32 devices in a mesh: groups: 2 (over y), wide: 16 (over z, x, core).
Axes of the slice: x: 2, y: 2, z: 4, core: 2. Of those that a mesh axis runs over, the one named last changes fastest.
Arguments:
- bfac: bfloat16 [32, 256, 4, 4096], P('wide', None, 'groups'), parts along dimension 2, may hold values from -2 to 2
- pair_mask: int32 [32, 3], P('wide'), may hold values 0 or 1
- dom_start: int32 [32, 3], P('wide'), may hold values from 0 to 16
Outputs:
- kband: float32 [64, 3, 256, 256], P(('groups', 'wide')), parts along dimension 0
- kmirror: float32 [64, 2, 256, 256], P(('groups', 'wide')), parts along dimension 0
The draws below stay inside these ranges and needn't reach their ends.
There are 2 independent parts, one for each index of `groups`. The reference program is written for one: setup_inputs(seed, part) draws one part's arguments, and reference() takes and returns one part's arrays. A program takes and returns all parts, laid end to end along the dimension named above; an argument that names none is the same for every part. Nothing has to cross between parts.
All inputs are finite; a program needn't handle non-finite values. No bound on the sum of `pair_mask` on one device may be relied on, other than what follows from the above.
Results may differ from the reference program's by a relative error of at most 0.0003.
Values may be sent and summed in bfloat16 or wider, within the bound.
No kernel may reach another device: no remote copies, remote signals or barrier semaphores. Data moves between devices by JAX's collectives and lax.ppermute only.
A program may use at most 128 MiB of HBM per device.

```python
import jax
import jax.numpy as jnp
from jax import lax

BS = 256
OCC = 2
NAUX = 4096
DOM = 2048
DSTEP = 128
REACH = 2
NBLK = 32


def with_ends(values, key, smallest, top_value):
    index_at = [jax.random.randint(jax.random.fold_in(key, axis), (), 0, length) for axis, length in enumerate(values.shape)]
    longest = values.shape.index(max(values.shape))
    neighbour = index_at[:longest] + [(index_at[longest] + 1) % values.shape[longest]] + index_at[longest + 1:]
    return values.at[tuple(index_at)].set(smallest).at[tuple(neighbour)].set(top_value)


def levels(rng, dims, split, smallest, largest):
    def one(axis_at, shards_of):
        heights = jax.random.uniform(jax.random.fold_in(jax.random.fold_in(rng, 6), axis_at), (shards_of,), jnp.float32, smallest / len(split), largest / len(split))
        return jnp.repeat(jnp.exp(heights), dims[axis_at] // shards_of).reshape((-1,) + (1,) * (len(dims) - axis_at - 1))

    factor_of = one(*split[0])
    for cut in split[1:]:
        factor_of = factor_of * one(*cut)
    return factor_of


def noise(own_key, extent, deviation, limit, split=(), kind=jnp.bfloat16):
    drawn = jax.random.normal(own_key, extent, jnp.float32) * deviation
    if len(split) > 0:
        drawn = levels(own_key, extent, split, -0.22, 0.18) * drawn
    return jnp.clip(drawn, min=-limit, max=limit).astype(kind)


def setup_inputs(seed: int = 0, part: int = 0) -> dict:
    key_of = jax.random.split(jax.random.key(seed), 4)
    part_keys = jax.random.split(jax.random.fold_in(key_of[3], part), 4)
    return {
        "bfac": noise(part_keys[0], (NBLK, BS, OCC, NAUX), 0.125, 2.0, ((0, 16),)),
        "pair_mask": with_ends((jax.random.randint(key_of[1], (NBLK, REACH + 1), 0, 3) < 2).astype(jnp.int32), jax.random.fold_in(key_of[1], 1), 0, 1),
        "dom_start": with_ends(jax.random.randint(key_of[2], (NBLK, REACH + 1), 0, (NAUX - DOM) // DSTEP + 1), jax.random.fold_in(key_of[2], 1), 0, ((NAUX - DOM) // DSTEP + 1) - 1).astype(jnp.int32),
    }


def pair_block(left, right, start):
    first = (start * DSTEP).astype(jnp.int32)
    part_left = lax.dynamic_slice_in_dim(left, first, DOM, 2)
    part_right = lax.dynamic_slice_in_dim(right, first, DOM, 2)
    return jnp.einsum("aip,bip->ab", part_left, part_right)


def reference(bfac, pair_mask, dom_start):
    padded = jnp.concatenate([bfac, jnp.zeros((REACH, BS, OCC, NAUX), jnp.bfloat16)], 0)

    def block_row(index):
        left = lax.dynamic_index_in_dim(bfac, index, 0, keepdims=False).astype(jnp.float32)
        mask_row = lax.dynamic_index_in_dim(pair_mask, index, 0, keepdims=False)
        start_row = lax.dynamic_index_in_dim(dom_start, index, 0, keepdims=False)
        blocks = []
        for offset in range(REACH + 1):
            right = lax.dynamic_index_in_dim(padded, index + offset, 0, keepdims=False).astype(jnp.float32)
            value = pair_block(left, right, start_row[offset])
            blocks.append(value * mask_row[offset].astype(jnp.float32))
        return jnp.stack(blocks)

    kband = lax.map(block_row, jnp.arange(NBLK, dtype=jnp.int32))
    lowered = []
    for offset in range(1, REACH + 1):
        moved = jnp.concatenate([jnp.zeros((offset, BS, BS), jnp.float32), kband[:NBLK - offset, offset]], 0)
        lowered.append(jnp.transpose(moved, (0, 2, 1)))
    kmirror = jnp.stack(lowered, axis=1)
    return kband, kmirror
```

```python
import jax
import jax.numpy as jnp
from jax import lax
from jax.sharding import PartitionSpec as P

DOM = 2048
DSTEP = 128
UNITS = DOM // DSTEP
LEVELS = (0, 1, 2, 3, 4, 6, 8)


def product(left, right):
    return jnp.einsum("aip,bip->ab", left, right, preferred_element_type=jnp.float32)


def window(blocks, which, unit, count):
    rows, orbitals = blocks.shape[1:3]
    return lax.dynamic_slice(
        blocks, (which, 0, 0, unit * DSTEP), (1, rows, orbitals, count * DSTEP)
    )[0]


def kept(values, unit, holds):
    units = unit + lax.iota(jnp.int32, values.shape[2] // DSTEP)
    flags = jnp.repeat(holds(units), DSTEP)
    return jnp.where(flags[None, None, :], values, jnp.zeros((), values.dtype))


def local_pairs(bfac, pair_mask, dom_start):
    keep = pair_mask.astype(jnp.float32)

    def pair(a, r):
        at = dom_start[a, r]
        return keep[a, r] * product(window(bfac, a, at, UNITS), window(bfac, a + r, at, UNITS))

    def swapped(a, r):
        at = dom_start[a, r]
        return keep[a, r] * product(window(bfac, a + r, at, UNITS), window(bfac, a, at, UNITS))

    return pair(0, 0), pair(0, 1), pair(1, 0), swapped(0, 1)


def per_device(bfac, pair_mask, dom_start):
    n = lax.axis_size("wide")
    me = lax.axis_index("wide")
    odd = me % 2 == 1
    total = bfac.shape[3] // DSTEP
    slow = [p for i in range(1, n - 1, 2) for p in ((i, i + 1), (i + 1, i))]
    fast = [p for i in range(0, n, 2) for p in ((i, i + 1), (i + 1, i))]

    screen = jnp.stack([pair_mask, dom_start])
    below = lax.ppermute(screen, "wide", [(i, i + 1) for i in range(n - 1)])

    def three(flags):
        return [(flags[0, 0, 2], flags[1, 0, 2]), (flags[0, 1, 1], flags[1, 1, 1]), (flags[0, 1, 2], flags[1, 1, 2])]

    exists = jnp.where(odd, me < n - 1, me > 0).astype(jnp.int32)
    (m1, s1), (m2, s2), (m3, s3) = three(jnp.where(odd, screen, below))
    w1 = jnp.where(m1 > 0, s1, s2)
    w3 = jnp.where(m3 > 0, s3, s2)
    near = odd.astype(jnp.int32)
    far = 1 - near
    send_at = jnp.where(odd, w3, w1)
    recv_at = jnp.where(odd, w1, w3)
    sent = window(bfac, near, send_at, UNITS)
    arrived = lax.ppermute(sent, "wide", slow)

    low, high = s2, s2 + UNITS
    for w in (w1, w3):
        low = jnp.where(w <= s2, jnp.maximum(low, w + UNITS), low)
        high = jnp.where(w > s2, jnp.minimum(high, w), high)
    rest = jnp.maximum(high - low, 0) * m2 * exists
    half = (rest + 1) // 2
    mid = low + half
    end = low + rest
    largest = lax.pmax(half, "wide")

    def extras(count):
        def run():
            if count == 0:
                return jnp.zeros((bfac.shape[1], bfac.shape[1]), jnp.float32), jnp.zeros(
                    (bfac.shape[1], bfac.shape[1]), jnp.float32
                )
            at_a = jnp.clip(low, 0, total - count)
            at_b = jnp.clip(mid, 0, total - count)
            got = lax.ppermute(window(bfac, near, jnp.where(odd, at_a, at_b), count), "wide", slow)
            at = jnp.where(odd, at_b, at_a)
            first, last = jnp.where(odd, mid, low), jnp.where(odd, end, mid)
            mine = kept(window(bfac, near, at, count), at, lambda u: (u >= first) & (u < last))
            return product(mine, got), product(got, mine)

        return run

    level = sum((largest > c).astype(jnp.int32) for c in LEVELS[:-1])
    near_near_extra, near_near_extra_t = lax.switch(level, [extras(c) for c in LEVELS])

    def assigned(u):
        inside = (u >= s2) & (u < s2 + UNITS)
        return inside & (odd | (u < w1) | (u >= w1 + UNITS))

    far_mine = window(bfac, far, recv_at, UNITS)
    near_mine = kept(window(bfac, near, recv_at, UNITS), recv_at, assigned)
    far_near_t = product(arrived, far_mine)
    near_far = lax.ppermute(far_near_t, "wide", slow)
    near_near_t = product(arrived, near_mine) + near_near_extra_t
    near_near_other = lax.ppermute(near_near_t, "wide", slow)
    far_near = product(far_mine, arrived)
    near_near = product(near_mine, arrived) + near_near_extra + near_near_other

    def flag(x):
        return (x * exists).astype(jnp.float32)

    slow_out = (
        far_near * flag(jnp.where(odd, m1, m3)),
        near_near * flag(m2),
        near_far * flag(jnp.where(odd, m3, m1)),
    )

    other = lax.ppermute(bfac, "wide", fast)
    (f1, t1), (f2, t2), (f3, t3) = three(jnp.where(odd, below, screen))
    fnear, ffar = far, near

    def fast_pair(mine, theirs, at, keep):
        value = product(window(bfac, mine, at, UNITS), window(other, theirs, at, UNITS))
        return value * keep.astype(jnp.float32)

    fast_out = (
        fast_pair(ffar, 1 - fnear, jnp.where(odd, t3, t1), jnp.where(odd, f3, f1)),
        fast_pair(fnear, 1 - fnear, t2, f2),
        fast_pair(fnear, fnear, jnp.where(odd, t1, t3), jnp.where(odd, f1, f3)),
    )

    k00, k01, k10, k01_t = local_pairs(bfac, pair_mask, dom_start)
    upper = [jnp.where(odd, s, f) for s, f in zip(slow_out, fast_out)]
    lower = [jnp.where(odd, f, s) for s, f in zip(slow_out, fast_out)]
    kband = jnp.stack([jnp.stack([k00, k01, upper[0]]), jnp.stack([k10, upper[1], upper[2]])])
    kmirror = jnp.stack([jnp.stack([lower[1], lower[2]]), jnp.stack([k01_t, lower[0]])])
    return kband, kmirror


def solution(mesh):
    placed = (P("wide", None, "groups", None), P("wide", None), P("wide", None))
    return jax.shard_map(
        per_device,
        mesh=mesh,
        in_specs=placed,
        out_specs=(
            P(("groups", "wide"), None, None, None),
            P(("groups", "wide"), None, None, None),
        ),
        check_vma=False,
    )
```

```python
import functools

import jax
import jax.numpy as jnp
from jax import lax
from jax.experimental import pallas as pl
from jax.experimental.pallas import tpu as pltpu
from jax.sharding import PartitionSpec as P

DOM = 2048
DSTEP = 128
UNITS = DOM // DSTEP
SPARE = UNITS // 2
LEVELS = (0, 1, 2, 3, 4, 6, 8)
PER = 12
VMEM = pl.BlockSpec(memory_space=pltpu.VMEM)
SMEM = pl.BlockSpec(memory_space=pltpu.SMEM)
HBM = pl.BlockSpec(memory_space=pl.ANY)


def flags(screen, device, block, r):
    at = device * PER + block * 3 + r
    return screen[at], screen[at + PER // 2]


def boundary(screen, device):
    m1, s1 = flags(screen, device, 0, 2)
    m2, s2 = flags(screen, device, 1, 1)
    m3, s3 = flags(screen, device, 1, 2)
    w1 = jnp.where(m1 > 0, s1, s2)
    w3 = jnp.where(m3 > 0, s3, s2)
    low, high = s2, s2 + UNITS
    for w in (w1, w3):
        low, high = (
            jnp.where(w <= s2, jnp.maximum(low, w + UNITS), low),
            jnp.where(w > s2, jnp.minimum(high, w), high),
        )
    rest = jnp.maximum(high - low, 0) * m2
    half = lax.shift_right_logical(rest + 1, 1)
    return dict(m1=m1, s1=s1, m2=m2, s2=s2, m3=m3, s3=s3, w1=w1, w3=w3, low=low, half=half, rest=rest)


def slow_plan(screen, n):
    me = lax.axis_index("wide")
    odd = lax.rem(me, 2)
    is_odd = odd == 1
    lower = jnp.where(is_odd, me, jnp.maximum(me - 1, 0))
    exists = jnp.where(is_odd, me < n - 1, me > 0).astype(jnp.int32)
    b = boundary(screen, lower)
    pick = lambda a, c: jnp.where(is_odd, a, c)
    mid = b["low"] + b["half"]
    other = b["rest"] - b["half"]
    recv_at = pick(b["w1"], b["w3"])
    first = jnp.maximum(b["s2"], recv_at)
    last = jnp.minimum(b["s2"] + UNITS, recv_at + UNITS)
    below_w1 = b["w1"] > first
    first_b = jnp.where(below_w1, first, jnp.maximum(first, b["w1"] + UNITS))
    last_b = jnp.where(below_w1, jnp.minimum(last, b["w1"]), last)
    return dict(
        is_odd=is_odd,
        near=odd,
        far=1 - odd,
        send_at=pick(b["w3"], b["w1"]),
        recv_at=recv_at,
        first=pick(first, first_b),
        last=pick(last, last_b),
        extra_send=pick(b["low"], mid),
        extra_recv=pick(mid, b["low"]),
        extra_count=pick(other, b["half"]) * exists,
        keep_far_near=pick(b["m1"], b["m3"]) * exists,
        keep_near_far=pick(b["m3"], b["m1"]) * exists,
        keep_near=b["m2"] * exists,
    )


def lanes(unit, count=1):
    return pl.ds(pl.multiple_of(unit * DSTEP, DSTEP), count * DSTEP)


def times(left, right):
    return lax.dot_general(left, right, (((1,), (1,)), ((), ())), preferred_element_type=jnp.float32)


def run(copies):
    for c in copies:
        c.start()
    for c in copies:
        c.wait()


def pack_kernel(n, screen, blocks, main, extra, level, sems):
    plan = slow_plan(screen, n)
    total = blocks.shape[3] // DSTEP
    near, at = plan["near"], plan["send_at"]
    copies = [
        pltpu.make_async_copy(blocks.at[near, :, :, lanes(at, UNITS)], main, sems.at[SPARE])
    ] + [
        pltpu.make_async_copy(
            blocks.at[near, :, :, lanes(jnp.minimum(plan["extra_send"] + u, total - 1))], extra.at[u], sems.at[u]
        )
        for u in range(SPARE)
    ]
    for c in copies:
        c.start()
    largest = lax.fori_loop(
        0,
        n // 2 - 1,
        lambda i, most: jnp.maximum(most, boundary(screen, 2 * i + 1)["half"]),
        jnp.int32(0),
    )
    level[0] = sum((largest > c).astype(jnp.int32) for c in LEVELS[:-1])
    for c in copies:
        c.wait()


def inner_kernel(n, screen, blocks, other, kband, kmirror, mine, theirs, out, sems):
    me = lax.axis_index("wide")
    is_odd = lax.rem(me, 2) == 1
    loads = [pltpu.make_async_copy(blocks.at[b], mine.at[b], sems.at[b]) for b in range(2)]
    loads += [pltpu.make_async_copy(other.at[b], theirs.at[b], sems.at[2 + b]) for b in range(2)]
    for c in loads:
        c.start()

    def product(left, a, right, b, at, keep):
        total = sum(times(left[a, i, :, lanes(at, UNITS)], right[b, i, :, lanes(at, UNITS)]) for i in range(2))
        return total * keep.astype(jnp.float32)

    stores = []

    def store(slot, value, ref, index):
        out[slot] = value
        c = pltpu.make_async_copy(out.at[slot], ref.at[index], sems.at[4 + slot])
        c.start()
        stores.append(c)

    loads[0].wait()
    loads[1].wait()
    k, s = flags(screen, me, 0, 0)
    store(0, product(mine, 0, mine, 0, s, k), kband, (0, 0))
    k, s = flags(screen, me, 0, 1)
    value = product(mine, 0, mine, 1, s, k)
    store(1, value, kband, (0, 1))
    store(2, value.T, kmirror, (1, 0))
    k, s = flags(screen, me, 1, 0)
    store(3, product(mine, 1, mine, 1, s, k), kband, (1, 0))

    loads[2].wait()
    loads[3].wait()
    lower = jnp.where(is_odd, me - 1, me)
    b = boundary(screen, lower)
    near = jnp.where(is_odd, 0, 1)
    pick = lambda x, y: jnp.where(is_odd, x, y)
    out[4] = product(mine, 1 - near, theirs, 1 - near, pick(b["s3"], b["s1"]), pick(b["m3"], b["m1"]))
    out[5] = product(mine, near, theirs, 1 - near, b["s2"], b["m2"])
    out[6] = product(mine, near, theirs, near, pick(b["s1"], b["s3"]), pick(b["m1"], b["m3"]))

    def put(targets):
        run([pltpu.make_async_copy(out.at[4 + j], ref, sems.at[8 + j]) for j, ref in enumerate(targets)])

    @pl.when(is_odd)
    def _():
        put([kmirror.at[1, 1], kmirror.at[0, 0], kmirror.at[0, 1]])

    @pl.when(jnp.logical_not(is_odd))
    def _():
        put([kband.at[0, 2], kband.at[1, 1], kband.at[1, 2]])

    for c in stores:
        c.wait()


def slow_kernel(
    n, screen, blocks, main, extra, kband_in, kmirror_in, kband, kmirror, partial, back,
    far, near, near_extra, got, got_extra, done, sems,
):
    plan = slow_plan(screen, n)
    total = blocks.shape[3] // DSTEP
    window = lanes(plan["recv_at"], UNITS)
    loads = [
        pltpu.make_async_copy(main, got, sems.at[0]),
        pltpu.make_async_copy(blocks.at[plan["far"], :, :, window], far, sems.at[1]),
        pltpu.make_async_copy(blocks.at[plan["near"], :, :, window], near, sems.at[2]),
        pltpu.make_async_copy(extra, got_extra, sems.at[3]),
    ] + [
        pltpu.make_async_copy(
            blocks.at[plan["near"], :, :, lanes(jnp.minimum(plan["extra_recv"] + u, total - 1))],
            near_extra.at[u],
            sems.at[4 + u],
        )
        for u in range(SPARE)
    ]
    for c in loads:
        c.start()
    loads[0].wait()
    loads[1].wait()
    value = times(far[0], got[0]) + times(far[1], got[1])
    back[0] = value.T
    done[...] = value * plan["keep_far_near"].astype(jnp.float32)

    @pl.when(plan["is_odd"])
    def _():
        pltpu.make_async_copy(done, kband.at[0, 2], sems.at[4 + SPARE]).start()

    @pl.when(jnp.logical_not(plan["is_odd"]))
    def _():
        pltpu.make_async_copy(done, kmirror.at[1, 1], sems.at[4 + SPARE]).start()

    for c in loads[2:]:
        c.wait()
    unit = plan["recv_at"] + lax.shift_right_logical(
        lax.broadcasted_iota(jnp.int32, (1, DOM), 1), DSTEP.bit_length() - 1
    )
    counts = jnp.where((unit >= plan["first"]) & (unit < plan["last"]), 1.0, 0.0).astype(jnp.bfloat16)
    partial[...] = times(near[0] * counts, got[0]) + times(near[1] * counts, got[1])

    def more(u, carry):
        partial[...] += times(near_extra[u, 0], got_extra[u, 0]) + times(near_extra[u, 1], got_extra[u, 1])
        return carry

    lax.fori_loop(0, plan["extra_count"], more, 0)
    back[1] = partial[...].T
    pltpu.make_async_copy(done, kband.at[0, 2], sems.at[4 + SPARE]).wait()


def last_kernel(n, screen, partial, back, kband_in, kmirror_in, kband, kmirror, out, sems):
    plan = slow_plan(screen, n)
    out[0] = (partial[...] + back[1]) * plan["keep_near"].astype(jnp.float32)
    out[1] = back[0] * plan["keep_near_far"].astype(jnp.float32)

    def put(targets):
        run([pltpu.make_async_copy(out.at[j], ref, sems.at[j]) for j, ref in enumerate(targets)])

    @pl.when(plan["is_odd"])
    def _():
        put([kband.at[1, 1], kband.at[1, 2]])

    @pl.when(jnp.logical_not(plan["is_odd"]))
    def _():
        put([kmirror.at[0, 0], kmirror.at[0, 1]])


def call(kernel, n, outs, ins, out_specs, scratch, flops, bytes_moved, aliases=None):
    return pl.pallas_call(
        functools.partial(kernel, n),
        out_shape=outs,
        in_specs=ins,
        out_specs=out_specs,
        scratch_shapes=scratch,
        input_output_aliases=aliases or {},
        compiler_params=pltpu.CompilerParams(vmem_limit_bytes=40 * 2**20),
        cost_estimate=pl.CostEstimate(flops=flops, bytes_accessed=bytes_moved, transcendentals=0),
        name=kernel.__name__,
    )


def per_device(bfac, pair_mask, dom_start):
    n = lax.axis_size("wide")
    _, rows, orbitals, fitting = bfac.shape
    slow = [p for i in range(1, n - 1, 2) for p in ((i, i + 1), (i + 1, i))]
    fast = [p for i in range(0, n, 2) for p in ((i, i + 1), (i + 1, i))]
    f32, bf16 = jnp.float32, bfac.dtype
    shape = jax.ShapeDtypeStruct
    dma = pltpu.SemaphoreType.DMA

    own = jnp.concatenate([pair_mask.reshape(-1), dom_start.reshape(-1)])
    screen = lax.all_gather(own, "wide", tiled=True)
    blocks = jnp.transpose(bfac, (0, 2, 1, 3))

    main, extra, level = call(
        pack_kernel,
        n,
        (
            shape((orbitals, rows, DOM), bf16),
            shape((SPARE, orbitals, rows, DSTEP), bf16),
            shape((1,), jnp.int32),
        ),
        [SMEM, HBM],
        (HBM, HBM, SMEM),
        [dma((SPARE + 1,))],
        0,
        6 * 2**20,
    )(screen, blocks)
    main_got = lax.ppermute(main, "wide", slow)
    other = lax.ppermute(lax.optimization_barrier((blocks, main))[0], "wide", fast)

    band = shape((2, 3, rows, rows), f32)
    mirror = shape((2, 2, rows, rows), f32)
    kband, kmirror = call(
        inner_kernel,
        n,
        (band, mirror),
        [SMEM, HBM, HBM],
        (HBM, HBM),
        [
            pltpu.VMEM((2, orbitals, rows, fitting), bf16),
            pltpu.VMEM((2, orbitals, rows, fitting), bf16),
            pltpu.VMEM((7, rows, rows), f32),
            dma((11,)),
        ],
        12 * rows * rows * orbitals * DOM,
        20 * 2**20,
    )(screen, blocks, other)

    extra, kband, kmirror = lax.optimization_barrier((extra, kband, kmirror))

    def extras(count):
        def branch(extra):
            if count == 0:
                return jnp.zeros_like(extra)
            got = lax.ppermute(extra[:count], "wide", slow)
            return lax.pad(got, jnp.zeros((), bf16), ((0, SPARE - count, 0),) + ((0, 0, 0),) * 3)

        return branch

    extra_got = lax.switch(level[0], [extras(c) for c in LEVELS], extra)

    kband, kmirror, partial, back = call(
        slow_kernel,
        n,
        (band, mirror, shape((rows, rows), f32), shape((2, rows, rows), f32)),
        [SMEM, HBM, HBM, HBM, HBM, HBM],
        (HBM, HBM, VMEM, VMEM),
        [
            pltpu.VMEM((orbitals, rows, DOM), bf16),
            pltpu.VMEM((orbitals, rows, DOM), bf16),
            pltpu.VMEM((SPARE, orbitals, rows, DSTEP), bf16),
            pltpu.VMEM((orbitals, rows, DOM), bf16),
            pltpu.VMEM((SPARE, orbitals, rows, DSTEP), bf16),
            pltpu.VMEM((rows, rows), f32),
            dma((5 + SPARE,)),
        ],
        4 * rows * rows * orbitals * DOM,
        8 * 2**20,
        {4: 0, 5: 1},
    )(screen, blocks, main_got, extra_got, kband, kmirror)
    back_got = lax.ppermute(back, "wide", slow)
    return call(
        last_kernel,
        n,
        (band, mirror),
        [SMEM, VMEM, VMEM, HBM, HBM],
        (HBM, HBM),
        [pltpu.VMEM((2, rows, rows), f32), dma((2,))],
        0,
        2**21,
        {3: 0, 4: 1},
    )(screen, partial, back_got, kband, kmirror)


def solution(mesh):
    placed = (P("wide", None, "groups", None), P("wide", None), P("wide", None))
    return jax.shard_map(
        per_device,
        mesh=mesh,
        in_specs=placed,
        out_specs=(
            P(("groups", "wide"), None, None, None),
            P(("groups", "wide"), None, None, None),
        ),
        check_vma=False,
    )
```

```python
import functools

import jax
import jax.numpy as jnp
from jax import lax
from jax.experimental import pallas as pl
from jax.experimental.pallas import tpu as pltpu
from jax.sharding import PartitionSpec as P

DOM = 2048
DSTEP = 128
UNITS = DOM // DSTEP
SPARE = UNITS // 2
LEVELS = (0, 1, 2, 3, 4, 6, 8)
PER = 12
VMEM = pl.BlockSpec(memory_space=pltpu.VMEM)
SMEM = pl.BlockSpec(memory_space=pltpu.SMEM)
HBM = pl.BlockSpec(memory_space=pltpu.HBM)


def flags(screen, device, block, r):
    at = block * 3 + r
    return screen[device, at], screen[device, at + PER // 2]


def boundary(screen, device):
    m1, s1 = flags(screen, device, 0, 2)
    m2, s2 = flags(screen, device, 1, 1)
    m3, s3 = flags(screen, device, 1, 2)
    w1 = jnp.where(m1 > 0, s1, s2)
    w3 = jnp.where(m3 > 0, s3, s2)
    low, high = s2, s2 + UNITS
    for w in (w1, w3):
        low, high = (
            jnp.where(w <= s2, jnp.maximum(low, w + UNITS), low),
            jnp.where(w > s2, jnp.minimum(high, w), high),
        )
    rest = jnp.maximum(high - low, 0) * m2
    half = lax.shift_right_logical(rest + 1, 1)
    return dict(m1=m1, s1=s1, m2=m2, s2=s2, m3=m3, s3=s3, w1=w1, w3=w3, low=low, half=half, rest=rest)


def slow_plan(screen, n):
    me = lax.axis_index("wide")
    odd = lax.rem(me, 2)
    is_odd = odd == 1
    lower = jnp.where(is_odd, me, jnp.maximum(me - 1, 0))
    exists = jnp.where(is_odd, me < n - 1, me > 0).astype(jnp.int32)
    b = boundary(screen, lower)
    pick = lambda a, c: jnp.where(is_odd, a, c)
    mid = b["low"] + b["half"]
    other = b["rest"] - b["half"]
    recv_at = pick(b["w1"], b["w3"])
    first = jnp.maximum(b["s2"], recv_at)
    last = jnp.minimum(b["s2"] + UNITS, recv_at + UNITS)
    below_w1 = b["w1"] > first
    first_b = jnp.where(below_w1, first, jnp.maximum(first, b["w1"] + UNITS))
    last_b = jnp.where(below_w1, jnp.minimum(last, b["w1"]), last)
    return dict(
        is_odd=is_odd,
        near=odd,
        far=1 - odd,
        send_at=pick(b["w3"], b["w1"]),
        recv_at=recv_at,
        first=pick(first, first_b),
        last=pick(last, last_b),
        extra_send=pick(b["low"], mid),
        extra_recv=pick(mid, b["low"]),
        extra_count=pick(other, b["half"]) * exists,
        keep_far_near=pick(b["m1"], b["m3"]) * exists,
        keep_near_far=pick(b["m3"], b["m1"]) * exists,
        keep_near=b["m2"] * exists,
    )


def lanes(unit, count=1):
    return pl.ds(pl.multiple_of(unit * DSTEP, DSTEP), count * DSTEP)


def times(left, right):
    return lax.dot_general(left, right, (((1,), (1,)), ((), ())), preferred_element_type=jnp.float32)


def run(copies):
    for c in copies:
        c.start()
    for c in copies:
        c.wait()


def screen_kernel(n, pair_mask, dom_start, out):
    me = lax.axis_index("wide")
    row = lax.broadcasted_iota(jnp.int32, out.shape, 0)
    column = lax.broadcasted_iota(jnp.int32, out.shape, 1)
    value = jnp.zeros(out.shape, jnp.int32)
    for at in range(PER):
        source = pair_mask if at < PER // 2 else dom_start
        block, r = divmod(at % (PER // 2), 3)
        value = jnp.where(column == at, source[block, r], value)
    out[...] = jnp.where(row == me, value, 0)


def pack_kernel(n, screen, bfac, main, extra, level, sems):
    plan = slow_plan(screen, n)
    total = bfac.shape[3] // DSTEP
    near, at = plan["near"], plan["send_at"]
    rows = bfac.shape[1] // 4
    copies = [
        pltpu.make_async_copy(
            bfac.at[near, pl.ds(q * rows, rows), :, lanes(at, UNITS)], main.at[pl.ds(q * rows, rows)], sems.at[SPARE + q]
        )
        for q in range(4)
    ] + [
        pltpu.make_async_copy(
            bfac.at[near, :, :, lanes(jnp.minimum(plan["extra_send"] + u, total - 1))], extra.at[u], sems.at[u]
        )
        for u in range(SPARE)
    ]
    for c in copies:
        c.start()
    largest = lax.fori_loop(
        0,
        n // 2 - 1,
        lambda i, most: jnp.maximum(most, boundary(screen, 2 * i + 1)["half"]),
        jnp.int32(0),
    )
    level[0] = sum((largest > c).astype(jnp.int32) for c in LEVELS[:-1])
    for c in copies:
        c.wait()


def inner_kernel(
    n, screen, blocks, other, kband, kmirror, far, near, near_extra, mine, theirs, out, sems
):
    me = lax.axis_index("wide")
    is_odd = lax.rem(me, 2) == 1
    loads = [pltpu.make_async_copy(blocks.at[b], mine.at[b], sems.at[b]) for b in range(2)]
    loads += [pltpu.make_async_copy(other.at[b], theirs.at[b], sems.at[2 + b]) for b in range(2)]
    for c in loads:
        c.start()

    def product(left, a, right, b, at, keep):
        total = sum(times(left[a, i, :, lanes(at, UNITS)], right[b, i, :, lanes(at, UNITS)]) for i in range(2))
        return total * keep.astype(jnp.float32)

    stores = []

    def store(slot, value, ref, index):
        out[slot] = value
        c = pltpu.make_async_copy(out.at[slot], ref.at[index], sems.at[4 + slot])
        c.start()
        stores.append(c)

    loads[0].wait()
    loads[1].wait()
    k, s = flags(screen, me, 0, 0)
    store(0, product(mine, 0, mine, 0, s, k), kband, (0, 0))
    k, s = flags(screen, me, 0, 1)
    value = product(mine, 0, mine, 1, s, k)
    store(1, value, kband, (0, 1))
    store(2, value.T, kmirror, (1, 0))
    k, s = flags(screen, me, 1, 0)
    store(3, product(mine, 1, mine, 1, s, k), kband, (1, 0))

    plan = slow_plan(screen, n)
    total = blocks.shape[3] // DSTEP
    window = lanes(plan["recv_at"], UNITS)
    unit = plan["recv_at"] + lax.shift_right_logical(
        lax.broadcasted_iota(jnp.int32, (1, DOM), 1), DSTEP.bit_length() - 1
    )
    counts = jnp.where((unit >= plan["first"]) & (unit < plan["last"]), 1.0, 0.0).astype(near.dtype)
    for i in range(2):
        far[i] = mine[plan["far"], i, :, window]
        near[i] = mine[plan["near"], i, :, window] * counts
        for u in range(SPARE):
            near_extra[u, i] = mine[plan["near"], i, :, lanes(jnp.minimum(plan["extra_recv"] + u, total - 1))]

    loads[2].wait()
    loads[3].wait()
    lower = jnp.where(is_odd, me - 1, me)
    b = boundary(screen, lower)
    close = jnp.where(is_odd, 0, 1)
    pick = lambda x, y: jnp.where(is_odd, x, y)
    out[4] = product(mine, 1 - close, theirs, 1 - close, pick(b["s3"], b["s1"]), pick(b["m3"], b["m1"]))
    out[5] = product(mine, close, theirs, 1 - close, b["s2"], b["m2"])
    out[6] = product(mine, close, theirs, close, pick(b["s1"], b["s3"]), pick(b["m1"], b["m3"]))

    def put(targets):
        run([pltpu.make_async_copy(out.at[4 + j], ref, sems.at[8 + j]) for j, ref in enumerate(targets)])

    @pl.when(is_odd)
    def _():
        put([kmirror.at[1, 1], kmirror.at[0, 0], kmirror.at[0, 1]])

    @pl.when(jnp.logical_not(is_odd))
    def _():
        put([kband.at[0, 2], kband.at[1, 1], kband.at[1, 2]])

    for c in stores:
        c.wait()


def extra_kernel(n, screen, near_extra, got, out):
    out[...] = jnp.zeros(out.shape, out.dtype)

    def more(u, carry):
        out[...] += times(near_extra[u, 0], got[u, 0]) + times(near_extra[u, 1], got[u, 1])
        return carry

    lax.fori_loop(0, slow_plan(screen, n)["extra_count"], more, 0)


def slow_kernel(n, got, far, near, extra, far_near, partial, back):
    value = times(far[0], got[0]) + times(far[1], got[1])
    far_near[...] = value
    back[0] = value.T
    value = extra[...] + times(near[0], got[0]) + times(near[1], got[1])
    partial[...] = value
    back[1] = value.T


def last_kernel(n, screen, far_near, partial, back, kband_in, kmirror_in, kband, kmirror, out, sems):
    plan = slow_plan(screen, n)
    out[0] = (partial[...] + back[1]) * plan["keep_near"].astype(jnp.float32)
    out[1] = back[0] * plan["keep_near_far"].astype(jnp.float32)
    out[2] = far_near[...] * plan["keep_far_near"].astype(jnp.float32)

    def put(targets):
        run([pltpu.make_async_copy(out.at[j], ref, sems.at[j]) for j, ref in enumerate(targets)])

    @pl.when(plan["is_odd"])
    def _():
        put([kband.at[1, 1], kband.at[1, 2], kband.at[0, 2]])

    @pl.when(jnp.logical_not(plan["is_odd"]))
    def _():
        put([kmirror.at[0, 0], kmirror.at[0, 1], kmirror.at[1, 1]])


def call(kernel, n, outs, ins, out_specs, scratch, flops, bytes_moved, aliases=None, vmem=40):
    return pl.pallas_call(
        functools.partial(kernel, n),
        out_shape=outs,
        in_specs=ins,
        out_specs=out_specs,
        scratch_shapes=scratch,
        input_output_aliases=aliases or {},
        compiler_params=pltpu.CompilerParams(vmem_limit_bytes=vmem * 2**20),
        cost_estimate=pl.CostEstimate(flops=flops, bytes_accessed=bytes_moved, transcendentals=0),
        name=kernel.__name__,
    )


def per_device(bfac, pair_mask, dom_start):
    n = lax.axis_size("wide")
    _, rows, orbitals, fitting = bfac.shape
    slow = [p for i in range(1, n - 1, 2) for p in ((i, i + 1), (i + 1, i))]
    fast = [p for i in range(0, n, 2) for p in ((i, i + 1), (i + 1, i))]
    f32, bf16 = jnp.float32, bfac.dtype
    shape = jax.ShapeDtypeStruct
    dma = pltpu.SemaphoreType.DMA

    own = call(screen_kernel, n, shape((n, 128), jnp.int32), [SMEM, SMEM], VMEM, [], 0, 2**14)(pair_mask, dom_start)
    screen = lax.psum(own, "wide")

    main, extra, level = call(
        pack_kernel,
        n,
        (
            shape((rows, orbitals, DOM), bf16),
            shape((SPARE, rows, orbitals, DSTEP), bf16),
            shape((1,), jnp.int32),
        ),
        [SMEM, HBM],
        (HBM, HBM, SMEM),
        [dma((SPARE + 4,))],
        0,
        6 * 2**20,
        vmem=63,
    )(screen, bfac)
    main = jnp.transpose(main, (1, 0, 2))
    main_got = lax.ppermute(main, "wide", slow)

    band = shape((2, 3, rows, rows), f32)
    mirror = shape((2, 2, rows, rows), f32)
    square = shape((rows, rows), f32)
    window = shape((orbitals, rows, DOM), bf16)
    inner_outs = (band, mirror, window, window, shape((SPARE, orbitals, rows, DSTEP), bf16))

    def inner(screen, bfac):
        blocks = jnp.transpose(bfac, (0, 2, 1, 3))
        other = lax.ppermute(blocks, "wide", fast)
        return call(
            inner_kernel,
            n,
            inner_outs,
            [SMEM, HBM, HBM],
            (HBM, HBM, VMEM, VMEM, VMEM),
            [
                pltpu.VMEM((2, orbitals, rows, fitting), bf16),
                pltpu.VMEM((2, orbitals, rows, fitting), bf16),
                pltpu.VMEM((7, rows, rows), f32),
                dma((11,)),
            ],
            12 * rows * rows * orbitals * DOM,
            25 * 2**20,
            vmem=52,
        )(screen, blocks, other)

    def unused(screen, bfac):
        return tuple(jnp.zeros(o.shape, o.dtype) for o in inner_outs)

    kband, kmirror, far, near, near_extra = lax.cond(level[0] >= 0, inner, unused, screen, bfac)
    extra = jnp.transpose(extra, (0, 2, 1, 3))

    def extras(count):
        def branch(screen, extra, near_extra):
            if count == 0:
                return jnp.zeros((rows, rows), f32)
            got = lax.ppermute(extra[:count], "wide", slow)
            return call(extra_kernel, n, square, [SMEM, VMEM, VMEM], VMEM, [], 2**26 * count, 2**19 * count)(
                screen, near_extra, got
            )

        return branch

    more = lax.switch(level[0], [extras(c) for c in LEVELS], screen, extra, near_extra)

    far_near, partial, back = call(
        slow_kernel,
        n,
        (square, square, shape((2, rows, rows), f32)),
        [VMEM] * 4,
        (VMEM, VMEM, VMEM),
        [],
        4 * rows * rows * orbitals * DOM,
        8 * 2**20,
    )(main_got, far, near, more)
    back_got = lax.ppermute(back, "wide", slow)
    return call(
        last_kernel,
        n,
        (band, mirror),
        [SMEM, VMEM, VMEM, VMEM, HBM, HBM],
        (HBM, HBM),
        [pltpu.VMEM((3, rows, rows), f32), dma((3,))],
        0,
        2**21,
        {4: 0, 5: 1},
    )(screen, far_near, partial, back_got, kband, kmirror)


def solution(mesh):
    placed = (P("wide", None, "groups", None), P("wide", None), P("wide", None))
    return jax.shard_map(
        per_device,
        mesh=mesh,
        in_specs=placed,
        out_specs=(
            P(("groups", "wide"), None, None, None),
            P(("groups", "wide"), None, None, None),
        ),
        check_vma=False,
    )
```

```python
import functools

import jax
import jax.numpy as jnp
from jax import lax
from jax.experimental import pallas as pl
from jax.experimental.pallas import tpu as pltpu
from jax.sharding import PartitionSpec as P

DOM = 2048
DSTEP = 128
UNITS = DOM // DSTEP
SPARE = UNITS // 2
LEVELS = (0, 1, 2, 3, 4, 6, 8)
PER = 12
VMEM = pl.BlockSpec(memory_space=pltpu.VMEM)
SMEM = pl.BlockSpec(memory_space=pltpu.SMEM)
HBM = pl.BlockSpec(memory_space=pltpu.HBM)


def flags(screen, device, block, r):
    at = block * 3 + r
    return screen[device, at], screen[device, at + PER // 2]


def boundary(screen, device):
    m1, s1 = flags(screen, device, 0, 2)
    m2, s2 = flags(screen, device, 1, 1)
    m3, s3 = flags(screen, device, 1, 2)
    w1 = jnp.where(m1 > 0, s1, s2)
    w3 = jnp.where(m3 > 0, s3, s2)
    low, high = s2, s2 + UNITS
    for w in (w1, w3):
        low, high = (
            jnp.where(w <= s2, jnp.maximum(low, w + UNITS), low),
            jnp.where(w > s2, jnp.minimum(high, w), high),
        )
    rest = jnp.maximum(high - low, 0) * m2
    half = lax.shift_right_logical(rest + 1, 1)
    return dict(m1=m1, s1=s1, m2=m2, s2=s2, m3=m3, s3=s3, w1=w1, w3=w3, low=low, half=half, rest=rest)


def slow_plan(screen, n):
    me = lax.axis_index("wide")
    odd = lax.rem(me, 2)
    is_odd = odd == 1
    lower = jnp.where(is_odd, me, jnp.maximum(me - 1, 0))
    exists = jnp.where(is_odd, me < n - 1, me > 0).astype(jnp.int32)
    b = boundary(screen, lower)
    pick = lambda a, c: jnp.where(is_odd, a, c)
    mid = b["low"] + b["half"]
    other = b["rest"] - b["half"]
    recv_at = pick(b["w1"], b["w3"])
    first = jnp.maximum(b["s2"], recv_at)
    last = jnp.minimum(b["s2"] + UNITS, recv_at + UNITS)
    below_w1 = b["w1"] > first
    first_b = jnp.where(below_w1, first, jnp.maximum(first, b["w1"] + UNITS))
    last_b = jnp.where(below_w1, jnp.minimum(last, b["w1"]), last)
    return dict(
        is_odd=is_odd,
        near=odd,
        far=1 - odd,
        send_at=pick(b["w3"], b["w1"]),
        recv_at=recv_at,
        first=pick(first, first_b),
        last=pick(last, last_b),
        extra_send=pick(b["low"], mid),
        extra_recv=pick(mid, b["low"]),
        extra_count=pick(other, b["half"]) * exists,
        keep_far_near=pick(b["m1"], b["m3"]) * exists,
        keep_near_far=pick(b["m3"], b["m1"]) * exists,
        keep_near=b["m2"] * exists,
    )


def lanes(unit, count=1):
    return pl.ds(pl.multiple_of(unit * DSTEP, DSTEP), count * DSTEP)


def times(left, right):
    return lax.dot_general(left, right, (((1,), (1,)), ((), ())), preferred_element_type=jnp.float32)


def run(copies):
    for c in copies:
        c.start()
    for c in copies:
        c.wait()


def screen_kernel(n, pair_mask, dom_start, out):
    me = lax.axis_index("wide")
    row = lax.broadcasted_iota(jnp.int32, out.shape, 0)
    column = lax.broadcasted_iota(jnp.int32, out.shape, 1)
    value = jnp.zeros(out.shape, jnp.int32)
    for at in range(PER):
        source = pair_mask if at < PER // 2 else dom_start
        block, r = divmod(at % (PER // 2), 3)
        value = jnp.where(column == at, source[block, r], value)
    out[...] = jnp.where(row == me, value, 0)


def swapped(values):
    return jnp.swapaxes(values, 0, 1)


def pack_kernel(n, screen, bfac, main, extra, level, raw, sems):
    plan = slow_plan(screen, n)
    total = bfac.shape[3] // DSTEP
    near, at = plan["near"], plan["send_at"]
    parts = sems.shape[0]
    step = bfac.shape[1] // parts
    loads = [
        pltpu.make_async_copy(bfac.at[near, pl.ds(q * step, step)], raw.at[pl.ds(q * step, step)], sems.at[q])
        for q in range(parts)
    ]
    for c in loads:
        c.start()
    largest = lax.fori_loop(
        0,
        n // 2 - 1,
        lambda i, most: jnp.maximum(most, boundary(screen, 2 * i + 1)["half"]),
        jnp.int32(0),
    )
    level[0] = sum((largest > c).astype(jnp.int32) for c in LEVELS[:-1])
    for q in range(parts):
        loads[q].wait()
        rows = pl.ds(q * step, step)
        main[:, rows, :] = swapped(raw[rows, :, lanes(at, UNITS)])

    def one(u, carry):
        unit = jnp.minimum(plan["extra_send"] + u, total - 1)
        extra[u] = swapped(raw[:, :, lanes(unit)])
        return carry

    lax.fori_loop(0, SPARE, one, 0)


def inner_kernel(
    n, screen, bfac, other, kband, kmirror, far, near, near_extra, mine, theirs, raw, out, sems
):
    me = lax.axis_index("wide")
    is_odd = lax.rem(me, 2) == 1
    total = bfac.shape[3] // DSTEP
    sources = [(bfac, 0, mine), (bfac, 1, mine), (other, 0, theirs), (other, 1, theirs)]
    loads = [
        pltpu.make_async_copy(source.at[b], raw.at[k % 2], sems.at[k]) for k, (source, b, _) in enumerate(sources)
    ]
    step = 32

    def relayout(k):
        _, b, target = sources[k]
        loads[k].wait()

        def some(q, carry):
            rows = pl.ds(pl.multiple_of(q * step, step), step)
            target[b, :, rows, :] = swapped(raw[k % 2, rows])
            return carry

        lax.fori_loop(0, bfac.shape[1] // step, some, 0)
        if k + 2 < len(loads):
            loads[k + 2].start()

    loads[0].start()
    loads[1].start()

    def product(left, a, right, b, at, keep):
        value = sum(times(left[a, i, :, lanes(at, UNITS)], right[b, i, :, lanes(at, UNITS)]) for i in range(2))
        return value * keep.astype(jnp.float32)

    stores = []

    def store(slot, value, ref, index):
        out[slot] = value
        c = pltpu.make_async_copy(out.at[slot], ref.at[index], sems.at[4 + slot])
        c.start()
        stores.append(c)

    relayout(0)
    relayout(1)
    k, s = flags(screen, me, 0, 0)
    store(0, product(mine, 0, mine, 0, s, k), kband, (0, 0))
    k, s = flags(screen, me, 0, 1)
    value = product(mine, 0, mine, 1, s, k)
    store(1, value, kband, (0, 1))
    store(2, value.T, kmirror, (1, 0))
    k, s = flags(screen, me, 1, 0)
    store(3, product(mine, 1, mine, 1, s, k), kband, (1, 0))

    plan = slow_plan(screen, n)
    window = lanes(plan["recv_at"], UNITS)
    unit = plan["recv_at"] + lax.shift_right_logical(
        lax.broadcasted_iota(jnp.int32, (1, DOM), 1), DSTEP.bit_length() - 1
    )
    counts = jnp.where((unit >= plan["first"]) & (unit < plan["last"]), 1.0, 0.0).astype(near.dtype)
    for i in range(2):
        far[i] = mine[plan["far"], i, :, window]
        near[i] = mine[plan["near"], i, :, window] * counts
        for u in range(SPARE):
            near_extra[u, i] = mine[plan["near"], i, :, lanes(jnp.minimum(plan["extra_recv"] + u, total - 1))]

    relayout(2)
    relayout(3)
    lower = jnp.where(is_odd, me - 1, me)
    b = boundary(screen, lower)
    close = jnp.where(is_odd, 0, 1)
    pick = lambda x, y: jnp.where(is_odd, x, y)
    out[4] = product(mine, 1 - close, theirs, 1 - close, pick(b["s3"], b["s1"]), pick(b["m3"], b["m1"]))
    out[5] = product(mine, close, theirs, 1 - close, b["s2"], b["m2"])
    out[6] = product(mine, close, theirs, close, pick(b["s1"], b["s3"]), pick(b["m1"], b["m3"]))

    def put(targets):
        run([pltpu.make_async_copy(out.at[4 + j], ref, sems.at[8 + j]) for j, ref in enumerate(targets)])

    @pl.when(is_odd)
    def _():
        put([kmirror.at[1, 1], kmirror.at[0, 0], kmirror.at[0, 1]])

    @pl.when(jnp.logical_not(is_odd))
    def _():
        put([kband.at[0, 2], kband.at[1, 1], kband.at[1, 2]])

    for c in stores:
        c.wait()


def extra_kernel(n, screen, near_extra, got, out):
    out[...] = jnp.zeros(out.shape, out.dtype)

    def more(u, carry):
        out[...] += times(near_extra[u, 0], got[u, 0]) + times(near_extra[u, 1], got[u, 1])
        return carry

    lax.fori_loop(0, slow_plan(screen, n)["extra_count"], more, 0)


def slow_kernel(n, got, far, near, extra, far_near, partial, back):
    value = times(far[0], got[0]) + times(far[1], got[1])
    far_near[...] = value
    back[0] = value.T
    value = extra[...] + times(near[0], got[0]) + times(near[1], got[1])
    partial[...] = value
    back[1] = value.T


def last_kernel(n, screen, far_near, partial, back, kband_in, kmirror_in, kband, kmirror, out, sems):
    plan = slow_plan(screen, n)
    out[0] = (partial[...] + back[1]) * plan["keep_near"].astype(jnp.float32)
    out[1] = back[0] * plan["keep_near_far"].astype(jnp.float32)
    out[2] = far_near[...] * plan["keep_far_near"].astype(jnp.float32)

    def put(targets):
        run([pltpu.make_async_copy(out.at[j], ref, sems.at[j]) for j, ref in enumerate(targets)])

    @pl.when(plan["is_odd"])
    def _():
        put([kband.at[1, 1], kband.at[1, 2], kband.at[0, 2]])

    @pl.when(jnp.logical_not(plan["is_odd"]))
    def _():
        put([kmirror.at[0, 0], kmirror.at[0, 1], kmirror.at[1, 1]])


def call(kernel, n, outs, ins, out_specs, scratch, flops, bytes_moved, aliases=None, vmem=40):
    return pl.pallas_call(
        functools.partial(kernel, n),
        out_shape=outs,
        in_specs=ins,
        out_specs=out_specs,
        scratch_shapes=scratch,
        input_output_aliases=aliases or {},
        compiler_params=pltpu.CompilerParams(vmem_limit_bytes=vmem * 2**20),
        cost_estimate=pl.CostEstimate(flops=flops, bytes_accessed=bytes_moved, transcendentals=0),
        name=kernel.__name__,
    )


def per_device(bfac, pair_mask, dom_start):
    n = lax.axis_size("wide")
    _, rows, orbitals, fitting = bfac.shape
    slow = [p for i in range(1, n - 1, 2) for p in ((i, i + 1), (i + 1, i))]
    fast = [p for i in range(0, n, 2) for p in ((i, i + 1), (i + 1, i))]
    f32, bf16 = jnp.float32, bfac.dtype
    shape = jax.ShapeDtypeStruct
    dma = pltpu.SemaphoreType.DMA

    own = call(screen_kernel, n, shape((n, 128), jnp.int32), [SMEM, SMEM], VMEM, [], 0, 2**14)(pair_mask, dom_start)
    screen = lax.psum(own, "wide")

    window = shape((orbitals, rows, DOM), bf16)
    spare = shape((SPARE, orbitals, rows, DSTEP), bf16)
    main, extra, level = call(
        pack_kernel,
        n,
        (window, spare, shape((1,), jnp.int32)),
        [SMEM, HBM],
        (VMEM, VMEM, SMEM),
        [pltpu.VMEM((rows, orbitals, fitting), bf16), dma((4,))],
        0,
        6 * 2**20,
        vmem=60,
    )(screen, bfac)
    main_got = lax.ppermute(main, "wide", slow)

    band = shape((2, 3, rows, rows), f32)
    mirror = shape((2, 2, rows, rows), f32)
    square = shape((rows, rows), f32)
    inner_outs = (band, mirror, window, window, spare)

    def inner(screen, bfac):
        other = lax.ppermute(bfac, "wide", fast)
        return call(
            inner_kernel,
            n,
            inner_outs,
            [SMEM, HBM, HBM],
            (HBM, HBM, VMEM, VMEM, VMEM),
            [
                pltpu.VMEM((2, orbitals, rows, fitting), bf16),
                pltpu.VMEM((2, orbitals, rows, fitting), bf16),
                pltpu.VMEM((2, rows, orbitals, fitting), bf16),
                pltpu.VMEM((7, rows, rows), f32),
                dma((11,)),
            ],
            12 * rows * rows * orbitals * DOM,
            25 * 2**20,
            vmem=52,
        )(screen, bfac, other)

    def unused(screen, bfac):
        return tuple(jnp.zeros(o.shape, o.dtype) for o in inner_outs)

    kband, kmirror, far, near, near_extra = lax.cond(level[0] >= 0, inner, unused, screen, bfac)
    def extras(count):
        def branch(screen, extra, near_extra):
            if count == 0:
                return jnp.zeros((rows, rows), f32)
            got = lax.ppermute(extra[:count], "wide", slow)
            return call(extra_kernel, n, square, [SMEM, VMEM, VMEM], VMEM, [], 2**26 * count, 2**19 * count)(
                screen, near_extra, got
            )

        return branch

    more = lax.switch(level[0], [extras(c) for c in LEVELS], screen, extra, near_extra)

    far_near, partial, back = call(
        slow_kernel,
        n,
        (square, square, shape((2, rows, rows), f32)),
        [VMEM] * 4,
        (VMEM, VMEM, VMEM),
        [],
        4 * rows * rows * orbitals * DOM,
        8 * 2**20,
    )(main_got, far, near, more)
    back_got = lax.ppermute(back, "wide", slow)
    return call(
        last_kernel,
        n,
        (band, mirror),
        [SMEM, VMEM, VMEM, VMEM, HBM, HBM],
        (HBM, HBM),
        [pltpu.VMEM((3, rows, rows), f32), dma((3,))],
        0,
        2**21,
        {4: 0, 5: 1},
    )(screen, far_near, partial, back_got, kband, kmirror)


def solution(mesh):
    placed = (P("wide", None, "groups", None), P("wide", None), P("wide", None))
    return jax.shard_map(
        per_device,
        mesh=mesh,
        in_specs=placed,
        out_specs=(
            P(("groups", "wide"), None, None, None),
            P(("groups", "wide"), None, None, None),
        ),
        check_vma=False,
    )
```

```python
import functools

import jax
import jax.numpy as jnp
from jax import lax
from jax.experimental import pallas as pl
from jax.experimental.pallas import tpu as pltpu
from jax.sharding import PartitionSpec as P

DOM = 2048
DSTEP = 128
UNITS = DOM // DSTEP
SPARE = UNITS // 2
LEVELS = (0, 1, 2, 3, 4, 6, 8)
PER = 12
VMEM = pl.BlockSpec(memory_space=pltpu.VMEM)
SMEM = pl.BlockSpec(memory_space=pltpu.SMEM)
HBM = pl.BlockSpec(memory_space=pltpu.HBM)


def flags(screen, block, r, row=0):
    at = block * 3 + r
    return screen[row, at], screen[row, at + PER // 2]


def choose(is_first, first, second):
    return tuple(jnp.where(is_first, a, b) for a, b in zip(first, second))


def boundary(get):
    m1, s1 = get(0, 2)
    m2, s2 = get(1, 1)
    m3, s3 = get(1, 2)
    w1 = jnp.where(m1 > 0, s1, s2)
    w3 = jnp.where(m3 > 0, s3, s2)
    low, high = s2, s2 + UNITS
    for w in (w1, w3):
        low, high = (
            jnp.where(w <= s2, jnp.maximum(low, w + UNITS), low),
            jnp.where(w > s2, jnp.minimum(high, w), high),
        )
    rest = jnp.maximum(high - low, 0) * m2
    half = lax.shift_right_logical(rest + 1, 1)
    return dict(m1=m1, s1=s1, m2=m2, s2=s2, m3=m3, s3=s3, w1=w1, w3=w3, low=low, half=half, rest=rest)


def slow_plan(own, below, n):
    me = lax.axis_index("wide")
    odd = lax.rem(me, 2)
    is_odd = odd == 1
    exists = jnp.where(is_odd, me < n - 1, me > 0).astype(jnp.int32)
    b = boundary(lambda block, r: choose(is_odd, flags(own, block, r), flags(below, block, r)))
    pick = lambda a, c: jnp.where(is_odd, a, c)
    mid = b["low"] + b["half"]
    other = b["rest"] - b["half"]
    recv_at = pick(b["w1"], b["w3"])
    first = jnp.maximum(b["s2"], recv_at)
    last = jnp.minimum(b["s2"] + UNITS, recv_at + UNITS)
    below_w1 = b["w1"] > first
    first_b = jnp.where(below_w1, first, jnp.maximum(first, b["w1"] + UNITS))
    last_b = jnp.where(below_w1, jnp.minimum(last, b["w1"]), last)
    return dict(
        is_odd=is_odd,
        near=odd,
        far=1 - odd,
        send_at=pick(b["w3"], b["w1"]),
        recv_at=recv_at,
        first=pick(first, first_b),
        last=pick(last, last_b),
        extra_send=pick(b["low"], mid),
        extra_recv=pick(mid, b["low"]),
        extra_count=pick(other, b["half"]) * exists,
        keep_far_near=pick(b["m1"], b["m3"]) * exists,
        keep_near_far=pick(b["m3"], b["m1"]) * exists,
        keep_near=b["m2"] * exists,
    )


def lanes(unit, count=1):
    return pl.ds(pl.multiple_of(unit * DSTEP, DSTEP), count * DSTEP)


def times(left, right):
    return lax.dot_general(left, right, (((1,), (1,)), ((), ())), preferred_element_type=jnp.float32)


def run(copies):
    for c in copies:
        c.start()
    for c in copies:
        c.wait()


def screen_kernel(n, pair_mask, dom_start, out, again, sem):
    column = lax.broadcasted_iota(jnp.int32, out.shape, 1)
    value = jnp.zeros(out.shape, jnp.int32)
    for at in range(PER):
        source = pair_mask if at < PER // 2 else dom_start
        block, r = divmod(at % (PER // 2), 3)
        value = jnp.where(column == at, source[block, r], value)
    out[...] = value
    run([pltpu.make_async_copy(out, again, sem)])


def level_kernel(n, screens, level):
    def one(i, most):
        row = (2 * i + 1) * 8
        return jnp.maximum(most, boundary(lambda block, r: flags(screens, block, r, row))["half"])

    largest = lax.fori_loop(0, n // 2 - 1, one, jnp.int32(0))
    level[0] = sum((largest > c).astype(jnp.int32) for c in LEVELS[:-1])


def swapped(values):
    return jnp.swapaxes(values, 0, 1)


def pack_kernel(n, own, below, bfac, main, raw, sems):
    plan = slow_plan(own, below, n)
    near, at = plan["near"], plan["send_at"]
    parts = sems.shape[0]
    step = bfac.shape[1] // parts
    loads = [
        pltpu.make_async_copy(bfac.at[near, pl.ds(q * step, step)], raw.at[pl.ds(q * step, step)], sems.at[q])
        for q in range(parts)
    ]
    for c in loads:
        c.start()
    for q in range(parts):
        loads[q].wait()
        rows = pl.ds(q * step, step)
        main[:, rows, :] = swapped(raw[rows, :, lanes(at, UNITS)])


def inner_kernel(
    n, own, below, bfac, other, kband, kmirror, far, near, near_extra, extra, mine, theirs, raw, out, sems
):
    me = lax.axis_index("wide")
    is_odd = lax.rem(me, 2) == 1
    total = bfac.shape[3] // DSTEP
    sources = [(bfac, 0, mine), (bfac, 1, mine), (other, 0, theirs), (other, 1, theirs)]
    loads = [
        pltpu.make_async_copy(source.at[b], raw.at[k % 2], sems.at[k]) for k, (source, b, _) in enumerate(sources)
    ]
    step = 32

    def relayout(k):
        _, b, target = sources[k]
        loads[k].wait()

        def some(q, carry):
            rows = pl.ds(pl.multiple_of(q * step, step), step)
            target[b, :, rows, :] = swapped(raw[k % 2, rows])
            return carry

        lax.fori_loop(0, bfac.shape[1] // step, some, 0)
        if k + 2 < len(loads):
            loads[k + 2].start()

    loads[0].start()
    loads[1].start()

    def product(left, a, right, b, at, keep):
        value = sum(times(left[a, i, :, lanes(at, UNITS)], right[b, i, :, lanes(at, UNITS)]) for i in range(2))
        return value * keep.astype(jnp.float32)

    stores = []

    def store(slot, value, ref, index):
        out[slot] = value
        c = pltpu.make_async_copy(out.at[slot], ref.at[index], sems.at[4 + slot])
        c.start()
        stores.append(c)

    relayout(0)
    relayout(1)
    k, s = flags(own, 0, 0)
    store(0, product(mine, 0, mine, 0, s, k), kband, (0, 0))
    k, s = flags(own, 0, 1)
    value = product(mine, 0, mine, 1, s, k)
    store(1, value, kband, (0, 1))
    store(2, value.T, kmirror, (1, 0))
    k, s = flags(own, 1, 0)
    store(3, product(mine, 1, mine, 1, s, k), kband, (1, 0))

    plan = slow_plan(own, below, n)
    window = lanes(plan["recv_at"], UNITS)
    unit = plan["recv_at"] + lax.shift_right_logical(
        lax.broadcasted_iota(jnp.int32, (1, DOM), 1), DSTEP.bit_length() - 1
    )
    counts = jnp.where((unit >= plan["first"]) & (unit < plan["last"]), 1.0, 0.0).astype(near.dtype)
    for i in range(2):
        far[i] = mine[plan["far"], i, :, window]
        near[i] = mine[plan["near"], i, :, window] * counts
        for u in range(SPARE):
            near_extra[u, i] = mine[plan["near"], i, :, lanes(jnp.minimum(plan["extra_recv"] + u, total - 1))]
            extra[u, i] = mine[plan["near"], i, :, lanes(jnp.minimum(plan["extra_send"] + u, total - 1))]

    relayout(2)
    relayout(3)
    b = boundary(lambda block, r: choose(is_odd, flags(below, block, r), flags(own, block, r)))
    close = jnp.where(is_odd, 0, 1)
    pick = lambda x, y: jnp.where(is_odd, x, y)
    out[4] = product(mine, 1 - close, theirs, 1 - close, pick(b["s3"], b["s1"]), pick(b["m3"], b["m1"]))
    out[5] = product(mine, close, theirs, 1 - close, b["s2"], b["m2"])
    out[6] = product(mine, close, theirs, close, pick(b["s1"], b["s3"]), pick(b["m1"], b["m3"]))

    def put(targets):
        run([pltpu.make_async_copy(out.at[4 + j], ref, sems.at[8 + j]) for j, ref in enumerate(targets)])

    @pl.when(is_odd)
    def _():
        put([kmirror.at[1, 1], kmirror.at[0, 0], kmirror.at[0, 1]])

    @pl.when(jnp.logical_not(is_odd))
    def _():
        put([kband.at[0, 2], kband.at[1, 1], kband.at[1, 2]])

    for c in stores:
        c.wait()


def extra_kernel(n, own, below, near_extra, got, out):
    out[...] = jnp.zeros(out.shape, out.dtype)

    def more(u, carry):
        out[...] += times(near_extra[u, 0], got[u, 0]) + times(near_extra[u, 1], got[u, 1])
        return carry

    lax.fori_loop(0, slow_plan(own, below, n)["extra_count"], more, 0)


def slow_kernel(n, got, far, near, extra, far_near, partial, back):
    value = times(far[0], got[0]) + times(far[1], got[1])
    far_near[...] = value
    back[0] = value.T
    value = extra[...] + times(near[0], got[0]) + times(near[1], got[1])
    partial[...] = value
    back[1] = value.T


def last_kernel(n, own, below, far_near, partial, back, kband_in, kmirror_in, kband, kmirror, out, sems):
    plan = slow_plan(own, below, n)
    out[0] = (partial[...] + back[1]) * plan["keep_near"].astype(jnp.float32)
    out[1] = back[0] * plan["keep_near_far"].astype(jnp.float32)
    out[2] = far_near[...] * plan["keep_far_near"].astype(jnp.float32)

    def put(targets):
        run([pltpu.make_async_copy(out.at[j], ref, sems.at[j]) for j, ref in enumerate(targets)])

    @pl.when(plan["is_odd"])
    def _():
        put([kband.at[1, 1], kband.at[1, 2], kband.at[0, 2]])

    @pl.when(jnp.logical_not(plan["is_odd"]))
    def _():
        put([kmirror.at[0, 0], kmirror.at[0, 1], kmirror.at[1, 1]])


def call(kernel, n, outs, ins, out_specs, scratch, flops, bytes_moved, aliases=None, vmem=40):
    return pl.pallas_call(
        functools.partial(kernel, n),
        out_shape=outs,
        in_specs=ins,
        out_specs=out_specs,
        scratch_shapes=scratch,
        input_output_aliases=aliases or {},
        compiler_params=pltpu.CompilerParams(vmem_limit_bytes=vmem * 2**20),
        cost_estimate=pl.CostEstimate(flops=flops, bytes_accessed=bytes_moved, transcendentals=0),
        name=kernel.__name__,
    )


def per_device(bfac, pair_mask, dom_start):
    n = lax.axis_size("wide")
    _, rows, orbitals, fitting = bfac.shape
    slow = [p for i in range(1, n - 1, 2) for p in ((i, i + 1), (i + 1, i))]
    fast = [p for i in range(0, n, 2) for p in ((i, i + 1), (i + 1, i))]
    f32, bf16 = jnp.float32, bfac.dtype
    shape = jax.ShapeDtypeStruct
    dma = pltpu.SemaphoreType.DMA

    window = shape((orbitals, rows, DOM), bf16)
    spare = shape((SPARE, orbitals, rows, DSTEP), bf16)
    ints = shape((8, 128), jnp.int32)
    own, again = call(screen_kernel, n, (ints, ints), [SMEM, SMEM], (VMEM, HBM), [dma(())], 0, 2**14, vmem=60)(
        pair_mask, dom_start
    )
    below = lax.ppermute(own, "wide", [(i, i + 1) for i in range(n - 1)])
    screens = lax.all_gather(again, "wide", tiled=True)

    main = call(
        pack_kernel,
        n,
        window,
        [SMEM, SMEM, HBM],
        VMEM,
        [pltpu.VMEM((rows, orbitals, fitting), bf16), dma((4,))],
        0,
        6 * 2**20,
        vmem=60,
    )(own, below, bfac)
    main_got = lax.ppermute(main, "wide", slow)

    band = shape((2, 3, rows, rows), f32)
    mirror = shape((2, 2, rows, rows), f32)
    square = shape((rows, rows), f32)
    inner_outs = (band, mirror, window, window, spare, spare)

    def inner(own, below, bfac):
        other = lax.ppermute(bfac, "wide", fast)
        return call(
            inner_kernel,
            n,
            inner_outs,
            [SMEM, SMEM, HBM, HBM],
            (HBM, HBM, VMEM, VMEM, VMEM, VMEM),
            [
                pltpu.VMEM((2, orbitals, rows, fitting), bf16),
                pltpu.VMEM((2, orbitals, rows, fitting), bf16),
                pltpu.VMEM((2, rows, orbitals, fitting), bf16),
                pltpu.VMEM((7, rows, rows), f32),
                dma((11,)),
            ],
            12 * rows * rows * orbitals * DOM,
            25 * 2**20,
            vmem=52,
        )(own, below, bfac, other)

    def unused(own, below, bfac):
        return tuple(jnp.zeros(o.shape, o.dtype) for o in inner_outs)

    level = call(level_kernel, n, shape((1,), jnp.int32), [SMEM], SMEM, [], 0, 2**16)(screens)
    own, below, bfac, _ = lax.optimization_barrier((own, below, bfac, main))
    kband, kmirror, far, near, near_extra, extra = lax.cond(level[0] >= 0, inner, unused, own, below, bfac)

    def extras(count):
        def branch(own, below, extra, near_extra):
            if count == 0:
                return jnp.zeros((rows, rows), f32)
            got = lax.ppermute(extra[:count], "wide", slow)
            return call(extra_kernel, n, square, [SMEM, SMEM, VMEM, VMEM], VMEM, [], 2**26 * count, 2**19 * count)(
                own, below, near_extra, got
            )

        return branch

    more = lax.switch(level[0], [extras(c) for c in LEVELS], own, below, extra, near_extra)

    far_near, partial, back = call(
        slow_kernel,
        n,
        (square, square, shape((2, rows, rows), f32)),
        [VMEM] * 4,
        (VMEM, VMEM, VMEM),
        [],
        4 * rows * rows * orbitals * DOM,
        8 * 2**20,
    )(main_got, far, near, more)
    back_got = lax.ppermute(back, "wide", slow)
    return call(
        last_kernel,
        n,
        (band, mirror),
        [SMEM, SMEM, VMEM, VMEM, VMEM, HBM, HBM],
        (HBM, HBM),
        [pltpu.VMEM((3, rows, rows), f32), dma((3,))],
        0,
        2**21,
        {5: 0, 6: 1},
    )(own, below, far_near, partial, back_got, kband, kmirror)


def solution(mesh):
    placed = (P("wide", None, "groups", None), P("wide", None), P("wide", None))
    return jax.shard_map(
        per_device,
        mesh=mesh,
        in_specs=placed,
        out_specs=(
            P(("groups", "wide"), None, None, None),
            P(("groups", "wide"), None, None, None),
        ),
        check_vma=False,
    )
```

```python
import functools

import jax
import jax.numpy as jnp
from jax import lax
from jax.experimental import pallas as pl
from jax.experimental.pallas import tpu as pltpu
from jax.sharding import PartitionSpec as P

DOM = 2048
DSTEP = 128
UNITS = DOM // DSTEP
SPARE = UNITS // 2
LEVELS = (0, 1, 2, 3, 4, 6, 8)
PER = 12
VMEM = pl.BlockSpec(memory_space=pltpu.VMEM)
SMEM = pl.BlockSpec(memory_space=pltpu.SMEM)
HBM = pl.BlockSpec(memory_space=pltpu.HBM)


def flags(screen, block, r, row=0):
    at = block * 3 + r
    return screen[row, at], screen[row, at + PER // 2]


def choose(is_first, first, second):
    return tuple(jnp.where(is_first, a, b) for a, b in zip(first, second))


def boundary(get):
    m1, s1 = get(0, 2)
    m2, s2 = get(1, 1)
    m3, s3 = get(1, 2)
    w1 = jnp.where(m1 > 0, s1, s2)
    w3 = jnp.where(m3 > 0, s3, s2)
    low, high = s2, s2 + UNITS
    for w in (w1, w3):
        low, high = (
            jnp.where(w <= s2, jnp.maximum(low, w + UNITS), low),
            jnp.where(w > s2, jnp.minimum(high, w), high),
        )
    rest = jnp.maximum(high - low, 0) * m2
    half = lax.shift_right_logical(rest + 1, 1)
    return dict(m1=m1, s1=s1, m2=m2, s2=s2, m3=m3, s3=s3, w1=w1, w3=w3, low=low, half=half, rest=rest)


def slow_plan(own, below, n):
    me = lax.axis_index("wide")
    odd = lax.rem(me, 2)
    is_odd = odd == 1
    exists = jnp.where(is_odd, me < n - 1, me > 0).astype(jnp.int32)
    b = boundary(lambda block, r: choose(is_odd, flags(own, block, r), flags(below, block, r)))
    pick = lambda a, c: jnp.where(is_odd, a, c)
    mid = b["low"] + b["half"]
    other = b["rest"] - b["half"]
    recv_at = pick(b["w1"], b["w3"])
    first = jnp.maximum(b["s2"], recv_at)
    last = jnp.minimum(b["s2"] + UNITS, recv_at + UNITS)
    below_w1 = b["w1"] > first
    first_b = jnp.where(below_w1, first, jnp.maximum(first, b["w1"] + UNITS))
    last_b = jnp.where(below_w1, jnp.minimum(last, b["w1"]), last)
    return dict(
        is_odd=is_odd,
        near=odd,
        far=1 - odd,
        send_at=pick(b["w3"], b["w1"]),
        recv_at=recv_at,
        first=pick(first, first_b),
        last=pick(last, last_b),
        extra_send=pick(b["low"], mid),
        extra_recv=pick(mid, b["low"]),
        extra_count=pick(other, b["half"]) * exists,
        keep_far_near=pick(b["m1"], b["m3"]) * exists,
        keep_near_far=pick(b["m3"], b["m1"]) * exists,
        keep_near=b["m2"] * exists,
    )


def lanes(unit, count=1):
    return pl.ds(pl.multiple_of(unit * DSTEP, DSTEP), count * DSTEP)


def times(left, right):
    return lax.dot_general(left, right, (((1,), (1,)), ((), ())), preferred_element_type=jnp.float32)


def run(copies):
    for c in copies:
        c.start()
    for c in copies:
        c.wait()


def screen_kernel(n, pair_mask, dom_start, out, again, sem):
    column = lax.broadcasted_iota(jnp.int32, out.shape, 1)
    value = jnp.zeros(out.shape, jnp.int32)
    for at in range(PER):
        source = pair_mask if at < PER // 2 else dom_start
        block, r = divmod(at % (PER // 2), 3)
        value = jnp.where(column == at, source[block, r], value)
    out[...] = value
    run([pltpu.make_async_copy(out, again, sem)])


def level_kernel(n, screens, level):
    def one(i, most):
        row = (2 * i + 1) * 8
        return jnp.maximum(most, boundary(lambda block, r: flags(screens, block, r, row))["half"])

    largest = lax.fori_loop(0, n // 2 - 1, one, jnp.int32(0))
    level[0] = sum((largest > c).astype(jnp.int32) for c in LEVELS[:-1])


def swapped(values):
    return jnp.swapaxes(values, 0, 1)


def pack_kernel(n, own, below, bfac, main, raw, sems):
    plan = slow_plan(own, below, n)
    near, at = plan["near"], plan["send_at"]
    parts = sems.shape[0]
    step = bfac.shape[1] // parts
    loads = [
        pltpu.make_async_copy(bfac.at[near, pl.ds(q * step, step)], raw.at[pl.ds(q * step, step)], sems.at[q])
        for q in range(parts)
    ]
    for c in loads:
        c.start()
    for q in range(parts):
        loads[q].wait()
        rows = pl.ds(q * step, step)
        main[:, rows, :] = swapped(raw[rows, :, lanes(at, UNITS)])


def inner_kernel(
    n, own, below, bfac, other, kband, kmirror, far, near, near_extra, extra, mine, theirs, raw, out, sems
):
    me = lax.axis_index("wide")
    is_odd = lax.rem(me, 2) == 1
    total = bfac.shape[3] // DSTEP
    sources = [(bfac, 0, mine), (bfac, 1, mine), (other, 0, theirs), (other, 1, theirs)]
    loads = [
        pltpu.make_async_copy(source.at[b], raw.at[k % 2], sems.at[k]) for k, (source, b, _) in enumerate(sources)
    ]
    step = 32

    def relayout(k):
        _, b, target = sources[k]
        loads[k].wait()

        def some(q, carry):
            rows = pl.ds(pl.multiple_of(q * step, step), step)
            target[b, :, rows, :] = swapped(raw[k % 2, rows])
            return carry

        lax.fori_loop(0, bfac.shape[1] // step, some, 0)
        if k + 2 < len(loads):
            loads[k + 2].start()

    loads[0].start()
    loads[1].start()

    def product(left, a, right, b, at, keep):
        value = sum(times(left[a, i, :, lanes(at, UNITS)], right[b, i, :, lanes(at, UNITS)]) for i in range(2))
        return value * keep.astype(jnp.float32)

    stores = []

    def store(slot, value, ref, index):
        out[slot] = value
        c = pltpu.make_async_copy(out.at[slot], ref.at[index], sems.at[4 + slot])
        c.start()
        stores.append(c)

    relayout(0)
    relayout(1)
    k, s = flags(own, 0, 0)
    store(0, product(mine, 0, mine, 0, s, k), kband, (0, 0))
    k, s = flags(own, 0, 1)
    value = product(mine, 0, mine, 1, s, k)
    store(1, value, kband, (0, 1))
    store(2, value.T, kmirror, (1, 0))
    k, s = flags(own, 1, 0)
    store(3, product(mine, 1, mine, 1, s, k), kband, (1, 0))

    plan = slow_plan(own, below, n)
    window = lanes(plan["recv_at"], UNITS)
    unit = plan["recv_at"] + lax.shift_right_logical(
        lax.broadcasted_iota(jnp.int32, (1, DOM), 1), DSTEP.bit_length() - 1
    )
    counts = jnp.where((unit >= plan["first"]) & (unit < plan["last"]), 1.0, 0.0).astype(near.dtype)
    for i in range(2):
        far[i] = mine[plan["far"], i, :, window]
        near[i] = mine[plan["near"], i, :, window] * counts
        for u in range(SPARE):
            near_extra[u, i] = mine[plan["near"], i, :, lanes(jnp.minimum(plan["extra_recv"] + u, total - 1))]
            extra[u, i] = mine[plan["near"], i, :, lanes(jnp.minimum(plan["extra_send"] + u, total - 1))]

    relayout(2)
    relayout(3)
    b = boundary(lambda block, r: choose(is_odd, flags(below, block, r), flags(own, block, r)))
    close = jnp.where(is_odd, 0, 1)
    pick = lambda x, y: jnp.where(is_odd, x, y)
    out[4] = product(mine, 1 - close, theirs, 1 - close, pick(b["s3"], b["s1"]), pick(b["m3"], b["m1"]))
    out[5] = product(mine, close, theirs, 1 - close, b["s2"], b["m2"])
    out[6] = product(mine, close, theirs, close, pick(b["s1"], b["s3"]), pick(b["m1"], b["m3"]))

    def put(targets):
        run([pltpu.make_async_copy(out.at[4 + j], ref, sems.at[8 + j]) for j, ref in enumerate(targets)])

    @pl.when(is_odd)
    def _():
        put([kmirror.at[1, 1], kmirror.at[0, 0], kmirror.at[0, 1]])

    @pl.when(jnp.logical_not(is_odd))
    def _():
        put([kband.at[0, 2], kband.at[1, 1], kband.at[1, 2]])

    for c in stores:
        c.wait()


def extra_kernel(n, own, below, near_extra, got, out):
    out[...] = jnp.zeros(out.shape, out.dtype)

    def more(u, carry):
        out[...] += times(near_extra[u, 0], got[u, 0]) + times(near_extra[u, 1], got[u, 1])
        return carry

    lax.fori_loop(0, slow_plan(own, below, n)["extra_count"], more, 0)


def slow_kernel(n, got, far, near, extra, far_near, partial, back):
    value = times(far[0], got[0]) + times(far[1], got[1])
    far_near[...] = value
    back[0] = value.T
    value = extra[...] + times(near[0], got[0]) + times(near[1], got[1])
    partial[...] = value
    back[1] = value.T


def last_kernel(n, own, below, far_near, partial, back, kband_in, kmirror_in, kband, kmirror, out, sems):
    plan = slow_plan(own, below, n)
    out[0] = (partial[...] + back[1]) * plan["keep_near"].astype(jnp.float32)
    out[1] = back[0] * plan["keep_near_far"].astype(jnp.float32)
    out[2] = far_near[...] * plan["keep_far_near"].astype(jnp.float32)

    def put(targets):
        run([pltpu.make_async_copy(out.at[j], ref, sems.at[j]) for j, ref in enumerate(targets)])

    @pl.when(plan["is_odd"])
    def _():
        put([kband.at[1, 1], kband.at[1, 2], kband.at[0, 2]])

    @pl.when(jnp.logical_not(plan["is_odd"]))
    def _():
        put([kmirror.at[0, 0], kmirror.at[0, 1], kmirror.at[1, 1]])


def call(kernel, n, outs, ins, out_specs, scratch, flops, bytes_moved, aliases=None, vmem=40):
    return pl.pallas_call(
        functools.partial(kernel, n),
        out_shape=outs,
        in_specs=ins,
        out_specs=out_specs,
        scratch_shapes=scratch,
        input_output_aliases=aliases or {},
        compiler_params=pltpu.CompilerParams(vmem_limit_bytes=vmem * 2**20),
        cost_estimate=pl.CostEstimate(flops=flops, bytes_accessed=bytes_moved, transcendentals=0),
        name=kernel.__name__,
    )


def per_device(bfac, pair_mask, dom_start):
    n = lax.axis_size("wide")
    _, rows, orbitals, fitting = bfac.shape
    slow = [p for i in range(1, n - 1, 2) for p in ((i, i + 1), (i + 1, i))]
    fast = [p for i in range(0, n, 2) for p in ((i, i + 1), (i + 1, i))]
    f32, bf16 = jnp.float32, bfac.dtype
    shape = jax.ShapeDtypeStruct
    dma = pltpu.SemaphoreType.DMA

    window = shape((orbitals, rows, DOM), bf16)
    spare = shape((SPARE, orbitals, rows, DSTEP), bf16)
    ints = shape((8, 128), jnp.int32)
    own, again = call(screen_kernel, n, (ints, ints), [SMEM, SMEM], (VMEM, HBM), [dma(())], 0, 2**14, vmem=60)(
        pair_mask, dom_start
    )
    below = lax.ppermute(own, "wide", [(i, i + 1) for i in range(n - 1)])
    screens = lax.all_gather(again, "wide", tiled=True)

    main = call(
        pack_kernel,
        n,
        window,
        [SMEM, SMEM, HBM],
        VMEM,
        [pltpu.VMEM((rows, orbitals, fitting), bf16), dma((4,))],
        0,
        6 * 2**20,
        vmem=60,
    )(own, below, bfac)
    main, screens = lax.optimization_barrier((main, screens))
    main_got = lax.ppermute(main, "wide", slow)

    band = shape((2, 3, rows, rows), f32)
    mirror = shape((2, 2, rows, rows), f32)
    square = shape((rows, rows), f32)
    inner_outs = (band, mirror, window, window, spare, spare)

    def inner(own, below, bfac):
        other = lax.ppermute(bfac, "wide", fast)
        return call(
            inner_kernel,
            n,
            inner_outs,
            [SMEM, SMEM, HBM, HBM],
            (HBM, HBM, VMEM, VMEM, VMEM, VMEM),
            [
                pltpu.VMEM((2, orbitals, rows, fitting), bf16),
                pltpu.VMEM((2, orbitals, rows, fitting), bf16),
                pltpu.VMEM((2, rows, orbitals, fitting), bf16),
                pltpu.VMEM((7, rows, rows), f32),
                dma((11,)),
            ],
            12 * rows * rows * orbitals * DOM,
            25 * 2**20,
            vmem=52,
        )(own, below, bfac, other)

    def unused(own, below, bfac):
        return tuple(jnp.zeros(o.shape, o.dtype) for o in inner_outs)

    level = call(level_kernel, n, shape((1,), jnp.int32), [SMEM], SMEM, [], 0, 2**16)(screens)
    own, below, bfac, _ = lax.optimization_barrier((own, below, bfac, main))
    kband, kmirror, far, near, near_extra, extra = lax.cond(level[0] >= 0, inner, unused, own, below, bfac)

    def extras(count):
        def branch(own, below, extra, near_extra):
            if count == 0:
                return jnp.zeros((rows, rows), f32)
            got = lax.ppermute(extra[:count], "wide", slow)
            return call(extra_kernel, n, square, [SMEM, SMEM, VMEM, VMEM], VMEM, [], 2**26 * count, 2**19 * count)(
                own, below, near_extra, got
            )

        return branch

    more = lax.switch(level[0], [extras(c) for c in LEVELS], own, below, extra, near_extra)

    far_near, partial, back = call(
        slow_kernel,
        n,
        (square, square, shape((2, rows, rows), f32)),
        [VMEM] * 4,
        (VMEM, VMEM, VMEM),
        [],
        4 * rows * rows * orbitals * DOM,
        8 * 2**20,
    )(main_got, far, near, more)
    back_got = lax.ppermute(back, "wide", slow)
    return call(
        last_kernel,
        n,
        (band, mirror),
        [SMEM, SMEM, VMEM, VMEM, VMEM, HBM, HBM],
        (HBM, HBM),
        [pltpu.VMEM((3, rows, rows), f32), dma((3,))],
        0,
        2**21,
        {5: 0, 6: 1},
    )(own, below, far_near, partial, back_got, kband, kmirror)


def solution(mesh):
    placed = (P("wide", None, "groups", None), P("wide", None), P("wide", None))
    return jax.shard_map(
        per_device,
        mesh=mesh,
        in_specs=placed,
        out_specs=(
            P(("groups", "wide"), None, None, None),
            P(("groups", "wide"), None, None, None),
        ),
        check_vma=False,
    )
```

```python
import functools

import jax
import jax.numpy as jnp
from jax import lax
from jax.experimental import pallas as pl
from jax.experimental.pallas import tpu as pltpu
from jax.sharding import PartitionSpec as P

DOM = 2048
DSTEP = 128
UNITS = DOM // DSTEP
SPARE = UNITS // 2
LEVELS = (1, 2, 3, 4, 6, 8)
PER = 12
VMEM = pl.BlockSpec(memory_space=pltpu.VMEM)
SMEM = pl.BlockSpec(memory_space=pltpu.SMEM)
HBM = pl.BlockSpec(memory_space=pltpu.HBM)


def flags(screen, block, r, row=0):
    at = block * 3 + r
    return screen[row, at], screen[row, at + PER // 2]


def choose(is_first, first, second):
    return tuple(jnp.where(is_first, a, b) for a, b in zip(first, second))


def boundary(get):
    m1, s1 = get(0, 2)
    m2, s2 = get(1, 1)
    m3, s3 = get(1, 2)
    w1 = jnp.where(m1 > 0, s1, s2)
    w3 = jnp.where(m3 > 0, s3, s2)
    low, high = s2, s2 + UNITS
    for w in (w1, w3):
        low, high = (
            jnp.where(w <= s2, jnp.maximum(low, w + UNITS), low),
            jnp.where(w > s2, jnp.minimum(high, w), high),
        )
    rest = jnp.maximum(high - low, 0) * m2
    half = lax.shift_right_logical(rest + 1, 1)
    return dict(m1=m1, s1=s1, m2=m2, s2=s2, m3=m3, s3=s3, w1=w1, w3=w3, low=low, half=half, rest=rest)


def slow_plan(own, below, n):
    me = lax.axis_index("wide")
    odd = lax.rem(me, 2)
    is_odd = odd == 1
    exists = jnp.where(is_odd, me < n - 1, me > 0).astype(jnp.int32)
    b = boundary(lambda block, r: choose(is_odd, flags(own, block, r), flags(below, block, r)))
    pick = lambda a, c: jnp.where(is_odd, a, c)
    mid = b["low"] + b["half"]
    other = b["rest"] - b["half"]
    recv_at = pick(b["w1"], b["w3"])
    first = jnp.maximum(b["s2"], recv_at)
    last = jnp.minimum(b["s2"] + UNITS, recv_at + UNITS)
    below_w1 = b["w1"] > first
    first_b = jnp.where(below_w1, first, jnp.maximum(first, b["w1"] + UNITS))
    last_b = jnp.where(below_w1, jnp.minimum(last, b["w1"]), last)
    level = sum((b["half"] > c).astype(jnp.int32) for c in LEVELS[:-1])
    lower = lax.shift_right_logical(jnp.where(is_odd, me, me - 1) - 1, 1)
    case = jnp.where(b["half"] * exists > 0, 1 + lower * len(LEVELS) + level, 0)
    return dict(
        case=case,
        is_odd=is_odd,
        near=odd,
        far=1 - odd,
        send_at=pick(b["w3"], b["w1"]),
        recv_at=recv_at,
        first=pick(first, first_b),
        last=pick(last, last_b),
        extra_send=pick(b["low"], mid),
        extra_recv=pick(mid, b["low"]),
        extra_count=pick(other, b["half"]) * exists,
        keep_far_near=pick(b["m1"], b["m3"]) * exists,
        keep_near_far=pick(b["m3"], b["m1"]) * exists,
        keep_near=b["m2"] * exists,
    )


def lanes(unit, count=1):
    return pl.ds(pl.multiple_of(unit * DSTEP, DSTEP), count * DSTEP)


def times(left, right):
    return lax.dot_general(left, right, (((1,), (1,)), ((), ())), preferred_element_type=jnp.float32)


def run(copies):
    for c in copies:
        c.start()
    for c in copies:
        c.wait()


def screen_kernel(n, pair_mask, dom_start, out):
    column = lax.broadcasted_iota(jnp.int32, out.shape, 1)
    value = jnp.zeros(out.shape, jnp.int32)
    for at in range(PER):
        source = pair_mask if at < PER // 2 else dom_start
        block, r = divmod(at % (PER // 2), 3)
        value = jnp.where(column == at, source[block, r], value)
    out[...] = value


def swapped(values):
    return jnp.swapaxes(values, 0, 1)


def pack_kernel(n, own, below, bfac, main, case, raw, sems):
    plan = slow_plan(own, below, n)
    near, at = plan["near"], plan["send_at"]
    parts = sems.shape[0]
    step = bfac.shape[1] // parts
    loads = [
        pltpu.make_async_copy(bfac.at[near, pl.ds(q * step, step)], raw.at[pl.ds(q * step, step)], sems.at[q])
        for q in range(parts)
    ]
    for c in loads:
        c.start()
    case[0] = plan["case"]
    for q in range(parts):
        loads[q].wait()
        rows = pl.ds(q * step, step)
        main[:, rows, :] = swapped(raw[rows, :, lanes(at, UNITS)])


def inner_kernel(
    n, own, below, bfac, other, kband, kmirror, far, near, near_extra, extra, mine, theirs, raw, out, sems
):
    me = lax.axis_index("wide")
    is_odd = lax.rem(me, 2) == 1
    total = bfac.shape[3] // DSTEP
    sources = [(bfac, 0, mine), (bfac, 1, mine), (other, 0, theirs), (other, 1, theirs)]
    loads = [
        pltpu.make_async_copy(source.at[b], raw.at[k % 2], sems.at[k]) for k, (source, b, _) in enumerate(sources)
    ]
    step = 32

    def relayout(k):
        _, b, target = sources[k]
        loads[k].wait()

        def some(q, carry):
            rows = pl.ds(pl.multiple_of(q * step, step), step)
            target[b, :, rows, :] = swapped(raw[k % 2, rows])
            return carry

        lax.fori_loop(0, bfac.shape[1] // step, some, 0)
        if k + 2 < len(loads):
            loads[k + 2].start()

    loads[0].start()
    loads[1].start()

    def product(left, a, right, b, at, keep):
        value = sum(times(left[a, i, :, lanes(at, UNITS)], right[b, i, :, lanes(at, UNITS)]) for i in range(2))
        return value * keep.astype(jnp.float32)

    stores = []

    def store(slot, value, ref, index):
        out[slot] = value
        c = pltpu.make_async_copy(out.at[slot], ref.at[index], sems.at[4 + slot])
        c.start()
        stores.append(c)

    relayout(0)
    relayout(1)
    k, s = flags(own, 0, 0)
    store(0, product(mine, 0, mine, 0, s, k), kband, (0, 0))
    k, s = flags(own, 0, 1)
    value = product(mine, 0, mine, 1, s, k)
    store(1, value, kband, (0, 1))
    store(2, value.T, kmirror, (1, 0))
    k, s = flags(own, 1, 0)
    store(3, product(mine, 1, mine, 1, s, k), kband, (1, 0))

    plan = slow_plan(own, below, n)
    window = lanes(plan["recv_at"], UNITS)
    unit = plan["recv_at"] + lax.shift_right_logical(
        lax.broadcasted_iota(jnp.int32, (1, DOM), 1), DSTEP.bit_length() - 1
    )
    counts = jnp.where((unit >= plan["first"]) & (unit < plan["last"]), 1.0, 0.0).astype(near.dtype)
    for i in range(2):
        far[i] = mine[plan["far"], i, :, window]
        near[i] = mine[plan["near"], i, :, window] * counts
        for u in range(SPARE):
            near_extra[u, i] = mine[plan["near"], i, :, lanes(jnp.minimum(plan["extra_recv"] + u, total - 1))]
            extra[u, i] = mine[plan["near"], i, :, lanes(jnp.minimum(plan["extra_send"] + u, total - 1))]

    relayout(2)
    relayout(3)
    b = boundary(lambda block, r: choose(is_odd, flags(below, block, r), flags(own, block, r)))
    close = jnp.where(is_odd, 0, 1)
    pick = lambda x, y: jnp.where(is_odd, x, y)
    out[4] = product(mine, 1 - close, theirs, 1 - close, pick(b["s3"], b["s1"]), pick(b["m3"], b["m1"]))
    out[5] = product(mine, close, theirs, 1 - close, b["s2"], b["m2"])
    out[6] = product(mine, close, theirs, close, pick(b["s1"], b["s3"]), pick(b["m1"], b["m3"]))

    def put(targets):
        run([pltpu.make_async_copy(out.at[4 + j], ref, sems.at[8 + j]) for j, ref in enumerate(targets)])

    @pl.when(is_odd)
    def _():
        put([kmirror.at[1, 1], kmirror.at[0, 0], kmirror.at[0, 1]])

    @pl.when(jnp.logical_not(is_odd))
    def _():
        put([kband.at[0, 2], kband.at[1, 1], kband.at[1, 2]])

    for c in stores:
        c.wait()


def extra_kernel(n, own, below, near_extra, got, out):
    out[...] = jnp.zeros(out.shape, out.dtype)

    def more(u, carry):
        out[...] += times(near_extra[u, 0], got[u, 0]) + times(near_extra[u, 1], got[u, 1])
        return carry

    lax.fori_loop(0, slow_plan(own, below, n)["extra_count"], more, 0)


def slow_kernel(n, got, far, near, extra, far_near, partial, back):
    value = times(far[0], got[0]) + times(far[1], got[1])
    far_near[...] = value
    back[0] = value.T
    value = extra[...] + times(near[0], got[0]) + times(near[1], got[1])
    partial[...] = value
    back[1] = value.T


def last_kernel(n, own, below, far_near, partial, back, kband_in, kmirror_in, kband, kmirror, out, sems):
    plan = slow_plan(own, below, n)
    out[0] = (partial[...] + back[1]) * plan["keep_near"].astype(jnp.float32)
    out[1] = back[0] * plan["keep_near_far"].astype(jnp.float32)
    out[2] = far_near[...] * plan["keep_far_near"].astype(jnp.float32)

    def put(targets):
        run([pltpu.make_async_copy(out.at[j], ref, sems.at[j]) for j, ref in enumerate(targets)])

    @pl.when(plan["is_odd"])
    def _():
        put([kband.at[1, 1], kband.at[1, 2], kband.at[0, 2]])

    @pl.when(jnp.logical_not(plan["is_odd"]))
    def _():
        put([kmirror.at[0, 0], kmirror.at[0, 1], kmirror.at[1, 1]])


def call(kernel, n, outs, ins, out_specs, scratch, flops, bytes_moved, aliases=None, vmem=40):
    return pl.pallas_call(
        functools.partial(kernel, n),
        out_shape=outs,
        in_specs=ins,
        out_specs=out_specs,
        scratch_shapes=scratch,
        input_output_aliases=aliases or {},
        compiler_params=pltpu.CompilerParams(vmem_limit_bytes=vmem * 2**20),
        cost_estimate=pl.CostEstimate(flops=flops, bytes_accessed=bytes_moved, transcendentals=0),
        name=kernel.__name__,
    )


def per_device(bfac, pair_mask, dom_start):
    n = lax.axis_size("wide")
    _, rows, orbitals, fitting = bfac.shape
    slow = [p for i in range(1, n - 1, 2) for p in ((i, i + 1), (i + 1, i))]
    fast = [p for i in range(0, n, 2) for p in ((i, i + 1), (i + 1, i))]
    f32, bf16 = jnp.float32, bfac.dtype
    shape = jax.ShapeDtypeStruct
    dma = pltpu.SemaphoreType.DMA

    window = shape((orbitals, rows, DOM), bf16)
    spare = shape((SPARE, orbitals, rows, DSTEP), bf16)
    own = call(screen_kernel, n, shape((8, 128), jnp.int32), [SMEM, SMEM], VMEM, [], 0, 2**14)(pair_mask, dom_start)
    below = lax.ppermute(own, "wide", [(i, i + 1) for i in range(n - 1)])

    main, case = call(
        pack_kernel,
        n,
        (window, shape((1,), jnp.int32)),
        [SMEM, SMEM, HBM],
        (VMEM, SMEM),
        [pltpu.VMEM((rows, orbitals, fitting), bf16), dma((4,))],
        0,
        6 * 2**20,
        vmem=60,
    )(own, below, bfac)
    main_got = lax.ppermute(main, "wide", slow)

    band = shape((2, 3, rows, rows), f32)
    mirror = shape((2, 2, rows, rows), f32)
    square = shape((rows, rows), f32)
    inner_outs = (band, mirror, window, window, spare, spare)

    def inner(own, below, bfac):
        other = lax.ppermute(bfac, "wide", fast)
        return call(
            inner_kernel,
            n,
            inner_outs,
            [SMEM, SMEM, HBM, HBM],
            (HBM, HBM, VMEM, VMEM, VMEM, VMEM),
            [
                pltpu.VMEM((2, orbitals, rows, fitting), bf16),
                pltpu.VMEM((2, orbitals, rows, fitting), bf16),
                pltpu.VMEM((2, rows, orbitals, fitting), bf16),
                pltpu.VMEM((7, rows, rows), f32),
                dma((11,)),
            ],
            12 * rows * rows * orbitals * DOM,
            25 * 2**20,
            vmem=52,
        )(own, below, bfac, other)

    def unused(own, below, bfac):
        return tuple(jnp.zeros(o.shape, o.dtype) for o in inner_outs)

    own, below, bfac, _ = lax.optimization_barrier((own, below, bfac, main))
    kband, kmirror, far, near, near_extra, extra = lax.cond(case[0] >= 0, inner, unused, own, below, bfac)

    def nothing(own, below, extra, near_extra):
        return jnp.zeros((rows, rows), f32)

    def extras(lower, count):
        def branch(own, below, extra, near_extra):
            got = lax.ppermute(extra[:count], "wide", [(lower, lower + 1), (lower + 1, lower)])
            return call(extra_kernel, n, square, [SMEM, SMEM, VMEM, VMEM], VMEM, [], 2**26 * count, 2**19 * count)(
                own, below, near_extra, got
            )

        return branch

    branches = [nothing] + [extras(i, c) for i in range(1, n - 1, 2) for c in LEVELS]
    more = lax.switch(case[0], branches, own, below, extra, near_extra)

    far_near, partial, back = call(
        slow_kernel,
        n,
        (square, square, shape((2, rows, rows), f32)),
        [VMEM] * 4,
        (VMEM, VMEM, VMEM),
        [],
        4 * rows * rows * orbitals * DOM,
        8 * 2**20,
    )(main_got, far, near, more)
    back_got = lax.ppermute(back, "wide", slow)
    return call(
        last_kernel,
        n,
        (band, mirror),
        [SMEM, SMEM, VMEM, VMEM, VMEM, HBM, HBM],
        (HBM, HBM),
        [pltpu.VMEM((3, rows, rows), f32), dma((3,))],
        0,
        2**21,
        {5: 0, 6: 1},
    )(own, below, far_near, partial, back_got, kband, kmirror)


def solution(mesh):
    placed = (P("wide", None, "groups", None), P("wide", None), P("wide", None))
    return jax.shard_map(
        per_device,
        mesh=mesh,
        in_specs=placed,
        out_specs=(
            P(("groups", "wide"), None, None, None),
            P(("groups", "wide"), None, None, None),
        ),
        check_vma=False,
    )
```

```python
import functools

import jax
import jax.numpy as jnp
from jax import lax
from jax.experimental import pallas as pl
from jax.experimental.pallas import tpu as pltpu
from jax.sharding import PartitionSpec as P

DOM = 2048
DSTEP = 128
UNITS = DOM // DSTEP
LEVELS = (2, 4, 6, 8, 12, 16)
PER = 12
NOTE = 16
VMEM = pl.BlockSpec(memory_space=pltpu.VMEM)
SMEM = pl.BlockSpec(memory_space=pltpu.SMEM)
HBM = pl.BlockSpec(memory_space=pltpu.HBM)


def flags(screen, block, r):
    at = block * 3 + r
    return screen[0, at], screen[0, at + PER // 2]


def boundary(get):
    m1, s1 = get(0, 2)
    m2, s2 = get(1, 1)
    m3, s3 = get(1, 2)
    first = jnp.where(m3 > 0, s3, s2)
    low = jnp.where(first <= s2, jnp.maximum(s2, first + UNITS), s2)
    high = jnp.where(first <= s2, s2 + UNITS, jnp.minimum(s2 + UNITS, first))
    rest = jnp.maximum(high - low, 0) * m2
    second = jnp.where(m1 > 0, s1, jnp.minimum(low, UNITS))
    return dict(m1=m1, s1=s1, m2=m2, s2=s2, m3=m3, s3=s3, first=first, low=low, rest=rest, second=second)


def position():
    me = lax.axis_index("wide")
    return me, lax.rem(me, 2) == 1


def slow_boundary(own, below):
    _, is_odd = position()

    def get(block, r):
        return tuple(jnp.where(is_odd, a, b) for a, b in zip(flags(own, block, r), flags(below, block, r)))

    return boundary(get)


def lanes(unit, count=1):
    return pl.ds(pl.multiple_of(unit * DSTEP, DSTEP), count * DSTEP)


def counted(unit, first, last):
    at = unit + lax.shift_right_logical(lax.broadcasted_iota(jnp.int32, (1, DOM), 1), DSTEP.bit_length() - 1)
    return jnp.where((at >= first) & (at < last), 1.0, 0.0).astype(jnp.bfloat16)


def times(left, right):
    return lax.dot_general(left, right, (((1,), (1,)), ((), ())), preferred_element_type=jnp.float32)


def swapped(values):
    return jnp.swapaxes(values, 0, 1)


def run(copies):
    for c in copies:
        c.start()
    for c in copies:
        c.wait()


def load_parts(block, raw, sems):
    parts = sems.shape[0]
    step = raw.shape[0] // parts
    return [
        pltpu.make_async_copy(block.at[pl.ds(q * step, step)], raw.at[pl.ds(q * step, step)], sems.at[q])
        for q in range(parts)
    ]


def first_kernel(pair_mask, dom_start, bfac, out, own, raw, sems):
    _, is_odd = position()
    rows = raw.shape[0]
    column = lax.broadcasted_iota(jnp.int32, own.shape, 1)
    value = jnp.zeros(own.shape, jnp.int32)
    for at in range(PER):
        source = pair_mask if at < PER // 2 else dom_start
        block, r = divmod(at % (PER // 2), 3)
        value = jnp.where(column == at, source[block, r], value)
    own[...] = value

    @pl.when(is_odd)
    def _():
        loads = load_parts(bfac.at[1], raw, sems)
        for c in loads:
            c.start()
        at = boundary(lambda block, r: (pair_mask[block, r], dom_start[block, r]))["first"]
        out[2 * rows :, :] = jnp.zeros((NOTE, DOM), out.dtype)
        out[2 * rows :, :DSTEP] = jnp.concatenate([value, value], 0).astype(jnp.float32).astype(out.dtype)
        step = rows // len(loads)
        for q, c in enumerate(loads):
            c.wait()
            part = swapped(raw[pl.ds(q * step, step), :, lanes(at, UNITS)])
            for i in range(2):
                out[pl.ds(i * rows + q * step, step), :] = part[i]


def second_kernel(own, bfac, out, raw, sems):
    _, is_odd = position()

    @pl.when(is_odd)
    def _():
        b = boundary(lambda block, r: flags(own, block, r))
        loads = load_parts(bfac.at[jnp.where(b["m1"] > 0, 0, 1)], raw, sems)
        for c in loads:
            c.start()
        step = raw.shape[0] // len(loads)
        for q, c in enumerate(loads):
            c.wait()
            rows = pl.ds(q * step, step)
            out[:, rows, :] = swapped(raw[rows, :, lanes(b["second"], UNITS)])


def inner_kernel(own, below, bfac, other, kband, kmirror, mine, extra, theirs, raw, out, sems):
    _, is_odd = position()
    total = bfac.shape[3] // DSTEP
    sources = [(bfac, 0, mine), (bfac, 1, mine), (other, 0, theirs), (other, 1, theirs)]
    loads = [
        pltpu.make_async_copy(source.at[b], raw.at[k % 2], sems.at[k]) for k, (source, b, _) in enumerate(sources)
    ]
    step = 32

    def relayout(k):
        _, b, target = sources[k]
        loads[k].wait()

        def some(q, carry):
            rows = pl.ds(pl.multiple_of(q * step, step), step)
            target[b, :, rows, :] = swapped(raw[k % 2, rows])
            return carry

        lax.fori_loop(0, bfac.shape[1] // step, some, 0)
        if k + 2 < len(loads):
            loads[k + 2].start()

    loads[0].start()
    loads[1].start()

    def product(left, a, right, b, at, keep):
        value = sum(times(left[a, i, :, lanes(at, UNITS)], right[b, i, :, lanes(at, UNITS)]) for i in range(2))
        return value * keep.astype(jnp.float32)

    stores = []

    def store(slot, value, ref, index):
        out[slot] = value
        c = pltpu.make_async_copy(out.at[slot], ref.at[index], sems.at[4 + slot])
        c.start()
        stores.append(c)

    relayout(0)
    relayout(1)
    k, s = flags(own, 0, 0)
    store(0, product(mine, 0, mine, 0, s, k), kband, (0, 0))
    k, s = flags(own, 0, 1)
    value = product(mine, 0, mine, 1, s, k)
    store(1, value, kband, (0, 1))
    store(2, value.T, kmirror, (1, 0))
    k, s = flags(own, 1, 0)
    store(3, product(mine, 1, mine, 1, s, k), kband, (1, 0))

    @pl.when(is_odd)
    def _():
        low = boundary(lambda block, r: flags(own, block, r))["low"]

        def some(u, carry):
            for i in range(2):
                extra[u, i] = mine[1, i, :, lanes(jnp.minimum(low + u, total - 1))]
            return carry

        lax.fori_loop(0, UNITS, some, 0)

    relayout(2)
    relayout(3)

    def get(block, r):
        return tuple(jnp.where(is_odd, a, b) for a, b in zip(flags(below, block, r), flags(own, block, r)))

    b = boundary(get)
    close = jnp.where(is_odd, 0, 1)
    pick = lambda x, y: jnp.where(is_odd, x, y)
    out[4] = product(mine, 1 - close, theirs, 1 - close, pick(b["s3"], b["s1"]), pick(b["m3"], b["m1"]))
    out[5] = product(mine, close, theirs, 1 - close, b["s2"], b["m2"])
    out[6] = product(mine, close, theirs, close, pick(b["s1"], b["s3"]), pick(b["m1"], b["m3"]))

    def put(targets):
        run([pltpu.make_async_copy(out.at[4 + j], ref, sems.at[8 + j]) for j, ref in enumerate(targets)])

    @pl.when(is_odd)
    def _():
        put([kmirror.at[1, 1], kmirror.at[0, 0], kmirror.at[0, 1]])

    @pl.when(jnp.logical_not(is_odd))
    def _():
        put([kband.at[0, 2], kband.at[1, 1], kband.at[1, 2]])

    for c in stores:
        c.wait()


def upper_first_kernel(n, own, below, got, mine, back, near, case):
    me, is_odd = position()
    b = slow_boundary(own, below)
    exists = jnp.where(is_odd, me < n - 1, me > 0)
    level = sum((b["rest"] > c).astype(jnp.int32) for c in LEVELS[:-1])
    which = lax.shift_right_logical(jnp.where(is_odd, me, me - 1) - 1, 1)
    case[0] = jnp.where(exists & (b["rest"] * b["m1"] > 0), 1 + which * len(LEVELS) + level, 0)

    @pl.when(jnp.logical_not(is_odd))
    def _():
        rows = mine.shape[2]
        window = lanes(b["first"], UNITS)
        counts = counted(b["first"], b["s2"], b["s2"] + UNITS * b["m2"])
        left = [got[pl.ds(i * rows, rows), :] for i in range(2)]
        back[...] = sum(times(left[i], mine[1, i, :, window]) for i in range(2)) * b["m3"].astype(jnp.float32)
        near[...] = sum(times(left[i], mine[0, i, :, window] * counts) for i in range(2))


def rest_kernel(own, below, got, mine, out):
    _, is_odd = position()
    b = slow_boundary(own, below)
    out[...] = jnp.zeros(out.shape, out.dtype)

    def some(u, carry):
        window = lanes(b["low"] + u)
        out[...] += times(got[u, 0], mine[0, 0, :, window]) + times(got[u, 1], mine[0, 1, :, window])
        return carry

    lax.fori_loop(0, jnp.where(is_odd, 0, b["rest"]), some, 0)


def upper_second_kernel(own, below, got, mine, near, more, back):
    _, is_odd = position()

    @pl.when(jnp.logical_not(is_odd))
    def _():
        b = slow_boundary(own, below)
        far_lives = b["m1"] > 0
        window = lanes(b["second"], UNITS)
        counts = counted(
            b["second"],
            jnp.where(far_lives, b["second"], b["low"]),
            jnp.where(far_lives, b["second"] + UNITS, b["low"] + b["rest"]),
        )
        value = sum(times(got[i], mine[0, i, :, window] * counts) for i in range(2))
        lives = b["m1"].astype(jnp.float32)
        back[0] = value * lives
        back[1] = near[...] + more[...] + value * (1.0 - lives)


def middle_kernel(first_got, first, second, kband_in, kmirror_in, kband, kmirror, out, sems):
    _, is_odd = position()

    @pl.when(is_odd)
    def _():
        run([pltpu.make_async_copy(first_got, kband.at[1, 2], sems.at[0])])

    @pl.when(jnp.logical_not(is_odd))
    def _():
        out[0] = first[...].T
        out[1] = second[0].T
        out[2] = second[1].T
        targets = [kmirror.at[1, 1], kmirror.at[0, 1], kmirror.at[0, 0]]
        run([pltpu.make_async_copy(out.at[j], ref, sems.at[j]) for j, ref in enumerate(targets)])


def last_kernel(got, kband_in, kband, sems):
    _, is_odd = position()

    @pl.when(is_odd)
    def _():
        targets = [kband.at[0, 2], kband.at[1, 1]]
        run([pltpu.make_async_copy(got.at[j], ref, sems.at[j]) for j, ref in enumerate(targets)])


def call(kernel, outs, ins, out_specs, scratch, flops=0, moved=0, aliases=None, vmem=40):
    inner = kernel.func if isinstance(kernel, functools.partial) else kernel
    return pl.pallas_call(
        kernel,
        out_shape=outs,
        in_specs=ins,
        out_specs=out_specs,
        scratch_shapes=scratch,
        input_output_aliases=aliases or {},
        compiler_params=pltpu.CompilerParams(vmem_limit_bytes=vmem * 2**20),
        cost_estimate=pl.CostEstimate(flops=flops, bytes_accessed=moved, transcendentals=0),
        name=inner.__name__,
    )


def per_device(bfac, pair_mask, dom_start):
    n = lax.axis_size("wide")
    _, rows, orbitals, fitting = bfac.shape
    upward = [(i, i + 1) for i in range(1, n - 1, 2)]
    downward = [(j, i) for i, j in upward]
    fast = [p for i in range(0, n, 2) for p in ((i, i + 1), (i + 1, i))]
    f32, bf16 = jnp.float32, bfac.dtype
    shape = jax.ShapeDtypeStruct
    dma = pltpu.SemaphoreType.DMA
    square = shape((rows, rows), f32)
    window = shape((orbitals, rows, DOM), bf16)
    raw_block = pltpu.VMEM((rows, orbitals, fitting), bf16)

    first, own = call(
        first_kernel,
        (shape((orbitals * rows + NOTE, DOM), bf16), shape((8, 128), jnp.int32)),
        [SMEM, SMEM, HBM],
        (VMEM, VMEM),
        [raw_block, dma((4,))],
        vmem=60,
    )(pair_mask, dom_start, bfac)
    first_got = lax.ppermute(first, "wide", upward)

    second = call(second_kernel, window, [SMEM, HBM], VMEM, [raw_block, dma((4,))], vmem=56)(own, bfac)
    second_got = lax.ppermute(second, "wide", upward)

    inner_outs = (
        shape((2, 3, rows, rows), f32),
        shape((2, 2, rows, rows), f32),
        shape((2, orbitals, rows, fitting), bf16),
        shape((UNITS, orbitals, rows, DSTEP), bf16),
    )

    def inner(own, bfac):
        below = lax.ppermute(own, "wide", [(i, i + 1) for i in range(0, n, 2)])
        other = lax.ppermute(bfac, "wide", fast)
        return call(
            inner_kernel,
            inner_outs,
            [SMEM, SMEM, HBM, HBM],
            (HBM, HBM, VMEM, VMEM),
            [
                pltpu.VMEM((2, orbitals, rows, fitting), bf16),
                pltpu.VMEM((2, rows, orbitals, fitting), bf16),
                pltpu.VMEM((7, rows, rows), f32),
                dma((11,)),
            ],
            12 * rows * rows * orbitals * DOM,
            25 * 2**20,
            vmem=44,
        )(own, below, bfac, other)

    def unused(own, bfac):
        return tuple(jnp.zeros(o.shape, o.dtype) for o in inner_outs)

    own, bfac, _ = lax.optimization_barrier((own, bfac, second))
    kband, kmirror, mine, extra = lax.cond(own[0, 0] >= 0, inner, unused, own, bfac)

    below = first_got[orbitals * rows : orbitals * rows + 8, :DSTEP].astype(jnp.int32)
    back, near, case = call(
        functools.partial(upper_first_kernel, n),
        (square, square, shape((1,), jnp.int32)),
        [SMEM, SMEM, VMEM, VMEM],
        (VMEM, VMEM, SMEM),
        [],
        2**31,
        2**22,
    )(own, below, first_got, mine)
    back_got = lax.ppermute(back, "wide", downward)

    def nothing(own, below, extra, mine):
        return jnp.zeros((rows, rows), f32)

    def rest(lower, count):
        def branch(own, below, extra, mine):
            got = lax.ppermute(extra[:count], "wide", [(lower, lower + 1)])
            return call(rest_kernel, square, [SMEM, SMEM, VMEM, VMEM], VMEM, [], 2**26 * count, 2**19 * count)(
                own, below, got, mine
            )

        return branch

    branches = [nothing] + [rest(i, c) for i in range(1, n - 1, 2) for c in LEVELS]
    more = lax.switch(case[0], branches, own, below, extra, mine)

    results = call(
        upper_second_kernel,
        shape((2, rows, rows), f32),
        [SMEM, SMEM, VMEM, VMEM, VMEM, VMEM],
        VMEM,
        [],
        2**30,
        2**22,
    )(own, below, second_got, mine, near, more)
    results_got = lax.ppermute(results, "wide", downward)
    kband, kmirror = call(
        middle_kernel,
        inner_outs[:2],
        [VMEM, VMEM, VMEM, HBM, HBM],
        (HBM, HBM),
        [pltpu.VMEM((3, rows, rows), f32), dma((3,))],
        0,
        2**21,
        {3: 0, 4: 1},
    )(back_got, back, results, kband, kmirror)
    kband = call(last_kernel, inner_outs[0], [VMEM, HBM], HBM, [dma((2,))], 0, 2**20, {1: 0})(results_got, kband)
    return kband, kmirror


def solution(mesh):
    placed = (P("wide", None, "groups", None), P("wide", None), P("wide", None))
    return jax.shard_map(
        per_device,
        mesh=mesh,
        in_specs=placed,
        out_specs=(
            P(("groups", "wide"), None, None, None),
            P(("groups", "wide"), None, None, None),
        ),
        check_vma=False,
    )
```

```python
import functools

import jax
import jax.numpy as jnp
from jax import lax
from jax.experimental import pallas as pl
from jax.experimental.pallas import tpu as pltpu
from jax.sharding import PartitionSpec as P

DOM = 2048
DSTEP = 128
UNITS = DOM // DSTEP
LEVELS = (2, 4, 6, 8, 12, 16)
PER = 12
NOTE = 16
STEPS = 32767.0
VMEM = pl.BlockSpec(memory_space=pltpu.VMEM)
SMEM = pl.BlockSpec(memory_space=pltpu.SMEM)
HBM = pl.BlockSpec(memory_space=pltpu.HBM)


def flags(screen, block, r):
    at = block * 3 + r
    return screen[0, at], screen[0, at + PER // 2]


def boundary(get):
    m1, s1 = get(0, 2)
    m2, s2 = get(1, 1)
    m3, s3 = get(1, 2)
    first = jnp.where(m3 > 0, s3, s2)
    low = jnp.where(first <= s2, jnp.maximum(s2, first + UNITS), s2)
    high = jnp.where(first <= s2, s2 + UNITS, jnp.minimum(s2 + UNITS, first))
    rest = jnp.maximum(high - low, 0) * m2
    second = jnp.where(m1 > 0, s1, jnp.minimum(low, UNITS))
    return dict(m1=m1, s1=s1, m2=m2, s2=s2, m3=m3, s3=s3, first=first, low=low, rest=rest, second=second)


def position():
    me = lax.axis_index("wide")
    return me, lax.rem(me, 2) == 1


def slow_boundary(own, below):
    _, is_odd = position()

    def get(block, r):
        return tuple(jnp.where(is_odd, a, b) for a, b in zip(flags(own, block, r), flags(below, block, r)))

    return boundary(get)


def lanes(unit, count=1):
    return pl.ds(pl.multiple_of(unit * DSTEP, DSTEP), count * DSTEP)


def counted(unit, first, last):
    at = unit + lax.shift_right_logical(lax.broadcasted_iota(jnp.int32, (1, DOM), 1), DSTEP.bit_length() - 1)
    return jnp.where((at >= first) & (at < last), 1.0, 0.0).astype(jnp.bfloat16)


def times(left, right):
    return lax.dot_general(left, right, (((1,), (1,)), ((), ())), preferred_element_type=jnp.float32)


def swapped(values):
    return jnp.swapaxes(values, 0, 1)


def run(copies):
    for c in copies:
        c.start()
    for c in copies:
        c.wait()


def load_parts(block, raw, sems):
    parts = sems.shape[0]
    step = raw.shape[0] // parts
    return [
        pltpu.make_async_copy(block.at[pl.ds(q * step, step)], raw.at[pl.ds(q * step, step)], sems.at[q])
        for q in range(parts)
    ]


def first_kernel(pair_mask, dom_start, bfac, out, own, raw, made, sems, out_sems):
    _, is_odd = position()
    rows = raw.shape[0]
    column = lax.broadcasted_iota(jnp.int32, own.shape, 1)
    value = jnp.zeros(own.shape, jnp.int32)
    for at in range(PER):
        source = pair_mask if at < PER // 2 else dom_start
        block, r = divmod(at % (PER // 2), 3)
        value = jnp.where(column == at, source[block, r], value)
    own[...] = value

    @pl.when(is_odd)
    def _():
        loads = load_parts(bfac.at[1], raw, sems)
        for c in loads:
            c.start()
        at = boundary(lambda block, r: (pair_mask[block, r], dom_start[block, r]))["first"]
        stores = []

        def store(first, count):
            piece = pl.ds(first, count)
            c = pltpu.make_async_copy(made.at[piece], out.at[piece], out_sems.at[len(stores)])
            c.start()
            stores.append(c)

        made[2 * rows :, :] = jnp.zeros((NOTE, DOM), made.dtype)
        made[2 * rows :, :DSTEP] = jnp.concatenate([value, value], 0).astype(jnp.float32).astype(made.dtype)
        store(2 * rows, NOTE)
        step = rows // len(loads)
        for q, c in enumerate(loads):
            c.wait()
            part = swapped(raw[pl.ds(q * step, step), :, lanes(at, UNITS)])
            for i in range(2):
                made[pl.ds(i * rows + q * step, step), :] = part[i]
                store(i * rows + q * step, step)
        for c in stores:
            c.wait()


def second_kernel(own, bfac, out, raw, sems):
    _, is_odd = position()

    @pl.when(is_odd)
    def _():
        b = boundary(lambda block, r: flags(own, block, r))
        loads = load_parts(bfac.at[jnp.where(b["m1"] > 0, 0, 1)], raw, sems)
        for c in loads:
            c.start()
        step = raw.shape[0] // len(loads)
        for q, c in enumerate(loads):
            c.wait()
            rows = pl.ds(q * step, step)
            out[:, rows, :] = swapped(raw[rows, :, lanes(b["second"], UNITS)])


def inner_kernel(own, below, bfac, other, kband, kmirror, mine, extra, theirs, raw, out, sems):
    _, is_odd = position()
    total = bfac.shape[3] // DSTEP
    sources = [(bfac, 0, mine), (bfac, 1, mine), (other, 0, theirs), (other, 1, theirs)]
    loads = [
        pltpu.make_async_copy(source.at[b], raw.at[k % 2], sems.at[k]) for k, (source, b, _) in enumerate(sources)
    ]
    step = 32

    def relayout(k):
        _, b, target = sources[k]
        loads[k].wait()

        def some(q, carry):
            rows = pl.ds(pl.multiple_of(q * step, step), step)
            target[b, :, rows, :] = swapped(raw[k % 2, rows])
            return carry

        lax.fori_loop(0, bfac.shape[1] // step, some, 0)
        if k + 2 < len(loads):
            loads[k + 2].start()

    loads[0].start()
    loads[1].start()

    def product(left, a, right, b, at, keep):
        value = sum(times(left[a, i, :, lanes(at, UNITS)], right[b, i, :, lanes(at, UNITS)]) for i in range(2))
        return value * keep.astype(jnp.float32)

    stores = []

    def store(slot, value, ref, index):
        out[slot] = value
        c = pltpu.make_async_copy(out.at[slot], ref.at[index], sems.at[4 + slot])
        c.start()
        stores.append(c)

    relayout(0)
    relayout(1)
    k, s = flags(own, 0, 0)
    store(0, product(mine, 0, mine, 0, s, k), kband, (0, 0))
    k, s = flags(own, 0, 1)
    value = product(mine, 0, mine, 1, s, k)
    store(1, value, kband, (0, 1))
    store(2, value.T, kmirror, (1, 0))
    k, s = flags(own, 1, 0)
    store(3, product(mine, 1, mine, 1, s, k), kband, (1, 0))

    @pl.when(is_odd)
    def _():
        low = boundary(lambda block, r: flags(own, block, r))["low"]

        def some(u, carry):
            for i in range(2):
                extra[i, :, lanes(u)] = mine[1, i, :, lanes(jnp.minimum(low + u, total - 1))]
            return carry

        lax.fori_loop(0, UNITS, some, 0)

    relayout(2)
    relayout(3)

    def get(block, r):
        return tuple(jnp.where(is_odd, a, b) for a, b in zip(flags(below, block, r), flags(own, block, r)))

    b = boundary(get)
    close = jnp.where(is_odd, 0, 1)
    pick = lambda x, y: jnp.where(is_odd, x, y)
    out[4] = product(mine, 1 - close, theirs, 1 - close, pick(b["s3"], b["s1"]), pick(b["m3"], b["m1"]))
    out[5] = product(mine, close, theirs, 1 - close, b["s2"], b["m2"])
    out[6] = product(mine, close, theirs, close, pick(b["s1"], b["s3"]), pick(b["m1"], b["m3"]))

    def put(targets):
        run([pltpu.make_async_copy(out.at[4 + j], ref, sems.at[8 + j]) for j, ref in enumerate(targets)])

    @pl.when(is_odd)
    def _():
        put([kmirror.at[1, 1], kmirror.at[0, 0], kmirror.at[0, 1]])

    @pl.when(jnp.logical_not(is_odd))
    def _():
        put([kband.at[0, 2], kband.at[1, 1], kband.at[1, 2]])

    for c in stores:
        c.wait()


def upper_first_kernel(n, own, below, got, mine, back, near, second, rest, case, far_window, near_window, sems):
    me, is_odd = position()
    b = slow_boundary(own, below)
    exists = jnp.where(is_odd, me < n - 1, me > 0)
    level = sum((b["rest"] > c).astype(jnp.int32) for c in LEVELS[:-1])
    which = lax.shift_right_logical(jnp.where(is_odd, me, me - 1) - 1, 1)
    case[0] = jnp.where(exists & (b["rest"] * b["m1"] > 0), 1 + which * len(LEVELS) + level, 0)

    @pl.when(jnp.logical_not(is_odd))
    def _():
        rows = mine.shape[2]
        low_at = jnp.minimum(b["low"], UNITS)
        at = b["first"]
        loads = [
            pltpu.make_async_copy(mine.at[1, :, :, lanes(at, UNITS)], far_window, sems.at[0]),
            pltpu.make_async_copy(mine.at[0, :, :, lanes(at, UNITS)], near_window, sems.at[1]),
            pltpu.make_async_copy(mine.at[0, :, :, lanes(b["second"], UNITS)], second, sems.at[2]),
        ]
        for c in loads:
            c.start()
        left = [got[pl.ds(i * rows, rows), :] for i in range(2)]
        loads[0].wait()
        back[...] = sum(times(left[i], far_window[i]) for i in range(2)) * b["m3"].astype(jnp.float32)
        last = pltpu.make_async_copy(mine.at[0, :, :, lanes(low_at, UNITS)], far_window, sems.at[3])
        last.start()
        loads[1].wait()
        counts = counted(at, b["s2"], b["s2"] + UNITS * b["m2"])
        near[...] = sum(times(left[i], near_window[i] * counts) for i in range(2))
        loads[2].wait()
        far_lives = b["m1"] > 0
        counts = counted(
            b["second"],
            jnp.where(far_lives, b["second"], b["low"]),
            jnp.where(far_lives, b["second"] + UNITS, b["low"] + b["rest"]),
        )
        for i in range(2):
            second[i] = second[i] * counts
        last.wait()

        def some(u, carry):
            alive = jnp.where(u < b["rest"], 1.0, 0.0).astype(rest.dtype)
            for i in range(2):
                rest[i, :, lanes(u)] = far_window[i, :, lanes(jnp.minimum(b["low"] - low_at + u, UNITS - 1))] * alive
            return carry

        lax.fori_loop(0, UNITS, some, 0)


def rest_kernel(got, rest, out):
    width = got.shape[2]
    out[...] = sum(times(got[i], rest[i, :, :width]) for i in range(2))


def coded(value):
    top = jnp.maximum(jnp.max(jnp.abs(value), axis=0, keepdims=True), 1e-30)
    power = jnp.ceil(jnp.log2(top)) - 14.0
    whole = jnp.clip(jnp.ceil(top / jnp.exp2(power)), 1.0, STEPS)
    steps = jnp.round(value * (STEPS / (whole * jnp.exp2(power))))
    return jnp.clip(steps, -STEPS, STEPS), whole, power


def decoded(steps, whole, power):
    return steps * (whole * jnp.exp2(power) * (1.0 / STEPS))


def whole_numbers(value):
    return value.astype(jnp.int32).astype(jnp.int16)


def upper_second_kernel(own, below, got, second, back, near, more, results, sent):
    _, is_odd = position()

    @pl.when(jnp.logical_not(is_odd))
    def _():
        b = slow_boundary(own, below)
        rows = back.shape[0]
        value = sum(times(got[i], second[i]) for i in range(2))
        lives = b["m1"].astype(jnp.float32)
        results[0] = value * lives
        results[1] = near[...] + more[...] + value * (1.0 - lives)
        row = lax.broadcasted_iota(jnp.int32, (NOTE, rows), 0)
        scales = jnp.zeros((NOTE, rows), jnp.float32)
        for k, block in enumerate((results[0], results[1], back[...])):
            steps, whole, power = coded(block)
            sent[pl.ds(k * rows, rows), :] = whole_numbers(steps)
            scales = jnp.where(row == 2 * k, whole, jnp.where(row == 2 * k + 1, power, scales))
        sent[pl.ds(3 * rows, NOTE), :] = whole_numbers(scales)


def middle_kernel(back, results, kmirror_in, kmirror, out, sems):
    _, is_odd = position()

    @pl.when(jnp.logical_not(is_odd))
    def _():
        out[0] = back[...].T
        out[1] = results[0].T
        out[2] = results[1].T
        targets = [kmirror.at[1, 1], kmirror.at[0, 1], kmirror.at[0, 0]]
        run([pltpu.make_async_copy(out.at[j], ref, sems.at[j]) for j, ref in enumerate(targets)])


def last_kernel(got, kband_in, kband, out, sems):
    _, is_odd = position()

    @pl.when(is_odd)
    def _():
        rows = out.shape[1]
        scales = got[pl.ds(3 * rows, NOTE), :].astype(jnp.int32).astype(jnp.float32)
        copies = []
        for k, ref in enumerate((kband.at[0, 2], kband.at[1, 1], kband.at[1, 2])):
            steps = got[pl.ds(k * rows, rows), :].astype(jnp.int32).astype(jnp.float32)
            out[k] = decoded(steps, scales[2 * k : 2 * k + 1], scales[2 * k + 1 : 2 * k + 2])
            copies.append(pltpu.make_async_copy(out.at[k], ref, sems.at[k]))
            copies[-1].start()
        for c in copies:
            c.wait()


def call(kernel, outs, ins, out_specs, scratch, flops=0, moved=0, aliases=None, vmem=40):
    inner = kernel.func if isinstance(kernel, functools.partial) else kernel
    return pl.pallas_call(
        kernel,
        out_shape=outs,
        in_specs=ins,
        out_specs=out_specs,
        scratch_shapes=scratch,
        input_output_aliases=aliases or {},
        compiler_params=pltpu.CompilerParams(vmem_limit_bytes=vmem * 2**20),
        cost_estimate=pl.CostEstimate(flops=flops, bytes_accessed=moved, transcendentals=0),
        name=inner.__name__,
    )


def per_device(bfac, pair_mask, dom_start):
    n = lax.axis_size("wide")
    _, rows, orbitals, fitting = bfac.shape
    upward = [(i, i + 1) for i in range(1, n - 1, 2)]
    downward = [(j, i) for i, j in upward]
    fast = [p for i in range(0, n, 2) for p in ((i, i + 1), (i + 1, i))]
    f32, bf16 = jnp.float32, bfac.dtype
    shape = jax.ShapeDtypeStruct
    dma = pltpu.SemaphoreType.DMA
    square = shape((rows, rows), f32)
    window = shape((orbitals, rows, DOM), bf16)
    raw_block = pltpu.VMEM((rows, orbitals, fitting), bf16)

    parts = 8
    whole = (orbitals * rows + NOTE, DOM)
    first, own = call(
        first_kernel,
        (shape(whole, bf16), shape((8, 128), jnp.int32)),
        [SMEM, SMEM, HBM],
        (HBM, VMEM),
        [raw_block, pltpu.VMEM(whole, bf16), dma((parts,)), dma((2 * parts + 1,))],
        vmem=60,
    )(pair_mask, dom_start, bfac)
    first_got = lax.ppermute(first, "wide", upward)

    second = call(second_kernel, window, [SMEM, HBM], VMEM, [raw_block, dma((4,))], vmem=56)(own, bfac)
    second_got = lax.ppermute(second, "wide", upward)

    inner_outs = (
        shape((2, 3, rows, rows), f32),
        shape((2, 2, rows, rows), f32),
        shape((2, orbitals, rows, fitting), bf16),
        window,
    )

    def inner(own, bfac):
        below = lax.ppermute(own, "wide", [(i, i + 1) for i in range(0, n, 2)])
        other = lax.ppermute(bfac, "wide", fast)
        return call(
            inner_kernel,
            inner_outs,
            [SMEM, SMEM, HBM, HBM],
            (HBM, HBM, VMEM, VMEM),
            [
                pltpu.VMEM((2, orbitals, rows, fitting), bf16),
                pltpu.VMEM((2, rows, orbitals, fitting), bf16),
                pltpu.VMEM((7, rows, rows), f32),
                dma((11,)),
            ],
            12 * rows * rows * orbitals * DOM,
            25 * 2**20,
            vmem=44,
        )(own, below, bfac, other)

    def unused(own, bfac):
        return tuple(jnp.zeros(o.shape, o.dtype) for o in inner_outs)

    own, bfac, _ = lax.optimization_barrier((own, bfac, second))
    kband, kmirror, mine, extra = lax.cond(own[0, 0] >= 0, inner, unused, own, bfac)

    below = first_got[orbitals * rows : orbitals * rows + 8, :DSTEP].astype(jnp.int32)
    back, near, second_window, rest_window, case = call(
        functools.partial(upper_first_kernel, n),
        (square, square, window, window, shape((1,), jnp.int32)),
        [SMEM, SMEM, VMEM, HBM],
        (VMEM, VMEM, VMEM, VMEM, SMEM),
        [pltpu.VMEM((orbitals, rows, DOM), bf16), pltpu.VMEM((orbitals, rows, DOM), bf16), dma((4,))],
        2**31,
        2**22,
        vmem=20,
    )(own, below, first_got, mine)

    def nothing(extra, rest_window):
        return jnp.zeros((rows, rows), f32)

    def rest(lower, count):
        def branch(extra, rest_window):
            got = lax.ppermute(extra[:, :, : count * DSTEP], "wide", [(lower, lower + 1)])
            return call(rest_kernel, square, [VMEM, VMEM], VMEM, [], 2**26 * count, 2**19 * count, vmem=16)(
                got, rest_window
            )

        return branch

    branches = [nothing] + [rest(i, c) for i in range(1, n - 1, 2) for c in LEVELS]
    more = lax.switch(case[0], branches, extra, rest_window)

    results, sent = call(
        upper_second_kernel,
        (shape((2, rows, rows), f32), shape((3 * rows + NOTE, rows), jnp.int16)),
        [SMEM, SMEM, VMEM, VMEM, VMEM, VMEM, VMEM],
        (VMEM, VMEM),
        [],
        2**30,
        2**22,
        vmem=20,
    )(own, below, second_got, second_window, back, near, more)
    sent_got = lax.ppermute(sent, "wide", downward)
    kmirror = call(
        middle_kernel,
        inner_outs[1],
        [VMEM, VMEM, HBM],
        HBM,
        [pltpu.VMEM((3, rows, rows), f32), dma((3,))],
        0,
        2**20,
        {2: 0},
        vmem=62,
    )(back, results, kmirror)
    kband = call(
        last_kernel,
        inner_outs[0],
        [VMEM, HBM],
        HBM,
        [pltpu.VMEM((3, rows, rows), f32), dma((3,))],
        0,
        2**20,
        {1: 0},
        vmem=62,
    )(sent_got, kband)
    return kband, kmirror


def solution(mesh):
    placed = (P("wide", None, "groups", None), P("wide", None), P("wide", None))
    return jax.shard_map(
        per_device,
        mesh=mesh,
        in_specs=placed,
        out_specs=(
            P(("groups", "wide"), None, None, None),
            P(("groups", "wide"), None, None, None),
        ),
        check_vma=False,
    )
```

```python
import functools

import jax
import jax.numpy as jnp
from jax import lax
from jax.experimental import pallas as pl
from jax.experimental.pallas import tpu as pltpu
from jax.sharding import PartitionSpec as P

DOM = 2048
DSTEP = 128
UNITS = DOM // DSTEP
LEVELS = (1, 2, 3, 4, 6, 8)
SPARE = 8
PER = 12
NOTE = 16
STEPS = 32767.0
VMEM = pl.BlockSpec(memory_space=pltpu.VMEM)
SMEM = pl.BlockSpec(memory_space=pltpu.SMEM)
HBM = pl.BlockSpec(memory_space=pltpu.HBM)


def flags(screen, block, r):
    at = block * 3 + r
    return screen[0, at], screen[0, at + PER // 2]


def boundary(get):
    m1, s1 = get(0, 2)
    m2, s2 = get(1, 1)
    m3, s3 = get(1, 2)
    first = jnp.where(m3 > 0, s3, s2)
    low = jnp.where(first <= s2, jnp.maximum(s2, first + UNITS), s2)
    high = jnp.where(first <= s2, s2 + UNITS, jnp.minimum(s2 + UNITS, first))
    rest = jnp.maximum(high - low, 0) * m2
    second = jnp.where(m1 > 0, s1, jnp.minimum(low, UNITS))
    split = rest * m1
    half = lax.shift_right_logical(split + 1, 1)
    return dict(
        m1=m1, s1=s1, m2=m2, s2=s2, m3=m3, s3=s3, first=first, low=low, rest=rest, second=second, split=split, half=half
    )


def position():
    me = lax.axis_index("wide")
    return me, lax.rem(me, 2) == 1


def slow_boundary(own, below):
    _, is_odd = position()

    def get(block, r):
        return tuple(jnp.where(is_odd, a, b) for a, b in zip(flags(own, block, r), flags(below, block, r)))

    return boundary(get)


def lanes(unit, count=1):
    return pl.ds(pl.multiple_of(unit * DSTEP, DSTEP), count * DSTEP)


def counted(unit, first, last):
    at = unit + lax.shift_right_logical(lax.broadcasted_iota(jnp.int32, (1, DOM), 1), DSTEP.bit_length() - 1)
    return jnp.where((at >= first) & (at < last), 1.0, 0.0).astype(jnp.bfloat16)


def times(left, right):
    return lax.dot_general(left, right, (((1,), (1,)), ((), ())), preferred_element_type=jnp.float32)


def swapped(values):
    return jnp.swapaxes(values, 0, 1)


def run(copies):
    for c in copies:
        c.start()
    for c in copies:
        c.wait()


def load_parts(block, raw, sems):
    parts = sems.shape[0]
    step = raw.shape[0] // parts
    return [
        pltpu.make_async_copy(block.at[pl.ds(q * step, step)], raw.at[pl.ds(q * step, step)], sems.at[q])
        for q in range(parts)
    ]


def first_kernel(pair_mask, dom_start, bfac, out, own, raw, made, sems, out_sems):
    _, is_odd = position()
    rows = raw.shape[0]
    column = lax.broadcasted_iota(jnp.int32, own.shape, 1)
    value = jnp.zeros(own.shape, jnp.int32)
    for at in range(PER):
        source = pair_mask if at < PER // 2 else dom_start
        block, r = divmod(at % (PER // 2), 3)
        value = jnp.where(column == at, source[block, r], value)
    own[...] = value

    @pl.when(is_odd)
    def _():
        loads = load_parts(bfac.at[1], raw, sems)
        for c in loads:
            c.start()
        at = boundary(lambda block, r: (pair_mask[block, r], dom_start[block, r]))["first"]
        stores = []

        def store(first, count):
            piece = pl.ds(first, count)
            c = pltpu.make_async_copy(made.at[piece], out.at[piece], out_sems.at[len(stores)])
            c.start()
            stores.append(c)

        made[2 * rows :, :] = jnp.zeros((NOTE, DOM), made.dtype)
        made[2 * rows :, :DSTEP] = jnp.concatenate([value, value], 0).astype(jnp.float32).astype(made.dtype)
        store(2 * rows, NOTE)
        step = rows // len(loads)
        for q, c in enumerate(loads):
            c.wait()
            part = swapped(raw[pl.ds(q * step, step), :, lanes(at, UNITS)])
            for i in range(2):
                made[pl.ds(i * rows + q * step, step), :] = part[i]
                store(i * rows + q * step, step)
        for c in stores:
            c.wait()


def second_kernel(own, bfac, out, raw, sems):
    _, is_odd = position()

    @pl.when(is_odd)
    def _():
        b = boundary(lambda block, r: flags(own, block, r))
        loads = load_parts(bfac.at[jnp.where(b["m1"] > 0, 0, 1)], raw, sems)
        for c in loads:
            c.start()
        step = raw.shape[0] // len(loads)
        for q, c in enumerate(loads):
            c.wait()
            rows = pl.ds(q * step, step)
            out[:, rows, :] = swapped(raw[rows, :, lanes(b["second"], UNITS)])


def relayouter(bfac, raw, target, loads):
    step = 32

    def relayout(b):
        loads[b].wait()

        def some(q, carry):
            rows = pl.ds(pl.multiple_of(q * step, step), step)
            target[b, :, rows, :] = swapped(raw[b, rows])
            return carry

        lax.fori_loop(0, bfac.shape[1] // step, some, 0)

    return relayout


def product(left, a, right, b, at, keep):
    value = sum(times(left[a, i, :, lanes(at, UNITS)], right[b, i, :, lanes(at, UNITS)]) for i in range(2))
    return value * keep.astype(jnp.float32)


def own_kernel(own, bfac, kband, kmirror, mine, held, raw, out, sems):
    loads = [pltpu.make_async_copy(bfac.at[b], raw.at[b], sems.at[b]) for b in range(2)]
    relayout = relayouter(bfac, raw, held, loads)
    stores = []

    def store(source, target):
        c = pltpu.make_async_copy(source, target, sems.at[2 + len(stores)])
        c.start()
        stores.append(c)

    def keep(slot, value, target):
        out[slot] = value
        store(out.at[slot], target)

    for c in loads:
        c.start()
    for b in range(2):
        relayout(b)
        store(held.at[b], mine.at[b])
    k, s = flags(own, 0, 0)
    keep(0, product(held, 0, held, 0, s, k), kband.at[0, 0])
    k, s = flags(own, 0, 1)
    value = product(held, 0, held, 1, s, k)
    keep(1, value, kband.at[0, 1])
    keep(2, value.T, kmirror.at[1, 0])
    k, s = flags(own, 1, 0)
    keep(3, product(held, 1, held, 1, s, k), kband.at[1, 0])
    for c in stores:
        c.wait()


def fast_kernel(own, below, mine, other, kband_in, kmirror_in, kband, kmirror, held, theirs, raw, out, sems):
    _, is_odd = position()
    loads = [pltpu.make_async_copy(other.at[b], raw.at[b], sems.at[b]) for b in range(2)]
    held_load = pltpu.make_async_copy(mine, held, sems.at[2])
    relayout = relayouter(other, raw, theirs, loads)
    for c in (*loads, held_load):
        c.start()

    def get(block, r):
        return tuple(jnp.where(is_odd, a, b) for a, b in zip(flags(below, block, r), flags(own, block, r)))

    b = boundary(get)
    relayout(0)
    relayout(1)
    held_load.wait()
    close = jnp.where(is_odd, 0, 1)
    pick = lambda x, y: jnp.where(is_odd, x, y)
    out[0] = product(held, 1 - close, theirs, 1 - close, pick(b["s3"], b["s1"]), pick(b["m3"], b["m1"]))
    out[1] = product(held, close, theirs, 1 - close, b["s2"], b["m2"])
    out[2] = product(held, close, theirs, close, pick(b["s1"], b["s3"]), pick(b["m1"], b["m3"]))

    def put(targets):
        run([pltpu.make_async_copy(out.at[j], ref, sems.at[3 + j]) for j, ref in enumerate(targets)])

    @pl.when(is_odd)
    def _():
        put([kmirror.at[1, 1], kmirror.at[0, 0], kmirror.at[0, 1]])

    @pl.when(jnp.logical_not(is_odd))
    def _():
        put([kband.at[0, 2], kband.at[1, 1], kband.at[1, 2]])


def first_products_kernel(
    n, own, below, got, mine, back, near, second, extra, rest, case, far_window, near_window, staged, sems
):
    me, is_odd = position()
    b = slow_boundary(own, below)
    exists = jnp.where(is_odd, me < n - 1, me > 0)
    level = sum((b["half"] > c).astype(jnp.int32) for c in LEVELS[:-1])
    which = lax.shift_right_logical(jnp.where(is_odd, me, me - 1) - 1, 1)
    splits = exists & (b["split"] > 0)
    case[0] = jnp.where(splits, 1 + which * len(LEVELS) + level, 0)
    case[1] = jnp.where(splits, 1 + which, 0)

    @pl.when(splits)
    def _():
        at = jnp.minimum(b["low"], UNITS)
        run([pltpu.make_async_copy(mine.at[jnp.where(is_odd, 1, 0), :, :, lanes(at, UNITS)], staged, sems.at[3])])
        lower, upper = b["low"] - at, b["low"] - at + b["half"]
        sent = jnp.where(is_odd, lower, upper)
        kept = jnp.where(is_odd, upper, lower)
        count = jnp.where(is_odd, b["split"] - b["half"], b["half"])

        def some(u, carry):
            alive = jnp.where(u < count, 1.0, 0.0).astype(rest.dtype)
            for i in range(2):
                extra[i, :, lanes(u)] = staged[i, :, lanes(jnp.minimum(sent + u, UNITS - 1))]
                rest[i, :, lanes(u)] = staged[i, :, lanes(jnp.minimum(kept + u, UNITS - 1))] * alive
            return carry

        lax.fori_loop(0, SPARE, some, 0)

    @pl.when(jnp.logical_not(is_odd))
    def _():
        rows = mine.shape[2]
        at = b["first"]
        loads = [
            pltpu.make_async_copy(mine.at[1, :, :, lanes(at, UNITS)], far_window, sems.at[0]),
            pltpu.make_async_copy(mine.at[0, :, :, lanes(at, UNITS)], near_window, sems.at[1]),
            pltpu.make_async_copy(mine.at[0, :, :, lanes(b["second"], UNITS)], second, sems.at[2]),
        ]
        for c in loads:
            c.start()
        left = [got[pl.ds(i * rows, rows), :] for i in range(2)]
        loads[0].wait()
        back[...] = sum(times(left[i], far_window[i]) for i in range(2)) * b["m3"].astype(jnp.float32)
        loads[1].wait()
        counts = counted(at, b["s2"], b["s2"] + UNITS * b["m2"])
        near[...] = sum(times(left[i], near_window[i] * counts) for i in range(2))
        loads[2].wait()
        far_lives = b["m1"] > 0
        counts = counted(
            b["second"],
            jnp.where(far_lives, b["second"], b["low"]),
            jnp.where(far_lives, b["second"] + UNITS, b["low"] + b["rest"]),
        )
        for i in range(2):
            second[i] = second[i] * counts


def rest_kernel(got, rest, out):
    _, is_odd = position()
    width = got.shape[2]

    @pl.when(is_odd)
    def _():
        out[...] = sum(times(rest[i, :, :width], got[i]) for i in range(2))

    @pl.when(jnp.logical_not(is_odd))
    def _():
        out[...] = sum(times(got[i], rest[i, :, :width]) for i in range(2))


def coded(value):
    top = jnp.maximum(jnp.max(jnp.abs(value), axis=0, keepdims=True), 1e-30)
    power = jnp.ceil(jnp.log2(top)) - 14.0
    whole = jnp.clip(jnp.ceil(top / jnp.exp2(power)), 1.0, STEPS)
    steps = jnp.round(value * (STEPS / (whole * jnp.exp2(power))))
    return jnp.clip(steps, -STEPS, STEPS), whole, power


def decoded(steps, whole, power):
    return steps * (whole * jnp.exp2(power) * (1.0 / STEPS))


def whole_numbers(value):
    return value.astype(jnp.int32).astype(jnp.int16)


def second_products_kernel(own, below, got, second, back, near, more, results, part, sent):
    _, is_odd = position()

    @pl.when(is_odd)
    def _():
        part[...] = more[...]

    @pl.when(jnp.logical_not(is_odd))
    def _():
        b = slow_boundary(own, below)
        rows = back.shape[0]
        value = sum(times(got[i], second[i]) for i in range(2))
        lives = b["m1"].astype(jnp.float32)
        results[...] = value * lives
        part[...] = near[...] + more[...] + value * (1.0 - lives)
        row = lax.broadcasted_iota(jnp.int32, (NOTE, rows), 0)
        scales = jnp.zeros((NOTE, rows), jnp.float32)
        for k, block in enumerate((results[...], part[...], back[...])):
            steps, whole, power = coded(block)
            sent[pl.ds(k * rows, rows), :] = whole_numbers(steps)
            scales = jnp.where(row == 2 * k, whole, jnp.where(row == 2 * k + 1, power, scales))
        sent[pl.ds(3 * rows, NOTE), :] = whole_numbers(scales)


def mirror_kernel(back, results, kmirror_in, kmirror, out, sems):
    _, is_odd = position()

    @pl.when(jnp.logical_not(is_odd))
    def _():
        out[0] = back[...].T
        out[1] = results[...].T
        targets = [kmirror.at[1, 1], kmirror.at[0, 1]]
        run([pltpu.make_async_copy(out.at[j], ref, sems.at[j]) for j, ref in enumerate(targets)])


def last_kernel(case, got, part, other, kband_in, kmirror_in, kband, kmirror, out, sems):
    _, is_odd = position()

    @pl.when(is_odd)
    def _():
        rows = out.shape[1]
        scales = got[pl.ds(3 * rows, NOTE), :].astype(jnp.int32).astype(jnp.float32)
        copies = []
        for k, ref in enumerate((kband.at[0, 2], kband.at[1, 1], kband.at[1, 2])):
            steps = got[pl.ds(k * rows, rows), :].astype(jnp.int32).astype(jnp.float32)
            out[k] = decoded(steps, scales[2 * k : 2 * k + 1], scales[2 * k + 1 : 2 * k + 2])
            if k == 1:

                @pl.when(case[1] > 0)
                def _():
                    out[1] = part[...] + other[...]

            copies.append(pltpu.make_async_copy(out.at[k], ref, sems.at[k]))
            copies[-1].start()
        for c in copies:
            c.wait()

    @pl.when(jnp.logical_not(is_odd))
    def _():
        out[0] = (part[...] + other[...]).T
        run([pltpu.make_async_copy(out.at[0], kmirror.at[0, 0], sems.at[0])])


def call(kernel, outs, ins, out_specs, scratch, flops=0, moved=0, aliases=None, vmem=40):
    inner = kernel.func if isinstance(kernel, functools.partial) else kernel
    return pl.pallas_call(
        kernel,
        out_shape=outs,
        in_specs=ins,
        out_specs=out_specs,
        scratch_shapes=scratch,
        input_output_aliases=aliases or {},
        compiler_params=pltpu.CompilerParams(vmem_limit_bytes=vmem * 2**20),
        cost_estimate=pl.CostEstimate(flops=flops, bytes_accessed=moved, transcendentals=0),
        name=inner.__name__,
    )


def per_device(bfac, pair_mask, dom_start):
    n = lax.axis_size("wide")
    _, rows, orbitals, fitting = bfac.shape
    upward = [(i, i + 1) for i in range(1, n - 1, 2)]
    downward = [(j, i) for i, j in upward]
    fast = [p for i in range(0, n, 2) for p in ((i, i + 1), (i + 1, i))]
    f32, bf16 = jnp.float32, bfac.dtype
    shape = jax.ShapeDtypeStruct
    dma = pltpu.SemaphoreType.DMA
    square = shape((rows, rows), f32)
    window = shape((orbitals, rows, DOM), bf16)
    raw_block = pltpu.VMEM((rows, orbitals, fitting), bf16)

    parts = 8
    whole = (orbitals * rows + NOTE, DOM)
    first, own = call(
        first_kernel,
        (shape(whole, bf16), shape((8, 128), jnp.int32)),
        [SMEM, SMEM, HBM],
        (HBM, VMEM),
        [raw_block, pltpu.VMEM(whole, bf16), dma((parts,)), dma((2 * parts + 1,))],
        vmem=60,
    )(pair_mask, dom_start, bfac)
    first_got = lax.ppermute(first, "wide", upward)

    second = call(second_kernel, window, [SMEM, HBM], VMEM, [raw_block, dma((4,))], vmem=56)(own, bfac)
    second_got = lax.ppermute(second, "wide", upward)

    band = shape((2, 3, rows, rows), f32)
    mirror = shape((2, 2, rows, rows), f32)
    both = shape((2, orbitals, rows, fitting), bf16)
    spare = shape((orbitals, rows, SPARE * DSTEP), bf16)
    blocks = pltpu.VMEM((2, orbitals, rows, fitting), bf16)
    raw_blocks = pltpu.VMEM((2, rows, orbitals, fitting), bf16)

    def inner(own, bfac):
        below = lax.ppermute(own, "wide", [(i, i + 1) for i in range(0, n, 2)])
        other = lax.ppermute(bfac, "wide", fast)
        kband, kmirror, mine = call(
            own_kernel,
            (band, mirror, both),
            [SMEM, HBM],
            (HBM, HBM, HBM),
            [blocks, raw_blocks, pltpu.VMEM((4, rows, rows), f32), dma((8,))],
            2**31,
            2**25,
            vmem=48,
        )(own, bfac)
        kband, kmirror = call(
            fast_kernel,
            (band, mirror),
            [SMEM, SMEM, HBM, HBM, HBM, HBM],
            (HBM, HBM),
            [blocks, blocks, raw_blocks, pltpu.VMEM((3, rows, rows), f32), dma((6,))],
            2**31,
            2**25,
            {4: 0, 5: 1},
            vmem=48,
        )(own, below, mine, other, kband, kmirror)
        return kband, kmirror, mine

    def unused(own, bfac):
        return tuple(jnp.zeros(o.shape, o.dtype) for o in (band, mirror, both))

    own, bfac, _ = lax.optimization_barrier((own, bfac, second))
    kband, kmirror, mine = lax.cond(own[0, 0] >= 0, inner, unused, own, bfac)

    below = first_got[orbitals * rows : orbitals * rows + 8, :DSTEP].astype(jnp.int32)
    staged = pltpu.VMEM((orbitals, rows, DOM), bf16)
    back, near, second_window, extra, rest_window, case = call(
        functools.partial(first_products_kernel, n),
        (square, square, window, spare, spare, shape((2,), jnp.int32)),
        [SMEM, SMEM, VMEM, HBM],
        (VMEM, VMEM, VMEM, VMEM, VMEM, SMEM),
        [staged, staged, staged, dma((4,))],
        2**31,
        2**22,
        vmem=20,
    )(own, below, first_got, mine)

    def nothing(*_):
        return jnp.zeros((rows, rows), f32)

    def pair_of(lower):
        return [(lower, lower + 1), (lower + 1, lower)]

    def rest(lower, count):
        def branch(extra, rest_window):
            got = lax.ppermute(extra[:, :, : count * DSTEP], "wide", pair_of(lower))
            return call(rest_kernel, square, [VMEM, VMEM], VMEM, [], 2**26 * count, 2**19 * count, vmem=16)(
                got, rest_window
            )

        return branch

    def parts_of(lower):
        return lambda part: lax.ppermute(part, "wide", pair_of(lower))

    lowers = range(1, n - 1, 2)
    branches = [nothing] + [rest(i, c) for i in lowers for c in LEVELS]
    more = lax.switch(case[0], branches, extra, rest_window)

    results, part, sent = call(
        second_products_kernel,
        (square, square, shape((3 * rows + NOTE, rows), jnp.int16)),
        [SMEM, SMEM, VMEM, VMEM, VMEM, VMEM, VMEM],
        (VMEM, VMEM, VMEM),
        [],
        2**30,
        2**22,
        vmem=20,
    )(own, below, second_got, second_window, back, near, more)
    sent_got = lax.ppermute(sent, "wide", downward)
    other_part = lax.switch(case[1], [nothing] + [parts_of(i) for i in lowers], part)
    kmirror = call(
        mirror_kernel,
        mirror,
        [VMEM, VMEM, HBM],
        HBM,
        [pltpu.VMEM((2, rows, rows), f32), dma((2,))],
        0,
        2**20,
        {2: 0},
        vmem=16,
    )(back, results, kmirror)
    return call(
        last_kernel,
        (band, mirror),
        [SMEM, VMEM, VMEM, VMEM, HBM, HBM],
        (HBM, HBM),
        [pltpu.VMEM((3, rows, rows), f32), dma((3,))],
        0,
        2**20,
        {4: 0, 5: 1},
        vmem=16,
    )(case, sent_got, part, other_part, kband, kmirror)


def solution(mesh):
    placed = (P("wide", None, "groups", None), P("wide", None), P("wide", None))
    return jax.shard_map(
        per_device,
        mesh=mesh,
        in_specs=placed,
        out_specs=(
            P(("groups", "wide"), None, None, None),
            P(("groups", "wide"), None, None, None),
        ),
        check_vma=False,
    )
```

```python
import functools

import jax
import jax.numpy as jnp
from jax import lax
from jax.experimental import pallas as pl
from jax.experimental.pallas import tpu as pltpu
from jax.sharding import PartitionSpec as P

DOM = 2048
DSTEP = 128
UNITS = DOM // DSTEP
LEVELS = (1, 2, 3, 4, 6, 8)
SPARE = 8
PER = 12
NOTE = 16
STEPS = 32767.0
VMEM = pl.BlockSpec(memory_space=pltpu.VMEM)
SMEM = pl.BlockSpec(memory_space=pltpu.SMEM)
HBM = pl.BlockSpec(memory_space=pltpu.HBM)


def flags(screen, block, r):
    at = block * 3 + r
    return screen[0, at], screen[0, at + PER // 2]


def boundary(get):
    m1, s1 = get(0, 2)
    m2, s2 = get(1, 1)
    m3, s3 = get(1, 2)
    first = jnp.where(m3 > 0, s3, s2)
    low = jnp.where(first <= s2, jnp.maximum(s2, first + UNITS), s2)
    high = jnp.where(first <= s2, s2 + UNITS, jnp.minimum(s2 + UNITS, first))
    rest = jnp.maximum(high - low, 0) * m2
    second = jnp.where(m1 > 0, s1, jnp.minimum(low, UNITS))
    split = rest * m1
    half = lax.shift_right_logical(split + 1, 1)
    return dict(
        m1=m1, s1=s1, m2=m2, s2=s2, m3=m3, s3=s3, first=first, low=low, rest=rest, second=second, split=split, half=half
    )


def position():
    me = lax.axis_index("wide")
    return me, lax.rem(me, 2) == 1


def slow_boundary(own, below):
    _, is_odd = position()

    def get(block, r):
        return tuple(jnp.where(is_odd, a, b) for a, b in zip(flags(own, block, r), flags(below, block, r)))

    return boundary(get)


def lanes(unit, count=1):
    return pl.ds(pl.multiple_of(unit * DSTEP, DSTEP), count * DSTEP)


def counted(unit, first, last):
    at = unit + lax.shift_right_logical(lax.broadcasted_iota(jnp.int32, (1, DOM), 1), DSTEP.bit_length() - 1)
    return jnp.where((at >= first) & (at < last), 1.0, 0.0).astype(jnp.bfloat16)


def times(left, right):
    return lax.dot_general(left, right, (((1,), (1,)), ((), ())), preferred_element_type=jnp.float32)


def swapped(values):
    return jnp.swapaxes(values, 0, 1)


def run(copies):
    for c in copies:
        c.start()
    for c in copies:
        c.wait()


def load_parts(block, raw, sems):
    parts = sems.shape[0]
    step = raw.shape[0] // parts
    return [
        pltpu.make_async_copy(block.at[pl.ds(q * step, step)], raw.at[pl.ds(q * step, step)], sems.at[q])
        for q in range(parts)
    ]


def first_kernel(pair_mask, dom_start, bfac, out, own, zero, raw, sems):
    _, is_odd = position()
    rows = raw.shape[0]
    column = lax.broadcasted_iota(jnp.int32, own.shape, 1)
    value = jnp.zeros(own.shape, jnp.int32)
    for at in range(PER):
        source = pair_mask if at < PER // 2 else dom_start
        block, r = divmod(at % (PER // 2), 3)
        value = jnp.where(column == at, source[block, r], value)
    own[...] = value
    zero[0] = jnp.minimum(pair_mask[0, 0], 0)

    @pl.when(is_odd)
    def _():
        loads = load_parts(bfac.at[1], raw, sems)
        for c in loads:
            c.start()
        at = boundary(lambda block, r: (pair_mask[block, r], dom_start[block, r]))["first"]
        out[2 * rows :, :] = jnp.zeros((NOTE, DOM), out.dtype)
        out[2 * rows :, :DSTEP] = jnp.concatenate([value, value], 0).astype(jnp.float32).astype(out.dtype)
        step = rows // len(loads)
        for q, c in enumerate(loads):
            c.wait()
            part = swapped(raw[pl.ds(q * step, step), :, lanes(at, UNITS)])
            for i in range(2):
                out[pl.ds(i * rows + q * step, step), :] = part[i]


def second_kernel(own, bfac, out, raw, sems):
    _, is_odd = position()

    @pl.when(is_odd)
    def _():
        b = boundary(lambda block, r: flags(own, block, r))
        loads = load_parts(bfac.at[jnp.where(b["m1"] > 0, 0, 1)], raw, sems)
        for c in loads:
            c.start()
        step = raw.shape[0] // len(loads)
        for q, c in enumerate(loads):
            c.wait()
            rows = pl.ds(q * step, step)
            out[:, rows, :] = swapped(raw[rows, :, lanes(b["second"], UNITS)])


def relayouter(bfac, raw, target, loads):
    step = 32

    def relayout(b):
        loads[b].wait()

        def some(q, carry):
            rows = pl.ds(pl.multiple_of(q * step, step), step)
            target[b, :, rows, :] = swapped(raw[b, rows])
            return carry

        lax.fori_loop(0, bfac.shape[1] // step, some, 0)

    return relayout


def product(left, a, right, b, at, keep):
    value = sum(times(left[a, i, :, lanes(at, UNITS)], right[b, i, :, lanes(at, UNITS)]) for i in range(2))
    return value * keep.astype(jnp.float32)


def own_kernel(own, bfac, kband, kmirror, mine, held, raw, out, sems):
    loads = [pltpu.make_async_copy(bfac.at[b], raw.at[b], sems.at[b]) for b in range(2)]
    relayout = relayouter(bfac, raw, held, loads)
    stores = []

    def store(source, target):
        c = pltpu.make_async_copy(source, target, sems.at[2 + len(stores)])
        c.start()
        stores.append(c)

    def keep(slot, value, target):
        out[slot] = value
        store(out.at[slot], target)

    for c in loads:
        c.start()
    for b in range(2):
        relayout(b)
        store(held.at[b], mine.at[b])
    k, s = flags(own, 0, 0)
    keep(0, product(held, 0, held, 0, s, k), kband.at[0, 0])
    k, s = flags(own, 0, 1)
    value = product(held, 0, held, 1, s, k)
    keep(1, value, kband.at[0, 1])
    keep(2, value.T, kmirror.at[1, 0])
    k, s = flags(own, 1, 0)
    keep(3, product(held, 1, held, 1, s, k), kband.at[1, 0])
    for c in stores:
        c.wait()


def fast_kernel(own, below, mine, other, kband_in, kmirror_in, kband, kmirror, held, theirs, raw, out, sems):
    _, is_odd = position()
    loads = [pltpu.make_async_copy(other.at[b], raw.at[b], sems.at[b]) for b in range(2)]
    held_load = pltpu.make_async_copy(mine, held, sems.at[2])
    relayout = relayouter(other, raw, theirs, loads)
    for c in (*loads, held_load):
        c.start()

    def get(block, r):
        return tuple(jnp.where(is_odd, a, b) for a, b in zip(flags(below, block, r), flags(own, block, r)))

    b = boundary(get)
    relayout(0)
    relayout(1)
    held_load.wait()
    close = jnp.where(is_odd, 0, 1)
    pick = lambda x, y: jnp.where(is_odd, x, y)
    out[0] = product(held, 1 - close, theirs, 1 - close, pick(b["s3"], b["s1"]), pick(b["m3"], b["m1"]))
    out[1] = product(held, close, theirs, 1 - close, b["s2"], b["m2"])
    out[2] = product(held, close, theirs, close, pick(b["s1"], b["s3"]), pick(b["m1"], b["m3"]))

    def put(targets):
        run([pltpu.make_async_copy(out.at[j], ref, sems.at[3 + j]) for j, ref in enumerate(targets)])

    @pl.when(is_odd)
    def _():
        put([kmirror.at[1, 1], kmirror.at[0, 0], kmirror.at[0, 1]])

    @pl.when(jnp.logical_not(is_odd))
    def _():
        put([kband.at[0, 2], kband.at[1, 1], kband.at[1, 2]])


def first_products_kernel(
    n, own, below, got, mine, back, near, second, extra, rest, case, far_window, near_window, staged, sems
):
    me, is_odd = position()
    b = slow_boundary(own, below)
    exists = jnp.where(is_odd, me < n - 1, me > 0)
    level = sum((b["half"] > c).astype(jnp.int32) for c in LEVELS[:-1])
    which = lax.shift_right_logical(jnp.where(is_odd, me, me - 1) - 1, 1)
    splits = exists & (b["split"] > 0)
    case[0] = jnp.where(splits, 1 + which * len(LEVELS) + level, 0)
    case[1] = jnp.where(splits, 1 + which, 0)

    @pl.when(splits)
    def _():
        at = jnp.minimum(b["low"], UNITS)
        run([pltpu.make_async_copy(mine.at[jnp.where(is_odd, 1, 0), :, :, lanes(at, UNITS)], staged, sems.at[3])])
        lower, upper = b["low"] - at, b["low"] - at + b["half"]
        sent = jnp.where(is_odd, lower, upper)
        kept = jnp.where(is_odd, upper, lower)
        count = jnp.where(is_odd, b["split"] - b["half"], b["half"])

        def some(u, carry):
            alive = jnp.where(u < count, 1.0, 0.0).astype(rest.dtype)
            for i in range(2):
                extra[i, :, lanes(u)] = staged[i, :, lanes(jnp.minimum(sent + u, UNITS - 1))]
                rest[i, :, lanes(u)] = staged[i, :, lanes(jnp.minimum(kept + u, UNITS - 1))] * alive
            return carry

        lax.fori_loop(0, SPARE, some, 0)

    @pl.when(jnp.logical_not(is_odd))
    def _():
        rows = mine.shape[2]
        at = b["first"]
        loads = [
            pltpu.make_async_copy(mine.at[1, :, :, lanes(at, UNITS)], far_window, sems.at[0]),
            pltpu.make_async_copy(mine.at[0, :, :, lanes(at, UNITS)], near_window, sems.at[1]),
            pltpu.make_async_copy(mine.at[0, :, :, lanes(b["second"], UNITS)], second, sems.at[2]),
        ]
        for c in loads:
            c.start()
        left = [got[pl.ds(i * rows, rows), :] for i in range(2)]
        loads[0].wait()
        back[...] = sum(times(left[i], far_window[i]) for i in range(2)) * b["m3"].astype(jnp.float32)
        loads[1].wait()
        counts = counted(at, b["s2"], b["s2"] + UNITS * b["m2"])
        near[...] = sum(times(left[i], near_window[i] * counts) for i in range(2))
        loads[2].wait()
        far_lives = b["m1"] > 0
        counts = counted(
            b["second"],
            jnp.where(far_lives, b["second"], b["low"]),
            jnp.where(far_lives, b["second"] + UNITS, b["low"] + b["rest"]),
        )
        for i in range(2):
            second[i] = second[i] * counts


def rest_kernel(got, rest, out):
    _, is_odd = position()
    width = got.shape[2]

    @pl.when(is_odd)
    def _():
        out[...] = sum(times(rest[i, :, :width], got[i]) for i in range(2))

    @pl.when(jnp.logical_not(is_odd))
    def _():
        out[...] = sum(times(got[i], rest[i, :, :width]) for i in range(2))


def coded(value):
    top = jnp.maximum(jnp.max(jnp.abs(value), axis=0, keepdims=True), 1e-30)
    power = jnp.ceil(jnp.log2(top)) - 14.0
    whole = jnp.clip(jnp.ceil(top / jnp.exp2(power)), 1.0, STEPS)
    steps = jnp.round(value * (STEPS / (whole * jnp.exp2(power))))
    return jnp.clip(steps, -STEPS, STEPS), whole, power


def decoded(steps, whole, power):
    return steps * (whole * jnp.exp2(power) * (1.0 / STEPS))


def whole_numbers(value):
    return value.astype(jnp.int32).astype(jnp.int16)


def second_products_kernel(own, below, got, second, back, near, more, results, part, sent):
    _, is_odd = position()

    @pl.when(is_odd)
    def _():
        part[...] = more[...]

    @pl.when(jnp.logical_not(is_odd))
    def _():
        b = slow_boundary(own, below)
        rows = back.shape[0]
        value = sum(times(got[i], second[i]) for i in range(2))
        lives = b["m1"].astype(jnp.float32)
        results[...] = value * lives
        part[...] = near[...] + more[...] + value * (1.0 - lives)
        row = lax.broadcasted_iota(jnp.int32, (NOTE, rows), 0)
        scales = jnp.zeros((NOTE, rows), jnp.float32)
        for k, block in enumerate((results[...], part[...], back[...])):
            steps, whole, power = coded(block)
            sent[pl.ds(k * rows, rows), :] = whole_numbers(steps)
            scales = jnp.where(row == 2 * k, whole, jnp.where(row == 2 * k + 1, power, scales))
        sent[pl.ds(3 * rows, NOTE), :] = whole_numbers(scales)


def mirror_kernel(back, results, kmirror_in, kmirror, out, sems):
    _, is_odd = position()

    @pl.when(jnp.logical_not(is_odd))
    def _():
        out[0] = back[...].T
        out[1] = results[...].T
        targets = [kmirror.at[1, 1], kmirror.at[0, 1]]
        run([pltpu.make_async_copy(out.at[j], ref, sems.at[j]) for j, ref in enumerate(targets)])


def last_kernel(case, got, part, other, kband_in, kmirror_in, kband, kmirror, out, sems):
    _, is_odd = position()

    @pl.when(is_odd)
    def _():
        rows = out.shape[1]
        scales = got[pl.ds(3 * rows, NOTE), :].astype(jnp.int32).astype(jnp.float32)
        copies = []
        for k, ref in enumerate((kband.at[0, 2], kband.at[1, 1], kband.at[1, 2])):
            steps = got[pl.ds(k * rows, rows), :].astype(jnp.int32).astype(jnp.float32)
            out[k] = decoded(steps, scales[2 * k : 2 * k + 1], scales[2 * k + 1 : 2 * k + 2])
            if k == 1:

                @pl.when(case[1] > 0)
                def _():
                    out[1] = part[...] + other[...]

            copies.append(pltpu.make_async_copy(out.at[k], ref, sems.at[k]))
            copies[-1].start()
        for c in copies:
            c.wait()

    @pl.when(jnp.logical_not(is_odd))
    def _():
        out[0] = (part[...] + other[...]).T
        run([pltpu.make_async_copy(out.at[0], kmirror.at[0, 0], sems.at[0])])


def call(kernel, outs, ins, out_specs, scratch, flops=0, moved=0, aliases=None, vmem=40):
    inner = kernel.func if isinstance(kernel, functools.partial) else kernel
    return pl.pallas_call(
        kernel,
        out_shape=outs,
        in_specs=ins,
        out_specs=out_specs,
        scratch_shapes=scratch,
        input_output_aliases=aliases or {},
        compiler_params=pltpu.CompilerParams(vmem_limit_bytes=vmem * 2**20),
        cost_estimate=pl.CostEstimate(flops=flops, bytes_accessed=moved, transcendentals=0),
        name=inner.__name__,
    )


def per_device(bfac, pair_mask, dom_start):
    n = lax.axis_size("wide")
    _, rows, orbitals, fitting = bfac.shape
    upward = [(i, i + 1) for i in range(1, n - 1, 2)]
    downward = [(j, i) for i, j in upward]
    fast = [p for i in range(0, n, 2) for p in ((i, i + 1), (i + 1, i))]
    f32, bf16 = jnp.float32, bfac.dtype
    shape = jax.ShapeDtypeStruct
    dma = pltpu.SemaphoreType.DMA
    square = shape((rows, rows), f32)
    window = shape((orbitals, rows, DOM), bf16)
    raw_block = pltpu.VMEM((rows, orbitals, fitting), bf16)

    first, own, zero = call(
        first_kernel,
        (shape((orbitals * rows + NOTE, DOM), bf16), shape((8, 128), jnp.int32), shape((1,), jnp.int32)),
        [SMEM, SMEM, HBM],
        (VMEM, VMEM, SMEM),
        [raw_block, dma((8,))],
        vmem=57,
    )(pair_mask, dom_start, bfac)
    first_got = lax.ppermute(first, "wide", upward)

    second = call(second_kernel, window, [SMEM, HBM], VMEM, [raw_block, dma((8,))], vmem=57)(own, bfac)
    second_got = lax.ppermute(second, "wide", upward)

    band = shape((2, 3, rows, rows), f32)
    mirror = shape((2, 2, rows, rows), f32)
    both = shape((2, orbitals, rows, fitting), bf16)
    spare = shape((orbitals, rows, SPARE * DSTEP), bf16)
    blocks = pltpu.VMEM((2, orbitals, rows, fitting), bf16)
    raw_blocks = pltpu.VMEM((2, rows, orbitals, fitting), bf16)

    own_outs = (band, mirror, both)
    own_work = call(
        own_kernel,
        own_outs,
        [SMEM, HBM],
        (HBM, HBM, HBM),
        [blocks, raw_blocks, pltpu.VMEM((4, rows, rows), f32), dma((8,))],
        2**31,
        2**25,
        vmem=48,
    )

    def unused(own, bfac):
        return tuple(jnp.zeros(o.shape, o.dtype) for o in own_outs)

    fast_below = lax.ppermute(
        lax.optimization_barrier((own, second))[0], "wide", [(i, i + 1) for i in range(0, n, 2)]
    )
    other = lax.ppermute(lax.optimization_barrier((bfac, second))[0], "wide", fast)

    own, bfac, _ = lax.optimization_barrier((own, bfac, second))
    kband, kmirror, mine = lax.cond(zero[0] == 0, own_work, unused, own, bfac)
    kband, kmirror = call(
        fast_kernel,
        (band, mirror),
        [SMEM, SMEM, HBM, HBM, HBM, HBM],
        (HBM, HBM),
        [blocks, blocks, raw_blocks, pltpu.VMEM((3, rows, rows), f32), dma((6,))],
        2**31,
        2**25,
        {4: 0, 5: 1},
        vmem=32,
    )(own, fast_below, mine, other, kband, kmirror)
    own, kband = lax.optimization_barrier((own, kband))

    below = first_got[orbitals * rows : orbitals * rows + 8, :DSTEP].astype(jnp.int32)
    staged = pltpu.VMEM((orbitals, rows, DOM), bf16)
    back, near, second_window, extra, rest_window, case = call(
        functools.partial(first_products_kernel, n),
        (square, square, window, spare, spare, shape((2,), jnp.int32)),
        [SMEM, SMEM, VMEM, HBM],
        (VMEM, VMEM, VMEM, VMEM, VMEM, SMEM),
        [staged, staged, staged, dma((4,))],
        2**31,
        2**22,
        vmem=20,
    )(own, below, first_got, mine)

    def nothing(*_):
        return jnp.zeros((rows, rows), f32)

    def pair_of(lower):
        return [(lower, lower + 1), (lower + 1, lower)]

    def rest(lower, count):
        def branch(extra, rest_window):
            got = lax.ppermute(extra[:, :, : count * DSTEP], "wide", pair_of(lower))
            return call(rest_kernel, square, [VMEM, VMEM], VMEM, [], 2**26 * count, 2**19 * count, vmem=16)(
                got, rest_window
            )

        return branch

    def parts_of(lower):
        return lambda part: lax.ppermute(part, "wide", pair_of(lower))

    lowers = range(1, n - 1, 2)
    branches = [nothing] + [rest(i, c) for i in lowers for c in LEVELS]
    more = lax.switch(case[0], branches, extra, rest_window)

    results, part, sent = call(
        second_products_kernel,
        (square, square, shape((3 * rows + NOTE, rows), jnp.int16)),
        [SMEM, SMEM, VMEM, VMEM, VMEM, VMEM, VMEM],
        (VMEM, VMEM, VMEM),
        [],
        2**30,
        2**22,
        vmem=20,
    )(own, below, second_got, second_window, back, near, more)
    sent_got = lax.ppermute(sent, "wide", downward)
    other_part = lax.switch(case[1], [nothing] + [parts_of(i) for i in lowers], part)
    kmirror = call(
        mirror_kernel,
        mirror,
        [VMEM, VMEM, HBM],
        HBM,
        [pltpu.VMEM((2, rows, rows), f32), dma((2,))],
        0,
        2**20,
        {2: 0},
        vmem=16,
    )(back, results, kmirror)
    return call(
        last_kernel,
        (band, mirror),
        [SMEM, VMEM, VMEM, VMEM, HBM, HBM],
        (HBM, HBM),
        [pltpu.VMEM((3, rows, rows), f32), dma((3,))],
        0,
        2**20,
        {4: 0, 5: 1},
        vmem=16,
    )(case, sent_got, part, other_part, kband, kmirror)


def solution(mesh):
    placed = (P("wide", None, "groups", None), P("wide", None), P("wide", None))
    return jax.shard_map(
        per_device,
        mesh=mesh,
        in_specs=placed,
        out_specs=(
            P(("groups", "wide"), None, None, None),
            P(("groups", "wide"), None, None, None),
        ),
        check_vma=False,
    )
```

```python
import functools

import jax
import jax.numpy as jnp
from jax import lax
from jax.experimental import pallas as pl
from jax.experimental.pallas import tpu as pltpu
from jax.sharding import PartitionSpec as P

DOM = 2048
DSTEP = 128
UNITS = DOM // DSTEP
LEVELS = (1, 2, 3, 4, 6, 8)
SPARE = 8
PER = 12
NOTE = 16
STEPS = 32767.0
VMEM = pl.BlockSpec(memory_space=pltpu.VMEM)
SMEM = pl.BlockSpec(memory_space=pltpu.SMEM)
HBM = pl.BlockSpec(memory_space=pltpu.HBM)


def flags(screen, block, r):
    at = block * 3 + r
    return screen[0, at], screen[0, at + PER // 2]


def boundary(get):
    m1, s1 = get(0, 2)
    m2, s2 = get(1, 1)
    m3, s3 = get(1, 2)
    first = jnp.where(m3 > 0, s3, s2)
    low = jnp.where(first <= s2, jnp.maximum(s2, first + UNITS), s2)
    high = jnp.where(first <= s2, s2 + UNITS, jnp.minimum(s2 + UNITS, first))
    rest = jnp.maximum(high - low, 0) * m2
    second = jnp.where(m1 > 0, s1, jnp.minimum(low, UNITS))
    split = rest * m1
    half = lax.shift_right_logical(split + 1, 1)
    return dict(
        m1=m1, s1=s1, m2=m2, s2=s2, m3=m3, s3=s3, first=first, low=low, rest=rest, second=second, split=split, half=half
    )


def position():
    me = lax.axis_index("wide")
    return me, lax.rem(me, 2) == 1


def slow_boundary(own, below):
    _, is_odd = position()

    def get(block, r):
        return tuple(jnp.where(is_odd, a, b) for a, b in zip(flags(own, block, r), flags(below, block, r)))

    return boundary(get)


def lanes(unit, count=1):
    return pl.ds(pl.multiple_of(unit * DSTEP, DSTEP), count * DSTEP)


def counted(unit, first, last):
    at = unit + lax.shift_right_logical(lax.broadcasted_iota(jnp.int32, (1, DOM), 1), DSTEP.bit_length() - 1)
    return jnp.where((at >= first) & (at < last), 1.0, 0.0).astype(jnp.bfloat16)


def times(left, right):
    return lax.dot_general(left, right, (((1,), (1,)), ((), ())), preferred_element_type=jnp.float32)


def swapped(values):
    return jnp.swapaxes(values, 0, 1)


def run(copies):
    for c in copies:
        c.start()
    for c in copies:
        c.wait()


def load_parts(block, raw, sems):
    parts = sems.shape[0]
    step = raw.shape[0] // parts
    return [
        pltpu.make_async_copy(block.at[pl.ds(q * step, step)], raw.at[pl.ds(q * step, step)], sems.at[q])
        for q in range(parts)
    ]


def first_kernel(pair_mask, dom_start, bfac, out, own, zero, raw, sems):
    _, is_odd = position()
    rows = raw.shape[0]
    column = lax.broadcasted_iota(jnp.int32, own.shape, 1)
    value = jnp.zeros(own.shape, jnp.int32)
    for at in range(PER):
        source = pair_mask if at < PER // 2 else dom_start
        block, r = divmod(at % (PER // 2), 3)
        value = jnp.where(column == at, source[block, r], value)
    own[...] = value
    zero[0] = jnp.minimum(pair_mask[0, 0], 0)

    @pl.when(is_odd)
    def _():
        loads = load_parts(bfac.at[1], raw, sems)
        for c in loads:
            c.start()
        at = boundary(lambda block, r: (pair_mask[block, r], dom_start[block, r]))["first"]
        out[2 * rows :, :] = jnp.zeros((NOTE, DOM), out.dtype)
        out[2 * rows :, :DSTEP] = jnp.concatenate([value, value], 0).astype(jnp.float32).astype(out.dtype)
        step = rows // len(loads)
        for q, c in enumerate(loads):
            c.wait()
            part = swapped(raw[pl.ds(q * step, step), :, lanes(at, UNITS)])
            for i in range(2):
                out[pl.ds(i * rows + q * step, step), :] = part[i]


def second_kernel(own, bfac, out, raw, sems):
    _, is_odd = position()

    @pl.when(is_odd)
    def _():
        b = boundary(lambda block, r: flags(own, block, r))
        loads = load_parts(bfac.at[jnp.where(b["m1"] > 0, 0, 1)], raw, sems)
        for c in loads:
            c.start()
        step = raw.shape[0] // len(loads)
        for q, c in enumerate(loads):
            c.wait()
            rows = pl.ds(q * step, step)
            out[:, rows, :] = swapped(raw[rows, :, lanes(b["second"], UNITS)])


def relayouter(bfac, raw, target, loads):
    step = 32

    def relayout(b):
        loads[b].wait()

        def some(q, carry):
            rows = pl.ds(pl.multiple_of(q * step, step), step)
            target[b, :, rows, :] = swapped(raw[b, rows])
            return carry

        lax.fori_loop(0, bfac.shape[1] // step, some, 0)

    return relayout


def product(left, a, right, b, at, keep):
    value = sum(times(left[a, i, :, lanes(at, UNITS)], right[b, i, :, lanes(at, UNITS)]) for i in range(2))
    return value * keep.astype(jnp.float32)


def own_kernel(own, bfac, kband, kmirror, mine, held, raw, out, sems):
    loads = [pltpu.make_async_copy(bfac.at[b], raw.at[b], sems.at[b]) for b in range(2)]
    relayout = relayouter(bfac, raw, held, loads)
    stores = []

    def store(source, target):
        c = pltpu.make_async_copy(source, target, sems.at[2 + len(stores)])
        c.start()
        stores.append(c)

    def keep(slot, value, target):
        out[slot] = value
        store(out.at[slot], target)

    for c in loads:
        c.start()
    for b in range(2):
        relayout(b)
        store(held.at[b], mine.at[b])
    k, s = flags(own, 0, 0)
    keep(0, product(held, 0, held, 0, s, k), kband.at[0, 0])
    k, s = flags(own, 0, 1)
    value = product(held, 0, held, 1, s, k)
    keep(1, value, kband.at[0, 1])
    keep(2, value.T, kmirror.at[1, 0])
    k, s = flags(own, 1, 0)
    keep(3, product(held, 1, held, 1, s, k), kband.at[1, 0])
    for c in stores:
        c.wait()


def fast_kernel(own, below, mine, other, kband_in, kmirror_in, kband, kmirror, held, theirs, raw, out, sems):
    _, is_odd = position()
    loads = [pltpu.make_async_copy(other.at[b], raw.at[b], sems.at[b]) for b in range(2)]
    held_load = pltpu.make_async_copy(mine, held, sems.at[2])
    relayout = relayouter(other, raw, theirs, loads)
    for c in (*loads, held_load):
        c.start()

    def get(block, r):
        return tuple(jnp.where(is_odd, a, b) for a, b in zip(flags(below, block, r), flags(own, block, r)))

    b = boundary(get)
    relayout(0)
    relayout(1)
    held_load.wait()
    close = jnp.where(is_odd, 0, 1)
    pick = lambda x, y: jnp.where(is_odd, x, y)
    out[0] = product(held, 1 - close, theirs, 1 - close, pick(b["s3"], b["s1"]), pick(b["m3"], b["m1"]))
    out[1] = product(held, close, theirs, 1 - close, b["s2"], b["m2"])
    out[2] = product(held, close, theirs, close, pick(b["s1"], b["s3"]), pick(b["m1"], b["m3"]))

    def put(targets):
        run([pltpu.make_async_copy(out.at[j], ref, sems.at[3 + j]) for j, ref in enumerate(targets)])

    @pl.when(is_odd)
    def _():
        put([kmirror.at[1, 1], kmirror.at[0, 0], kmirror.at[0, 1]])

    @pl.when(jnp.logical_not(is_odd))
    def _():
        put([kband.at[0, 2], kband.at[1, 1], kband.at[1, 2]])


def first_products_kernel(
    n, own, below, got, mine, back, near, second, extra, rest, case, far_window, near_window, staged, sems
):
    me, is_odd = position()
    b = slow_boundary(own, below)
    exists = jnp.where(is_odd, me < n - 1, me > 0)
    level = sum((b["half"] > c).astype(jnp.int32) for c in LEVELS[:-1])
    which = lax.shift_right_logical(jnp.where(is_odd, me, me - 1) - 1, 1)
    splits = exists & (b["split"] > 0)
    case[0] = jnp.where(splits, 1 + which * len(LEVELS) + level, 0)
    case[1] = jnp.where(splits, 1 + which, 0)

    @pl.when(splits)
    def _():
        at = jnp.minimum(b["low"], UNITS)
        run([pltpu.make_async_copy(mine.at[jnp.where(is_odd, 1, 0), :, :, lanes(at, UNITS)], staged, sems.at[3])])
        lower, upper = b["low"] - at, b["low"] - at + b["half"]
        sent = jnp.where(is_odd, lower, upper)
        kept = jnp.where(is_odd, upper, lower)
        count = jnp.where(is_odd, b["split"] - b["half"], b["half"])

        def some(u, carry):
            alive = jnp.where(u < count, 1.0, 0.0).astype(rest.dtype)
            for i in range(2):
                extra[i, :, lanes(u)] = staged[i, :, lanes(jnp.minimum(sent + u, UNITS - 1))]
                rest[i, :, lanes(u)] = staged[i, :, lanes(jnp.minimum(kept + u, UNITS - 1))] * alive
            return carry

        lax.fori_loop(0, SPARE, some, 0)

    @pl.when(jnp.logical_not(is_odd))
    def _():
        rows = mine.shape[2]
        at = b["first"]
        loads = [
            pltpu.make_async_copy(mine.at[1, :, :, lanes(at, UNITS)], far_window, sems.at[0]),
            pltpu.make_async_copy(mine.at[0, :, :, lanes(at, UNITS)], near_window, sems.at[1]),
            pltpu.make_async_copy(mine.at[0, :, :, lanes(b["second"], UNITS)], second, sems.at[2]),
        ]
        for c in loads:
            c.start()
        left = [got[pl.ds(i * rows, rows), :] for i in range(2)]
        loads[0].wait()
        back[...] = sum(times(left[i], far_window[i]) for i in range(2)) * b["m3"].astype(jnp.float32)
        loads[1].wait()
        counts = counted(at, b["s2"], b["s2"] + UNITS * b["m2"])
        near[...] = sum(times(left[i], near_window[i] * counts) for i in range(2))
        loads[2].wait()
        far_lives = b["m1"] > 0
        counts = counted(
            b["second"],
            jnp.where(far_lives, b["second"], b["low"]),
            jnp.where(far_lives, b["second"] + UNITS, b["low"] + b["rest"]),
        )
        for i in range(2):
            second[i] = second[i] * counts


def rest_kernel(got, rest, out):
    _, is_odd = position()
    width = got.shape[2]

    @pl.when(is_odd)
    def _():
        out[...] = sum(times(rest[i, :, :width], got[i]) for i in range(2))

    @pl.when(jnp.logical_not(is_odd))
    def _():
        out[...] = sum(times(got[i], rest[i, :, :width]) for i in range(2))


def coded(value):
    top = jnp.maximum(jnp.max(jnp.abs(value), axis=0, keepdims=True), 1e-30)
    power = jnp.ceil(jnp.log2(top)) - 14.0
    whole = jnp.clip(jnp.ceil(top / jnp.exp2(power)), 1.0, STEPS)
    steps = jnp.round(value * (STEPS / (whole * jnp.exp2(power))))
    return jnp.clip(steps, -STEPS, STEPS), whole, power


def decoded(steps, whole, power):
    return steps * (whole * jnp.exp2(power) * (1.0 / STEPS))


def whole_numbers(value):
    return value.astype(jnp.int32).astype(jnp.int16)


def second_products_kernel(own, below, got, second, back, near, more, results, part, sent):
    _, is_odd = position()

    @pl.when(is_odd)
    def _():
        part[...] = more[...]

    @pl.when(jnp.logical_not(is_odd))
    def _():
        b = slow_boundary(own, below)
        rows = back.shape[0]
        value = sum(times(got[i], second[i]) for i in range(2))
        lives = b["m1"].astype(jnp.float32)
        results[...] = value * lives
        part[...] = near[...] + more[...] + value * (1.0 - lives)
        row = lax.broadcasted_iota(jnp.int32, (NOTE, rows), 0)
        scales = jnp.zeros((NOTE, rows), jnp.float32)
        for k, block in enumerate((results[...], part[...], back[...])):
            steps, whole, power = coded(block)
            sent[pl.ds(k * rows, rows), :] = whole_numbers(steps)
            scales = jnp.where(row == 2 * k, whole, jnp.where(row == 2 * k + 1, power, scales))
        sent[pl.ds(3 * rows, NOTE), :] = whole_numbers(scales)


def mirror_kernel(back, results, kmirror_in, kmirror, out, sems):
    _, is_odd = position()

    @pl.when(jnp.logical_not(is_odd))
    def _():
        out[0] = back[...].T
        out[1] = results[...].T
        targets = [kmirror.at[1, 1], kmirror.at[0, 1]]
        run([pltpu.make_async_copy(out.at[j], ref, sems.at[j]) for j, ref in enumerate(targets)])


def last_kernel(case, got, part, other, kband_in, kmirror_in, kband, kmirror, out, sems):
    _, is_odd = position()

    @pl.when(is_odd)
    def _():
        rows = out.shape[1]
        scales = got[pl.ds(3 * rows, NOTE), :].astype(jnp.int32).astype(jnp.float32)
        copies = []
        for k, ref in enumerate((kband.at[0, 2], kband.at[1, 1], kband.at[1, 2])):
            steps = got[pl.ds(k * rows, rows), :].astype(jnp.int32).astype(jnp.float32)
            out[k] = decoded(steps, scales[2 * k : 2 * k + 1], scales[2 * k + 1 : 2 * k + 2])
            if k == 1:

                @pl.when(case[1] > 0)
                def _():
                    out[1] = part[...] + other[...]

            copies.append(pltpu.make_async_copy(out.at[k], ref, sems.at[k]))
            copies[-1].start()
        for c in copies:
            c.wait()

    @pl.when(jnp.logical_not(is_odd))
    def _():
        out[0] = (part[...] + other[...]).T
        run([pltpu.make_async_copy(out.at[0], kmirror.at[0, 0], sems.at[0])])


def call(kernel, outs, ins, out_specs, scratch, flops=0, moved=0, aliases=None, vmem=40):
    inner = kernel.func if isinstance(kernel, functools.partial) else kernel
    return pl.pallas_call(
        kernel,
        out_shape=outs,
        in_specs=ins,
        out_specs=out_specs,
        scratch_shapes=scratch,
        input_output_aliases=aliases or {},
        compiler_params=pltpu.CompilerParams(vmem_limit_bytes=vmem * 2**20),
        cost_estimate=pl.CostEstimate(flops=flops, bytes_accessed=moved, transcendentals=0),
        name=inner.__name__,
    )


def per_device(bfac, pair_mask, dom_start):
    n = lax.axis_size("wide")
    _, rows, orbitals, fitting = bfac.shape
    upward = [(i, i + 1) for i in range(1, n - 1, 2)]
    downward = [(j, i) for i, j in upward]
    fast = [p for i in range(0, n, 2) for p in ((i, i + 1), (i + 1, i))]
    f32, bf16 = jnp.float32, bfac.dtype
    shape = jax.ShapeDtypeStruct
    dma = pltpu.SemaphoreType.DMA
    square = shape((rows, rows), f32)
    window = shape((orbitals, rows, DOM), bf16)
    raw_block = pltpu.VMEM((rows, orbitals, fitting), bf16)

    first, own, zero = call(
        first_kernel,
        (shape((orbitals * rows + NOTE, DOM), bf16), shape((8, 128), jnp.int32), shape((1,), jnp.int32)),
        [SMEM, SMEM, HBM],
        (VMEM, VMEM, SMEM),
        [raw_block, dma((8,))],
        vmem=57,
    )(pair_mask, dom_start, bfac)
    first_got = lax.ppermute(first, "wide", upward)

    second = call(second_kernel, window, [SMEM, HBM], VMEM, [raw_block, dma((8,))], vmem=57)(own, bfac)
    second_got = lax.ppermute(second, "wide", upward)

    band = shape((2, 3, rows, rows), f32)
    mirror = shape((2, 2, rows, rows), f32)
    both = shape((2, orbitals, rows, fitting), bf16)
    spare = shape((orbitals, rows, SPARE * DSTEP), bf16)
    blocks = pltpu.VMEM((2, orbitals, rows, fitting), bf16)
    raw_blocks = pltpu.VMEM((2, rows, orbitals, fitting), bf16)

    def inner(own, bfac):
        below = lax.ppermute(own, "wide", [(i, i + 1) for i in range(0, n, 2)])
        other = lax.ppermute(bfac, "wide", fast)
        kband, kmirror, mine = call(
            own_kernel,
            (band, mirror, both),
            [SMEM, HBM],
            (HBM, HBM, HBM),
            [blocks, raw_blocks, pltpu.VMEM((4, rows, rows), f32), dma((8,))],
            2**31,
            2**25,
            vmem=40,
        )(own, bfac)
        kband, kmirror = call(
            fast_kernel,
            (band, mirror),
            [SMEM, SMEM, HBM, HBM, HBM, HBM],
            (HBM, HBM),
            [blocks, blocks, raw_blocks, pltpu.VMEM((3, rows, rows), f32), dma((6,))],
            2**31,
            2**25,
            {4: 0, 5: 1},
            vmem=32,
        )(own, below, mine, other, kband, kmirror)
        return kband, kmirror, mine

    def unused(own, bfac):
        return tuple(jnp.zeros(o.shape, o.dtype) for o in (band, mirror, both))

    own, bfac, _ = lax.optimization_barrier((own, bfac, second))
    kband, kmirror, mine = lax.cond(zero[0] == 0, inner, unused, own, bfac)

    below = first_got[orbitals * rows : orbitals * rows + 8, :DSTEP].astype(jnp.int32)
    staged = pltpu.VMEM((orbitals, rows, DOM), bf16)
    back, near, second_window, extra, rest_window, case = call(
        functools.partial(first_products_kernel, n),
        (square, square, window, spare, spare, shape((2,), jnp.int32)),
        [SMEM, SMEM, VMEM, HBM],
        (VMEM, VMEM, VMEM, VMEM, VMEM, SMEM),
        [staged, staged, staged, dma((4,))],
        2**31,
        2**22,
        vmem=16,
    )(own, below, first_got, mine)

    def nothing(*_):
        return jnp.zeros((rows, rows), f32)

    def pair_of(lower):
        return [(lower, lower + 1), (lower + 1, lower)]

    def rest(lower, count):
        def branch(extra, rest_window):
            got = lax.ppermute(extra[:, :, : count * DSTEP], "wide", pair_of(lower))
            return call(rest_kernel, square, [VMEM, VMEM], VMEM, [], 2**26 * count, 2**19 * count, vmem=8)(
                got, rest_window
            )

        return branch

    def parts_of(lower):
        return lambda part: lax.ppermute(part, "wide", pair_of(lower))

    lowers = range(1, n - 1, 2)
    branches = [nothing] + [rest(i, c) for i in lowers for c in LEVELS]
    more = lax.switch(case[0], branches, extra, rest_window)

    results, part, sent = call(
        second_products_kernel,
        (square, square, shape((3 * rows + NOTE, rows), jnp.int16)),
        [SMEM, SMEM, VMEM, VMEM, VMEM, VMEM, VMEM],
        (VMEM, VMEM, VMEM),
        [],
        2**30,
        2**22,
        vmem=12,
    )(own, below, second_got, second_window, back, near, more)
    sent_got = lax.ppermute(sent, "wide", downward)
    other_part = lax.switch(case[1], [nothing] + [parts_of(i) for i in lowers], part)
    kmirror = call(
        mirror_kernel,
        mirror,
        [VMEM, VMEM, HBM],
        HBM,
        [pltpu.VMEM((2, rows, rows), f32), dma((2,))],
        0,
        2**20,
        {2: 0},
        vmem=8,
    )(back, results, kmirror)
    return call(
        last_kernel,
        (band, mirror),
        [SMEM, VMEM, VMEM, VMEM, HBM, HBM],
        (HBM, HBM),
        [pltpu.VMEM((3, rows, rows), f32), dma((3,))],
        0,
        2**20,
        {4: 0, 5: 1},
        vmem=8,
    )(case, sent_got, part, other_part, kband, kmirror)


def solution(mesh):
    placed = (P("wide", None, "groups", None), P("wide", None), P("wide", None))
    return jax.shard_map(
        per_device,
        mesh=mesh,
        in_specs=placed,
        out_specs=(
            P(("groups", "wide"), None, None, None),
            P(("groups", "wide"), None, None, None),
        ),
        check_vma=False,
    )
```

```python
import functools

import jax
import jax.numpy as jnp
from jax import lax
from jax.experimental import pallas as pl
from jax.experimental.pallas import tpu as pltpu
from jax.sharding import PartitionSpec as P

DOM = 2048
DSTEP = 128
UNITS = DOM // DSTEP
UP = (1, 2, 4, 6, 8)
BOTH = (6, 8)
SPARE = 8
PER = 12
NOTE = 16
STEPS = 32767.0
VMEM = pl.BlockSpec(memory_space=pltpu.VMEM)
SMEM = pl.BlockSpec(memory_space=pltpu.SMEM)
HBM = pl.BlockSpec(memory_space=pltpu.HBM)


def flags(screen, block, r):
    at = block * 3 + r
    return screen[0, at], screen[0, at + PER // 2]


def boundary(get):
    m1, s1 = get(0, 2)
    m2, s2 = get(1, 1)
    m3, s3 = get(1, 2)
    first = jnp.where(m3 > 0, s3, s2)
    low = jnp.where(first <= s2, jnp.maximum(s2, first + UNITS), s2)
    high = jnp.where(first <= s2, s2 + UNITS, jnp.minimum(s2 + UNITS, first))
    rest = jnp.maximum(high - low, 0) * m2
    second = jnp.where(m1 > 0, s1, jnp.minimum(low, UNITS))
    split = rest * m1
    half = jnp.where(split > SPARE, lax.shift_right_logical(split + 1, 1), split)
    return dict(
        m1=m1, s1=s1, m2=m2, s2=s2, m3=m3, s3=s3, first=first, low=low, rest=rest, second=second, split=split, half=half
    )


def position():
    me = lax.axis_index("wide")
    return me, lax.rem(me, 2) == 1


def slow_boundary(own, below):
    _, is_odd = position()

    def get(block, r):
        return tuple(jnp.where(is_odd, a, b) for a, b in zip(flags(own, block, r), flags(below, block, r)))

    return boundary(get)


def lanes(unit, count=1):
    return pl.ds(pl.multiple_of(unit * DSTEP, DSTEP), count * DSTEP)


def counted(unit, first, last):
    at = unit + lax.shift_right_logical(lax.broadcasted_iota(jnp.int32, (1, DOM), 1), DSTEP.bit_length() - 1)
    return jnp.where((at >= first) & (at < last), 1.0, 0.0).astype(jnp.bfloat16)


def times(left, right):
    return lax.dot_general(left, right, (((1,), (1,)), ((), ())), preferred_element_type=jnp.float32)


def swapped(values):
    return jnp.swapaxes(values, 0, 1)


def run(copies):
    for c in copies:
        c.start()
    for c in copies:
        c.wait()


def load_parts(block, raw, sems):
    parts = sems.shape[0]
    step = raw.shape[0] // parts
    return [
        pltpu.make_async_copy(block.at[pl.ds(q * step, step)], raw.at[pl.ds(q * step, step)], sems.at[q])
        for q in range(parts)
    ]


def first_kernel(pair_mask, dom_start, bfac, out, own, zero, raw, made, sems, out_sems):
    _, is_odd = position()
    rows = raw.shape[0]
    column = lax.broadcasted_iota(jnp.int32, own.shape, 1)
    value = jnp.zeros(own.shape, jnp.int32)
    for at in range(PER):
        source = pair_mask if at < PER // 2 else dom_start
        block, r = divmod(at % (PER // 2), 3)
        value = jnp.where(column == at, source[block, r], value)
    own[...] = value
    zero[0] = jnp.minimum(pair_mask[0, 0], 0)

    @pl.when(is_odd)
    def _():
        loads = load_parts(bfac.at[1], raw, sems)
        for c in loads:
            c.start()
        at = boundary(lambda block, r: (pair_mask[block, r], dom_start[block, r]))["first"]
        width = made.shape[1]
        pieces = DOM // width
        stores = []

        def store(first, count):
            piece = pl.ds(first, count)
            c = pltpu.make_async_copy(made.at[piece], out.at[piece], out_sems.at[len(stores)])
            c.start()
            stores.append(c)

        note = made.shape[0] - NOTE
        made[note:, :] = jnp.zeros((NOTE, width), made.dtype)
        made[note:, :DSTEP] = jnp.concatenate([value, value], 0).astype(jnp.float32).astype(made.dtype)
        store(note, NOTE)
        step = rows // len(loads)
        for q, c in enumerate(loads):
            c.wait()
            part = swapped(raw[pl.ds(q * step, step), :, lanes(at, UNITS)])
            for k in range(pieces):
                for i in range(2):
                    first = (k * 2 + i) * rows + q * step
                    made[pl.ds(first, step), :] = part[i, :, k * width : (k + 1) * width]
                    store(first, step)
        for c in stores:
            c.wait()


def second_kernel(own, bfac, out, raw, sems):
    _, is_odd = position()

    @pl.when(is_odd)
    def _():
        b = boundary(lambda block, r: flags(own, block, r))
        loads = load_parts(bfac.at[jnp.where(b["m1"] > 0, 0, 1)], raw, sems)
        for c in loads:
            c.start()
        step = raw.shape[0] // len(loads)
        for q, c in enumerate(loads):
            c.wait()
            rows = pl.ds(q * step, step)
            out[:, rows, :] = swapped(raw[rows, :, lanes(b["second"], UNITS)])


def relayouter(bfac, raw, target, loads):
    step = 32

    def relayout(b):
        loads[b].wait()

        def some(q, carry):
            rows = pl.ds(pl.multiple_of(q * step, step), step)
            target[b, :, rows, :] = swapped(raw[b, rows])
            return carry

        lax.fori_loop(0, bfac.shape[1] // step, some, 0)

    return relayout


def product(left, a, right, b, at, keep):
    value = sum(times(left[a, i, :, lanes(at, UNITS)], right[b, i, :, lanes(at, UNITS)]) for i in range(2))
    return value * keep.astype(jnp.float32)


def own_kernel(own, bfac, kband, kmirror, mine, held, raw, out, sems):
    loads = [pltpu.make_async_copy(bfac.at[b], raw.at[b], sems.at[b]) for b in range(2)]
    relayout = relayouter(bfac, raw, held, loads)
    stores = []

    def store(source, target):
        c = pltpu.make_async_copy(source, target, sems.at[2 + len(stores)])
        c.start()
        stores.append(c)

    def keep(slot, value, target):
        out[slot] = value
        store(out.at[slot], target)

    for c in loads:
        c.start()
    for b in range(2):
        relayout(b)
        store(held.at[b], mine.at[b])
    k, s = flags(own, 0, 0)
    keep(0, product(held, 0, held, 0, s, k), kband.at[0, 0])
    k, s = flags(own, 0, 1)
    value = product(held, 0, held, 1, s, k)
    keep(1, value, kband.at[0, 1])
    keep(2, value.T, kmirror.at[1, 0])
    k, s = flags(own, 1, 0)
    keep(3, product(held, 1, held, 1, s, k), kband.at[1, 0])
    for c in stores:
        c.wait()


def fast_kernel(own, below, mine, other, kband_in, kmirror_in, kband, kmirror, held, theirs, raw, out, sems):
    _, is_odd = position()
    loads = [pltpu.make_async_copy(other.at[b], raw.at[b], sems.at[b]) for b in range(2)]
    held_load = pltpu.make_async_copy(mine, held, sems.at[2])
    relayout = relayouter(other, raw, theirs, loads)
    for c in (*loads, held_load):
        c.start()

    def get(block, r):
        return tuple(jnp.where(is_odd, a, b) for a, b in zip(flags(below, block, r), flags(own, block, r)))

    b = boundary(get)
    relayout(0)
    relayout(1)
    held_load.wait()
    close = jnp.where(is_odd, 0, 1)
    pick = lambda x, y: jnp.where(is_odd, x, y)
    out[0] = product(held, 1 - close, theirs, 1 - close, pick(b["s3"], b["s1"]), pick(b["m3"], b["m1"]))
    out[1] = product(held, close, theirs, 1 - close, b["s2"], b["m2"])
    out[2] = product(held, close, theirs, close, pick(b["s1"], b["s3"]), pick(b["m1"], b["m3"]))

    def put(targets):
        run([pltpu.make_async_copy(out.at[j], ref, sems.at[3 + j]) for j, ref in enumerate(targets)])

    @pl.when(is_odd)
    def _():
        put([kmirror.at[1, 1], kmirror.at[0, 0], kmirror.at[0, 1]])

    @pl.when(jnp.logical_not(is_odd))
    def _():
        put([kband.at[0, 2], kband.at[1, 1], kband.at[1, 2]])


def first_products_kernel(
    n, own, below, got, mine, back, near, second, extra, rest, case, far_window, near_window, staged, sems
):
    me, is_odd = position()
    b = slow_boundary(own, below)
    exists = jnp.where(is_odd, me < n - 1, me > 0)
    short = sum((b["half"] > c).astype(jnp.int32) for c in UP[:-1])
    long = len(UP) + sum((b["half"] > c).astype(jnp.int32) for c in BOTH[:-1])
    which = lax.shift_right_logical(jnp.where(is_odd, me, me - 1) - 1, 1)
    splits = exists & (b["split"] > 0)
    is_long = b["split"] > SPARE
    case[0] = jnp.where(splits, 1 + which * len(UP + BOTH) + jnp.where(is_long, long, short), 0)
    case[1] = jnp.where(splits & is_long, 1 + which, 0)

    @pl.when(splits)
    def _():
        at = jnp.minimum(b["low"], UNITS)
        run([pltpu.make_async_copy(mine.at[jnp.where(is_odd, 1, 0), :, :, lanes(at, UNITS)], staged, sems.at[3])])
        lower, upper = b["low"] - at, b["low"] - at + b["half"]
        sent = jnp.where(is_odd, lower, upper)
        kept = jnp.where(is_odd, upper, lower)
        count = jnp.where(is_odd, b["split"] - b["half"], b["half"])

        def some(u, carry):
            alive = jnp.where(u < count, 1.0, 0.0).astype(rest.dtype)
            for i in range(2):
                extra[i, :, lanes(u)] = staged[i, :, lanes(jnp.minimum(sent + u, UNITS - 1))]
                rest[i, :, lanes(u)] = staged[i, :, lanes(jnp.minimum(kept + u, UNITS - 1))] * alive
            return carry

        lax.fori_loop(0, SPARE, some, 0)

    @pl.when(jnp.logical_not(is_odd))
    def _():
        rows = mine.shape[2]
        at = b["first"]
        loads = [
            pltpu.make_async_copy(mine.at[1, :, :, lanes(at, UNITS)], far_window, sems.at[0]),
            pltpu.make_async_copy(mine.at[0, :, :, lanes(at, UNITS)], near_window, sems.at[1]),
            pltpu.make_async_copy(mine.at[0, :, :, lanes(b["second"], UNITS)], second, sems.at[2]),
        ]
        for c in loads:
            c.start()
        width = got.shape[1]

        def against(ref, scale):
            total = 0.0
            for k in range(DOM // width):
                for i in range(2):
                    right = ref[i, :, k * width : (k + 1) * width] * scale[:, k * width : (k + 1) * width]
                    total = total + times(got[pl.ds((k * 2 + i) * rows, rows), :], right)
            return total

        loads[0].wait()
        back[...] = against(far_window, counted(at, at, at + UNITS * b["m3"]))
        loads[1].wait()
        near[...] = against(near_window, counted(at, b["s2"], b["s2"] + UNITS * b["m2"]))
        loads[2].wait()
        far_lives = b["m1"] > 0
        counts = counted(
            b["second"],
            jnp.where(far_lives, b["second"], b["low"]),
            jnp.where(far_lives, b["second"] + UNITS, b["low"] + b["rest"]),
        )
        for i in range(2):
            second[i] = second[i] * counts


def rest_kernel(got, rest, out):
    _, is_odd = position()
    width = got.shape[2]

    @pl.when(is_odd)
    def _():
        out[...] = sum(times(rest[i, :, :width], got[i]) for i in range(2))

    @pl.when(jnp.logical_not(is_odd))
    def _():
        out[...] = sum(times(got[i], rest[i, :, :width]) for i in range(2))


def coded(value):
    top = jnp.maximum(jnp.max(jnp.abs(value), axis=0, keepdims=True), 1e-30)
    power = jnp.ceil(jnp.log2(top)) - 14.0
    whole = jnp.clip(jnp.ceil(top / jnp.exp2(power)), 1.0, STEPS)
    steps = jnp.round(value * (STEPS / (whole * jnp.exp2(power))))
    return jnp.clip(steps, -STEPS, STEPS), whole, power


def decoded(steps, whole, power):
    return steps * (whole * jnp.exp2(power) * (1.0 / STEPS))


def whole_numbers(value):
    return value.astype(jnp.int32).astype(jnp.int16)


def second_products_kernel(own, below, got, second, back, near, more, results, part, sent):
    _, is_odd = position()

    @pl.when(is_odd)
    def _():
        part[...] = more[...]

    @pl.when(jnp.logical_not(is_odd))
    def _():
        b = slow_boundary(own, below)
        rows = back.shape[0]
        value = sum(times(got[i], second[i]) for i in range(2))
        lives = b["m1"].astype(jnp.float32)
        results[...] = value * lives
        part[...] = near[...] + more[...] + value * (1.0 - lives)
        row = lax.broadcasted_iota(jnp.int32, (NOTE, rows), 0)
        scales = jnp.zeros((NOTE, rows), jnp.float32)
        for k, block in enumerate((results[...], part[...], back[...])):
            steps, whole, power = coded(block)
            sent[pl.ds(k * rows, rows), :] = whole_numbers(steps)
            scales = jnp.where(row == 2 * k, whole, jnp.where(row == 2 * k + 1, power, scales))
        sent[pl.ds(3 * rows, NOTE), :] = whole_numbers(scales)


def mirror_kernel(back, results, kmirror_in, kmirror, out, sems):
    _, is_odd = position()

    @pl.when(jnp.logical_not(is_odd))
    def _():
        out[0] = back[...].T
        out[1] = results[...].T
        targets = [kmirror.at[1, 1], kmirror.at[0, 1]]
        run([pltpu.make_async_copy(out.at[j], ref, sems.at[j]) for j, ref in enumerate(targets)])


def last_kernel(case, got, part, other, kband_in, kmirror_in, kband, kmirror, out, sems):
    _, is_odd = position()

    @pl.when(is_odd)
    def _():
        rows = out.shape[1]
        scales = got[pl.ds(3 * rows, NOTE), :].astype(jnp.int32).astype(jnp.float32)
        copies = []
        for k, ref in enumerate((kband.at[0, 2], kband.at[1, 1], kband.at[1, 2])):
            steps = got[pl.ds(k * rows, rows), :].astype(jnp.int32).astype(jnp.float32)
            out[k] = decoded(steps, scales[2 * k : 2 * k + 1], scales[2 * k + 1 : 2 * k + 2])
            if k == 1:

                @pl.when(case[1] > 0)
                def _():
                    out[1] = part[...] + other[...]

            copies.append(pltpu.make_async_copy(out.at[k], ref, sems.at[k]))
            copies[-1].start()
        for c in copies:
            c.wait()

    @pl.when(jnp.logical_not(is_odd))
    def _():
        out[0] = (part[...] + other[...]).T
        run([pltpu.make_async_copy(out.at[0], kmirror.at[0, 0], sems.at[0])])


def call(kernel, outs, ins, out_specs, scratch, flops=0, moved=0, aliases=None, vmem=40):
    inner = kernel.func if isinstance(kernel, functools.partial) else kernel
    return pl.pallas_call(
        kernel,
        out_shape=outs,
        in_specs=ins,
        out_specs=out_specs,
        scratch_shapes=scratch,
        input_output_aliases=aliases or {},
        compiler_params=pltpu.CompilerParams(vmem_limit_bytes=vmem * 2**20),
        cost_estimate=pl.CostEstimate(flops=flops, bytes_accessed=moved, transcendentals=0),
        name=inner.__name__,
    )


def per_device(bfac, pair_mask, dom_start):
    n = lax.axis_size("wide")
    _, rows, orbitals, fitting = bfac.shape
    upward = [(i, i + 1) for i in range(1, n - 1, 2)]
    downward = [(j, i) for i, j in upward]
    fast = [p for i in range(0, n, 2) for p in ((i, i + 1), (i + 1, i))]
    f32, bf16 = jnp.float32, bfac.dtype
    shape = jax.ShapeDtypeStruct
    dma = pltpu.SemaphoreType.DMA
    square = shape((rows, rows), f32)
    window = shape((orbitals, rows, DOM), bf16)
    raw_block = pltpu.VMEM((rows, orbitals, fitting), bf16)

    width = 512
    whole = (DOM // width * orbitals * rows + NOTE, width)
    parts = 8
    first, own, zero = call(
        first_kernel,
        (shape(whole, bf16), shape((8, 128), jnp.int32), shape((1,), jnp.int32)),
        [SMEM, SMEM, HBM],
        (HBM, VMEM, SMEM),
        [raw_block, pltpu.VMEM(whole, bf16), dma((parts,)), dma((parts * orbitals * DOM // width + 1,))],
        vmem=60,
    )(pair_mask, dom_start, bfac)
    first_got = lax.ppermute(first, "wide", upward)

    second = call(second_kernel, window, [SMEM, HBM], VMEM, [raw_block, dma((8,))], vmem=57)(own, bfac)
    second_got = lax.ppermute(second, "wide", upward)

    band = shape((2, 3, rows, rows), f32)
    mirror = shape((2, 2, rows, rows), f32)
    both = shape((2, orbitals, rows, fitting), bf16)
    spare = shape((orbitals, rows, SPARE * DSTEP), bf16)
    blocks = pltpu.VMEM((2, orbitals, rows, fitting), bf16)
    raw_blocks = pltpu.VMEM((2, rows, orbitals, fitting), bf16)

    def inner(own, bfac):
        below = lax.ppermute(own, "wide", [(i, i + 1) for i in range(0, n, 2)])
        other = lax.ppermute(bfac, "wide", fast)
        kband, kmirror, mine = call(
            own_kernel,
            (band, mirror, both),
            [SMEM, HBM],
            (HBM, HBM, HBM),
            [blocks, raw_blocks, pltpu.VMEM((4, rows, rows), f32), dma((8,))],
            2**31,
            2**25,
            vmem=40,
        )(own, bfac)
        kband, kmirror = call(
            fast_kernel,
            (band, mirror),
            [SMEM, SMEM, HBM, HBM, HBM, HBM],
            (HBM, HBM),
            [blocks, blocks, raw_blocks, pltpu.VMEM((3, rows, rows), f32), dma((6,))],
            2**31,
            2**25,
            {4: 0, 5: 1},
            vmem=32,
        )(own, below, mine, other, kband, kmirror)
        return kband, kmirror, mine

    def unused(own, bfac):
        return tuple(jnp.zeros(o.shape, o.dtype) for o in (band, mirror, both))

    own, bfac, _ = lax.optimization_barrier((own, bfac, second))
    kband, kmirror, mine = lax.cond(zero[0] == 0, inner, unused, own, bfac)

    below = first_got[whole[0] - NOTE : whole[0] - NOTE + 8, :DSTEP].astype(jnp.int32)
    staged = pltpu.VMEM((orbitals, rows, DOM), bf16)
    back, near, second_window, extra, rest_window, case = call(
        functools.partial(first_products_kernel, n),
        (square, square, window, spare, spare, shape((2,), jnp.int32)),
        [SMEM, SMEM, VMEM, HBM],
        (VMEM, VMEM, VMEM, VMEM, VMEM, SMEM),
        [staged, staged, staged, dma((4,))],
        2**31,
        2**22,
        vmem=16,
    )(own, below, first_got, mine)

    def nothing(*_):
        return jnp.zeros((rows, rows), f32)

    def pair_of(lower):
        return [(lower, lower + 1), (lower + 1, lower)]

    def rest(lower, count, pairs):
        def branch(extra, rest_window):
            got = lax.ppermute(extra[:, :, : count * DSTEP], "wide", pairs)
            return call(rest_kernel, square, [VMEM, VMEM], VMEM, [], 2**26 * count, 2**19 * count, vmem=8)(
                got, rest_window
            )

        return branch

    def parts_of(lower):
        return lambda part: lax.ppermute(part, "wide", pair_of(lower))

    lowers = range(1, n - 1, 2)
    branches = [nothing]
    for i in lowers:
        branches += [rest(i, c, [(i, i + 1)]) for c in UP] + [rest(i, c, pair_of(i)) for c in BOTH]
    more = lax.switch(case[0], branches, extra, rest_window)

    results, part, sent = call(
        second_products_kernel,
        (square, square, shape((3 * rows + NOTE, rows), jnp.int16)),
        [SMEM, SMEM, VMEM, VMEM, VMEM, VMEM, VMEM],
        (VMEM, VMEM, VMEM),
        [],
        2**30,
        2**22,
        vmem=12,
    )(own, below, second_got, second_window, back, near, more)
    sent_got = lax.ppermute(sent, "wide", downward)
    other_part = lax.switch(case[1], [nothing] + [parts_of(i) for i in lowers], part)
    kmirror = call(
        mirror_kernel,
        mirror,
        [VMEM, VMEM, HBM],
        HBM,
        [pltpu.VMEM((2, rows, rows), f32), dma((2,))],
        0,
        2**20,
        {2: 0},
        vmem=8,
    )(back, results, kmirror)
    return call(
        last_kernel,
        (band, mirror),
        [SMEM, VMEM, VMEM, VMEM, HBM, HBM],
        (HBM, HBM),
        [pltpu.VMEM((3, rows, rows), f32), dma((3,))],
        0,
        2**20,
        {4: 0, 5: 1},
        vmem=8,
    )(case, sent_got, part, other_part, kband, kmirror)


def solution(mesh):
    placed = (P("wide", None, "groups", None), P("wide", None), P("wide", None))
    return jax.shard_map(
        per_device,
        mesh=mesh,
        in_specs=placed,
        out_specs=(
            P(("groups", "wide"), None, None, None),
            P(("groups", "wide"), None, None, None),
        ),
        check_vma=False,
    )
```

```python
import functools

import jax
import jax.numpy as jnp
from jax import lax
from jax.experimental import pallas as pl
from jax.experimental.pallas import tpu as pltpu
from jax.sharding import PartitionSpec as P

DOM = 2048
DSTEP = 128
UNITS = DOM // DSTEP
UP = (2, 4, 8)
BOTH = (6, 8)
SPARE = 8
PER = 12
NOTE = 16
STEPS = 32767.0
VMEM = pl.BlockSpec(memory_space=pltpu.VMEM)
SMEM = pl.BlockSpec(memory_space=pltpu.SMEM)
HBM = pl.BlockSpec(memory_space=pltpu.HBM)


def flags(screen, block, r):
    at = block * 3 + r
    return screen[0, at], screen[0, at + PER // 2]


def boundary(get):
    m1, s1 = get(0, 2)
    m2, s2 = get(1, 1)
    m3, s3 = get(1, 2)
    first = jnp.where(m3 > 0, s3, s2)
    low = jnp.where(first <= s2, jnp.maximum(s2, first + UNITS), s2)
    high = jnp.where(first <= s2, s2 + UNITS, jnp.minimum(s2 + UNITS, first))
    rest = jnp.maximum(high - low, 0) * m2
    second = jnp.where(m1 > 0, s1, jnp.minimum(low, UNITS))
    split = rest * m1
    half = jnp.where(split > SPARE, lax.shift_right_logical(split + 1, 1), split)
    return dict(
        m1=m1, s1=s1, m2=m2, s2=s2, m3=m3, s3=s3, first=first, low=low, rest=rest, second=second, split=split, half=half
    )


def position():
    me = lax.axis_index("wide")
    return me, lax.rem(me, 2) == 1


def slow_boundary(own, below):
    _, is_odd = position()

    def get(block, r):
        return tuple(jnp.where(is_odd, a, b) for a, b in zip(flags(own, block, r), flags(below, block, r)))

    return boundary(get)


def lanes(unit, count=1):
    return pl.ds(pl.multiple_of(unit * DSTEP, DSTEP), count * DSTEP)


def counted(unit, first, last):
    at = unit + lax.shift_right_logical(lax.broadcasted_iota(jnp.int32, (1, DOM), 1), DSTEP.bit_length() - 1)
    return jnp.where((at >= first) & (at < last), 1.0, 0.0).astype(jnp.bfloat16)


def times(left, right):
    return lax.dot_general(left, right, (((1,), (1,)), ((), ())), preferred_element_type=jnp.float32)


def swapped(values):
    return jnp.swapaxes(values, 0, 1)


def run(copies):
    for c in copies:
        c.start()
    for c in copies:
        c.wait()


def load_parts(block, raw, sems):
    parts = sems.shape[0]
    step = raw.shape[0] // parts
    return [
        pltpu.make_async_copy(block.at[pl.ds(q * step, step)], raw.at[pl.ds(q * step, step)], sems.at[q])
        for q in range(parts)
    ]


def first_kernel(pair_mask, dom_start, bfac, out, own, zero, raw, made, sems, out_sems):
    _, is_odd = position()
    rows = raw.shape[0]
    column = lax.broadcasted_iota(jnp.int32, own.shape, 1)
    value = jnp.zeros(own.shape, jnp.int32)
    for at in range(PER):
        source = pair_mask if at < PER // 2 else dom_start
        block, r = divmod(at % (PER // 2), 3)
        value = jnp.where(column == at, source[block, r], value)
    own[...] = value
    zero[0] = jnp.minimum(pair_mask[0, 0], 0)

    @pl.when(is_odd)
    def _():
        loads = load_parts(bfac.at[1], raw, sems)
        for c in loads:
            c.start()
        at = boundary(lambda block, r: (pair_mask[block, r], dom_start[block, r]))["first"]
        stores = []

        def store(first, count):
            piece = pl.ds(first, count)
            c = pltpu.make_async_copy(made.at[piece], out.at[piece], out_sems.at[len(stores)])
            c.start()
            stores.append(c)

        made[2 * rows :, :] = jnp.zeros((NOTE, DOM), made.dtype)
        made[2 * rows :, :DSTEP] = jnp.concatenate([value, value], 0).astype(jnp.float32).astype(made.dtype)
        store(2 * rows, NOTE)
        step = rows // len(loads)
        for q, c in enumerate(loads):
            c.wait()
            part = swapped(raw[pl.ds(q * step, step), :, lanes(at, UNITS)])
            for i in range(2):
                made[pl.ds(i * rows + q * step, step), :] = part[i]
                store(i * rows + q * step, step)
        for c in stores:
            c.wait()


def second_kernel(own, bfac, out, raw, sems):
    _, is_odd = position()

    @pl.when(is_odd)
    def _():
        b = boundary(lambda block, r: flags(own, block, r))
        loads = load_parts(bfac.at[jnp.where(b["m1"] > 0, 0, 1)], raw, sems)
        for c in loads:
            c.start()
        step = raw.shape[0] // len(loads)
        for q, c in enumerate(loads):
            c.wait()
            rows = pl.ds(q * step, step)
            out[:, rows, :] = swapped(raw[rows, :, lanes(b["second"], UNITS)])


def relayouter(bfac, raw, target, loads):
    step = 32

    def relayout(b):
        loads[b].wait()

        def some(q, carry):
            rows = pl.ds(pl.multiple_of(q * step, step), step)
            target[b, :, rows, :] = swapped(raw[b, rows])
            return carry

        lax.fori_loop(0, bfac.shape[1] // step, some, 0)

    return relayout


def product(left, a, right, b, at, keep):
    value = sum(times(left[a, i, :, lanes(at, UNITS)], right[b, i, :, lanes(at, UNITS)]) for i in range(2))
    return value * keep.astype(jnp.float32)


def own_kernel(own, bfac, kband, kmirror, mine, held, raw, out, sems):
    loads = [pltpu.make_async_copy(bfac.at[b], raw.at[b], sems.at[b]) for b in range(2)]
    relayout = relayouter(bfac, raw, held, loads)
    stores = []

    def store(source, target):
        c = pltpu.make_async_copy(source, target, sems.at[2 + len(stores)])
        c.start()
        stores.append(c)

    def keep(slot, value, target):
        out[slot] = value
        store(out.at[slot], target)

    for c in loads:
        c.start()
    for b in range(2):
        relayout(b)
        store(held.at[b], mine.at[b])
    k, s = flags(own, 0, 0)
    keep(0, product(held, 0, held, 0, s, k), kband.at[0, 0])
    k, s = flags(own, 0, 1)
    value = product(held, 0, held, 1, s, k)
    keep(1, value, kband.at[0, 1])
    keep(2, value.T, kmirror.at[1, 0])
    k, s = flags(own, 1, 0)
    keep(3, product(held, 1, held, 1, s, k), kband.at[1, 0])
    for c in stores:
        c.wait()


def fast_kernel(own, below, mine, other, kband_in, kmirror_in, kband, kmirror, held, theirs, raw, out, sems):
    _, is_odd = position()
    loads = [pltpu.make_async_copy(other.at[b], raw.at[b], sems.at[b]) for b in range(2)]
    held_load = pltpu.make_async_copy(mine, held, sems.at[2])
    relayout = relayouter(other, raw, theirs, loads)
    for c in (*loads, held_load):
        c.start()

    def get(block, r):
        return tuple(jnp.where(is_odd, a, b) for a, b in zip(flags(below, block, r), flags(own, block, r)))

    b = boundary(get)
    relayout(0)
    relayout(1)
    held_load.wait()
    close = jnp.where(is_odd, 0, 1)
    pick = lambda x, y: jnp.where(is_odd, x, y)
    out[0] = product(held, 1 - close, theirs, 1 - close, pick(b["s3"], b["s1"]), pick(b["m3"], b["m1"]))
    out[1] = product(held, close, theirs, 1 - close, b["s2"], b["m2"])
    out[2] = product(held, close, theirs, close, pick(b["s1"], b["s3"]), pick(b["m1"], b["m3"]))

    def put(targets):
        run([pltpu.make_async_copy(out.at[j], ref, sems.at[3 + j]) for j, ref in enumerate(targets)])

    @pl.when(is_odd)
    def _():
        put([kmirror.at[1, 1], kmirror.at[0, 0], kmirror.at[0, 1]])

    @pl.when(jnp.logical_not(is_odd))
    def _():
        put([kband.at[0, 2], kband.at[1, 1], kband.at[1, 2]])


def first_products_kernel(
    n, own, below, got, mine, back, near, second, extra, rest, lives, case, far_window, near_window, staged, sems
):
    me, is_odd = position()
    b = slow_boundary(own, below)
    exists = jnp.where(is_odd, me < n - 1, me > 0)
    short = sum((b["half"] > c).astype(jnp.int32) for c in UP[:-1])
    long = len(UP) + sum((b["half"] > c).astype(jnp.int32) for c in BOTH[:-1])
    which = lax.shift_right_logical(jnp.where(is_odd, me, me - 1) - 1, 1)
    splits = exists & (b["split"] > 0)
    is_long = b["split"] > SPARE
    case[0] = jnp.where(splits, 1 + which * len(UP + BOTH) + jnp.where(is_long, long, short), 0)
    case[1] = jnp.where(splits & is_long, 1 + which, 0)

    @pl.when(splits)
    def _():
        at = jnp.minimum(b["low"], UNITS)
        run([pltpu.make_async_copy(mine.at[jnp.where(is_odd, 1, 0), :, :, lanes(at, UNITS)], staged, sems.at[3])])
        lower, upper = b["low"] - at, b["low"] - at + b["half"]
        sent = jnp.where(is_odd, lower, upper)
        kept = jnp.where(is_odd, upper, lower)
        count = jnp.where(is_odd, b["split"] - b["half"], b["half"])

        def some(u, carry):
            alive = jnp.where(u < count, 1.0, 0.0).astype(rest.dtype)
            for i in range(2):
                extra[i, :, lanes(u)] = staged[i, :, lanes(jnp.minimum(sent + u, UNITS - 1))]
                rest[i, :, lanes(u)] = staged[i, :, lanes(jnp.minimum(kept + u, UNITS - 1))] * alive
            return carry

        lax.fori_loop(0, SPARE, some, 0)

    @pl.when(jnp.logical_not(is_odd))
    def _():
        rows = mine.shape[2]
        at = b["first"]
        loads = [
            pltpu.make_async_copy(mine.at[1, :, :, lanes(at, UNITS)], far_window, sems.at[0]),
            pltpu.make_async_copy(mine.at[0, :, :, lanes(at, UNITS)], near_window, sems.at[1]),
            pltpu.make_async_copy(mine.at[0, :, :, lanes(b["second"], UNITS)], second, sems.at[2]),
        ]
        for c in loads:
            c.start()
        left = [got[pl.ds(i * rows, rows), :] for i in range(2)]

        def against(ref, scale):
            return sum(times(left[i], ref[i] * scale) for i in range(2))

        loads[0].wait()
        back[...] = against(far_window, counted(at, at, at + UNITS * b["m3"]))
        loads[1].wait()
        near[...] = against(near_window, counted(at, b["s2"], b["s2"] + UNITS * b["m2"]))
        loads[2].wait()
        far_lives = b["m1"] > 0
        lives[...] = jnp.zeros(lives.shape, lives.dtype) + b["m1"].astype(lives.dtype)
        counts = counted(
            b["second"],
            jnp.where(far_lives, b["second"], b["low"]),
            jnp.where(far_lives, b["second"] + UNITS, b["low"] + b["rest"]),
        )
        for i in range(2):
            second[i] = second[i] * counts


def rest_kernel(got, rest, out):
    _, is_odd = position()
    out[...] = jnp.zeros(out.shape, out.dtype)

    def some(k, carry):
        for i in range(2):
            out[...] += times(got[i, :, lanes(2 * k, 2)], rest[i, :, lanes(2 * k, 2)])
        return carry

    lax.fori_loop(0, got.shape[2] // (2 * DSTEP), some, 0)

    @pl.when(is_odd)
    def _():
        out[...] = out[...].T


def coded(value):
    top = jnp.maximum(jnp.max(jnp.abs(value), axis=0, keepdims=True), 1e-30)
    power = jnp.ceil(jnp.log2(top)) - 14.0
    whole = jnp.clip(jnp.ceil(top / jnp.exp2(power)), 1.0, STEPS)
    steps = jnp.round(value * (STEPS / (whole * jnp.exp2(power))))
    return jnp.clip(steps, -STEPS, STEPS), whole, power


def decoded(steps, whole, power):
    return steps * (whole * jnp.exp2(power) * (1.0 / STEPS))


def whole_numbers(value):
    return value.astype(jnp.int32).astype(jnp.int16)


def second_products_kernel(got, second, back, near, more, lives, results, part, sent, arrived, sems):
    _, is_odd = position()

    @pl.when(is_odd)
    def _():
        part[...] = more[...]

    @pl.when(jnp.logical_not(is_odd))
    def _():
        rows = back.shape[0]
        width = DOM // sems.shape[0]
        spans = [slice(k * width, (k + 1) * width) for k in range(sems.shape[0])]
        loads = [
            pltpu.make_async_copy(got.at[:, :, span], arrived.at[:, :, span], sems.at[k]) for k, span in enumerate(spans)
        ]
        for c in loads:
            c.start()
        row = lax.broadcasted_iota(jnp.int32, (NOTE, rows), 0)
        scales = jnp.zeros((NOTE, rows), jnp.float32)

        def put(k, block, scales):
            steps, whole, power = coded(block)
            sent[pl.ds(k * rows, rows), :] = whole_numbers(steps)
            return jnp.where(row == 2 * k, whole, jnp.where(row == 2 * k + 1, power, scales))

        scales = put(2, back[...], scales)
        value = 0.0
        for c, span in zip(loads, spans):
            c.wait()
            value = value + sum(times(arrived[i, :, span], second[i, :, span]) for i in range(2))
        lived = lives[0:1, :]
        results[...] = value * lived
        part[...] = near[...] + more[...] + value * (1.0 - lived)
        scales = put(0, results[...], scales)
        scales = put(1, part[...], scales)
        sent[pl.ds(3 * rows, NOTE), :] = whole_numbers(scales)


def mirror_kernel(back, results, kmirror_in, kmirror, out, sems):
    _, is_odd = position()

    @pl.when(jnp.logical_not(is_odd))
    def _():
        out[0] = back[...].T
        out[1] = results[...].T
        targets = [kmirror.at[1, 1], kmirror.at[0, 1]]
        run([pltpu.make_async_copy(out.at[j], ref, sems.at[j]) for j, ref in enumerate(targets)])


def last_kernel(case, got, part, other, kband_in, kmirror_in, kband, kmirror, out, sems):
    _, is_odd = position()

    @pl.when(is_odd)
    def _():
        rows = out.shape[1]
        scales = got[pl.ds(3 * rows, NOTE), :].astype(jnp.int32).astype(jnp.float32)
        copies = []
        for k, ref in enumerate((kband.at[0, 2], kband.at[1, 1], kband.at[1, 2])):
            steps = got[pl.ds(k * rows, rows), :].astype(jnp.int32).astype(jnp.float32)
            out[k] = decoded(steps, scales[2 * k : 2 * k + 1], scales[2 * k + 1 : 2 * k + 2])
            if k == 1:

                @pl.when(case[1] > 0)
                def _():
                    out[1] = part[...] + other[...]

            copies.append(pltpu.make_async_copy(out.at[k], ref, sems.at[k]))
            copies[-1].start()
        for c in copies:
            c.wait()

    @pl.when(jnp.logical_not(is_odd))
    def _():
        out[0] = (part[...] + other[...]).T
        run([pltpu.make_async_copy(out.at[0], kmirror.at[0, 0], sems.at[0])])


def call(kernel, outs, ins, out_specs, scratch, flops=0, moved=0, aliases=None, vmem=40):
    inner = kernel.func if isinstance(kernel, functools.partial) else kernel
    return pl.pallas_call(
        kernel,
        out_shape=outs,
        in_specs=ins,
        out_specs=out_specs,
        scratch_shapes=scratch,
        input_output_aliases=aliases or {},
        compiler_params=pltpu.CompilerParams(vmem_limit_bytes=vmem * 2**20),
        cost_estimate=pl.CostEstimate(flops=flops, bytes_accessed=moved, transcendentals=0),
        name=inner.__name__,
    )


def per_device(bfac, pair_mask, dom_start):
    n = lax.axis_size("wide")
    _, rows, orbitals, fitting = bfac.shape
    upward = [(i, i + 1) for i in range(1, n - 1, 2)]
    downward = [(j, i) for i, j in upward]
    fast = [p for i in range(0, n, 2) for p in ((i, i + 1), (i + 1, i))]
    f32, bf16 = jnp.float32, bfac.dtype
    shape = jax.ShapeDtypeStruct
    dma = pltpu.SemaphoreType.DMA
    square = shape((rows, rows), f32)
    window = shape((orbitals, rows, DOM), bf16)
    raw_block = pltpu.VMEM((rows, orbitals, fitting), bf16)

    whole = (orbitals * rows + NOTE, DOM)
    parts = 8
    first, own, zero = call(
        first_kernel,
        (shape(whole, bf16), shape((8, 128), jnp.int32), shape((1,), jnp.int32)),
        [SMEM, SMEM, HBM],
        (HBM, VMEM, SMEM),
        [raw_block, pltpu.VMEM(whole, bf16), dma((parts,)), dma((parts * orbitals + 1,))],
        vmem=60,
    )(pair_mask, dom_start, bfac)
    first_got = lax.ppermute(first, "wide", upward)

    second = call(second_kernel, window, [SMEM, HBM], VMEM, [raw_block, dma((8,))], vmem=57)(own, bfac)
    second_got = lax.ppermute(second, "wide", upward)

    band = shape((2, 3, rows, rows), f32)
    mirror = shape((2, 2, rows, rows), f32)
    both = shape((2, orbitals, rows, fitting), bf16)
    spare = shape((orbitals, rows, SPARE * DSTEP), bf16)
    blocks = pltpu.VMEM((2, orbitals, rows, fitting), bf16)
    raw_blocks = pltpu.VMEM((2, rows, orbitals, fitting), bf16)

    def inner(own, bfac):
        below = lax.ppermute(own, "wide", [(i, i + 1) for i in range(0, n, 2)])
        other = lax.ppermute(bfac, "wide", fast)
        kband, kmirror, mine = call(
            own_kernel,
            (band, mirror, both),
            [SMEM, HBM],
            (HBM, HBM, HBM),
            [blocks, raw_blocks, pltpu.VMEM((4, rows, rows), f32), dma((8,))],
            2**31,
            2**25,
            vmem=40,
        )(own, bfac)
        kband, kmirror = call(
            fast_kernel,
            (band, mirror),
            [SMEM, SMEM, HBM, HBM, HBM, HBM],
            (HBM, HBM),
            [blocks, blocks, raw_blocks, pltpu.VMEM((3, rows, rows), f32), dma((6,))],
            2**31,
            2**25,
            {4: 0, 5: 1},
            vmem=32,
        )(own, below, mine, other, kband, kmirror)
        return kband, kmirror, mine

    def unused(own, bfac):
        return tuple(jnp.zeros(o.shape, o.dtype) for o in (band, mirror, both))

    own, bfac, _ = lax.optimization_barrier((own, bfac, second))
    kband, kmirror, mine = lax.cond(zero[0] == 0, inner, unused, own, bfac)

    below = first_got[orbitals * rows : orbitals * rows + 8, :DSTEP].astype(jnp.int32)
    staged = pltpu.VMEM((orbitals, rows, DOM), bf16)
    back, near, second_window, extra, rest_window, lives, case = call(
        functools.partial(first_products_kernel, n),
        (square, square, window, spare, spare, shape((8, rows), f32), shape((2,), jnp.int32)),
        [SMEM, SMEM, VMEM, HBM],
        (VMEM, VMEM, VMEM, VMEM, VMEM, VMEM, SMEM),
        [staged, staged, staged, dma((4,))],
        2**31,
        2**22,
        vmem=16,
    )(own, below, first_got, mine)

    def nothing(*_):
        return jnp.zeros((rows, rows), f32)

    def pair_of(lower):
        return [(lower, lower + 1), (lower + 1, lower)]

    def rest(lower, count, pairs):
        def branch(extra, rest_window):
            got = lax.ppermute(extra[:, :, : count * DSTEP], "wide", pairs)
            return call(rest_kernel, square, [VMEM, VMEM], VMEM, [], 2**26 * count, 2**19 * count, vmem=8)(
                got, rest_window
            )

        return branch

    def parts_of(lower):
        return lambda part: lax.ppermute(part, "wide", pair_of(lower))

    lowers = range(1, n - 1, 2)
    branches = [nothing]
    for i in lowers:
        branches += [rest(i, c, [(i, i + 1)]) for c in UP] + [rest(i, c, pair_of(i)) for c in BOTH]
    more = lax.switch(case[0], branches, extra, rest_window)

    results, part, sent = call(
        second_products_kernel,
        (square, square, shape((3 * rows + NOTE, rows), jnp.int16)),
        [HBM, VMEM, VMEM, VMEM, VMEM, VMEM],
        (VMEM, VMEM, VMEM),
        [pltpu.VMEM((orbitals, rows, DOM), bf16), dma((4,))],
        2**30,
        2**22,
        vmem=12,
    )(second_got, second_window, back, near, more, lives)
    sent_got = lax.ppermute(sent, "wide", downward)
    other_part = lax.switch(case[1], [nothing] + [parts_of(i) for i in lowers], part)
    kmirror = call(
        mirror_kernel,
        mirror,
        [VMEM, VMEM, HBM],
        HBM,
        [pltpu.VMEM((2, rows, rows), f32), dma((2,))],
        0,
        2**20,
        {2: 0},
        vmem=8,
    )(back, results, kmirror)
    return call(
        last_kernel,
        (band, mirror),
        [SMEM, VMEM, VMEM, VMEM, HBM, HBM],
        (HBM, HBM),
        [pltpu.VMEM((3, rows, rows), f32), dma((3,))],
        0,
        2**20,
        {4: 0, 5: 1},
        vmem=8,
    )(case, sent_got, part, other_part, kband, kmirror)


def solution(mesh):
    placed = (P("wide", None, "groups", None), P("wide", None), P("wide", None))
    return jax.shard_map(
        per_device,
        mesh=mesh,
        in_specs=placed,
        out_specs=(
            P(("groups", "wide"), None, None, None),
            P(("groups", "wide"), None, None, None),
        ),
        check_vma=False,
    )
```

```python
import functools

import jax
import jax.numpy as jnp
from jax import lax
from jax.experimental import pallas as pl
from jax.experimental.pallas import tpu as pltpu
from jax.sharding import PartitionSpec as P

DOM = 2048
DSTEP = 128
UNITS = DOM // DSTEP
UP = (2, 4, 8)
BOTH = (6, 8)
SPARE = 8
PER = 12
NOTE = 16
STEPS = 32767.0
ROUND = 1.5 * 2.0**23
VMEM = pl.BlockSpec(memory_space=pltpu.VMEM)
SMEM = pl.BlockSpec(memory_space=pltpu.SMEM)
HBM = pl.BlockSpec(memory_space=pltpu.HBM)


def flags(screen, block, r):
    at = block * 3 + r
    return screen[0, at], screen[0, at + PER // 2]


def boundary(get):
    m1, s1 = get(0, 2)
    m2, s2 = get(1, 1)
    m3, s3 = get(1, 2)
    first = jnp.where(m3 > 0, s3, s2)
    low = jnp.where(first <= s2, jnp.maximum(s2, first + UNITS), s2)
    high = jnp.where(first <= s2, s2 + UNITS, jnp.minimum(s2 + UNITS, first))
    rest = jnp.maximum(high - low, 0) * m2
    second = jnp.where(m1 > 0, s1, jnp.minimum(low, UNITS))
    split = rest * m1
    half = jnp.where(split > SPARE, lax.shift_right_logical(split + 1, 1), split)
    return dict(
        m1=m1, s1=s1, m2=m2, s2=s2, m3=m3, s3=s3, first=first, low=low, rest=rest, second=second, split=split, half=half
    )


def position():
    me = lax.axis_index("wide")
    return me, lax.rem(me, 2) == 1


def slow_boundary(own, below):
    _, is_odd = position()

    def get(block, r):
        return tuple(jnp.where(is_odd, a, b) for a, b in zip(flags(own, block, r), flags(below, block, r)))

    return boundary(get)


def lanes(unit, count=1):
    return pl.ds(pl.multiple_of(unit * DSTEP, DSTEP), count * DSTEP)


def counted(unit, first, last):
    at = unit + lax.shift_right_logical(lax.broadcasted_iota(jnp.int32, (1, DOM), 1), DSTEP.bit_length() - 1)
    return jnp.where((at >= first) & (at < last), 1.0, 0.0).astype(jnp.bfloat16)


def times(left, right):
    return lax.dot_general(left, right, (((1,), (1,)), ((), ())), preferred_element_type=jnp.float32)


def swapped(values):
    return jnp.swapaxes(values, 0, 1)


def run(copies):
    for c in copies:
        c.start()
    for c in copies:
        c.wait()


def load_parts(block, raw, sems):
    parts = sems.shape[0]
    step = raw.shape[0] // parts
    return [
        pltpu.make_async_copy(block.at[pl.ds(q * step, step)], raw.at[pl.ds(q * step, step)], sems.at[q])
        for q in range(parts)
    ]


def first_kernel(pair_mask, dom_start, bfac, out, own, raw, made, sems, out_sems):
    _, is_odd = position()
    rows = raw.shape[0]
    column = lax.broadcasted_iota(jnp.int32, own.shape, 1)
    value = jnp.zeros(own.shape, jnp.int32)
    for at in range(PER):
        source = pair_mask if at < PER // 2 else dom_start
        block, r = divmod(at % (PER // 2), 3)
        value = jnp.where(column == at, source[block, r], value)
    own[...] = value

    @pl.when(is_odd)
    def _():
        loads = load_parts(bfac.at[1], raw, sems)
        for c in loads:
            c.start()
        at = boundary(lambda block, r: (pair_mask[block, r], dom_start[block, r]))["first"]
        stores = []

        def store(first, count):
            piece = pl.ds(first, count)
            c = pltpu.make_async_copy(made.at[piece], out.at[piece], out_sems.at[len(stores)])
            c.start()
            stores.append(c)

        made[2 * rows :, :] = jnp.zeros((NOTE, DOM), made.dtype)
        made[2 * rows :, :DSTEP] = jnp.concatenate([value, value], 0).astype(jnp.float32).astype(made.dtype)
        store(2 * rows, NOTE)
        step = rows // len(loads)
        for q, c in enumerate(loads):
            c.wait()
            part = swapped(raw[pl.ds(q * step, step), :, lanes(at, UNITS)])
            for i in range(2):
                made[pl.ds(i * rows + q * step, step), :] = part[i]
                store(i * rows + q * step, step)
        for c in stores:
            c.wait()


def second_kernel(own, bfac, out, zero, raw, sems):
    _, is_odd = position()
    zero[0] = jnp.minimum(own[0, 0], 0)

    @pl.when(is_odd)
    def _():
        b = boundary(lambda block, r: flags(own, block, r))
        loads = load_parts(bfac.at[jnp.where(b["m1"] > 0, 0, 1)], raw, sems)
        for c in loads:
            c.start()
        step = raw.shape[0] // len(loads)
        for q, c in enumerate(loads):
            c.wait()
            rows = pl.ds(q * step, step)
            out[:, rows, :] = swapped(raw[rows, :, lanes(b["second"], UNITS)])


def relayouter(bfac, raw, target, loads):
    step = 32

    def relayout(b):
        loads[b].wait()

        def some(q, carry):
            rows = pl.ds(pl.multiple_of(q * step, step), step)
            target[b, :, rows, :] = swapped(raw[b, rows])
            return carry

        lax.fori_loop(0, bfac.shape[1] // step, some, 0)

    return relayout


def product(left, a, right, b, at, keep):
    value = sum(times(left[a, i, :, lanes(at, UNITS)], right[b, i, :, lanes(at, UNITS)]) for i in range(2))
    return value * keep.astype(jnp.float32)


def own_kernel(own, bfac, kband, kmirror, mine, held, raw, out, sems):
    loads = [pltpu.make_async_copy(bfac.at[b], raw.at[b], sems.at[b]) for b in range(2)]
    relayout = relayouter(bfac, raw, held, loads)
    stores = []

    def store(source, target):
        c = pltpu.make_async_copy(source, target, sems.at[2 + len(stores)])
        c.start()
        stores.append(c)

    def keep(slot, value, target):
        out[slot] = value
        store(out.at[slot], target)

    for c in loads:
        c.start()
    for b in range(2):
        relayout(b)
        store(held.at[b], mine.at[b])
    k, s = flags(own, 0, 0)
    keep(0, product(held, 0, held, 0, s, k), kband.at[0, 0])
    k, s = flags(own, 0, 1)
    value = product(held, 0, held, 1, s, k)
    keep(1, value, kband.at[0, 1])
    keep(2, value.T, kmirror.at[1, 0])
    k, s = flags(own, 1, 0)
    keep(3, product(held, 1, held, 1, s, k), kband.at[1, 0])
    for c in stores:
        c.wait()


def fast_kernel(own, below, mine, other, kband_in, kmirror_in, kband, kmirror, held, theirs, raw, out, sems):
    _, is_odd = position()
    loads = [pltpu.make_async_copy(other.at[b], raw.at[b], sems.at[b]) for b in range(2)]
    held_load = pltpu.make_async_copy(mine, held, sems.at[2])
    relayout = relayouter(other, raw, theirs, loads)
    for c in (*loads, held_load):
        c.start()

    def get(block, r):
        return tuple(jnp.where(is_odd, a, b) for a, b in zip(flags(below, block, r), flags(own, block, r)))

    b = boundary(get)
    relayout(0)
    relayout(1)
    held_load.wait()
    close = jnp.where(is_odd, 0, 1)
    pick = lambda x, y: jnp.where(is_odd, x, y)
    out[0] = product(held, 1 - close, theirs, 1 - close, pick(b["s3"], b["s1"]), pick(b["m3"], b["m1"]))
    out[1] = product(held, close, theirs, 1 - close, b["s2"], b["m2"])
    out[2] = product(held, close, theirs, close, pick(b["s1"], b["s3"]), pick(b["m1"], b["m3"]))

    def put(targets):
        run([pltpu.make_async_copy(out.at[j], ref, sems.at[3 + j]) for j, ref in enumerate(targets)])

    @pl.when(is_odd)
    def _():
        put([kmirror.at[1, 1], kmirror.at[0, 0], kmirror.at[0, 1]])

    @pl.when(jnp.logical_not(is_odd))
    def _():
        put([kband.at[0, 2], kband.at[1, 1], kband.at[1, 2]])


def first_products_kernel(
    n, own, below, got, mine, back, steps, near, second, extra, rest, lives, case, far_window, near_window, staged, sems
):
    me, is_odd = position()
    b = slow_boundary(own, below)
    exists = jnp.where(is_odd, me < n - 1, me > 0)
    short = sum((b["half"] > c).astype(jnp.int32) for c in UP[:-1])
    long = len(UP) + sum((b["half"] > c).astype(jnp.int32) for c in BOTH[:-1])
    which = lax.shift_right_logical(jnp.where(is_odd, me, me - 1) - 1, 1)
    splits = exists & (b["split"] > 0)
    is_long = b["split"] > SPARE
    case[0] = jnp.where(splits, 1 + which * len(UP + BOTH) + jnp.where(is_long, long, short), 0)
    case[1] = jnp.where(splits & is_long, 1 + which, 0)

    @pl.when(splits)
    def _():
        at = jnp.minimum(b["low"], UNITS)
        run([pltpu.make_async_copy(mine.at[jnp.where(is_odd, 1, 0), :, :, lanes(at, UNITS)], staged, sems.at[3])])
        lower, upper = b["low"] - at, b["low"] - at + b["half"]
        sent = jnp.where(is_odd, lower, upper)
        kept = jnp.where(is_odd, upper, lower)
        count = jnp.where(is_odd, b["split"] - b["half"], b["half"])

        def some(u, carry):
            alive = jnp.where(u < count, 1.0, 0.0).astype(rest.dtype)
            for i in range(2):
                extra[i, :, lanes(u)] = staged[i, :, lanes(jnp.minimum(sent + u, UNITS - 1))]
                rest[i, :, lanes(u)] = staged[i, :, lanes(jnp.minimum(kept + u, UNITS - 1))] * alive
            return carry

        lax.fori_loop(0, SPARE, some, 0)

    @pl.when(jnp.logical_not(is_odd))
    def _():
        rows = mine.shape[2]
        at = b["first"]
        loads = [
            pltpu.make_async_copy(mine.at[1, :, :, lanes(at, UNITS)], far_window, sems.at[0]),
            pltpu.make_async_copy(mine.at[0, :, :, lanes(at, UNITS)], near_window, sems.at[1]),
            pltpu.make_async_copy(mine.at[0, :, :, lanes(b["second"], UNITS)], second, sems.at[2]),
        ]
        for c in loads:
            c.start()
        left = [got[pl.ds(i * rows, rows), :] for i in range(2)]

        def against(ref, scale):
            return sum(times(left[i], ref[i] * scale) for i in range(2))

        loads[0].wait()
        value = against(far_window, counted(at, at, at + UNITS * b["m3"]))
        back[...] = value
        steps[...], whole, power = coded(value)
        lives[0:1, :] = jnp.zeros((1, rows), lives.dtype) + b["m1"].astype(lives.dtype)
        lives[1:2, :] = whole
        lives[2:3, :] = power
        loads[1].wait()
        near[...] = against(near_window, counted(at, b["s2"], b["s2"] + UNITS * b["m2"]))
        loads[2].wait()
        far_lives = b["m1"] > 0
        counts = counted(
            b["second"],
            jnp.where(far_lives, b["second"], b["low"]),
            jnp.where(far_lives, b["second"] + UNITS, b["low"] + b["rest"]),
        )
        for i in range(2):
            second[i] = second[i] * counts


def rest_kernel(got, rest, out):
    _, is_odd = position()
    out[...] = jnp.zeros(out.shape, out.dtype)

    def some(k, carry):
        for i in range(2):
            out[...] += times(got[i, :, lanes(2 * k, 2)], rest[i, :, lanes(2 * k, 2)])
        return carry

    lax.fori_loop(0, got.shape[2] // (2 * DSTEP), some, 0)

    @pl.when(is_odd)
    def _():
        out[...] = out[...].T


def coded(value):
    top = jnp.maximum(jnp.max(jnp.abs(value), axis=0, keepdims=True), 1e-30)
    power = jnp.ceil(jnp.log2(top)) - 14.0
    unit = jnp.exp2(power)
    whole = jnp.clip(jnp.ceil(top / unit), 1.0, STEPS)
    steps = value * (STEPS / (whole * unit)) + ROUND
    return (steps - ROUND).astype(jnp.int32).astype(jnp.int16), whole, power


def decoded(steps, whole, power):
    return steps * (whole * jnp.exp2(power) * (1.0 / STEPS))


def second_products_kernel(got, second, steps, near, more, lives, results, part, sent, arrived, sems):
    _, is_odd = position()

    @pl.when(is_odd)
    def _():
        part[...] = more[...]

    @pl.when(jnp.logical_not(is_odd))
    def _():
        rows = steps.shape[0]
        width = DOM // sems.shape[0]
        spans = [slice(k * width, (k + 1) * width) for k in range(sems.shape[0])]
        loads = [
            pltpu.make_async_copy(got.at[:, :, span], arrived.at[:, :, span], sems.at[k]) for k, span in enumerate(spans)
        ]
        for c in loads:
            c.start()
        sent[pl.ds(2 * rows, rows), :] = steps[...]
        lived, whole, power = (lives[k : k + 1, :] for k in range(3))
        row = lax.broadcasted_iota(jnp.int32, (NOTE, rows), 0)
        scales = jnp.where(row == 4, whole, jnp.where(row == 5, power, 0.0))
        value = 0.0
        for c, span in zip(loads, spans):
            c.wait()
            value = value + sum(times(arrived[i, :, span], second[i, :, span]) for i in range(2))
        for k, block in enumerate((value * lived, near[...] + more[...] + value * (1.0 - lived))):
            (results, part)[k][...] = block
            sent[pl.ds(k * rows, rows), :], whole, power = coded(block)
            scales = jnp.where(row == 2 * k, whole, jnp.where(row == 2 * k + 1, power, scales))
        sent[pl.ds(3 * rows, NOTE), :] = scales.astype(jnp.int32).astype(jnp.int16)


def mirror_kernel(case, back, results, part, kmirror_in, kmirror, out, sems):
    _, is_odd = position()

    @pl.when(jnp.logical_not(is_odd))
    def _():
        out[0] = back[...].T
        out[1] = results[...].T
        targets = [kmirror.at[1, 1], kmirror.at[0, 1]]
        run([pltpu.make_async_copy(out.at[j], ref, sems.at[j]) for j, ref in enumerate(targets)])

        @pl.when(case[1] == 0)
        def _():
            out[2] = part[...].T
            run([pltpu.make_async_copy(out.at[2], kmirror.at[0, 0], sems.at[2])])


def last_kernel(case, got, part, other, kband_in, kmirror_in, kband, kmirror, out, mine, theirs, sems):
    _, is_odd = position()
    due = case[1] > 0

    @pl.when(due)
    def _():
        run([pltpu.make_async_copy(part, mine, sems.at[3]), pltpu.make_async_copy(other, theirs, sems.at[4])])

    @pl.when(is_odd)
    def _():
        rows = out.shape[1]
        scales = got[pl.ds(3 * rows, NOTE), :].astype(jnp.int32).astype(jnp.float32)
        copies = []
        for k, ref in enumerate((kband.at[0, 2], kband.at[1, 1], kband.at[1, 2])):
            steps = got[pl.ds(k * rows, rows), :].astype(jnp.int32).astype(jnp.float32)
            out[k] = decoded(steps, scales[2 * k : 2 * k + 1], scales[2 * k + 1 : 2 * k + 2])
            if k == 1:

                @pl.when(due)
                def _():
                    out[1] = mine[...] + theirs[...]

            copies.append(pltpu.make_async_copy(out.at[k], ref, sems.at[k]))
            copies[-1].start()
        for c in copies:
            c.wait()

    @pl.when(jnp.logical_not(is_odd) & due)
    def _():
        out[0] = (mine[...] + theirs[...]).T
        run([pltpu.make_async_copy(out.at[0], kmirror.at[0, 0], sems.at[0])])


def call(kernel, outs, ins, out_specs, scratch, flops=0, moved=0, aliases=None, vmem=40):
    inner = kernel.func if isinstance(kernel, functools.partial) else kernel
    return pl.pallas_call(
        kernel,
        out_shape=outs,
        in_specs=ins,
        out_specs=out_specs,
        scratch_shapes=scratch,
        input_output_aliases=aliases or {},
        compiler_params=pltpu.CompilerParams(vmem_limit_bytes=vmem * 2**20),
        cost_estimate=pl.CostEstimate(flops=flops, bytes_accessed=moved, transcendentals=0),
        name=inner.__name__,
    )


def per_device(bfac, pair_mask, dom_start):
    n = lax.axis_size("wide")
    _, rows, orbitals, fitting = bfac.shape
    upward = [(i, i + 1) for i in range(1, n - 1, 2)]
    downward = [(j, i) for i, j in upward]
    fast = [p for i in range(0, n, 2) for p in ((i, i + 1), (i + 1, i))]
    f32, bf16 = jnp.float32, bfac.dtype
    shape = jax.ShapeDtypeStruct
    dma = pltpu.SemaphoreType.DMA
    square = shape((rows, rows), f32)
    window = shape((orbitals, rows, DOM), bf16)
    raw_block = pltpu.VMEM((rows, orbitals, fitting), bf16)

    whole = (orbitals * rows + NOTE, DOM)
    parts = 8
    first, own = call(
        first_kernel,
        (shape(whole, bf16), shape((8, 128), jnp.int32)),
        [SMEM, SMEM, HBM],
        (HBM, VMEM),
        [raw_block, pltpu.VMEM(whole, bf16), dma((parts,)), dma((parts * orbitals + 1,))],
        vmem=60,
    )(pair_mask, dom_start, bfac)
    first_got = lax.ppermute(first, "wide", upward)

    second, zero = call(
        second_kernel,
        (window, shape((1,), jnp.int32)),
        [SMEM, HBM],
        (VMEM, SMEM),
        [raw_block, dma((8,))],
        vmem=57,
    )(own, bfac)
    second_got = lax.ppermute(second, "wide", upward)

    band = shape((2, 3, rows, rows), f32)
    mirror = shape((2, 2, rows, rows), f32)
    both = shape((2, orbitals, rows, fitting), bf16)
    spare = shape((orbitals, rows, SPARE * DSTEP), bf16)
    blocks = pltpu.VMEM((2, orbitals, rows, fitting), bf16)
    raw_blocks = pltpu.VMEM((2, rows, orbitals, fitting), bf16)

    def inner(own, bfac):
        below = lax.ppermute(own, "wide", [(i, i + 1) for i in range(0, n, 2)])
        other = lax.ppermute(bfac, "wide", fast)
        kband, kmirror, mine = call(
            own_kernel,
            (band, mirror, both),
            [SMEM, HBM],
            (HBM, HBM, HBM),
            [blocks, raw_blocks, pltpu.VMEM((4, rows, rows), f32), dma((8,))],
            2**31,
            2**25,
            vmem=40,
        )(own, bfac)
        kband, kmirror = call(
            fast_kernel,
            (band, mirror),
            [SMEM, SMEM, HBM, HBM, HBM, HBM],
            (HBM, HBM),
            [blocks, blocks, raw_blocks, pltpu.VMEM((3, rows, rows), f32), dma((6,))],
            2**31,
            2**25,
            {4: 0, 5: 1},
            vmem=32,
        )(own, below, mine, other, kband, kmirror)
        return kband, kmirror, mine

    def unused(own, bfac):
        return tuple(jnp.zeros(o.shape, o.dtype) for o in (band, mirror, both))

    own, bfac, _ = lax.optimization_barrier((own, bfac, second))
    kband, kmirror, mine = lax.cond(zero[0] == 0, inner, unused, own, bfac)

    below = first_got[orbitals * rows : orbitals * rows + 8, :DSTEP].astype(jnp.int32)
    staged = pltpu.VMEM((orbitals, rows, DOM), bf16)
    back, steps, near, second_window, extra, rest_window, lives, case = call(
        functools.partial(first_products_kernel, n),
        (
            square,
            shape((rows, rows), jnp.int16),
            square,
            window,
            spare,
            spare,
            shape((8, rows), f32),
            shape((2,), jnp.int32),
        ),
        [SMEM, SMEM, VMEM, HBM],
        (VMEM, VMEM, VMEM, VMEM, VMEM, VMEM, VMEM, SMEM),
        [staged, staged, staged, dma((4,))],
        2**31,
        2**22,
        vmem=16,
    )(own, below, first_got, mine)

    def nothing(*_):
        return jnp.zeros((rows, rows), f32)

    def pair_of(lower):
        return [(lower, lower + 1), (lower + 1, lower)]

    def rest(lower, count, pairs):
        def branch(extra, rest_window):
            got = lax.ppermute(extra[:, :, : count * DSTEP], "wide", pairs)
            return call(rest_kernel, square, [VMEM, VMEM], VMEM, [], 2**26 * count, 2**19 * count, vmem=8)(
                got, rest_window
            )

        return branch

    def parts_of(lower):
        return lambda part: lax.ppermute(part, "wide", pair_of(lower))

    lowers = range(1, n - 1, 2)
    branches = [nothing]
    for i in lowers:
        branches += [rest(i, c, [(i, i + 1)]) for c in UP] + [rest(i, c, pair_of(i)) for c in BOTH]
    more = lax.switch(case[0], branches, extra, rest_window)

    results, part, sent = call(
        second_products_kernel,
        (square, square, shape((3 * rows + NOTE, rows), jnp.int16)),
        [HBM, VMEM, VMEM, VMEM, VMEM, VMEM],
        (VMEM, VMEM, VMEM),
        [pltpu.VMEM((orbitals, rows, DOM), bf16), dma((2,))],
        2**30,
        2**22,
        vmem=12,
    )(second_got, second_window, steps, near, more, lives)
    sent_got = lax.ppermute(sent, "wide", downward)
    other_part = lax.switch(case[1], [nothing] + [parts_of(i) for i in lowers], part)
    kmirror = call(
        mirror_kernel,
        mirror,
        [SMEM, VMEM, VMEM, VMEM, HBM],
        HBM,
        [pltpu.VMEM((3, rows, rows), f32), dma((3,))],
        0,
        2**20,
        {4: 0},
        vmem=8,
    )(case, back, results, part, kmirror)
    return call(
        last_kernel,
        (band, mirror),
        [SMEM, VMEM, HBM, HBM, HBM, HBM],
        (HBM, HBM),
        [
            pltpu.VMEM((3, rows, rows), f32),
            pltpu.VMEM((rows, rows), f32),
            pltpu.VMEM((rows, rows), f32),
            dma((5,)),
        ],
        0,
        2**20,
        {4: 0, 5: 1},
        vmem=8,
    )(case, sent_got, part, other_part, kband, kmirror)


def solution(mesh):
    placed = (P("wide", None, "groups", None), P("wide", None), P("wide", None))
    return jax.shard_map(
        per_device,
        mesh=mesh,
        in_specs=placed,
        out_specs=(
            P(("groups", "wide"), None, None, None),
            P(("groups", "wide"), None, None, None),
        ),
        check_vma=False,
    )
```

```python
import functools

import jax
import jax.numpy as jnp
from jax import lax
from jax.experimental import pallas as pl
from jax.experimental.pallas import tpu as pltpu
from jax.sharding import PartitionSpec as P

DOM = 2048
DSTEP = 128
UNITS = DOM // DSTEP
UP = (2, 4)
BOTH = (4, 6, 8)
SPARE = 8
PER = 12
NOTE = 16
STEPS = 32767.0
ROUND = 1.5 * 2.0**23
VMEM = pl.BlockSpec(memory_space=pltpu.VMEM)
SMEM = pl.BlockSpec(memory_space=pltpu.SMEM)
HBM = pl.BlockSpec(memory_space=pltpu.HBM)


def flags(screen, block, r):
    at = block * 3 + r
    return screen[0, at], screen[0, at + PER // 2]


def boundary(get):
    m1, s1 = get(0, 2)
    m2, s2 = get(1, 1)
    m3, s3 = get(1, 2)
    first = jnp.where(m3 > 0, s3, s2)
    low = jnp.where(first <= s2, jnp.maximum(s2, first + UNITS), s2)
    high = jnp.where(first <= s2, s2 + UNITS, jnp.minimum(s2 + UNITS, first))
    rest = jnp.maximum(high - low, 0) * m2
    second = jnp.where(m1 > 0, s1, jnp.minimum(low, UNITS))
    split = rest * m1
    half = jnp.where(split > UP[-1], lax.shift_right_logical(split + 1, 1), split)
    return dict(
        m1=m1, s1=s1, m2=m2, s2=s2, m3=m3, s3=s3, first=first, low=low, rest=rest, second=second, split=split, half=half
    )


def position():
    me = lax.axis_index("wide")
    return me, lax.rem(me, 2) == 1


def slow_boundary(own, below):
    _, is_odd = position()

    def get(block, r):
        return tuple(jnp.where(is_odd, a, b) for a, b in zip(flags(own, block, r), flags(below, block, r)))

    return boundary(get)


def lanes(unit, count=1):
    return pl.ds(pl.multiple_of(unit * DSTEP, DSTEP), count * DSTEP)


def counted(unit, first, last):
    at = unit + lax.shift_right_logical(lax.broadcasted_iota(jnp.int32, (1, DOM), 1), DSTEP.bit_length() - 1)
    return jnp.where((at >= first) & (at < last), 1.0, 0.0).astype(jnp.bfloat16)


def times(left, right):
    return lax.dot_general(left, right, (((1,), (1,)), ((), ())), preferred_element_type=jnp.float32)


def swapped(values):
    return jnp.swapaxes(values, 0, 1)


def run(copies):
    for c in copies:
        c.start()
    for c in copies:
        c.wait()


def load_parts(block, raw, sems):
    parts = sems.shape[0]
    step = raw.shape[0] // parts
    return [
        pltpu.make_async_copy(block.at[pl.ds(q * step, step)], raw.at[pl.ds(q * step, step)], sems.at[q])
        for q in range(parts)
    ]


def first_kernel(pair_mask, dom_start, bfac, out, own, raw, made, sems, out_sems):
    _, is_odd = position()
    rows = raw.shape[0]
    column = lax.broadcasted_iota(jnp.int32, own.shape, 1)
    value = jnp.zeros(own.shape, jnp.int32)
    for at in range(PER):
        source = pair_mask if at < PER // 2 else dom_start
        block, r = divmod(at % (PER // 2), 3)
        value = jnp.where(column == at, source[block, r], value)
    own[...] = value

    @pl.when(is_odd)
    def _():
        loads = load_parts(bfac.at[1], raw, sems)
        for c in loads:
            c.start()
        at = boundary(lambda block, r: (pair_mask[block, r], dom_start[block, r]))["first"]
        stores = []

        def store(first, count):
            piece = pl.ds(first, count)
            c = pltpu.make_async_copy(made.at[piece], out.at[piece], out_sems.at[len(stores)])
            c.start()
            stores.append(c)

        made[2 * rows :, :] = jnp.zeros((NOTE, DOM), made.dtype)
        made[2 * rows :, :DSTEP] = jnp.concatenate([value, value], 0).astype(jnp.float32).astype(made.dtype)
        store(2 * rows, NOTE)
        step = rows // len(loads)
        for q, c in enumerate(loads):
            c.wait()
            part = swapped(raw[pl.ds(q * step, step), :, lanes(at, UNITS)])
            for i in range(2):
                made[pl.ds(i * rows + q * step, step), :] = part[i]
                store(i * rows + q * step, step)
        for c in stores:
            c.wait()


def second_kernel(own, bfac, out, zero, raw, sems):
    _, is_odd = position()
    zero[0] = jnp.minimum(own[0, 0], 0)

    @pl.when(is_odd)
    def _():
        b = boundary(lambda block, r: flags(own, block, r))
        loads = load_parts(bfac.at[jnp.where(b["m1"] > 0, 0, 1)], raw, sems)
        for c in loads:
            c.start()
        step = raw.shape[0] // len(loads)
        for q, c in enumerate(loads):
            c.wait()
            rows = pl.ds(q * step, step)
            out[:, rows, :] = swapped(raw[rows, :, lanes(b["second"], UNITS)])


def relayouter(bfac, raw, target, loads):
    step = 32

    def relayout(b):
        loads[b].wait()

        def some(q, carry):
            rows = pl.ds(pl.multiple_of(q * step, step), step)
            target[b, :, rows, :] = swapped(raw[b, rows])
            return carry

        lax.fori_loop(0, bfac.shape[1] // step, some, 0)

    return relayout


def product(left, a, right, b, at, keep):
    value = sum(times(left[a, i, :, lanes(at, UNITS)], right[b, i, :, lanes(at, UNITS)]) for i in range(2))
    return value * keep.astype(jnp.float32)


def own_kernel(own, bfac, kband, kmirror, mine, held, raw, out, sems):
    loads = [pltpu.make_async_copy(bfac.at[b], raw.at[b], sems.at[b]) for b in range(2)]
    relayout = relayouter(bfac, raw, held, loads)
    stores = []

    def store(source, target):
        c = pltpu.make_async_copy(source, target, sems.at[2 + len(stores)])
        c.start()
        stores.append(c)

    def keep(slot, value, target):
        out[slot] = value
        store(out.at[slot], target)

    for c in loads:
        c.start()
    for b in range(2):
        relayout(b)
        store(held.at[b], mine.at[b])
    k, s = flags(own, 0, 0)
    keep(0, product(held, 0, held, 0, s, k), kband.at[0, 0])
    k, s = flags(own, 0, 1)
    value = product(held, 0, held, 1, s, k)
    keep(1, value, kband.at[0, 1])
    keep(2, value.T, kmirror.at[1, 0])
    k, s = flags(own, 1, 0)
    keep(3, product(held, 1, held, 1, s, k), kband.at[1, 0])
    for c in stores:
        c.wait()


def fast_kernel(own, below, mine, other, kband_in, kmirror_in, kband, kmirror, held, theirs, raw, out, sems):
    _, is_odd = position()
    loads = [pltpu.make_async_copy(other.at[b], raw.at[b], sems.at[b]) for b in range(2)]
    held_load = pltpu.make_async_copy(mine, held, sems.at[2])
    relayout = relayouter(other, raw, theirs, loads)
    for c in (*loads, held_load):
        c.start()

    def get(block, r):
        return tuple(jnp.where(is_odd, a, b) for a, b in zip(flags(below, block, r), flags(own, block, r)))

    b = boundary(get)
    relayout(0)
    relayout(1)
    held_load.wait()
    close = jnp.where(is_odd, 0, 1)
    pick = lambda x, y: jnp.where(is_odd, x, y)
    out[0] = product(held, 1 - close, theirs, 1 - close, pick(b["s3"], b["s1"]), pick(b["m3"], b["m1"]))
    out[1] = product(held, close, theirs, 1 - close, b["s2"], b["m2"])
    out[2] = product(held, close, theirs, close, pick(b["s1"], b["s3"]), pick(b["m1"], b["m3"]))

    def put(targets):
        run([pltpu.make_async_copy(out.at[j], ref, sems.at[3 + j]) for j, ref in enumerate(targets)])

    @pl.when(is_odd)
    def _():
        put([kmirror.at[1, 1], kmirror.at[0, 0], kmirror.at[0, 1]])

    @pl.when(jnp.logical_not(is_odd))
    def _():
        put([kband.at[0, 2], kband.at[1, 1], kband.at[1, 2]])


def first_products_kernel(
    n, own, below, got, mine, back, steps, near, second, extra, rest, lives, case, far_window, near_window, staged, sems
):
    me, is_odd = position()
    b = slow_boundary(own, below)
    exists = jnp.where(is_odd, me < n - 1, me > 0)
    short = sum((b["half"] > c).astype(jnp.int32) for c in UP[:-1])
    long = len(UP) + sum((b["half"] > c).astype(jnp.int32) for c in BOTH[:-1])
    which = lax.shift_right_logical(jnp.where(is_odd, me, me - 1) - 1, 1)
    splits = exists & (b["split"] > 0)
    is_long = b["split"] > UP[-1]
    case[0] = jnp.where(splits, 1 + which * len(UP + BOTH) + jnp.where(is_long, long, short), 0)
    case[1] = jnp.where(splits & is_long, 1 + which, 0)

    @pl.when(splits)
    def _():
        at = jnp.minimum(b["low"], UNITS)
        run([pltpu.make_async_copy(mine.at[jnp.where(is_odd, 1, 0), :, :, lanes(at, UNITS)], staged, sems.at[3])])
        lower, upper = b["low"] - at, b["low"] - at + b["half"]
        sent = jnp.where(is_odd, lower, upper)
        kept = jnp.where(is_odd, upper, lower)
        count = jnp.where(is_odd, b["split"] - b["half"], b["half"])

        def some(u, carry):
            alive = jnp.where(u < count, 1.0, 0.0).astype(rest.dtype)
            for i in range(2):
                extra[i, :, lanes(u)] = staged[i, :, lanes(jnp.minimum(sent + u, UNITS - 1))]
                rest[i, :, lanes(u)] = staged[i, :, lanes(jnp.minimum(kept + u, UNITS - 1))] * alive
            return carry

        lax.fori_loop(0, SPARE, some, 0)

    @pl.when(jnp.logical_not(is_odd))
    def _():
        rows = mine.shape[2]
        at = b["first"]
        loads = [
            pltpu.make_async_copy(mine.at[1, :, :, lanes(at, UNITS)], far_window, sems.at[0]),
            pltpu.make_async_copy(mine.at[0, :, :, lanes(at, UNITS)], near_window, sems.at[1]),
            pltpu.make_async_copy(mine.at[0, :, :, lanes(b["second"], UNITS)], second, sems.at[2]),
        ]
        for c in loads:
            c.start()
        left = [got[pl.ds(i * rows, rows), :] for i in range(2)]

        def against(ref, scale):
            return sum(times(left[i], ref[i] * scale) for i in range(2))

        loads[0].wait()
        value = against(far_window, counted(at, at, at + UNITS * b["m3"]))
        back[...] = value
        steps[...], whole, power = coded(value)
        lives[0:1, :] = jnp.zeros((1, rows), lives.dtype) + b["m1"].astype(lives.dtype)
        lives[1:2, :] = whole
        lives[2:3, :] = power
        loads[1].wait()
        near[...] = against(near_window, counted(at, b["s2"], b["s2"] + UNITS * b["m2"]))
        loads[2].wait()
        far_lives = b["m1"] > 0
        counts = counted(
            b["second"],
            jnp.where(far_lives, b["second"], b["low"]),
            jnp.where(far_lives, b["second"] + UNITS, b["low"] + b["rest"]),
        )
        for i in range(2):
            second[i] = second[i] * counts


def rest_kernel(got, rest, out):
    _, is_odd = position()
    width = got.shape[2]
    step = min(width, 4 * DSTEP)
    out[...] = jnp.zeros(out.shape, out.dtype)
    for k in range(0, width, step):
        span = slice(k, min(k + step, width))
        out[...] += sum(times(got[i, :, span], rest[i, :, span]) for i in range(2))

    @pl.when(is_odd)
    def _():
        out[...] = out[...].T


def coded(value):
    top = jnp.maximum(jnp.max(jnp.abs(value), axis=0, keepdims=True), 1e-30)
    power = jnp.ceil(jnp.log2(top)) - 14.0
    unit = jnp.exp2(power)
    whole = jnp.clip(jnp.ceil(top / unit), 1.0, STEPS)
    steps = value * (STEPS / (whole * unit)) + ROUND
    return (steps - ROUND).astype(jnp.int32).astype(jnp.int16), whole, power


def decoded(steps, whole, power):
    return steps * (whole * jnp.exp2(power) * (1.0 / STEPS))


def second_products_kernel(got, second, steps, near, more, lives, results, part, sent):
    _, is_odd = position()

    @pl.when(is_odd)
    def _():
        part[...] = more[...]

    @pl.when(jnp.logical_not(is_odd))
    def _():
        rows = steps.shape[0]
        sent[pl.ds(2 * rows, rows), :] = steps[...]
        lived, whole, power = (lives[k : k + 1, :] for k in range(3))
        row = lax.broadcasted_iota(jnp.int32, (NOTE, rows), 0)
        scales = jnp.where(row == 4, whole, jnp.where(row == 5, power, 0.0))
        value = sum(times(got[i], second[i]) for i in range(2))
        for k, block in enumerate((value * lived, near[...] + more[...] + value * (1.0 - lived))):
            (results, part)[k][...] = block
            sent[pl.ds(k * rows, rows), :], whole, power = coded(block)
            scales = jnp.where(row == 2 * k, whole, jnp.where(row == 2 * k + 1, power, scales))
        sent[pl.ds(3 * rows, NOTE), :] = scales.astype(jnp.int32).astype(jnp.int16)


def mirror_kernel(case, back, results, part, kmirror_in, kmirror, out, sems):
    _, is_odd = position()

    @pl.when(jnp.logical_not(is_odd))
    def _():
        out[0] = back[...].T
        out[1] = results[...].T
        targets = [kmirror.at[1, 1], kmirror.at[0, 1]]
        run([pltpu.make_async_copy(out.at[j], ref, sems.at[j]) for j, ref in enumerate(targets)])

        @pl.when(case[1] == 0)
        def _():
            out[2] = part[...].T
            run([pltpu.make_async_copy(out.at[2], kmirror.at[0, 0], sems.at[2])])


def last_kernel(case, got, part, other, kband_in, kmirror_in, kband, kmirror, out, mine, theirs, sems):
    _, is_odd = position()
    due = case[1] > 0

    @pl.when(due)
    def _():
        run([pltpu.make_async_copy(part, mine, sems.at[3]), pltpu.make_async_copy(other, theirs, sems.at[4])])

    @pl.when(is_odd)
    def _():
        rows = out.shape[1]
        scales = got[pl.ds(3 * rows, NOTE), :].astype(jnp.int32).astype(jnp.float32)
        copies = []
        for k, ref in enumerate((kband.at[0, 2], kband.at[1, 1], kband.at[1, 2])):
            steps = got[pl.ds(k * rows, rows), :].astype(jnp.int32).astype(jnp.float32)
            out[k] = decoded(steps, scales[2 * k : 2 * k + 1], scales[2 * k + 1 : 2 * k + 2])
            if k == 1:

                @pl.when(due)
                def _():
                    out[1] = mine[...] + theirs[...]

            copies.append(pltpu.make_async_copy(out.at[k], ref, sems.at[k]))
            copies[-1].start()
        for c in copies:
            c.wait()

    @pl.when(jnp.logical_not(is_odd) & due)
    def _():
        out[0] = (mine[...] + theirs[...]).T
        run([pltpu.make_async_copy(out.at[0], kmirror.at[0, 0], sems.at[0])])


def call(kernel, outs, ins, out_specs, scratch, flops=0, moved=0, aliases=None, vmem=40):
    inner = kernel.func if isinstance(kernel, functools.partial) else kernel
    return pl.pallas_call(
        kernel,
        out_shape=outs,
        in_specs=ins,
        out_specs=out_specs,
        scratch_shapes=scratch,
        input_output_aliases=aliases or {},
        compiler_params=pltpu.CompilerParams(vmem_limit_bytes=vmem * 2**20),
        cost_estimate=pl.CostEstimate(flops=flops, bytes_accessed=moved, transcendentals=0),
        name=inner.__name__,
    )


def per_device(bfac, pair_mask, dom_start):
    n = lax.axis_size("wide")
    _, rows, orbitals, fitting = bfac.shape
    upward = [(i, i + 1) for i in range(1, n - 1, 2)]
    downward = [(j, i) for i, j in upward]
    fast = [p for i in range(0, n, 2) for p in ((i, i + 1), (i + 1, i))]
    f32, bf16 = jnp.float32, bfac.dtype
    shape = jax.ShapeDtypeStruct
    dma = pltpu.SemaphoreType.DMA
    square = shape((rows, rows), f32)
    window = shape((orbitals, rows, DOM), bf16)
    raw_block = pltpu.VMEM((rows, orbitals, fitting), bf16)

    whole = (orbitals * rows + NOTE, DOM)
    parts = 8
    first, own = call(
        first_kernel,
        (shape(whole, bf16), shape((8, 128), jnp.int32)),
        [SMEM, SMEM, HBM],
        (HBM, VMEM),
        [raw_block, pltpu.VMEM(whole, bf16), dma((parts,)), dma((parts * orbitals + 1,))],
        vmem=60,
    )(pair_mask, dom_start, bfac)
    first_got = lax.ppermute(first, "wide", upward)

    second, zero = call(
        second_kernel,
        (window, shape((1,), jnp.int32)),
        [SMEM, HBM],
        (VMEM, SMEM),
        [raw_block, dma((8,))],
        vmem=57,
    )(own, bfac)
    second_got = lax.ppermute(second, "wide", upward)

    band = shape((2, 3, rows, rows), f32)
    mirror = shape((2, 2, rows, rows), f32)
    both = shape((2, orbitals, rows, fitting), bf16)
    spare = shape((orbitals, rows, SPARE * DSTEP), bf16)
    blocks = pltpu.VMEM((2, orbitals, rows, fitting), bf16)
    raw_blocks = pltpu.VMEM((2, rows, orbitals, fitting), bf16)

    def inner(own, bfac):
        below = lax.ppermute(own, "wide", [(i, i + 1) for i in range(0, n, 2)])
        other = lax.ppermute(bfac, "wide", fast)
        kband, kmirror, mine = call(
            own_kernel,
            (band, mirror, both),
            [SMEM, HBM],
            (HBM, HBM, HBM),
            [blocks, raw_blocks, pltpu.VMEM((4, rows, rows), f32), dma((8,))],
            2**31,
            2**25,
            vmem=40,
        )(own, bfac)
        kband, kmirror = call(
            fast_kernel,
            (band, mirror),
            [SMEM, SMEM, HBM, HBM, HBM, HBM],
            (HBM, HBM),
            [blocks, blocks, raw_blocks, pltpu.VMEM((3, rows, rows), f32), dma((6,))],
            2**31,
            2**25,
            {4: 0, 5: 1},
            vmem=32,
        )(own, below, mine, other, kband, kmirror)
        return kband, kmirror, mine

    def unused(own, bfac):
        return tuple(jnp.zeros(o.shape, o.dtype) for o in (band, mirror, both))

    own, bfac, _ = lax.optimization_barrier((own, bfac, second))
    kband, kmirror, mine = lax.cond(zero[0] == 0, inner, unused, own, bfac)

    below = first_got[orbitals * rows : orbitals * rows + 8, :DSTEP].astype(jnp.int32)
    staged = pltpu.VMEM((orbitals, rows, DOM), bf16)
    back, steps, near, second_window, extra, rest_window, lives, case = call(
        functools.partial(first_products_kernel, n),
        (
            square,
            shape((rows, rows), jnp.int16),
            square,
            window,
            spare,
            spare,
            shape((8, rows), f32),
            shape((2,), jnp.int32),
        ),
        [SMEM, SMEM, VMEM, HBM],
        (VMEM, VMEM, VMEM, VMEM, VMEM, VMEM, VMEM, SMEM),
        [staged, staged, staged, dma((4,))],
        2**31,
        2**22,
        vmem=16,
    )(own, below, first_got, mine)

    def nothing(*_):
        return jnp.zeros((rows, rows), f32)

    def pair_of(lower):
        return [(lower, lower + 1), (lower + 1, lower)]

    def rest(lower, count, pairs):
        def branch(extra, rest_window):
            got = lax.ppermute(extra[:, :, : count * DSTEP], "wide", pairs)
            return call(rest_kernel, square, [VMEM, VMEM], VMEM, [], 2**26 * count, 2**19 * count, vmem=8)(
                got, rest_window
            )

        return branch

    def parts_of(lower):
        return lambda part: lax.ppermute(part, "wide", pair_of(lower))

    lowers = range(1, n - 1, 2)
    branches = [nothing]
    for i in lowers:
        branches += [rest(i, c, [(i, i + 1)]) for c in UP] + [rest(i, c, pair_of(i)) for c in BOTH]
    more = lax.switch(case[0], branches, extra, rest_window)

    results, part, sent = call(
        second_products_kernel,
        (square, square, shape((3 * rows + NOTE, rows), jnp.int16)),
        [VMEM] * 6,
        (VMEM, VMEM, VMEM),
        [],
        2**30,
        2**22,
        vmem=12,
    )(second_got, second_window, steps, near, more, lives)
    sent_got = lax.ppermute(sent, "wide", downward)
    other_part = lax.switch(case[1], [nothing] + [parts_of(i) for i in lowers], part)
    kmirror = call(
        mirror_kernel,
        mirror,
        [SMEM, VMEM, VMEM, VMEM, HBM],
        HBM,
        [pltpu.VMEM((3, rows, rows), f32), dma((3,))],
        0,
        2**20,
        {4: 0},
        vmem=8,
    )(case, back, results, part, kmirror)
    return call(
        last_kernel,
        (band, mirror),
        [SMEM, VMEM, HBM, HBM, HBM, HBM],
        (HBM, HBM),
        [
            pltpu.VMEM((3, rows, rows), f32),
            pltpu.VMEM((rows, rows), f32),
            pltpu.VMEM((rows, rows), f32),
            dma((5,)),
        ],
        0,
        2**20,
        {4: 0, 5: 1},
        vmem=8,
    )(case, sent_got, part, other_part, kband, kmirror)


def solution(mesh):
    placed = (P("wide", None, "groups", None), P("wide", None), P("wide", None))
    return jax.shard_map(
        per_device,
        mesh=mesh,
        in_specs=placed,
        out_specs=(
            P(("groups", "wide"), None, None, None),
            P(("groups", "wide"), None, None, None),
        ),
        check_vma=False,
    )
```

```python
import functools

import jax
import jax.numpy as jnp
from jax import lax
from jax.experimental import pallas as pl
from jax.experimental.pallas import tpu as pltpu
from jax.sharding import PartitionSpec as P

DOM = 2048
DSTEP = 128
UNITS = DOM // DSTEP
UP = (2, 4)
BOTH = (3, 4, 6, 8)
SPARE = 8
PER = 12
NOTE = 16
STEPS = 32767.0
ROUND = 1.5 * 2.0**23
VMEM = pl.BlockSpec(memory_space=pltpu.VMEM)
SMEM = pl.BlockSpec(memory_space=pltpu.SMEM)
HBM = pl.BlockSpec(memory_space=pltpu.HBM)


def flags(screen, block, r):
    at = block * 3 + r
    return screen[0, at], screen[0, at + PER // 2]


def boundary(get):
    m1, s1 = get(0, 2)
    m2, s2 = get(1, 1)
    m3, s3 = get(1, 2)
    first = jnp.where(m3 > 0, s3, s2)
    low = jnp.where(first <= s2, jnp.maximum(s2, first + UNITS), s2)
    high = jnp.where(first <= s2, s2 + UNITS, jnp.minimum(s2 + UNITS, first))
    rest = jnp.maximum(high - low, 0) * m2
    second = jnp.where(m1 > 0, s1, jnp.minimum(low, UNITS))
    split = rest * m1
    half = jnp.where(split > UP[-1], lax.shift_right_logical(split + 1, 1), split)
    return dict(
        m1=m1, s1=s1, m2=m2, s2=s2, m3=m3, s3=s3, first=first, low=low, rest=rest, second=second, split=split, half=half
    )


def position():
    me = lax.axis_index("wide")
    return me, lax.rem(me, 2) == 1


def slow_boundary(own, below):
    _, is_odd = position()

    def get(block, r):
        return tuple(jnp.where(is_odd, a, b) for a, b in zip(flags(own, block, r), flags(below, block, r)))

    return boundary(get)


def lanes(unit, count=1):
    return pl.ds(pl.multiple_of(unit * DSTEP, DSTEP), count * DSTEP)


def counted(unit, first, last):
    at = unit + lax.shift_right_logical(lax.broadcasted_iota(jnp.int32, (1, DOM), 1), DSTEP.bit_length() - 1)
    return jnp.where((at >= first) & (at < last), 1.0, 0.0).astype(jnp.bfloat16)


def times(left, right):
    return lax.dot_general(left, right, (((1,), (1,)), ((), ())), preferred_element_type=jnp.float32)


def swapped(values):
    return jnp.swapaxes(values, 0, 1)


def run(copies):
    for c in copies:
        c.start()
    for c in copies:
        c.wait()


def load_parts(block, raw, sems):
    parts = sems.shape[0]
    step = raw.shape[0] // parts
    return [
        pltpu.make_async_copy(block.at[pl.ds(q * step, step)], raw.at[pl.ds(q * step, step)], sems.at[q])
        for q in range(parts)
    ]


def first_kernel(pair_mask, dom_start, bfac, out, own, raw, made, sems, out_sems):
    _, is_odd = position()
    rows = raw.shape[0]
    column = lax.broadcasted_iota(jnp.int32, own.shape, 1)
    value = jnp.zeros(own.shape, jnp.int32)
    for at in range(PER):
        source = pair_mask if at < PER // 2 else dom_start
        block, r = divmod(at % (PER // 2), 3)
        value = jnp.where(column == at, source[block, r], value)
    own[...] = value

    @pl.when(is_odd)
    def _():
        loads = load_parts(bfac.at[1], raw, sems)
        for c in loads:
            c.start()
        at = boundary(lambda block, r: (pair_mask[block, r], dom_start[block, r]))["first"]
        stores = []

        def store(first, count):
            piece = pl.ds(first, count)
            c = pltpu.make_async_copy(made.at[piece], out.at[piece], out_sems.at[len(stores)])
            c.start()
            stores.append(c)

        made[2 * rows :, :] = jnp.zeros((NOTE, DOM), made.dtype)
        made[2 * rows :, :DSTEP] = jnp.concatenate([value, value], 0).astype(jnp.float32).astype(made.dtype)
        store(2 * rows, NOTE)
        step = rows // len(loads)
        for q, c in enumerate(loads):
            c.wait()
            part = swapped(raw[pl.ds(q * step, step), :, lanes(at, UNITS)])
            for i in range(2):
                made[pl.ds(i * rows + q * step, step), :] = part[i]
                store(i * rows + q * step, step)
        for c in stores:
            c.wait()


def second_kernel(own, bfac, out, zero, raw, sems):
    _, is_odd = position()
    zero[0] = jnp.minimum(own[0, 0], 0)

    @pl.when(is_odd)
    def _():
        b = boundary(lambda block, r: flags(own, block, r))
        loads = load_parts(bfac.at[jnp.where(b["m1"] > 0, 0, 1)], raw, sems)
        for c in loads:
            c.start()
        step = raw.shape[0] // len(loads)
        for q, c in enumerate(loads):
            c.wait()
            rows = pl.ds(q * step, step)
            out[:, rows, :] = swapped(raw[rows, :, lanes(b["second"], UNITS)])


def relayouter(bfac, raw, target, loads):
    step = 32

    def relayout(b):
        loads[b].wait()

        def some(q, carry):
            rows = pl.ds(pl.multiple_of(q * step, step), step)
            target[b, :, rows, :] = swapped(raw[b, rows])
            return carry

        lax.fori_loop(0, bfac.shape[1] // step, some, 0)

    return relayout


def product(left, a, right, b, at, keep):
    value = sum(times(left[a, i, :, lanes(at, UNITS)], right[b, i, :, lanes(at, UNITS)]) for i in range(2))
    return value * keep.astype(jnp.float32)


def own_kernel(own, bfac, kband, kmirror, mine, held, raw, out, sems):
    loads = [pltpu.make_async_copy(bfac.at[b], raw.at[b], sems.at[b]) for b in range(2)]
    relayout = relayouter(bfac, raw, held, loads)
    stores = []

    def store(source, target):
        c = pltpu.make_async_copy(source, target, sems.at[2 + len(stores)])
        c.start()
        stores.append(c)

    def keep(slot, value, target):
        out[slot] = value
        store(out.at[slot], target)

    for c in loads:
        c.start()
    for b in range(2):
        relayout(b)
        store(held.at[b], mine.at[b])
    k, s = flags(own, 0, 0)
    keep(0, product(held, 0, held, 0, s, k), kband.at[0, 0])
    k, s = flags(own, 0, 1)
    value = product(held, 0, held, 1, s, k)
    keep(1, value, kband.at[0, 1])
    keep(2, value.T, kmirror.at[1, 0])
    k, s = flags(own, 1, 0)
    keep(3, product(held, 1, held, 1, s, k), kband.at[1, 0])
    for c in stores:
        c.wait()


def fast_kernel(own, below, mine, other, kband_in, kmirror_in, kband, kmirror, held, theirs, raw, out, sems):
    _, is_odd = position()
    loads = [pltpu.make_async_copy(other.at[b], raw.at[b], sems.at[b]) for b in range(2)]
    held_load = pltpu.make_async_copy(mine, held, sems.at[2])
    relayout = relayouter(other, raw, theirs, loads)
    for c in (*loads, held_load):
        c.start()

    def get(block, r):
        return tuple(jnp.where(is_odd, a, b) for a, b in zip(flags(below, block, r), flags(own, block, r)))

    b = boundary(get)
    relayout(0)
    relayout(1)
    held_load.wait()
    close = jnp.where(is_odd, 0, 1)
    pick = lambda x, y: jnp.where(is_odd, x, y)
    out[0] = product(held, 1 - close, theirs, 1 - close, pick(b["s3"], b["s1"]), pick(b["m3"], b["m1"]))
    out[1] = product(held, close, theirs, 1 - close, b["s2"], b["m2"])
    out[2] = product(held, close, theirs, close, pick(b["s1"], b["s3"]), pick(b["m1"], b["m3"]))

    def put(targets):
        run([pltpu.make_async_copy(out.at[j], ref, sems.at[3 + j]) for j, ref in enumerate(targets)])

    @pl.when(is_odd)
    def _():
        put([kmirror.at[1, 1], kmirror.at[0, 0], kmirror.at[0, 1]])

    @pl.when(jnp.logical_not(is_odd))
    def _():
        put([kband.at[0, 2], kband.at[1, 1], kband.at[1, 2]])


def first_products_kernel(
    n, own, below, got, mine, back, steps, near, second, extra, rest, lives, case, far_window, near_window, staged, sems
):
    me, is_odd = position()
    b = slow_boundary(own, below)
    exists = jnp.where(is_odd, me < n - 1, me > 0)
    short = sum((b["half"] > c).astype(jnp.int32) for c in UP[:-1])
    long = len(UP) + sum((b["half"] > c).astype(jnp.int32) for c in BOTH[:-1])
    which = lax.shift_right_logical(jnp.where(is_odd, me, me - 1) - 1, 1)
    splits = exists & (b["split"] > 0)
    is_long = b["split"] > UP[-1]
    case[0] = jnp.where(splits, 1 + which * len(UP + BOTH) + jnp.where(is_long, long, short), 0)
    case[1] = jnp.where(splits & is_long, 1 + which, 0)

    @pl.when(splits)
    def _():
        at = jnp.minimum(b["low"], UNITS)
        run([pltpu.make_async_copy(mine.at[jnp.where(is_odd, 1, 0), :, :, lanes(at, UNITS)], staged, sems.at[3])])
        lower, upper = b["low"] - at, b["low"] - at + b["half"]
        sent = jnp.where(is_odd, lower, upper)
        kept = jnp.where(is_odd, upper, lower)
        count = jnp.where(is_odd, b["split"] - b["half"], b["half"])

        def some(u, carry):
            alive = jnp.where(u < count, 1.0, 0.0).astype(rest.dtype)
            for i in range(2):
                extra[i, :, lanes(u)] = staged[i, :, lanes(jnp.minimum(sent + u, UNITS - 1))]
                rest[i, :, lanes(u)] = staged[i, :, lanes(jnp.minimum(kept + u, UNITS - 1))] * alive
            return carry

        lax.fori_loop(0, SPARE, some, 0)

    @pl.when(jnp.logical_not(is_odd))
    def _():
        rows = mine.shape[2]
        at = b["first"]
        loads = [
            pltpu.make_async_copy(mine.at[1, :, :, lanes(at, UNITS)], far_window, sems.at[0]),
            pltpu.make_async_copy(mine.at[0, :, :, lanes(at, UNITS)], near_window, sems.at[1]),
            pltpu.make_async_copy(mine.at[0, :, :, lanes(b["second"], UNITS)], second, sems.at[2]),
        ]
        for c in loads:
            c.start()
        left = [got[pl.ds(i * rows, rows), :] for i in range(2)]

        def against(ref, scale):
            return sum(times(left[i], ref[i] * scale) for i in range(2))

        loads[0].wait()
        value = against(far_window, counted(at, at, at + UNITS * b["m3"]))
        back[...] = value
        steps[...], whole, power = coded(value)
        lives[0:1, :] = jnp.zeros((1, rows), lives.dtype) + b["m1"].astype(lives.dtype)
        lives[1:2, :] = whole
        lives[2:3, :] = power
        loads[1].wait()
        near[...] = against(near_window, counted(at, b["s2"], b["s2"] + UNITS * b["m2"]))
        loads[2].wait()
        far_lives = b["m1"] > 0
        counts = counted(
            b["second"],
            jnp.where(far_lives, b["second"], b["low"]),
            jnp.where(far_lives, b["second"] + UNITS, b["low"] + b["rest"]),
        )
        for i in range(2):
            second[i] = second[i] * counts


def rest_kernel(got, rest, out):
    width = got.shape[2]
    out[...] = sum(times(got[i], rest[i, :, :width]) for i in range(2))


def coded(value):
    top = jnp.maximum(jnp.max(jnp.abs(value), axis=0, keepdims=True), 1e-30)
    power = jnp.ceil(jnp.log2(top)) - 14.0
    unit = jnp.exp2(power)
    whole = jnp.clip(jnp.ceil(top / unit), 1.0, STEPS)
    steps = value * (STEPS / (whole * unit)) + ROUND
    return (steps - ROUND).astype(jnp.int32).astype(jnp.int16), whole, power


def decoded(steps, whole, power):
    return steps * (whole * jnp.exp2(power) * (1.0 / STEPS))


def second_products_kernel(got, second, steps, near, more, lives, results, part, sent):
    _, is_odd = position()

    @pl.when(is_odd)
    def _():
        part[...] = more[...].T

    @pl.when(jnp.logical_not(is_odd))
    def _():
        rows = steps.shape[0]
        sent[pl.ds(2 * rows, rows), :] = steps[...]
        lived, whole, power = (lives[k : k + 1, :] for k in range(3))
        row = lax.broadcasted_iota(jnp.int32, (NOTE, rows), 0)
        scales = jnp.where(row == 4, whole, jnp.where(row == 5, power, 0.0))
        value = sum(times(got[i], second[i]) for i in range(2))
        for k, block in enumerate((value * lived, near[...] + more[...] + value * (1.0 - lived))):
            (results, part)[k][...] = block
            sent[pl.ds(k * rows, rows), :], whole, power = coded(block)
            scales = jnp.where(row == 2 * k, whole, jnp.where(row == 2 * k + 1, power, scales))
        sent[pl.ds(3 * rows, NOTE), :] = scales.astype(jnp.int32).astype(jnp.int16)


def mirror_kernel(case, back, results, part, kmirror_in, kmirror, out, sems):
    _, is_odd = position()

    @pl.when(jnp.logical_not(is_odd))
    def _():
        out[0] = back[...].T
        out[1] = results[...].T
        targets = [kmirror.at[1, 1], kmirror.at[0, 1]]
        run([pltpu.make_async_copy(out.at[j], ref, sems.at[j]) for j, ref in enumerate(targets)])

        @pl.when(case[1] == 0)
        def _():
            out[2] = part[...].T
            run([pltpu.make_async_copy(out.at[2], kmirror.at[0, 0], sems.at[2])])


def last_kernel(case, got, part, other, kband_in, kmirror_in, kband, kmirror, out, mine, theirs, sems):
    _, is_odd = position()
    due = case[1] > 0

    loads = [pltpu.make_async_copy(part, mine, sems.at[3]), pltpu.make_async_copy(other, theirs, sems.at[4])]

    @pl.when(due)
    def _():
        for c in loads:
            c.start()

    @pl.when(is_odd)
    def _():
        rows = out.shape[1]
        scales = got[pl.ds(3 * rows, NOTE), :].astype(jnp.int32).astype(jnp.float32)
        copies = [
            pltpu.make_async_copy(out.at[k], kband.at[index], sems.at[k])
            for k, index in enumerate(((0, 2), (1, 1), (1, 2)))
        ]
        for k in (0, 2, 1):
            steps = got[pl.ds(k * rows, rows), :].astype(jnp.int32).astype(jnp.float32)
            out[k] = decoded(steps, scales[2 * k : 2 * k + 1], scales[2 * k + 1 : 2 * k + 2])
            if k == 1:

                @pl.when(due)
                def _():
                    for c in loads:
                        c.wait()
                    out[1] = mine[...] + theirs[...]

            copies[k].start()
        for c in copies:
            c.wait()

    @pl.when(jnp.logical_not(is_odd) & due)
    def _():
        for c in loads:
            c.wait()
        out[0] = (mine[...] + theirs[...]).T
        run([pltpu.make_async_copy(out.at[0], kmirror.at[0, 0], sems.at[0])])


def call(kernel, outs, ins, out_specs, scratch, flops=0, moved=0, aliases=None, vmem=40):
    inner = kernel.func if isinstance(kernel, functools.partial) else kernel
    return pl.pallas_call(
        kernel,
        out_shape=outs,
        in_specs=ins,
        out_specs=out_specs,
        scratch_shapes=scratch,
        input_output_aliases=aliases or {},
        compiler_params=pltpu.CompilerParams(vmem_limit_bytes=vmem * 2**20),
        cost_estimate=pl.CostEstimate(flops=flops, bytes_accessed=moved, transcendentals=0),
        name=inner.__name__,
    )


def per_device(bfac, pair_mask, dom_start):
    n = lax.axis_size("wide")
    _, rows, orbitals, fitting = bfac.shape
    upward = [(i, i + 1) for i in range(1, n - 1, 2)]
    downward = [(j, i) for i, j in upward]
    fast = [p for i in range(0, n, 2) for p in ((i, i + 1), (i + 1, i))]
    f32, bf16 = jnp.float32, bfac.dtype
    shape = jax.ShapeDtypeStruct
    dma = pltpu.SemaphoreType.DMA
    square = shape((rows, rows), f32)
    window = shape((orbitals, rows, DOM), bf16)
    raw_block = pltpu.VMEM((rows, orbitals, fitting), bf16)

    whole = (orbitals * rows + NOTE, DOM)
    parts = 8
    first, own = call(
        first_kernel,
        (shape(whole, bf16), shape((8, 128), jnp.int32)),
        [SMEM, SMEM, HBM],
        (HBM, VMEM),
        [raw_block, pltpu.VMEM(whole, bf16), dma((parts,)), dma((parts * orbitals + 1,))],
        vmem=60,
    )(pair_mask, dom_start, bfac)
    first_got = lax.ppermute(first, "wide", upward)

    second, zero = call(
        second_kernel,
        (window, shape((1,), jnp.int32)),
        [SMEM, HBM],
        (VMEM, SMEM),
        [raw_block, dma((8,))],
        vmem=57,
    )(own, bfac)
    second_got = lax.ppermute(second, "wide", upward)

    band = shape((2, 3, rows, rows), f32)
    mirror = shape((2, 2, rows, rows), f32)
    both = shape((2, orbitals, rows, fitting), bf16)
    spare = shape((orbitals, rows, SPARE * DSTEP), bf16)
    blocks = pltpu.VMEM((2, orbitals, rows, fitting), bf16)
    raw_blocks = pltpu.VMEM((2, rows, orbitals, fitting), bf16)

    def inner(own, bfac):
        below = lax.ppermute(own, "wide", [(i, i + 1) for i in range(0, n, 2)])
        other = lax.ppermute(bfac, "wide", fast)
        kband, kmirror, mine = call(
            own_kernel,
            (band, mirror, both),
            [SMEM, HBM],
            (HBM, HBM, HBM),
            [blocks, raw_blocks, pltpu.VMEM((4, rows, rows), f32), dma((8,))],
            2**31,
            2**25,
            vmem=40,
        )(own, bfac)
        kband, kmirror = call(
            fast_kernel,
            (band, mirror),
            [SMEM, SMEM, HBM, HBM, HBM, HBM],
            (HBM, HBM),
            [blocks, blocks, raw_blocks, pltpu.VMEM((3, rows, rows), f32), dma((6,))],
            2**31,
            2**25,
            {4: 0, 5: 1},
            vmem=32,
        )(own, below, mine, other, kband, kmirror)
        return kband, kmirror, mine

    def unused(own, bfac):
        return tuple(jnp.zeros(o.shape, o.dtype) for o in (band, mirror, both))

    own, bfac, _ = lax.optimization_barrier((own, bfac, second))
    kband, kmirror, mine = lax.cond(zero[0] == 0, inner, unused, own, bfac)

    below = first_got[orbitals * rows : orbitals * rows + 8, :DSTEP].astype(jnp.int32)
    staged = pltpu.VMEM((orbitals, rows, DOM), bf16)
    back, steps, near, second_window, extra, rest_window, lives, case = call(
        functools.partial(first_products_kernel, n),
        (
            square,
            shape((rows, rows), jnp.int16),
            square,
            window,
            spare,
            spare,
            shape((8, rows), f32),
            shape((2,), jnp.int32),
        ),
        [SMEM, SMEM, VMEM, HBM],
        (VMEM, VMEM, VMEM, VMEM, VMEM, VMEM, VMEM, SMEM),
        [staged, staged, staged, dma((4,))],
        2**31,
        2**22,
        vmem=16,
    )(own, below, first_got, mine)

    def nothing(*_):
        return jnp.zeros((rows, rows), f32)

    def pair_of(lower):
        return [(lower, lower + 1), (lower + 1, lower)]

    def rest(lower, count, pairs):
        def branch(extra, rest_window):
            got = lax.ppermute(extra[:, :, : count * DSTEP], "wide", pairs)
            return call(rest_kernel, square, [VMEM, VMEM], VMEM, [], 2**26 * count, 2**19 * count, vmem=8)(
                got, rest_window
            )

        return branch

    def parts_of(lower):
        return lambda part: lax.ppermute(part, "wide", pair_of(lower))

    lowers = range(1, n - 1, 2)
    branches = [nothing]
    for i in lowers:
        branches += [rest(i, c, [(i, i + 1)]) for c in UP] + [rest(i, c, pair_of(i)) for c in BOTH]
    more = lax.switch(case[0], branches, extra, rest_window)

    results, part, sent = call(
        second_products_kernel,
        (square, square, shape((3 * rows + NOTE, rows), jnp.int16)),
        [VMEM] * 6,
        (VMEM, VMEM, VMEM),
        [],
        2**30,
        2**22,
        vmem=12,
    )(second_got, second_window, steps, near, more, lives)
    sent_got = lax.ppermute(sent, "wide", downward)
    other_part = lax.switch(case[1], [nothing] + [parts_of(i) for i in lowers], part)
    kmirror = call(
        mirror_kernel,
        mirror,
        [SMEM, VMEM, VMEM, VMEM, HBM],
        HBM,
        [pltpu.VMEM((3, rows, rows), f32), dma((3,))],
        0,
        2**20,
        {4: 0},
        vmem=8,
    )(case, back, results, part, kmirror)
    return call(
        last_kernel,
        (band, mirror),
        [SMEM, VMEM, HBM, HBM, HBM, HBM],
        (HBM, HBM),
        [
            pltpu.VMEM((3, rows, rows), f32),
            pltpu.VMEM((rows, rows), f32),
            pltpu.VMEM((rows, rows), f32),
            dma((5,)),
        ],
        0,
        2**20,
        {4: 0, 5: 1},
        vmem=8,
    )(case, sent_got, part, other_part, kband, kmirror)


def solution(mesh):
    placed = (P("wide", None, "groups", None), P("wide", None), P("wide", None))
    return jax.shard_map(
        per_device,
        mesh=mesh,
        in_specs=placed,
        out_specs=(
            P(("groups", "wide"), None, None, None),
            P(("groups", "wide"), None, None, None),
        ),
        check_vma=False,
    )
```

```python
import functools

import jax
import jax.numpy as jnp
from jax import lax
from jax.experimental import pallas as pl
from jax.experimental.pallas import tpu as pltpu
from jax.sharding import PartitionSpec as P

DOM = 2048
DSTEP = 128
UNITS = DOM // DSTEP
UP = (2, 4)
BOTH = (3, 4, 6, 8)
SPARE = 8
PER = 12
NOTE = 16
STEPS = 32767.0
ROUND = 1.5 * 2.0**23
VMEM = pl.BlockSpec(memory_space=pltpu.VMEM)
SMEM = pl.BlockSpec(memory_space=pltpu.SMEM)
HBM = pl.BlockSpec(memory_space=pltpu.HBM)


def flags(screen, block, r):
    at = block * 3 + r
    return screen[0, at], screen[0, at + PER // 2]


def boundary(get):
    m1, s1 = get(0, 2)
    m2, s2 = get(1, 1)
    m3, s3 = get(1, 2)
    first = jnp.where(m3 > 0, s3, s2)
    low = jnp.where(first <= s2, jnp.maximum(s2, first + UNITS), s2)
    high = jnp.where(first <= s2, s2 + UNITS, jnp.minimum(s2 + UNITS, first))
    rest = jnp.maximum(high - low, 0) * m2
    second = jnp.where(m1 > 0, s1, jnp.minimum(low, UNITS))
    split = rest * m1
    half = jnp.where(split > UP[-1], lax.shift_right_logical(split + 1, 1), split)
    return dict(
        m1=m1, s1=s1, m2=m2, s2=s2, m3=m3, s3=s3, first=first, low=low, rest=rest, second=second, split=split, half=half
    )


def position():
    me = lax.axis_index("wide")
    return me, lax.rem(me, 2) == 1


def slow_boundary(own, below):
    _, is_odd = position()

    def get(block, r):
        return tuple(jnp.where(is_odd, a, b) for a, b in zip(flags(own, block, r), flags(below, block, r)))

    return boundary(get)


def lanes(unit, count=1):
    return pl.ds(pl.multiple_of(unit * DSTEP, DSTEP), count * DSTEP)


def counted(unit, first, last):
    at = unit + lax.shift_right_logical(lax.broadcasted_iota(jnp.int32, (1, DOM), 1), DSTEP.bit_length() - 1)
    return jnp.where((at >= first) & (at < last), 1.0, 0.0).astype(jnp.bfloat16)


def times(left, right):
    return lax.dot_general(left, right, (((1,), (1,)), ((), ())), preferred_element_type=jnp.float32)


def swapped(values):
    return jnp.swapaxes(values, 0, 1)


def run(copies):
    for c in copies:
        c.start()
    for c in copies:
        c.wait()


def load_parts(block, raw, sems):
    parts = sems.shape[0]
    step = raw.shape[0] // parts
    return [
        pltpu.make_async_copy(block.at[pl.ds(q * step, step)], raw.at[pl.ds(q * step, step)], sems.at[q])
        for q in range(parts)
    ]


def screen_rows(pair_mask, dom_start):
    column = lax.broadcasted_iota(jnp.int32, (8, DSTEP), 1)
    value = jnp.zeros((8, DSTEP), jnp.int32)
    for at in range(PER):
        source = pair_mask if at < PER // 2 else dom_start
        block, r = divmod(at % (PER // 2), 3)
        value = jnp.where(column == at, source[block, r], value)
    return value


def first_kernel(pair_mask, dom_start, bfac, out, raw, made, sems, out_sems):
    _, is_odd = position()
    rows = raw.shape[0]

    @pl.when(is_odd)
    def _():
        loads = load_parts(bfac.at[1], raw, sems)
        for c in loads:
            c.start()
        at = boundary(lambda block, r: (pair_mask[block, r], dom_start[block, r]))["first"]
        stores = []

        def store(first, count):
            piece = pl.ds(first, count)
            c = pltpu.make_async_copy(made.at[piece], out.at[piece], out_sems.at[len(stores)])
            c.start()
            stores.append(c)

        value = screen_rows(pair_mask, dom_start)
        made[2 * rows :, :] = jnp.zeros((NOTE, DOM), made.dtype)
        made[2 * rows :, :DSTEP] = jnp.concatenate([value, value], 0).astype(jnp.float32).astype(made.dtype)
        store(2 * rows, NOTE)
        step = rows // len(loads)
        for q, c in enumerate(loads):
            c.wait()
            part = swapped(raw[pl.ds(q * step, step), :, lanes(at, UNITS)])
            for i in range(2):
                made[pl.ds(i * rows + q * step, step), :] = part[i]
                store(i * rows + q * step, step)
        for c in stores:
            c.wait()


def second_kernel(pair_mask, dom_start, bfac, out, own, zero, raw, sems):
    _, is_odd = position()
    own[...] = screen_rows(pair_mask, dom_start)
    zero[0] = jnp.minimum(pair_mask[0, 0], 0)

    @pl.when(is_odd)
    def _():
        b = boundary(lambda block, r: (pair_mask[block, r], dom_start[block, r]))
        loads = load_parts(bfac.at[jnp.where(b["m1"] > 0, 0, 1)], raw, sems)
        for c in loads:
            c.start()
        step = raw.shape[0] // len(loads)
        for q, c in enumerate(loads):
            c.wait()
            rows = pl.ds(q * step, step)
            out[:, rows, :] = swapped(raw[rows, :, lanes(b["second"], UNITS)])


def relayouter(bfac, raw, target, loads):
    step = 32

    def relayout(b):
        loads[b].wait()

        def some(q, carry):
            rows = pl.ds(pl.multiple_of(q * step, step), step)
            target[b, :, rows, :] = swapped(raw[b, rows])
            return carry

        lax.fori_loop(0, bfac.shape[1] // step, some, 0)

    return relayout


def product(left, a, right, b, at, keep):
    value = sum(times(left[a, i, :, lanes(at, UNITS)], right[b, i, :, lanes(at, UNITS)]) for i in range(2))
    return value * keep.astype(jnp.float32)


def own_kernel(own, bfac, kband, kmirror, mine, held, raw, out, sems):
    loads = [pltpu.make_async_copy(bfac.at[b], raw.at[b], sems.at[b]) for b in range(2)]
    relayout = relayouter(bfac, raw, held, loads)
    stores = []

    def store(source, target):
        c = pltpu.make_async_copy(source, target, sems.at[2 + len(stores)])
        c.start()
        stores.append(c)

    def keep(slot, value, target):
        out[slot] = value
        store(out.at[slot], target)

    for c in loads:
        c.start()
    for b in range(2):
        relayout(b)
        store(held.at[b], mine.at[b])
    k, s = flags(own, 0, 0)
    keep(0, product(held, 0, held, 0, s, k), kband.at[0, 0])
    k, s = flags(own, 0, 1)
    value = product(held, 0, held, 1, s, k)
    keep(1, value, kband.at[0, 1])
    keep(2, value.T, kmirror.at[1, 0])
    k, s = flags(own, 1, 0)
    keep(3, product(held, 1, held, 1, s, k), kband.at[1, 0])
    for c in stores:
        c.wait()


def fast_kernel(own, below, mine, other, kband_in, kmirror_in, kband, kmirror, held, theirs, raw, out, sems):
    _, is_odd = position()
    loads = [pltpu.make_async_copy(other.at[b], raw.at[b], sems.at[b]) for b in range(2)]
    held_load = pltpu.make_async_copy(mine, held, sems.at[2])
    relayout = relayouter(other, raw, theirs, loads)
    for c in (*loads, held_load):
        c.start()

    def get(block, r):
        return tuple(jnp.where(is_odd, a, b) for a, b in zip(flags(below, block, r), flags(own, block, r)))

    b = boundary(get)
    relayout(0)
    relayout(1)
    held_load.wait()
    close = jnp.where(is_odd, 0, 1)
    pick = lambda x, y: jnp.where(is_odd, x, y)
    out[0] = product(held, 1 - close, theirs, 1 - close, pick(b["s3"], b["s1"]), pick(b["m3"], b["m1"]))
    out[1] = product(held, close, theirs, 1 - close, b["s2"], b["m2"])
    out[2] = product(held, close, theirs, close, pick(b["s1"], b["s3"]), pick(b["m1"], b["m3"]))

    def put(targets):
        run([pltpu.make_async_copy(out.at[j], ref, sems.at[3 + j]) for j, ref in enumerate(targets)])

    @pl.when(is_odd)
    def _():
        put([kmirror.at[1, 1], kmirror.at[0, 0], kmirror.at[0, 1]])

    @pl.when(jnp.logical_not(is_odd))
    def _():
        put([kband.at[0, 2], kband.at[1, 1], kband.at[1, 2]])


def first_products_kernel(
    n, own, below, got, mine, back, steps, near, second, extra, rest, lives, case, far_window, near_window, staged, sems
):
    me, is_odd = position()
    b = slow_boundary(own, below)
    exists = jnp.where(is_odd, me < n - 1, me > 0)
    short = sum((b["half"] > c).astype(jnp.int32) for c in UP[:-1])
    long = len(UP) + sum((b["half"] > c).astype(jnp.int32) for c in BOTH[:-1])
    which = lax.shift_right_logical(jnp.where(is_odd, me, me - 1) - 1, 1)
    splits = exists & (b["split"] > 0)
    is_long = b["split"] > UP[-1]
    case[0] = jnp.where(splits, 1 + which * len(UP + BOTH) + jnp.where(is_long, long, short), 0)
    case[1] = jnp.where(splits & is_long, 1 + which, 0)

    @pl.when(splits)
    def _():
        at = jnp.minimum(b["low"], UNITS)
        run([pltpu.make_async_copy(mine.at[jnp.where(is_odd, 1, 0), :, :, lanes(at, UNITS)], staged, sems.at[3])])
        lower, upper = b["low"] - at, b["low"] - at + b["half"]
        sent = jnp.where(is_odd, lower, upper)
        kept = jnp.where(is_odd, upper, lower)
        count = jnp.where(is_odd, b["split"] - b["half"], b["half"])

        def some(u, carry):
            alive = jnp.where(u < count, 1.0, 0.0).astype(rest.dtype)
            for i in range(2):
                extra[i, :, lanes(u)] = staged[i, :, lanes(jnp.minimum(sent + u, UNITS - 1))]
                rest[i, :, lanes(u)] = staged[i, :, lanes(jnp.minimum(kept + u, UNITS - 1))] * alive
            return carry

        lax.fori_loop(0, SPARE, some, 0)

    @pl.when(jnp.logical_not(is_odd))
    def _():
        rows = mine.shape[2]
        at = b["first"]
        loads = [
            pltpu.make_async_copy(mine.at[1, :, :, lanes(at, UNITS)], far_window, sems.at[0]),
            pltpu.make_async_copy(mine.at[0, :, :, lanes(at, UNITS)], near_window, sems.at[1]),
            pltpu.make_async_copy(mine.at[0, :, :, lanes(b["second"], UNITS)], second, sems.at[2]),
        ]
        for c in loads:
            c.start()
        left = [got[pl.ds(i * rows, rows), :] for i in range(2)]

        def against(ref, scale):
            return sum(times(left[i], ref[i] * scale) for i in range(2))

        loads[0].wait()
        value = against(far_window, counted(at, at, at + UNITS * b["m3"]))
        back[...] = value
        steps[...], whole, power = coded(value)
        lives[0:1, :] = jnp.zeros((1, rows), lives.dtype) + b["m1"].astype(lives.dtype)
        lives[1:2, :] = whole
        lives[2:3, :] = power
        loads[1].wait()
        near[...] = against(near_window, counted(at, b["s2"], b["s2"] + UNITS * b["m2"]))
        loads[2].wait()
        far_lives = b["m1"] > 0
        counts = counted(
            b["second"],
            jnp.where(far_lives, b["second"], b["low"]),
            jnp.where(far_lives, b["second"] + UNITS, b["low"] + b["rest"]),
        )
        for i in range(2):
            second[i] = second[i] * counts


def rest_kernel(got, rest, out):
    width = got.shape[2]
    out[...] = sum(times(got[i], rest[i, :, :width]) for i in range(2))


def coded(value):
    top = jnp.maximum(jnp.max(jnp.abs(value), axis=0, keepdims=True), 1e-30)
    power = jnp.ceil(jnp.log2(top)) - 14.0
    unit = jnp.exp2(power)
    whole = jnp.clip(jnp.ceil(top / unit), 1.0, STEPS)
    steps = value * (STEPS / (whole * unit)) + ROUND
    return (steps - ROUND).astype(jnp.int32).astype(jnp.int16), whole, power


def decoded(steps, whole, power):
    return steps * (whole * jnp.exp2(power) * (1.0 / STEPS))


def second_products_kernel(got, second, steps, near, more, lives, results, part, sent):
    _, is_odd = position()

    @pl.when(is_odd)
    def _():
        part[...] = more[...].T

    @pl.when(jnp.logical_not(is_odd))
    def _():
        rows = steps.shape[0]
        sent[pl.ds(2 * rows, rows), :] = steps[...]
        lived, whole, power = (lives[k : k + 1, :] for k in range(3))
        row = lax.broadcasted_iota(jnp.int32, (NOTE, rows), 0)
        scales = jnp.where(row == 4, whole, jnp.where(row == 5, power, 0.0))
        value = sum(times(got[i], second[i]) for i in range(2))
        for k, block in enumerate((value * lived, near[...] + more[...] + value * (1.0 - lived))):
            (results, part)[k][...] = block
            sent[pl.ds(k * rows, rows), :], whole, power = coded(block)
            scales = jnp.where(row == 2 * k, whole, jnp.where(row == 2 * k + 1, power, scales))
        sent[pl.ds(3 * rows, NOTE), :] = scales.astype(jnp.int32).astype(jnp.int16)


def mirror_kernel(case, back, results, part, kmirror_in, kmirror, out, sems):
    _, is_odd = position()

    @pl.when(jnp.logical_not(is_odd))
    def _():
        out[0] = back[...].T
        out[1] = results[...].T
        targets = [kmirror.at[1, 1], kmirror.at[0, 1]]
        run([pltpu.make_async_copy(out.at[j], ref, sems.at[j]) for j, ref in enumerate(targets)])

        @pl.when(case[1] == 0)
        def _():
            out[2] = part[...].T
            run([pltpu.make_async_copy(out.at[2], kmirror.at[0, 0], sems.at[2])])


def last_kernel(case, got, part, other, kband_in, kmirror_in, kband, kmirror, out, mine, theirs, sems):
    _, is_odd = position()
    due = case[1] > 0

    loads = [pltpu.make_async_copy(part, mine, sems.at[3]), pltpu.make_async_copy(other, theirs, sems.at[4])]

    @pl.when(due)
    def _():
        for c in loads:
            c.start()

    @pl.when(is_odd)
    def _():
        rows = out.shape[1]
        scales = got[pl.ds(3 * rows, NOTE), :].astype(jnp.int32).astype(jnp.float32)
        copies = [
            pltpu.make_async_copy(out.at[k], kband.at[index], sems.at[k])
            for k, index in enumerate(((0, 2), (1, 1), (1, 2)))
        ]
        for k in (0, 2, 1):
            steps = got[pl.ds(k * rows, rows), :].astype(jnp.int32).astype(jnp.float32)
            out[k] = decoded(steps, scales[2 * k : 2 * k + 1], scales[2 * k + 1 : 2 * k + 2])
            if k == 1:

                @pl.when(due)
                def _():
                    for c in loads:
                        c.wait()
                    out[1] = mine[...] + theirs[...]

            copies[k].start()
        for c in copies:
            c.wait()

    @pl.when(jnp.logical_not(is_odd) & due)
    def _():
        for c in loads:
            c.wait()
        out[0] = (mine[...] + theirs[...]).T
        run([pltpu.make_async_copy(out.at[0], kmirror.at[0, 0], sems.at[0])])


def call(kernel, outs, ins, out_specs, scratch, flops=0, moved=0, aliases=None, vmem=40):
    inner = kernel.func if isinstance(kernel, functools.partial) else kernel
    return pl.pallas_call(
        kernel,
        out_shape=outs,
        in_specs=ins,
        out_specs=out_specs,
        scratch_shapes=scratch,
        input_output_aliases=aliases or {},
        compiler_params=pltpu.CompilerParams(vmem_limit_bytes=vmem * 2**20),
        cost_estimate=pl.CostEstimate(flops=flops, bytes_accessed=moved, transcendentals=0),
        name=inner.__name__,
    )


def per_device(bfac, pair_mask, dom_start):
    n = lax.axis_size("wide")
    _, rows, orbitals, fitting = bfac.shape
    upward = [(i, i + 1) for i in range(1, n - 1, 2)]
    downward = [(j, i) for i, j in upward]
    fast = [p for i in range(0, n, 2) for p in ((i, i + 1), (i + 1, i))]
    f32, bf16 = jnp.float32, bfac.dtype
    shape = jax.ShapeDtypeStruct
    dma = pltpu.SemaphoreType.DMA
    square = shape((rows, rows), f32)
    window = shape((orbitals, rows, DOM), bf16)
    raw_block = pltpu.VMEM((rows, orbitals, fitting), bf16)

    whole = (orbitals * rows + NOTE, DOM)
    parts = 8
    first = call(
        first_kernel,
        shape(whole, bf16),
        [SMEM, SMEM, HBM],
        HBM,
        [raw_block, pltpu.VMEM(whole, bf16), dma((parts,)), dma((parts * orbitals + 1,))],
        vmem=60,
    )(pair_mask, dom_start, bfac)
    first_got = lax.ppermute(first, "wide", upward)

    second, own, zero = call(
        second_kernel,
        (window, shape((8, DSTEP), jnp.int32), shape((1,), jnp.int32)),
        [SMEM, SMEM, HBM],
        (VMEM, VMEM, SMEM),
        [raw_block, dma((8,))],
        vmem=57,
    )(pair_mask, dom_start, lax.optimization_barrier((bfac, first))[0])
    second_got = lax.ppermute(second, "wide", upward)

    band = shape((2, 3, rows, rows), f32)
    mirror = shape((2, 2, rows, rows), f32)
    both = shape((2, orbitals, rows, fitting), bf16)
    spare = shape((orbitals, rows, SPARE * DSTEP), bf16)
    blocks = pltpu.VMEM((2, orbitals, rows, fitting), bf16)
    raw_blocks = pltpu.VMEM((2, rows, orbitals, fitting), bf16)

    def inner(own, bfac):
        below = lax.ppermute(own, "wide", [(i, i + 1) for i in range(0, n, 2)])
        other = lax.ppermute(bfac, "wide", fast)
        kband, kmirror, mine = call(
            own_kernel,
            (band, mirror, both),
            [SMEM, HBM],
            (HBM, HBM, HBM),
            [blocks, raw_blocks, pltpu.VMEM((4, rows, rows), f32), dma((8,))],
            2**31,
            2**25,
            vmem=40,
        )(own, bfac)
        kband, kmirror = call(
            fast_kernel,
            (band, mirror),
            [SMEM, SMEM, HBM, HBM, HBM, HBM],
            (HBM, HBM),
            [blocks, blocks, raw_blocks, pltpu.VMEM((3, rows, rows), f32), dma((6,))],
            2**31,
            2**25,
            {4: 0, 5: 1},
            vmem=32,
        )(own, below, mine, other, kband, kmirror)
        return kband, kmirror, mine

    def unused(own, bfac):
        return tuple(jnp.zeros(o.shape, o.dtype) for o in (band, mirror, both))

    own, bfac, _ = lax.optimization_barrier((own, bfac, second))
    kband, kmirror, mine = lax.cond(zero[0] == 0, inner, unused, own, bfac)

    below = first_got[orbitals * rows : orbitals * rows + 8, :DSTEP].astype(jnp.int32)
    staged = pltpu.VMEM((orbitals, rows, DOM), bf16)
    back, steps, near, second_window, extra, rest_window, lives, case = call(
        functools.partial(first_products_kernel, n),
        (
            square,
            shape((rows, rows), jnp.int16),
            square,
            window,
            spare,
            spare,
            shape((8, rows), f32),
            shape((2,), jnp.int32),
        ),
        [SMEM, SMEM, VMEM, HBM],
        (VMEM, VMEM, VMEM, VMEM, VMEM, VMEM, VMEM, SMEM),
        [staged, staged, staged, dma((4,))],
        2**31,
        2**22,
        vmem=16,
    )(own, below, first_got, mine)

    def nothing(*_):
        return jnp.zeros((rows, rows), f32)

    def pair_of(lower):
        return [(lower, lower + 1), (lower + 1, lower)]

    def rest(lower, count, pairs):
        def branch(extra, rest_window):
            got = lax.ppermute(extra[:, :, : count * DSTEP], "wide", pairs)
            return call(rest_kernel, square, [VMEM, VMEM], VMEM, [], 2**26 * count, 2**19 * count, vmem=8)(
                got, rest_window
            )

        return branch

    def parts_of(lower):
        return lambda part: lax.ppermute(part, "wide", pair_of(lower))

    lowers = range(1, n - 1, 2)
    branches = [nothing]
    for i in lowers:
        branches += [rest(i, c, [(i, i + 1)]) for c in UP] + [rest(i, c, pair_of(i)) for c in BOTH]
    more = lax.switch(case[0], branches, extra, rest_window)

    results, part, sent = call(
        second_products_kernel,
        (square, square, shape((3 * rows + NOTE, rows), jnp.int16)),
        [VMEM] * 6,
        (VMEM, VMEM, VMEM),
        [],
        2**30,
        2**22,
        vmem=12,
    )(second_got, second_window, steps, near, more, lives)
    sent_got = lax.ppermute(sent, "wide", downward)
    kmirror = call(
        mirror_kernel,
        mirror,
        [SMEM, VMEM, VMEM, VMEM, HBM],
        HBM,
        [pltpu.VMEM((3, rows, rows), f32), dma((3,))],
        0,
        2**20,
        {4: 0},
        vmem=8,
    )(case, back, results, part, kmirror)
    part, kmirror = lax.optimization_barrier((part, kmirror))
    other_part = lax.switch(case[1], [nothing] + [parts_of(i) for i in lowers], part)
    return call(
        last_kernel,
        (band, mirror),
        [SMEM, VMEM, HBM, HBM, HBM, HBM],
        (HBM, HBM),
        [
            pltpu.VMEM((3, rows, rows), f32),
            pltpu.VMEM((rows, rows), f32),
            pltpu.VMEM((rows, rows), f32),
            dma((5,)),
        ],
        0,
        2**20,
        {4: 0, 5: 1},
        vmem=8,
    )(case, sent_got, part, other_part, kband, kmirror)


def solution(mesh):
    placed = (P("wide", None, "groups", None), P("wide", None), P("wide", None))
    return jax.shard_map(
        per_device,
        mesh=mesh,
        in_specs=placed,
        out_specs=(
            P(("groups", "wide"), None, None, None),
            P(("groups", "wide"), None, None, None),
        ),
        check_vma=False,
    )
```

```python
import functools

import jax
import jax.numpy as jnp
from jax import lax
from jax.experimental import pallas as pl
from jax.experimental.pallas import tpu as pltpu
from jax.sharding import PartitionSpec as P

DOM = 2048
DSTEP = 128
UNITS = DOM // DSTEP
UP = (2, 4)
BOTH = (3, 4, 6, 8)
SPARE = 8
PER = 12
NOTE = 16
STEPS = 32767.0
ROUND = 1.5 * 2.0**23
VMEM = pl.BlockSpec(memory_space=pltpu.VMEM)
SMEM = pl.BlockSpec(memory_space=pltpu.SMEM)
HBM = pl.BlockSpec(memory_space=pltpu.HBM)


def flags(screen, block, r):
    at = block * 3 + r
    return screen[0, at], screen[0, at + PER // 2]


def boundary(get):
    m1, s1 = get(0, 2)
    m2, s2 = get(1, 1)
    m3, s3 = get(1, 2)
    first = jnp.where(m3 > 0, s3, s2)
    low = jnp.where(first <= s2, jnp.maximum(s2, first + UNITS), s2)
    high = jnp.where(first <= s2, s2 + UNITS, jnp.minimum(s2 + UNITS, first))
    rest = jnp.maximum(high - low, 0) * m2
    second = jnp.where(m1 > 0, s1, jnp.minimum(low, UNITS))
    split = rest * m1
    half = jnp.where(split > UP[-1], lax.shift_right_logical(split + 1, 1), split)
    return dict(
        m1=m1, s1=s1, m2=m2, s2=s2, m3=m3, s3=s3, first=first, low=low, rest=rest, second=second, split=split, half=half
    )


def position():
    me = lax.axis_index("wide")
    return me, lax.rem(me, 2) == 1


def slow_boundary(own, below):
    _, is_odd = position()

    def get(block, r):
        return tuple(jnp.where(is_odd, a, b) for a, b in zip(flags(own, block, r), flags(below, block, r)))

    return boundary(get)


def lanes(unit, count=1):
    return pl.ds(pl.multiple_of(unit * DSTEP, DSTEP), count * DSTEP)


def counted(unit, first, last):
    at = unit + lax.shift_right_logical(lax.broadcasted_iota(jnp.int32, (1, DOM), 1), DSTEP.bit_length() - 1)
    return jnp.where((at >= first) & (at < last), 1.0, 0.0).astype(jnp.bfloat16)


def times(left, right):
    return lax.dot_general(left, right, (((1,), (1,)), ((), ())), preferred_element_type=jnp.float32)


def swapped(values):
    return jnp.swapaxes(values, 0, 1)


def run(copies):
    for c in copies:
        c.start()
    for c in copies:
        c.wait()


def load_parts(block, raw, sems):
    parts = sems.shape[0]
    step = raw.shape[0] // parts
    return [
        pltpu.make_async_copy(block.at[pl.ds(q * step, step)], raw.at[pl.ds(q * step, step)], sems.at[q])
        for q in range(parts)
    ]


def screen_rows(pair_mask, dom_start):
    column = lax.broadcasted_iota(jnp.int32, (8, DSTEP), 1)
    value = jnp.zeros((8, DSTEP), jnp.int32)
    for at in range(PER):
        source = pair_mask if at < PER // 2 else dom_start
        block, r = divmod(at % (PER // 2), 3)
        value = jnp.where(column == at, source[block, r], value)
    return value


def first_kernel(pair_mask, dom_start, bfac, out, raw, made, sems, out_sems):
    _, is_odd = position()
    rows = raw.shape[0]

    @pl.when(is_odd)
    def _():
        loads = load_parts(bfac.at[1], raw, sems)
        for c in loads:
            c.start()
        at = boundary(lambda block, r: (pair_mask[block, r], dom_start[block, r]))["first"]
        stores = []

        def store(first, count):
            piece = pl.ds(first, count)
            c = pltpu.make_async_copy(made.at[piece], out.at[piece], out_sems.at[len(stores)])
            c.start()
            stores.append(c)

        value = screen_rows(pair_mask, dom_start)
        made[2 * rows :, :] = jnp.zeros((NOTE, DOM), made.dtype)
        made[2 * rows :, :DSTEP] = jnp.concatenate([value, value], 0).astype(jnp.float32).astype(made.dtype)
        store(2 * rows, NOTE)
        step = rows // len(loads)
        for q, c in enumerate(loads):
            c.wait()
            part = swapped(raw[pl.ds(q * step, step), :, lanes(at, UNITS)])
            for i in range(2):
                made[pl.ds(i * rows + q * step, step), :] = part[i]
                store(i * rows + q * step, step)
        for c in stores:
            c.wait()


def second_kernel(pair_mask, dom_start, bfac, out, own, zero, raw, sems):
    _, is_odd = position()
    own[...] = screen_rows(pair_mask, dom_start)
    zero[0] = jnp.minimum(pair_mask[0, 0], 0)

    @pl.when(is_odd)
    def _():
        b = boundary(lambda block, r: (pair_mask[block, r], dom_start[block, r]))
        loads = load_parts(bfac.at[jnp.where(b["m1"] > 0, 0, 1)], raw, sems)
        for c in loads:
            c.start()
        step = raw.shape[0] // len(loads)
        for q, c in enumerate(loads):
            c.wait()
            rows = pl.ds(q * step, step)
            out[:, rows, :] = swapped(raw[rows, :, lanes(b["second"], UNITS)])


def relayouter(bfac, raw, target, loads):
    step = 32

    def relayout(b):
        loads[b].wait()

        def some(q, carry):
            rows = pl.ds(pl.multiple_of(q * step, step), step)
            target[b, :, rows, :] = swapped(raw[b, rows])
            return carry

        lax.fori_loop(0, bfac.shape[1] // step, some, 0)

    return relayout


def product(left, a, right, b, at, keep):
    value = sum(times(left[a, i, :, lanes(at, UNITS)], right[b, i, :, lanes(at, UNITS)]) for i in range(2))
    return value * keep.astype(jnp.float32)


def own_kernel(own, bfac, kband, kmirror, mine, held, raw, out, sems):
    loads = [pltpu.make_async_copy(bfac.at[b], raw.at[b], sems.at[b]) for b in range(2)]
    relayout = relayouter(bfac, raw, held, loads)
    stores = []

    def store(source, target):
        c = pltpu.make_async_copy(source, target, sems.at[2 + len(stores)])
        c.start()
        stores.append(c)

    def keep(slot, value, target):
        out[slot] = value
        store(out.at[slot], target)

    for c in loads:
        c.start()
    for b in range(2):
        relayout(b)
        store(held.at[b], mine.at[b])
    k, s = flags(own, 0, 0)
    keep(0, product(held, 0, held, 0, s, k), kband.at[0, 0])
    k, s = flags(own, 0, 1)
    value = product(held, 0, held, 1, s, k)
    keep(1, value, kband.at[0, 1])
    keep(2, value.T, kmirror.at[1, 0])
    k, s = flags(own, 1, 0)
    keep(3, product(held, 1, held, 1, s, k), kband.at[1, 0])
    for c in stores:
        c.wait()


def fast_kernel(own, below, mine, other, kband_in, kmirror_in, kband, kmirror, held, theirs, raw, out, sems):
    _, is_odd = position()
    loads = [pltpu.make_async_copy(other.at[b], raw.at[b], sems.at[b]) for b in range(2)]
    held_load = pltpu.make_async_copy(mine, held, sems.at[2])
    relayout = relayouter(other, raw, theirs, loads)
    for c in (*loads, held_load):
        c.start()

    def get(block, r):
        return tuple(jnp.where(is_odd, a, b) for a, b in zip(flags(below, block, r), flags(own, block, r)))

    b = boundary(get)
    relayout(0)
    relayout(1)
    held_load.wait()
    close = jnp.where(is_odd, 0, 1)
    pick = lambda x, y: jnp.where(is_odd, x, y)
    out[0] = product(held, 1 - close, theirs, 1 - close, pick(b["s3"], b["s1"]), pick(b["m3"], b["m1"]))
    out[1] = product(held, close, theirs, 1 - close, b["s2"], b["m2"])
    out[2] = product(held, close, theirs, close, pick(b["s1"], b["s3"]), pick(b["m1"], b["m3"]))

    def put(targets):
        run([pltpu.make_async_copy(out.at[j], ref, sems.at[3 + j]) for j, ref in enumerate(targets)])

    @pl.when(is_odd)
    def _():
        put([kmirror.at[1, 1], kmirror.at[0, 0], kmirror.at[0, 1]])

    @pl.when(jnp.logical_not(is_odd))
    def _():
        put([kband.at[0, 2], kband.at[1, 1], kband.at[1, 2]])


def first_products_kernel(
    n, own, below, got, mine, back, steps, near, second, extra, rest, lives, case, far_window, near_window, second_window, staged, sems
):
    me, is_odd = position()
    b = slow_boundary(own, below)
    exists = jnp.where(is_odd, me < n - 1, me > 0)
    short = sum((b["half"] > c).astype(jnp.int32) for c in UP[:-1])
    long = len(UP) + sum((b["half"] > c).astype(jnp.int32) for c in BOTH[:-1])
    which = lax.shift_right_logical(jnp.where(is_odd, me, me - 1) - 1, 1)
    splits = exists & (b["split"] > 0)
    is_long = b["split"] > UP[-1]
    case[0] = jnp.where(splits, 1 + which * len(UP + BOTH) + jnp.where(is_long, long, short), 0)
    case[1] = jnp.where(splits & is_long, 1 + which, 0)

    @pl.when(splits)
    def _():
        at = jnp.minimum(b["low"], UNITS)
        run([pltpu.make_async_copy(mine.at[jnp.where(is_odd, 1, 0), :, :, lanes(at, UNITS)], staged, sems.at[3])])
        lower, upper = b["low"] - at, b["low"] - at + b["half"]
        sent = jnp.where(is_odd, lower, upper)
        kept = jnp.where(is_odd, upper, lower)
        count = jnp.where(is_odd, b["split"] - b["half"], b["half"])

        def some(u, carry):
            alive = jnp.where(u < count, 1.0, 0.0).astype(rest.dtype)
            for i in range(2):
                extra[i, :, lanes(u)] = staged[i, :, lanes(jnp.minimum(sent + u, UNITS - 1))]
                rest[i, :, lanes(u)] = staged[i, :, lanes(jnp.minimum(kept + u, UNITS - 1))] * alive
            return carry

        lax.fori_loop(0, SPARE, some, 0)

    @pl.when(jnp.logical_not(is_odd))
    def _():
        rows = mine.shape[2]
        at = b["first"]
        loads = [
            pltpu.make_async_copy(mine.at[1, :, :, lanes(at, UNITS)], far_window, sems.at[0]),
            pltpu.make_async_copy(mine.at[0, :, :, lanes(at, UNITS)], near_window, sems.at[1]),
            pltpu.make_async_copy(mine.at[0, :, :, lanes(b["second"], UNITS)], second_window, sems.at[2]),
        ]
        for c in loads:
            c.start()
        left = [got[pl.ds(i * rows, rows), :] for i in range(2)]

        def against(ref, scale):
            return sum(times(left[i], ref[i] * scale) for i in range(2))

        loads[0].wait()
        value = against(far_window, counted(at, at, at + UNITS * b["m3"]))
        back[...] = value
        steps[...], whole, power = coded(value)
        lives[0:1, :] = jnp.zeros((1, rows), lives.dtype) + b["m1"].astype(lives.dtype)
        lives[1:2, :] = whole
        lives[2:3, :] = power
        loads[1].wait()
        near[...] = against(near_window, counted(at, b["s2"], b["s2"] + UNITS * b["m2"]))
        loads[2].wait()
        far_lives = b["m1"] > 0
        counts = counted(
            b["second"],
            jnp.where(far_lives, b["second"], b["low"]),
            jnp.where(far_lives, b["second"] + UNITS, b["low"] + b["rest"]),
        )
        for i in range(2):
            second[i] = (second_window[i] * counts).T


def rest_kernel(got, rest, out):
    width = got.shape[2]
    out[...] = sum(times(got[i], rest[i, :, :width]) for i in range(2))


def coded(value):
    top = jnp.maximum(jnp.max(jnp.abs(value), axis=0, keepdims=True), 1e-30)
    power = jnp.ceil(jnp.log2(top)) - 14.0
    unit = jnp.exp2(power)
    whole = jnp.clip(jnp.ceil(top / unit), 1.0, STEPS)
    steps = value * (STEPS / (whole * unit)) + ROUND
    return (steps - ROUND).astype(jnp.int32).astype(jnp.int16), whole, power


def decoded(steps, whole, power):
    return steps * (whole * jnp.exp2(power) * (1.0 / STEPS))


def second_products_kernel(got, second, steps, near, more, lives, results, part, sent):
    _, is_odd = position()

    @pl.when(is_odd)
    def _():
        part[...] = more[...].T

    @pl.when(jnp.logical_not(is_odd))
    def _():
        rows = steps.shape[0]
        sent[pl.ds(2 * rows, rows), :] = steps[...]
        lived, whole, power = (lives[k : k + 1, :] for k in range(3))
        row = lax.broadcasted_iota(jnp.int32, (NOTE, rows), 0)
        scales = jnp.where(row == 4, whole, jnp.where(row == 5, power, 0.0))
        value = sum(jnp.dot(got[i], second[i], preferred_element_type=jnp.float32) for i in range(2))
        for k, block in enumerate((value * lived, near[...] + more[...] + value * (1.0 - lived))):
            (results, part)[k][...] = block
            sent[pl.ds(k * rows, rows), :], whole, power = coded(block)
            scales = jnp.where(row == 2 * k, whole, jnp.where(row == 2 * k + 1, power, scales))
        sent[pl.ds(3 * rows, NOTE), :] = scales.astype(jnp.int32).astype(jnp.int16)


def mirror_kernel(case, back, results, part, kmirror_in, kmirror, out, sems):
    _, is_odd = position()

    @pl.when(jnp.logical_not(is_odd))
    def _():
        out[0] = back[...].T
        out[1] = results[...].T
        targets = [kmirror.at[1, 1], kmirror.at[0, 1]]
        run([pltpu.make_async_copy(out.at[j], ref, sems.at[j]) for j, ref in enumerate(targets)])

        @pl.when(case[1] == 0)
        def _():
            out[2] = part[...].T
            run([pltpu.make_async_copy(out.at[2], kmirror.at[0, 0], sems.at[2])])


def last_kernel(case, got, part, other, kband_in, kmirror_in, kband, kmirror, out, mine, theirs, sems):
    _, is_odd = position()
    due = case[1] > 0

    loads = [pltpu.make_async_copy(part, mine, sems.at[3]), pltpu.make_async_copy(other, theirs, sems.at[4])]

    @pl.when(due)
    def _():
        for c in loads:
            c.start()

    @pl.when(is_odd)
    def _():
        rows = out.shape[1]
        scales = got[pl.ds(3 * rows, NOTE), :].astype(jnp.int32).astype(jnp.float32)
        copies = [
            pltpu.make_async_copy(out.at[k], kband.at[index], sems.at[k])
            for k, index in enumerate(((0, 2), (1, 1), (1, 2)))
        ]
        for k in (0, 2, 1):
            steps = got[pl.ds(k * rows, rows), :].astype(jnp.int32).astype(jnp.float32)
            out[k] = decoded(steps, scales[2 * k : 2 * k + 1], scales[2 * k + 1 : 2 * k + 2])
            if k == 1:

                @pl.when(due)
                def _():
                    for c in loads:
                        c.wait()
                    out[1] = mine[...] + theirs[...]

            copies[k].start()
        for c in copies:
            c.wait()

    @pl.when(jnp.logical_not(is_odd) & due)
    def _():
        for c in loads:
            c.wait()
        out[0] = (mine[...] + theirs[...]).T
        run([pltpu.make_async_copy(out.at[0], kmirror.at[0, 0], sems.at[0])])


def call(kernel, outs, ins, out_specs, scratch, flops=0, moved=0, aliases=None, vmem=40):
    inner = kernel.func if isinstance(kernel, functools.partial) else kernel
    return pl.pallas_call(
        kernel,
        out_shape=outs,
        in_specs=ins,
        out_specs=out_specs,
        scratch_shapes=scratch,
        input_output_aliases=aliases or {},
        compiler_params=pltpu.CompilerParams(vmem_limit_bytes=vmem * 2**20),
        cost_estimate=pl.CostEstimate(flops=flops, bytes_accessed=moved, transcendentals=0),
        name=inner.__name__,
    )


def per_device(bfac, pair_mask, dom_start):
    n = lax.axis_size("wide")
    _, rows, orbitals, fitting = bfac.shape
    upward = [(i, i + 1) for i in range(1, n - 1, 2)]
    downward = [(j, i) for i, j in upward]
    fast = [p for i in range(0, n, 2) for p in ((i, i + 1), (i + 1, i))]
    f32, bf16 = jnp.float32, bfac.dtype
    shape = jax.ShapeDtypeStruct
    dma = pltpu.SemaphoreType.DMA
    square = shape((rows, rows), f32)
    window = shape((orbitals, rows, DOM), bf16)
    raw_block = pltpu.VMEM((rows, orbitals, fitting), bf16)

    whole = (orbitals * rows + NOTE, DOM)
    parts = 8
    first = call(
        first_kernel,
        shape(whole, bf16),
        [SMEM, SMEM, HBM],
        HBM,
        [raw_block, pltpu.VMEM(whole, bf16), dma((parts,)), dma((parts * orbitals + 1,))],
        vmem=60,
    )(pair_mask, dom_start, bfac)
    first_got = lax.ppermute(first, "wide", upward)

    second, own, zero = call(
        second_kernel,
        (window, shape((8, DSTEP), jnp.int32), shape((1,), jnp.int32)),
        [SMEM, SMEM, HBM],
        (VMEM, VMEM, SMEM),
        [raw_block, dma((8,))],
        vmem=57,
    )(pair_mask, dom_start, lax.optimization_barrier((bfac, first))[0])
    second_got = lax.ppermute(second, "wide", upward)

    band = shape((2, 3, rows, rows), f32)
    mirror = shape((2, 2, rows, rows), f32)
    both = shape((2, orbitals, rows, fitting), bf16)
    spare = shape((orbitals, rows, SPARE * DSTEP), bf16)
    blocks = pltpu.VMEM((2, orbitals, rows, fitting), bf16)
    raw_blocks = pltpu.VMEM((2, rows, orbitals, fitting), bf16)

    def inner(own, bfac):
        below = lax.ppermute(own, "wide", [(i, i + 1) for i in range(0, n, 2)])
        other = lax.ppermute(bfac, "wide", fast)
        kband, kmirror, mine = call(
            own_kernel,
            (band, mirror, both),
            [SMEM, HBM],
            (HBM, HBM, HBM),
            [blocks, raw_blocks, pltpu.VMEM((4, rows, rows), f32), dma((8,))],
            2**31,
            2**25,
            vmem=40,
        )(own, bfac)
        kband, kmirror = call(
            fast_kernel,
            (band, mirror),
            [SMEM, SMEM, HBM, HBM, HBM, HBM],
            (HBM, HBM),
            [blocks, blocks, raw_blocks, pltpu.VMEM((3, rows, rows), f32), dma((6,))],
            2**31,
            2**25,
            {4: 0, 5: 1},
            vmem=32,
        )(own, below, mine, other, kband, kmirror)
        return kband, kmirror, mine

    def unused(own, bfac):
        return tuple(jnp.zeros(o.shape, o.dtype) for o in (band, mirror, both))

    own, bfac, _ = lax.optimization_barrier((own, bfac, second))
    kband, kmirror, mine = lax.cond(zero[0] == 0, inner, unused, own, bfac)

    below = first_got[orbitals * rows : orbitals * rows + 8, :DSTEP].astype(jnp.int32)
    staged = pltpu.VMEM((orbitals, rows, DOM), bf16)
    back, steps, near, second_window, extra, rest_window, lives, case = call(
        functools.partial(first_products_kernel, n),
        (
            square,
            shape((rows, rows), jnp.int16),
            square,
            shape((orbitals, DOM, rows), bf16),
            spare,
            spare,
            shape((8, rows), f32),
            shape((2,), jnp.int32),
        ),
        [SMEM, SMEM, VMEM, HBM],
        (VMEM, VMEM, VMEM, VMEM, VMEM, VMEM, VMEM, SMEM),
        [staged, staged, staged, staged, dma((4,))],
        2**31,
        2**22,
        vmem=16,
    )(own, below, first_got, mine)

    def nothing(*_):
        return jnp.zeros((rows, rows), f32)

    def pair_of(lower):
        return [(lower, lower + 1), (lower + 1, lower)]

    def rest(lower, count, pairs):
        def branch(extra, rest_window):
            got = lax.ppermute(extra[:, :, : count * DSTEP], "wide", pairs)
            return call(rest_kernel, square, [VMEM, VMEM], VMEM, [], 2**26 * count, 2**19 * count, vmem=8)(
                got, rest_window
            )

        return branch

    def parts_of(lower):
        return lambda part: lax.ppermute(part, "wide", pair_of(lower))

    lowers = range(1, n - 1, 2)
    branches = [nothing]
    for i in lowers:
        branches += [rest(i, c, [(i, i + 1)]) for c in UP] + [rest(i, c, pair_of(i)) for c in BOTH]
    more = lax.switch(case[0], branches, extra, rest_window)

    results, part, sent = call(
        second_products_kernel,
        (square, square, shape((3 * rows + NOTE, rows), jnp.int16)),
        [VMEM] * 6,
        (VMEM, VMEM, VMEM),
        [],
        2**30,
        2**22,
        vmem=12,
    )(second_got, second_window, steps, near, more, lives)
    sent_got = lax.ppermute(sent, "wide", downward)
    kmirror = call(
        mirror_kernel,
        mirror,
        [SMEM, VMEM, VMEM, VMEM, HBM],
        HBM,
        [pltpu.VMEM((3, rows, rows), f32), dma((3,))],
        0,
        2**20,
        {4: 0},
        vmem=8,
    )(case, back, results, part, kmirror)
    part, kmirror = lax.optimization_barrier((part, kmirror))
    other_part = lax.switch(case[1], [nothing] + [parts_of(i) for i in lowers], part)
    return call(
        last_kernel,
        (band, mirror),
        [SMEM, VMEM, HBM, HBM, HBM, HBM],
        (HBM, HBM),
        [
            pltpu.VMEM((3, rows, rows), f32),
            pltpu.VMEM((rows, rows), f32),
            pltpu.VMEM((rows, rows), f32),
            dma((5,)),
        ],
        0,
        2**20,
        {4: 0, 5: 1},
        vmem=8,
    )(case, sent_got, part, other_part, kband, kmirror)


def solution(mesh):
    placed = (P("wide", None, "groups", None), P("wide", None), P("wide", None))
    return jax.shard_map(
        per_device,
        mesh=mesh,
        in_specs=placed,
        out_specs=(
            P(("groups", "wide"), None, None, None),
            P(("groups", "wide"), None, None, None),
        ),
        check_vma=False,
    )
```

```python
import functools

import jax
import jax.numpy as jnp
from jax import lax
from jax.experimental import pallas as pl
from jax.experimental.pallas import tpu as pltpu
from jax.sharding import PartitionSpec as P

DOM = 2048
DSTEP = 128
UNITS = DOM // DSTEP
UP = (2, 4)
BOTH = (3, 4, 6, 8)
SPARE = 8
PER = 12
NOTE = 16
STEPS = 32767.0
ROUND = 1.5 * 2.0**23
VMEM = pl.BlockSpec(memory_space=pltpu.VMEM)
SMEM = pl.BlockSpec(memory_space=pltpu.SMEM)
HBM = pl.BlockSpec(memory_space=pltpu.HBM)


def flags(screen, block, r):
    at = block * 3 + r
    return screen[0, at], screen[0, at + PER // 2]


def boundary(get):
    m1, s1 = get(0, 2)
    m2, s2 = get(1, 1)
    m3, s3 = get(1, 2)
    first = jnp.where(m3 > 0, s3, s2)
    low = jnp.where(first <= s2, jnp.maximum(s2, first + UNITS), s2)
    high = jnp.where(first <= s2, s2 + UNITS, jnp.minimum(s2 + UNITS, first))
    rest = jnp.maximum(high - low, 0) * m2
    second = jnp.where(m1 > 0, s1, jnp.minimum(low, UNITS))
    split = rest * m1
    half = jnp.where(split > UP[-1], lax.shift_right_logical(split + 1, 1), split)
    return dict(
        m1=m1, s1=s1, m2=m2, s2=s2, m3=m3, s3=s3, first=first, low=low, rest=rest, second=second, split=split, half=half
    )


def position():
    me = lax.axis_index("wide")
    return me, lax.rem(me, 2) == 1


def slow_boundary(own, below):
    _, is_odd = position()

    def get(block, r):
        return tuple(jnp.where(is_odd, a, b) for a, b in zip(flags(own, block, r), flags(below, block, r)))

    return boundary(get)


def lanes(unit, count=1):
    return pl.ds(pl.multiple_of(unit * DSTEP, DSTEP), count * DSTEP)


def counted(unit, first, last):
    at = unit + lax.shift_right_logical(lax.broadcasted_iota(jnp.int32, (1, DOM), 1), DSTEP.bit_length() - 1)
    return jnp.where((at >= first) & (at < last), 1.0, 0.0).astype(jnp.bfloat16)


def times(left, right):
    return lax.dot_general(left, right, (((1,), (1,)), ((), ())), preferred_element_type=jnp.float32)


def swapped(values):
    return jnp.swapaxes(values, 0, 1)


def run(copies):
    for c in copies:
        c.start()
    for c in copies:
        c.wait()


def load_parts(block, raw, sems):
    parts = sems.shape[0]
    step = raw.shape[0] // parts
    return [
        pltpu.make_async_copy(block.at[pl.ds(q * step, step)], raw.at[pl.ds(q * step, step)], sems.at[q])
        for q in range(parts)
    ]


def screen_rows(pair_mask, dom_start):
    column = lax.broadcasted_iota(jnp.int32, (8, DSTEP), 1)
    value = jnp.zeros((8, DSTEP), jnp.int32)
    for at in range(PER):
        source = pair_mask if at < PER // 2 else dom_start
        block, r = divmod(at % (PER // 2), 3)
        value = jnp.where(column == at, source[block, r], value)
    return value


def first_kernel(pair_mask, dom_start, bfac, out, raw, made, sems, out_sems):
    _, is_odd = position()
    rows = raw.shape[0]

    @pl.when(is_odd)
    def _():
        loads = load_parts(bfac.at[1], raw, sems)
        for c in loads:
            c.start()
        at = boundary(lambda block, r: (pair_mask[block, r], dom_start[block, r]))["first"]
        stores = []

        def store(first, count):
            piece = pl.ds(first, count)
            c = pltpu.make_async_copy(made.at[piece], out.at[piece], out_sems.at[len(stores)])
            c.start()
            stores.append(c)

        value = screen_rows(pair_mask, dom_start)
        made[2 * rows :, :] = jnp.zeros((NOTE, DOM), made.dtype)
        made[2 * rows :, :DSTEP] = jnp.concatenate([value, value], 0).astype(jnp.float32).astype(made.dtype)
        store(2 * rows, NOTE)
        step = rows // len(loads)
        for q, c in enumerate(loads):
            c.wait()
            part = swapped(raw[pl.ds(q * step, step), :, lanes(at, UNITS)])
            for i in range(2):
                made[pl.ds(i * rows + q * step, step), :] = part[i]
                store(i * rows + q * step, step)
        for c in stores:
            c.wait()


def second_kernel(pair_mask, dom_start, bfac, out, own, zero, raw, sems):
    _, is_odd = position()
    own[...] = screen_rows(pair_mask, dom_start)
    zero[0] = jnp.minimum(pair_mask[0, 0], 0)

    @pl.when(is_odd)
    def _():
        b = boundary(lambda block, r: (pair_mask[block, r], dom_start[block, r]))
        loads = load_parts(bfac.at[jnp.where(b["m1"] > 0, 0, 1)], raw, sems)
        for c in loads:
            c.start()
        step = raw.shape[0] // len(loads)
        for q, c in enumerate(loads):
            c.wait()
            rows = pl.ds(q * step, step)
            out[:, rows, :] = swapped(raw[rows, :, lanes(b["second"], UNITS)])


def relayouter(bfac, raw, target, loads):
    step = 32

    def relayout(b):
        loads[b].wait()

        def some(q, carry):
            rows = pl.ds(pl.multiple_of(q * step, step), step)
            target[b, :, rows, :] = swapped(raw[b, rows])
            return carry

        lax.fori_loop(0, bfac.shape[1] // step, some, 0)

    return relayout


def product(left, a, right, b, at, keep):
    value = sum(times(left[a, i, :, lanes(at, UNITS)], right[b, i, :, lanes(at, UNITS)]) for i in range(2))
    return value * keep.astype(jnp.float32)


def own_kernel(own, bfac, kband, kmirror, mine, held, raw, out, sems):
    loads = [pltpu.make_async_copy(bfac.at[b], raw.at[b], sems.at[b]) for b in range(2)]
    relayout = relayouter(bfac, raw, held, loads)
    stores = []

    def store(source, target):
        c = pltpu.make_async_copy(source, target, sems.at[2 + len(stores)])
        c.start()
        stores.append(c)

    def keep(slot, value, target):
        out[slot] = value
        store(out.at[slot], target)

    for c in loads:
        c.start()
    for b in range(2):
        relayout(b)
        store(held.at[b], mine.at[b])
    k, s = flags(own, 0, 0)
    keep(0, product(held, 0, held, 0, s, k), kband.at[0, 0])
    k, s = flags(own, 0, 1)
    value = product(held, 0, held, 1, s, k)
    keep(1, value, kband.at[0, 1])
    keep(2, value.T, kmirror.at[1, 0])
    k, s = flags(own, 1, 0)
    keep(3, product(held, 1, held, 1, s, k), kband.at[1, 0])
    for c in stores:
        c.wait()


def fast_kernel(own, below, mine, other, kband_in, kmirror_in, kband, kmirror, held, theirs, raw, out, sems):
    _, is_odd = position()
    loads = [pltpu.make_async_copy(other.at[b], raw.at[b], sems.at[b]) for b in range(2)]
    held_load = pltpu.make_async_copy(mine, held, sems.at[2])
    relayout = relayouter(other, raw, theirs, loads)
    for c in (*loads, held_load):
        c.start()

    def get(block, r):
        return tuple(jnp.where(is_odd, a, b) for a, b in zip(flags(below, block, r), flags(own, block, r)))

    b = boundary(get)
    relayout(0)
    relayout(1)
    held_load.wait()
    close = jnp.where(is_odd, 0, 1)
    pick = lambda x, y: jnp.where(is_odd, x, y)
    out[0] = product(held, 1 - close, theirs, 1 - close, pick(b["s3"], b["s1"]), pick(b["m3"], b["m1"]))
    out[1] = product(held, close, theirs, 1 - close, b["s2"], b["m2"])
    out[2] = product(held, close, theirs, close, pick(b["s1"], b["s3"]), pick(b["m1"], b["m3"]))

    def put(targets):
        run([pltpu.make_async_copy(out.at[j], ref, sems.at[3 + j]) for j, ref in enumerate(targets)])

    @pl.when(is_odd)
    def _():
        put([kmirror.at[1, 1], kmirror.at[0, 0], kmirror.at[0, 1]])

    @pl.when(jnp.logical_not(is_odd))
    def _():
        put([kband.at[0, 2], kband.at[1, 1], kband.at[1, 2]])


def first_products_kernel(
    n, own, below, got, mine, back, steps, near, second, extra, rest, lives, case, far_window, near_window, second_window, staged, sems
):
    me, is_odd = position()
    b = slow_boundary(own, below)
    exists = jnp.where(is_odd, me < n - 1, me > 0)
    short = sum((b["half"] > c).astype(jnp.int32) for c in UP[:-1])
    long = len(UP) + sum((b["half"] > c).astype(jnp.int32) for c in BOTH[:-1])
    which = lax.shift_right_logical(jnp.where(is_odd, me, me - 1) - 1, 1)
    splits = exists & (b["split"] > 0)
    is_long = b["split"] > UP[-1]
    case[0] = jnp.where(splits, 1 + which * len(UP + BOTH) + jnp.where(is_long, long, short), 0)
    case[1] = jnp.where(splits & is_long, 1 + which, 0)

    @pl.when(splits)
    def _():
        at = jnp.minimum(b["low"], UNITS)
        run([pltpu.make_async_copy(mine.at[jnp.where(is_odd, 1, 0), :, :, lanes(at, UNITS)], staged, sems.at[3])])
        lower, upper = b["low"] - at, b["low"] - at + b["half"]
        sent = jnp.where(is_odd, lower, upper)
        kept = jnp.where(is_odd, upper, lower)
        count = jnp.where(is_odd, b["split"] - b["half"], b["half"])

        def some(u, carry):
            alive = jnp.where(u < count, 1.0, 0.0).astype(rest.dtype)
            for i in range(2):
                extra[i, :, lanes(u)] = staged[i, :, lanes(jnp.minimum(sent + u, UNITS - 1))]
                rest[i, :, lanes(u)] = staged[i, :, lanes(jnp.minimum(kept + u, UNITS - 1))] * alive
            return carry

        lax.fori_loop(0, SPARE, some, 0)

    @pl.when(jnp.logical_not(is_odd))
    def _():
        rows = mine.shape[2]
        at = b["first"]
        loads = [
            pltpu.make_async_copy(mine.at[1, :, :, lanes(at, UNITS)], far_window, sems.at[0]),
            pltpu.make_async_copy(mine.at[0, :, :, lanes(at, UNITS)], near_window, sems.at[1]),
            pltpu.make_async_copy(mine.at[0, :, :, lanes(b["second"], UNITS)], second_window, sems.at[2]),
        ]
        for c in loads:
            c.start()
        left = [got[pl.ds(i * rows, rows), :] for i in range(2)]

        def against(ref, scale):
            return sum(times(left[i], ref[i] * scale) for i in range(2))

        loads[0].wait()
        value = against(far_window, counted(at, at, at + UNITS * b["m3"]))
        back[...] = value
        steps[...], whole, power = coded(value)
        lives[0:1, :] = jnp.zeros((1, rows), lives.dtype) + b["m1"].astype(lives.dtype)
        lives[1:2, :] = whole
        lives[2:3, :] = power
        loads[1].wait()
        near[...] = against(near_window, counted(at, b["s2"], b["s2"] + UNITS * b["m2"]))
        loads[2].wait()
        far_lives = b["m1"] > 0
        counts = counted(
            b["second"],
            jnp.where(far_lives, b["second"], b["low"]),
            jnp.where(far_lives, b["second"] + UNITS, b["low"] + b["rest"]),
        )
        for i in range(2):
            second[i] = (second_window[i] * counts).T


def rest_kernel(got, rest, out):
    width = got.shape[2]
    out[...] = sum(times(got[i], rest[i, :, :width]) for i in range(2))


def coded(value):
    top = jnp.maximum(jnp.max(jnp.abs(value), axis=0, keepdims=True), 1e-30)
    power = jnp.ceil(jnp.log2(top)) - 14.0
    unit = jnp.exp2(power)
    whole = jnp.clip(jnp.ceil(top / unit), 1.0, STEPS)
    steps = value * (STEPS / (whole * unit)) + ROUND
    return (steps - ROUND).astype(jnp.int32).astype(jnp.int16), whole, power


def decoded(steps, whole, power):
    return steps * (whole * jnp.exp2(power) * (1.0 / STEPS))


def second_products_kernel(got, second, steps, near, more, lives, results, part, sent):
    _, is_odd = position()

    @pl.when(is_odd)
    def _():
        part[...] = more[...].T

    @pl.when(jnp.logical_not(is_odd))
    def _():
        rows = steps.shape[0]
        sent[pl.ds(2 * rows, rows), :] = steps[...]
        lived, whole, power = (lives[k : k + 1, :] for k in range(3))
        row = lax.broadcasted_iota(jnp.int32, (NOTE, rows), 0)
        scales = jnp.where(row == 4, whole, jnp.where(row == 5, power, 0.0))
        value = sum(jnp.dot(got[i], second[i], preferred_element_type=jnp.float32) for i in range(2))
        for k, block in enumerate((value * lived, near[...] + more[...] + value * (1.0 - lived))):
            (results, part)[k][...] = block
            sent[pl.ds(k * rows, rows), :], whole, power = coded(block)
            scales = jnp.where(row == 2 * k, whole, jnp.where(row == 2 * k + 1, power, scales))
        sent[pl.ds(3 * rows, NOTE), :] = scales.astype(jnp.int32).astype(jnp.int16)


def mirror_kernel(case, back, results, part, kmirror_in, kmirror, out, sems):
    _, is_odd = position()

    @pl.when(jnp.logical_not(is_odd))
    def _():
        out[0] = back[...].T
        out[1] = results[...].T
        targets = [kmirror.at[1, 1], kmirror.at[0, 1]]
        run([pltpu.make_async_copy(out.at[j], ref, sems.at[j]) for j, ref in enumerate(targets)])

        @pl.when(case[1] == 0)
        def _():
            out[2] = part[...].T
            run([pltpu.make_async_copy(out.at[2], kmirror.at[0, 0], sems.at[2])])


def last_kernel(case, got, part, other, kband_in, kmirror_in, kband, kmirror, out, theirs, sems):
    _, is_odd = position()
    due = case[1] > 0

    load = pltpu.make_async_copy(other, theirs, sems.at[3])

    @pl.when(due)
    def _():
        load.start()

    @pl.when(is_odd)
    def _():
        rows = out.shape[1]
        scales = got[pl.ds(3 * rows, NOTE), :].astype(jnp.int32).astype(jnp.float32)
        copies = [
            pltpu.make_async_copy(out.at[k], kband.at[index], sems.at[k])
            for k, index in enumerate(((0, 2), (1, 1), (1, 2)))
        ]
        for k in (0, 2, 1):
            steps = got[pl.ds(k * rows, rows), :].astype(jnp.int32).astype(jnp.float32)
            out[k] = decoded(steps, scales[2 * k : 2 * k + 1], scales[2 * k + 1 : 2 * k + 2])
            if k == 1:

                @pl.when(due)
                def _():
                    load.wait()
                    out[1] = part[...] + theirs[...]

            copies[k].start()
        for c in copies:
            c.wait()

    @pl.when(jnp.logical_not(is_odd) & due)
    def _():
        load.wait()
        out[0] = (part[...] + theirs[...]).T
        run([pltpu.make_async_copy(out.at[0], kmirror.at[0, 0], sems.at[0])])


def call(kernel, outs, ins, out_specs, scratch, flops=0, moved=0, aliases=None, vmem=40):
    inner = kernel.func if isinstance(kernel, functools.partial) else kernel
    return pl.pallas_call(
        kernel,
        out_shape=outs,
        in_specs=ins,
        out_specs=out_specs,
        scratch_shapes=scratch,
        input_output_aliases=aliases or {},
        compiler_params=pltpu.CompilerParams(vmem_limit_bytes=vmem * 2**20),
        cost_estimate=pl.CostEstimate(flops=flops, bytes_accessed=moved, transcendentals=0),
        name=inner.__name__,
    )


def per_device(bfac, pair_mask, dom_start):
    n = lax.axis_size("wide")
    _, rows, orbitals, fitting = bfac.shape
    upward = [(i, i + 1) for i in range(1, n - 1, 2)]
    downward = [(j, i) for i, j in upward]
    fast = [p for i in range(0, n, 2) for p in ((i, i + 1), (i + 1, i))]
    f32, bf16 = jnp.float32, bfac.dtype
    shape = jax.ShapeDtypeStruct
    dma = pltpu.SemaphoreType.DMA
    square = shape((rows, rows), f32)
    window = shape((orbitals, rows, DOM), bf16)
    raw_block = pltpu.VMEM((rows, orbitals, fitting), bf16)

    whole = (orbitals * rows + NOTE, DOM)
    parts = 16
    first = call(
        first_kernel,
        shape(whole, bf16),
        [SMEM, SMEM, HBM],
        HBM,
        [raw_block, pltpu.VMEM(whole, bf16), dma((parts,)), dma((parts * orbitals + 1,))],
        vmem=60,
    )(pair_mask, dom_start, bfac)
    first_got = lax.ppermute(first, "wide", upward)

    second, own, zero = call(
        second_kernel,
        (window, shape((8, DSTEP), jnp.int32), shape((1,), jnp.int32)),
        [SMEM, SMEM, HBM],
        (VMEM, VMEM, SMEM),
        [raw_block, dma((8,))],
        vmem=57,
    )(pair_mask, dom_start, lax.optimization_barrier((bfac, first))[0])
    second_got = lax.ppermute(second, "wide", upward)

    band = shape((2, 3, rows, rows), f32)
    mirror = shape((2, 2, rows, rows), f32)
    both = shape((2, orbitals, rows, fitting), bf16)
    spare = shape((orbitals, rows, SPARE * DSTEP), bf16)
    blocks = pltpu.VMEM((2, orbitals, rows, fitting), bf16)
    raw_blocks = pltpu.VMEM((2, rows, orbitals, fitting), bf16)

    def inner(own, bfac):
        below = lax.ppermute(own, "wide", [(i, i + 1) for i in range(0, n, 2)])
        other = lax.ppermute(bfac, "wide", fast)
        kband, kmirror, mine = call(
            own_kernel,
            (band, mirror, both),
            [SMEM, HBM],
            (HBM, HBM, HBM),
            [blocks, raw_blocks, pltpu.VMEM((4, rows, rows), f32), dma((8,))],
            2**31,
            2**25,
            vmem=40,
        )(own, bfac)
        kband, kmirror = call(
            fast_kernel,
            (band, mirror),
            [SMEM, SMEM, HBM, HBM, HBM, HBM],
            (HBM, HBM),
            [blocks, blocks, raw_blocks, pltpu.VMEM((3, rows, rows), f32), dma((6,))],
            2**31,
            2**25,
            {4: 0, 5: 1},
            vmem=32,
        )(own, below, mine, other, kband, kmirror)
        return kband, kmirror, mine

    def unused(own, bfac):
        return tuple(jnp.zeros(o.shape, o.dtype) for o in (band, mirror, both))

    own, bfac, _ = lax.optimization_barrier((own, bfac, second))
    kband, kmirror, mine = lax.cond(zero[0] == 0, inner, unused, own, bfac)

    below = first_got[orbitals * rows : orbitals * rows + 8, :DSTEP].astype(jnp.int32)
    staged = pltpu.VMEM((orbitals, rows, DOM), bf16)
    back, steps, near, second_window, extra, rest_window, lives, case = call(
        functools.partial(first_products_kernel, n),
        (
            square,
            shape((rows, rows), jnp.int16),
            square,
            shape((orbitals, DOM, rows), bf16),
            spare,
            spare,
            shape((8, rows), f32),
            shape((2,), jnp.int32),
        ),
        [SMEM, SMEM, VMEM, HBM],
        (VMEM, VMEM, VMEM, VMEM, VMEM, VMEM, VMEM, SMEM),
        [staged, staged, staged, staged, dma((4,))],
        2**31,
        2**22,
        vmem=16,
    )(own, below, first_got, mine)

    def nothing(*_):
        return jnp.zeros((rows, rows), f32)

    def pair_of(lower):
        return [(lower, lower + 1), (lower + 1, lower)]

    def rest(lower, count, pairs):
        def branch(extra, rest_window):
            got = lax.ppermute(extra[:, :, : count * DSTEP], "wide", pairs)
            return call(rest_kernel, square, [VMEM, VMEM], VMEM, [], 2**26 * count, 2**19 * count, vmem=8)(
                got, rest_window
            )

        return branch

    def parts_of(lower):
        return lambda part: lax.ppermute(part, "wide", pair_of(lower))

    lowers = range(1, n - 1, 2)
    branches = [nothing]
    for i in lowers:
        branches += [rest(i, c, [(i, i + 1)]) for c in UP] + [rest(i, c, pair_of(i)) for c in BOTH]
    more = lax.switch(case[0], branches, extra, rest_window)

    results, part, sent = call(
        second_products_kernel,
        (square, square, shape((3 * rows + NOTE, rows), jnp.int16)),
        [VMEM] * 6,
        (VMEM, VMEM, VMEM),
        [],
        2**30,
        2**22,
        vmem=12,
    )(second_got, second_window, steps, near, more, lives)
    sent_got = lax.ppermute(sent, "wide", downward)
    kmirror = call(
        mirror_kernel,
        mirror,
        [SMEM, VMEM, VMEM, VMEM, HBM],
        HBM,
        [pltpu.VMEM((3, rows, rows), f32), dma((3,))],
        0,
        2**20,
        {4: 0},
        vmem=8,
    )(case, back, results, part, kmirror)
    part, kmirror = lax.optimization_barrier((part, kmirror))
    other_part = lax.switch(case[1], [nothing] + [parts_of(i) for i in lowers], part)
    return call(
        last_kernel,
        (band, mirror),
        [SMEM, VMEM, VMEM, HBM, HBM, HBM],
        (HBM, HBM),
        [pltpu.VMEM((3, rows, rows), f32), pltpu.VMEM((rows, rows), f32), dma((4,))],
        0,
        2**20,
        {4: 0, 5: 1},
        vmem=8,
    )(case, sent_got, part, other_part, kband, kmirror)


def solution(mesh):
    placed = (P("wide", None, "groups", None), P("wide", None), P("wide", None))
    return jax.shard_map(
        per_device,
        mesh=mesh,
        in_specs=placed,
        out_specs=(
            P(("groups", "wide"), None, None, None),
            P(("groups", "wide"), None, None, None),
        ),
        check_vma=False,
    )
```

```python
import functools

import jax
import jax.numpy as jnp
from jax import lax
from jax.experimental import pallas as pl
from jax.experimental.pallas import tpu as pltpu
from jax.sharding import PartitionSpec as P

DOM = 2048
DSTEP = 128
UNITS = DOM // DSTEP
UP = (2, 4)
BOTH = (3, 4, 6, 8)
SPARE = 8
PER = 12
NOTE = 16
STEPS = 32767.0
ROUND = 1.5 * 2.0**23
VMEM = pl.BlockSpec(memory_space=pltpu.VMEM)
SMEM = pl.BlockSpec(memory_space=pltpu.SMEM)
HBM = pl.BlockSpec(memory_space=pltpu.HBM)


def flags(screen, block, r):
    at = block * 3 + r
    return screen[0, at], screen[0, at + PER // 2]


def boundary(get):
    m1, s1 = get(0, 2)
    m2, s2 = get(1, 1)
    m3, s3 = get(1, 2)
    first = jnp.where(m3 > 0, s3, s2)
    low = jnp.where(first <= s2, jnp.maximum(s2, first + UNITS), s2)
    high = jnp.where(first <= s2, s2 + UNITS, jnp.minimum(s2 + UNITS, first))
    rest = jnp.maximum(high - low, 0) * m2
    second = jnp.where(m1 > 0, s1, jnp.minimum(low, UNITS))
    split = rest * m1
    half = jnp.where(split > UP[-1], lax.shift_right_logical(split + 1, 1), split)
    return dict(
        m1=m1, s1=s1, m2=m2, s2=s2, m3=m3, s3=s3, first=first, low=low, rest=rest, second=second, split=split, half=half
    )


def position():
    me = lax.axis_index("wide")
    return me, lax.rem(me, 2) == 1


def slow_boundary(own, below):
    _, is_odd = position()

    def get(block, r):
        return tuple(jnp.where(is_odd, a, b) for a, b in zip(flags(own, block, r), flags(below, block, r)))

    return boundary(get)


def lanes(unit, count=1):
    return pl.ds(pl.multiple_of(unit * DSTEP, DSTEP), count * DSTEP)


def counted(unit, first, last):
    at = unit + lax.shift_right_logical(lax.broadcasted_iota(jnp.int32, (1, DOM), 1), DSTEP.bit_length() - 1)
    return jnp.where((at >= first) & (at < last), 1.0, 0.0).astype(jnp.bfloat16)


def times(left, right):
    return lax.dot_general(left, right, (((1,), (1,)), ((), ())), preferred_element_type=jnp.float32)


def swapped(values):
    return jnp.swapaxes(values, 0, 1)


def run(copies):
    for c in copies:
        c.start()
    for c in copies:
        c.wait()


def load_parts(block, raw, sems):
    parts = sems.shape[0]
    step = raw.shape[0] // parts
    return [
        pltpu.make_async_copy(block.at[pl.ds(q * step, step)], raw.at[pl.ds(q * step, step)], sems.at[q])
        for q in range(parts)
    ]


def screen_rows(pair_mask, dom_start):
    column = lax.broadcasted_iota(jnp.int32, (8, DSTEP), 1)
    value = jnp.zeros((8, DSTEP), jnp.int32)
    for at in range(PER):
        source = pair_mask if at < PER // 2 else dom_start
        block, r = divmod(at % (PER // 2), 3)
        value = jnp.where(column == at, source[block, r], value)
    return value


def first_kernel(pair_mask, dom_start, bfac, out, raw, made, sems, out_sems):
    _, is_odd = position()
    rows = raw.shape[0]

    @pl.when(is_odd)
    def _():
        loads = load_parts(bfac.at[1], raw, sems)
        for c in loads:
            c.start()
        at = boundary(lambda block, r: (pair_mask[block, r], dom_start[block, r]))["first"]
        stores = []

        def store(first, count):
            piece = pl.ds(first, count)
            c = pltpu.make_async_copy(made.at[piece], out.at[piece], out_sems.at[len(stores)])
            c.start()
            stores.append(c)

        value = screen_rows(pair_mask, dom_start)
        made[2 * rows :, :] = jnp.zeros((NOTE, DOM), made.dtype)
        made[2 * rows :, :DSTEP] = jnp.concatenate([value, value], 0).astype(jnp.float32).astype(made.dtype)
        store(2 * rows, NOTE)
        step = rows // len(loads)
        for q, c in enumerate(loads):
            c.wait()
            part = swapped(raw[pl.ds(q * step, step), :, lanes(at, UNITS)])
            for i in range(2):
                made[pl.ds(i * rows + q * step, step), :] = part[i]
                store(i * rows + q * step, step)
        for c in stores:
            c.wait()


def second_kernel(pair_mask, dom_start, bfac, out, own, zero, raw, sems):
    _, is_odd = position()
    own[...] = screen_rows(pair_mask, dom_start)
    zero[0] = jnp.minimum(pair_mask[0, 0], 0)

    @pl.when(is_odd)
    def _():
        b = boundary(lambda block, r: (pair_mask[block, r], dom_start[block, r]))
        loads = load_parts(bfac.at[jnp.where(b["m1"] > 0, 0, 1)], raw, sems)
        for c in loads:
            c.start()
        step = raw.shape[0] // len(loads)
        for q, c in enumerate(loads):
            c.wait()
            rows = pl.ds(q * step, step)
            out[:, rows, :] = swapped(raw[rows, :, lanes(b["second"], UNITS)])


def relayouter(bfac, raw, target, loads):
    step = 32

    def relayout(b):
        loads[b].wait()

        def some(q, carry):
            rows = pl.ds(pl.multiple_of(q * step, step), step)
            target[b, :, rows, :] = swapped(raw[b, rows])
            return carry

        lax.fori_loop(0, bfac.shape[1] // step, some, 0)

    return relayout


def product(left, a, right, b, at, keep):
    value = sum(times(left[a, i, :, lanes(at, UNITS)], right[b, i, :, lanes(at, UNITS)]) for i in range(2))
    return value * keep.astype(jnp.float32)


def own_kernel(own, bfac, kband, kmirror, mine, held, raw, out, sems):
    loads = [pltpu.make_async_copy(bfac.at[b], raw.at[b], sems.at[b]) for b in range(2)]
    relayout = relayouter(bfac, raw, held, loads)
    stores = []

    def store(source, target):
        c = pltpu.make_async_copy(source, target, sems.at[2 + len(stores)])
        c.start()
        stores.append(c)

    def keep(slot, value, target):
        out[slot] = value
        store(out.at[slot], target)

    for c in loads:
        c.start()
    for b in range(2):
        relayout(b)
        store(held.at[b], mine.at[b])
    k, s = flags(own, 0, 0)
    keep(0, product(held, 0, held, 0, s, k), kband.at[0, 0])
    k, s = flags(own, 0, 1)
    value = product(held, 0, held, 1, s, k)
    keep(1, value, kband.at[0, 1])
    keep(2, value.T, kmirror.at[1, 0])
    k, s = flags(own, 1, 0)
    keep(3, product(held, 1, held, 1, s, k), kband.at[1, 0])
    for c in stores:
        c.wait()


def fast_kernel(own, below, mine, other, kband_in, kmirror_in, kband, kmirror, held, theirs, raw, out, sems):
    _, is_odd = position()
    loads = [pltpu.make_async_copy(other.at[b], raw.at[b], sems.at[b]) for b in range(2)]
    held_load = pltpu.make_async_copy(mine, held, sems.at[2])
    relayout = relayouter(other, raw, theirs, loads)
    for c in (*loads, held_load):
        c.start()

    def get(block, r):
        return tuple(jnp.where(is_odd, a, b) for a, b in zip(flags(below, block, r), flags(own, block, r)))

    b = boundary(get)
    relayout(0)
    relayout(1)
    held_load.wait()
    close = jnp.where(is_odd, 0, 1)
    pick = lambda x, y: jnp.where(is_odd, x, y)
    out[0] = product(held, 1 - close, theirs, 1 - close, pick(b["s3"], b["s1"]), pick(b["m3"], b["m1"]))
    out[1] = product(held, close, theirs, 1 - close, b["s2"], b["m2"])
    out[2] = product(held, close, theirs, close, pick(b["s1"], b["s3"]), pick(b["m1"], b["m3"]))

    def put(targets):
        run([pltpu.make_async_copy(out.at[j], ref, sems.at[3 + j]) for j, ref in enumerate(targets)])

    @pl.when(is_odd)
    def _():
        put([kmirror.at[1, 1], kmirror.at[0, 0], kmirror.at[0, 1]])

    @pl.when(jnp.logical_not(is_odd))
    def _():
        put([kband.at[0, 2], kband.at[1, 1], kband.at[1, 2]])


def first_products_kernel(
    n, own, below, got, mine, kmirror_in, steps, near, second, extra, rest, lives, kmirror, case,
    far_window, near_window, second_window, staged, turned, sems,
):
    me, is_odd = position()
    b = slow_boundary(own, below)
    exists = jnp.where(is_odd, me < n - 1, me > 0)
    short = sum((b["half"] > c).astype(jnp.int32) for c in UP[:-1])
    long = len(UP) + sum((b["half"] > c).astype(jnp.int32) for c in BOTH[:-1])
    which = lax.shift_right_logical(jnp.where(is_odd, me, me - 1) - 1, 1)
    splits = exists & (b["split"] > 0)
    is_long = b["split"] > UP[-1]
    case[0] = jnp.where(splits, 1 + which * len(UP + BOTH) + jnp.where(is_long, long, short), 0)
    parts_due = splits & is_long
    case[1] = jnp.where(exists, 1 + which + jnp.where(parts_due, n // 2 - 1, 0), 0)
    case[2] = jnp.where(parts_due, 1, 0)

    @pl.when(splits)
    def _():
        at = jnp.minimum(b["low"], UNITS)
        run([pltpu.make_async_copy(mine.at[jnp.where(is_odd, 1, 0), :, :, lanes(at, UNITS)], staged, sems.at[3])])
        lower, upper = b["low"] - at, b["low"] - at + b["half"]
        sent = jnp.where(is_odd, lower, upper)
        kept = jnp.where(is_odd, upper, lower)
        count = jnp.where(is_odd, b["split"] - b["half"], b["half"])

        def some(u, carry):
            alive = jnp.where(u < count, 1.0, 0.0).astype(rest.dtype)
            for i in range(2):
                extra[i, :, lanes(u)] = staged[i, :, lanes(jnp.minimum(sent + u, UNITS - 1))]
                rest[i, :, lanes(u)] = staged[i, :, lanes(jnp.minimum(kept + u, UNITS - 1))] * alive
            return carry

        lax.fori_loop(0, SPARE, some, 0)

    @pl.when(jnp.logical_not(is_odd))
    def _():
        rows = mine.shape[2]
        at = b["first"]
        loads = [
            pltpu.make_async_copy(mine.at[1, :, :, lanes(at, UNITS)], far_window, sems.at[0]),
            pltpu.make_async_copy(mine.at[0, :, :, lanes(at, UNITS)], near_window, sems.at[1]),
            pltpu.make_async_copy(mine.at[0, :, :, lanes(b["second"], UNITS)], second_window, sems.at[2]),
        ]
        for c in loads:
            c.start()
        left = [got[pl.ds(i * rows, rows), :] for i in range(2)]

        def against(ref, scale):
            return sum(times(left[i], ref[i] * scale) for i in range(2))

        loads[0].wait()
        value = against(far_window, counted(at, at, at + UNITS * b["m3"]))
        turned[...] = value.T
        mirrored = pltpu.make_async_copy(turned, kmirror.at[1, 1], sems.at[4])
        mirrored.start()
        steps[...], whole, power = coded(value)
        lives[0:1, :] = jnp.zeros((1, rows), lives.dtype) + b["m1"].astype(lives.dtype)
        lives[1:2, :] = whole
        lives[2:3, :] = power
        loads[1].wait()
        near[...] = against(near_window, counted(at, b["s2"], b["s2"] + UNITS * b["m2"]))
        loads[2].wait()
        far_lives = b["m1"] > 0
        counts = counted(
            b["second"],
            jnp.where(far_lives, b["second"], b["low"]),
            jnp.where(far_lives, b["second"] + UNITS, b["low"] + b["rest"]),
        )
        for i in range(2):
            second[i] = (second_window[i] * counts).T
        mirrored.wait()


def rest_kernel(got, rest, out):
    width = got.shape[2]
    out[...] = sum(times(got[i], rest[i, :, :width]) for i in range(2))


def coded(value):
    top = jnp.maximum(jnp.max(jnp.abs(value), axis=0, keepdims=True), 1e-30)
    power = jnp.ceil(jnp.log2(top)) - 14.0
    unit = jnp.exp2(power)
    whole = jnp.clip(jnp.ceil(top / unit), 1.0, STEPS)
    steps = value * (STEPS / (whole * unit)) + ROUND
    return (steps - ROUND).astype(jnp.int32).astype(jnp.int16), whole, power


def decoded(steps, whole, power):
    return steps * (whole * jnp.exp2(power) * (1.0 / STEPS))


def second_products_kernel(got, second, steps, near, more, lives, results, part, sent, near_sent):
    _, is_odd = position()

    @pl.when(is_odd)
    def _():
        part[...] = more[...].T

    @pl.when(jnp.logical_not(is_odd))
    def _():
        rows = steps.shape[0]
        row = lax.broadcasted_iota(jnp.int32, (NOTE, rows), 0)

        def scales(*values):
            total = jnp.zeros((NOTE, rows), jnp.float32)
            for k, value in enumerate(values):
                total = jnp.where(row == k, value, total)
            return total.astype(jnp.int32).astype(jnp.int16)

        lived, far_whole, far_power = (lives[k : k + 1, :] for k in range(3))
        value = sum(jnp.dot(got[i], second[i], preferred_element_type=jnp.float32) for i in range(2))
        block = value * lived
        results[...] = block
        sent[pl.ds(0, rows), :], whole, power = coded(block)
        sent[pl.ds(rows, rows), :] = steps[...]
        sent[pl.ds(2 * rows, NOTE), :] = scales(whole, power, far_whole, far_power)
        block = near[...] + more[...] + value * (1.0 - lived)
        part[...] = block
        near_sent[pl.ds(0, rows), :], whole, power = coded(block)
        near_sent[pl.ds(rows, NOTE), :] = scales(whole, power)


def last_kernel(
    case, got, near_got, part, other, results, kband_in, kmirror_in, kband, kmirror, out, near, mine, theirs, own, sems
):
    _, is_odd = position()
    is_even = jnp.logical_not(is_odd)
    due = case[2] > 0
    part_load = pltpu.make_async_copy(part, mine, sems.at[3])
    other_load = pltpu.make_async_copy(other, theirs, sems.at[4])
    results_load = pltpu.make_async_copy(results, own, sems.at[5])
    near_load = pltpu.make_async_copy(near_got, near, sems.at[6])

    @pl.when(is_even)
    def _():
        results_load.start()

    @pl.when(is_even | due)
    def _():
        part_load.start()

    @pl.when(due)
    def _():
        other_load.start()

    @pl.when(is_odd & jnp.logical_not(due))
    def _():
        near_load.start()

    rows = out.shape[1]

    def block(ref, at, scale_at, k):
        scales = ref[pl.ds(scale_at, NOTE), :].astype(jnp.int32).astype(jnp.float32)
        steps = ref[pl.ds(at, rows), :].astype(jnp.int32).astype(jnp.float32)
        return decoded(steps, scales[2 * k : 2 * k + 1], scales[2 * k + 1 : 2 * k + 2])

    @pl.when(is_odd)
    def _():
        copies = [
            pltpu.make_async_copy(out.at[k], kband.at[index], sems.at[k])
            for k, index in enumerate(((0, 2), (1, 2), (1, 1)))
        ]
        for k in range(2):
            out[k] = block(got, k * rows, 2 * rows, k)
            copies[k].start()

        @pl.when(due)
        def _():
            part_load.wait()
            other_load.wait()
            out[2] = mine[...] + theirs[...]

        @pl.when(jnp.logical_not(due))
        def _():
            near_load.wait()
            out[2] = block(near, 0, rows, 0)

        copies[2].start()
        for c in copies:
            c.wait()

    @pl.when(is_even)
    def _():
        copies = [
            pltpu.make_async_copy(out.at[k], kmirror.at[index], sems.at[k]) for k, index in enumerate(((0, 1), (0, 0)))
        ]
        results_load.wait()
        out[0] = own[...].T
        copies[0].start()
        part_load.wait()

        @pl.when(due)
        def _():
            other_load.wait()
            out[1] = (mine[...] + theirs[...]).T

        @pl.when(jnp.logical_not(due))
        def _():
            out[1] = mine[...].T

        copies[1].start()
        for c in copies:
            c.wait()


def call(kernel, outs, ins, out_specs, scratch, flops=0, moved=0, aliases=None, vmem=40):
    inner = kernel.func if isinstance(kernel, functools.partial) else kernel
    return pl.pallas_call(
        kernel,
        out_shape=outs,
        in_specs=ins,
        out_specs=out_specs,
        scratch_shapes=scratch,
        input_output_aliases=aliases or {},
        compiler_params=pltpu.CompilerParams(vmem_limit_bytes=vmem * 2**20),
        cost_estimate=pl.CostEstimate(flops=flops, bytes_accessed=moved, transcendentals=0),
        name=inner.__name__,
    )


def per_device(bfac, pair_mask, dom_start):
    n = lax.axis_size("wide")
    _, rows, orbitals, fitting = bfac.shape
    upward = [(i, i + 1) for i in range(1, n - 1, 2)]
    downward = [(j, i) for i, j in upward]
    fast = [p for i in range(0, n, 2) for p in ((i, i + 1), (i + 1, i))]
    f32, bf16 = jnp.float32, bfac.dtype
    shape = jax.ShapeDtypeStruct
    dma = pltpu.SemaphoreType.DMA
    square = shape((rows, rows), f32)
    window = shape((orbitals, rows, DOM), bf16)
    raw_block = pltpu.VMEM((rows, orbitals, fitting), bf16)

    whole = (orbitals * rows + NOTE, DOM)
    parts = 8
    first = call(
        first_kernel,
        shape(whole, bf16),
        [SMEM, SMEM, HBM],
        HBM,
        [raw_block, pltpu.VMEM(whole, bf16), dma((parts,)), dma((parts * orbitals + 1,))],
        vmem=60,
    )(pair_mask, dom_start, bfac)
    first_got = lax.ppermute(first, "wide", upward)

    second, own, zero = call(
        second_kernel,
        (window, shape((8, DSTEP), jnp.int32), shape((1,), jnp.int32)),
        [SMEM, SMEM, HBM],
        (VMEM, VMEM, SMEM),
        [raw_block, dma((8,))],
        vmem=57,
    )(pair_mask, dom_start, lax.optimization_barrier((bfac, first))[0])
    second_got = lax.ppermute(second, "wide", upward)

    band = shape((2, 3, rows, rows), f32)
    mirror = shape((2, 2, rows, rows), f32)
    both = shape((2, orbitals, rows, fitting), bf16)
    spare = shape((orbitals, rows, SPARE * DSTEP), bf16)
    blocks = pltpu.VMEM((2, orbitals, rows, fitting), bf16)
    raw_blocks = pltpu.VMEM((2, rows, orbitals, fitting), bf16)

    def inner(own, bfac):
        below = lax.ppermute(own, "wide", [(i, i + 1) for i in range(0, n, 2)])
        other = lax.ppermute(bfac, "wide", fast)
        kband, kmirror, mine = call(
            own_kernel,
            (band, mirror, both),
            [SMEM, HBM],
            (HBM, HBM, HBM),
            [blocks, raw_blocks, pltpu.VMEM((4, rows, rows), f32), dma((8,))],
            2**31,
            2**25,
            vmem=40,
        )(own, bfac)
        kband, kmirror = call(
            fast_kernel,
            (band, mirror),
            [SMEM, SMEM, HBM, HBM, HBM, HBM],
            (HBM, HBM),
            [blocks, blocks, raw_blocks, pltpu.VMEM((3, rows, rows), f32), dma((6,))],
            2**31,
            2**25,
            {4: 0, 5: 1},
            vmem=32,
        )(own, below, mine, other, kband, kmirror)
        return kband, kmirror, mine

    def unused(own, bfac):
        return tuple(jnp.zeros(o.shape, o.dtype) for o in (band, mirror, both))

    own, bfac, _ = lax.optimization_barrier((own, bfac, second))
    kband, kmirror, mine = lax.cond(zero[0] == 0, inner, unused, own, bfac)

    below = first_got[orbitals * rows : orbitals * rows + 8, :DSTEP].astype(jnp.int32)
    staged = pltpu.VMEM((orbitals, rows, DOM), bf16)
    steps, near, second_window, extra, rest_window, lives, kmirror, case = call(
        functools.partial(first_products_kernel, n),
        (
            shape((rows, rows), jnp.int16),
            square,
            shape((orbitals, DOM, rows), bf16),
            spare,
            spare,
            shape((8, rows), f32),
            mirror,
            shape((3,), jnp.int32),
        ),
        [SMEM, SMEM, VMEM, HBM, HBM],
        (VMEM, VMEM, VMEM, VMEM, VMEM, VMEM, HBM, SMEM),
        [staged, staged, staged, staged, pltpu.VMEM((rows, rows), f32), dma((5,))],
        2**31,
        2**22,
        {4: 6},
        vmem=20,
    )(own, below, first_got, mine, kmirror)

    def nothing(*_):
        return jnp.zeros((rows, rows), f32)

    def pair_of(lower):
        return [(lower, lower + 1), (lower + 1, lower)]

    def rest(lower, count, pairs):
        def branch(extra, rest_window):
            got = lax.ppermute(extra[:, :, : count * DSTEP], "wide", pairs)
            return call(rest_kernel, square, [VMEM, VMEM], VMEM, [], 2**26 * count, 2**19 * count, vmem=8)(
                got, rest_window
            )

        return branch

    lowers = range(1, n - 1, 2)
    branches = [nothing]
    for i in lowers:
        branches += [rest(i, c, [(i, i + 1)]) for c in UP] + [rest(i, c, pair_of(i)) for c in BOTH]
    more = lax.switch(case[0], branches, extra, rest_window)

    near_shape = (rows + NOTE, rows)
    results, part, sent, near_sent = call(
        second_products_kernel,
        (square, square, shape((2 * rows + NOTE, rows), jnp.int16), shape(near_shape, jnp.int16)),
        [VMEM] * 6,
        (VMEM, VMEM, VMEM, VMEM),
        [],
        2**30,
        2**22,
        vmem=12,
    )(second_got, second_window, steps, near, more, lives)
    sent_got = lax.ppermute(sent, "wide", downward)

    def no_near(near_sent, part):
        return jnp.zeros(near_shape, jnp.int16), jnp.zeros((rows, rows), f32)

    def whole_near(lower):
        def branch(near_sent, part):
            return lax.ppermute(near_sent, "wide", [(lower + 1, lower)]), jnp.zeros((rows, rows), f32)

        return branch

    def parts_of_near(lower):
        def branch(near_sent, part):
            return jnp.zeros(near_shape, jnp.int16), lax.ppermute(part, "wide", pair_of(lower))

        return branch

    near_branches = [no_near] + [whole_near(i) for i in lowers] + [parts_of_near(i) for i in lowers]
    near_got, other_part = lax.switch(case[1], near_branches, near_sent, part)
    part_block = pltpu.VMEM((rows, rows), f32)
    return call(
        last_kernel,
        (band, mirror),
        [SMEM, VMEM, HBM, HBM, HBM, HBM, HBM, HBM],
        (HBM, HBM),
        [
            pltpu.VMEM((3, rows, rows), f32),
            pltpu.VMEM(near_shape, jnp.int16),
            part_block,
            part_block,
            part_block,
            dma((7,)),
        ],
        0,
        2**20,
        {6: 0, 7: 1},
        vmem=8,
    )(case, sent_got, near_got, part, other_part, results, kband, kmirror)


def solution(mesh):
    placed = (P("wide", None, "groups", None), P("wide", None), P("wide", None))
    return jax.shard_map(
        per_device,
        mesh=mesh,
        in_specs=placed,
        out_specs=(
            P(("groups", "wide"), None, None, None),
            P(("groups", "wide"), None, None, None),
        ),
        check_vma=False,
    )
```

```python
import functools

import jax
import jax.numpy as jnp
from jax import lax
from jax.experimental import pallas as pl
from jax.experimental.pallas import tpu as pltpu
from jax.sharding import PartitionSpec as P

DOM = 2048
DSTEP = 128
UNITS = DOM // DSTEP
UP = (2, 4)
BOTH = (3, 4, 6, 8)
SPARE = 8
PER = 12
NOTE = 16
STEPS = 32767.0
ROUND = 1.5 * 2.0**23
VMEM = pl.BlockSpec(memory_space=pltpu.VMEM)
SMEM = pl.BlockSpec(memory_space=pltpu.SMEM)
HBM = pl.BlockSpec(memory_space=pltpu.HBM)


def flags(screen, block, r):
    at = block * 3 + r
    return screen[0, at], screen[0, at + PER // 2]


def boundary(get):
    m1, s1 = get(0, 2)
    m2, s2 = get(1, 1)
    m3, s3 = get(1, 2)
    first = jnp.where(m3 > 0, s3, s2)
    low = jnp.where(first <= s2, jnp.maximum(s2, first + UNITS), s2)
    high = jnp.where(first <= s2, s2 + UNITS, jnp.minimum(s2 + UNITS, first))
    rest = jnp.maximum(high - low, 0) * m2
    second = jnp.where(m1 > 0, s1, jnp.minimum(low, UNITS))
    split = rest * m1
    half = jnp.where(split > UP[-1], lax.shift_right_logical(split + 1, 1), split)
    return dict(
        m1=m1, s1=s1, m2=m2, s2=s2, m3=m3, s3=s3, first=first, low=low, rest=rest, second=second, split=split, half=half
    )


def position():
    me = lax.axis_index("wide")
    return me, lax.rem(me, 2) == 1


def slow_boundary(own, below):
    _, is_odd = position()

    def get(block, r):
        return tuple(jnp.where(is_odd, a, b) for a, b in zip(flags(own, block, r), flags(below, block, r)))

    return boundary(get)


def lanes(unit, count=1):
    return pl.ds(pl.multiple_of(unit * DSTEP, DSTEP), count * DSTEP)


def counted(unit, first, last):
    at = unit + lax.shift_right_logical(lax.broadcasted_iota(jnp.int32, (1, DOM), 1), DSTEP.bit_length() - 1)
    return jnp.where((at >= first) & (at < last), 1.0, 0.0).astype(jnp.bfloat16)


def times(left, right):
    return lax.dot_general(left, right, (((1,), (1,)), ((), ())), preferred_element_type=jnp.float32)


def swapped(values):
    return jnp.swapaxes(values, 0, 1)


def run(copies):
    for c in copies:
        c.start()
    for c in copies:
        c.wait()


def load_parts(block, raw, sems):
    parts = sems.shape[0]
    step = raw.shape[0] // parts
    return [
        pltpu.make_async_copy(block.at[pl.ds(q * step, step)], raw.at[pl.ds(q * step, step)], sems.at[q])
        for q in range(parts)
    ]


def screen_rows(pair_mask, dom_start):
    column = lax.broadcasted_iota(jnp.int32, (8, DSTEP), 1)
    value = jnp.zeros((8, DSTEP), jnp.int32)
    for at in range(PER):
        source = pair_mask if at < PER // 2 else dom_start
        block, r = divmod(at % (PER // 2), 3)
        value = jnp.where(column == at, source[block, r], value)
    return value


def first_kernel(pair_mask, dom_start, bfac, out, raw, made, sems, out_sems):
    _, is_odd = position()
    rows = raw.shape[0]

    @pl.when(is_odd)
    def _():
        loads = load_parts(bfac.at[1], raw, sems)
        for c in loads:
            c.start()
        at = boundary(lambda block, r: (pair_mask[block, r], dom_start[block, r]))["first"]
        stores = []

        def store(first, count):
            piece = pl.ds(first, count)
            c = pltpu.make_async_copy(made.at[piece], out.at[piece], out_sems.at[len(stores)])
            c.start()
            stores.append(c)

        value = screen_rows(pair_mask, dom_start)
        made[2 * rows :, :] = jnp.zeros((NOTE, DOM), made.dtype)
        made[2 * rows :, :DSTEP] = jnp.concatenate([value, value], 0).astype(jnp.float32).astype(made.dtype)
        store(2 * rows, NOTE)
        step = rows // len(loads)
        for q, c in enumerate(loads):
            c.wait()
            part = swapped(raw[pl.ds(q * step, step), :, lanes(at, UNITS)])
            for i in range(2):
                made[pl.ds(i * rows + q * step, step), :] = part[i]
                store(i * rows + q * step, step)
        for c in stores:
            c.wait()


def second_kernel(pair_mask, dom_start, bfac, out, own, zero, raw, sems):
    _, is_odd = position()
    own[...] = screen_rows(pair_mask, dom_start)
    zero[0] = jnp.minimum(pair_mask[0, 0], 0)

    @pl.when(is_odd)
    def _():
        b = boundary(lambda block, r: (pair_mask[block, r], dom_start[block, r]))
        loads = load_parts(bfac.at[jnp.where(b["m1"] > 0, 0, 1)], raw, sems)
        for c in loads:
            c.start()
        step = raw.shape[0] // len(loads)
        for q, c in enumerate(loads):
            c.wait()
            rows = pl.ds(q * step, step)
            out[:, rows, :] = swapped(raw[rows, :, lanes(b["second"], UNITS)])


def relayouter(bfac, raw, target, loads):
    step = 32

    def relayout(b):
        loads[b].wait()

        def some(q, carry):
            rows = pl.ds(pl.multiple_of(q * step, step), step)
            target[b, :, rows, :] = swapped(raw[b, rows])
            return carry

        lax.fori_loop(0, bfac.shape[1] // step, some, 0)

    return relayout


def product(left, a, right, b, at, keep):
    value = sum(times(left[a, i, :, lanes(at, UNITS)], right[b, i, :, lanes(at, UNITS)]) for i in range(2))
    return value * keep.astype(jnp.float32)


def own_kernel(own, bfac, kband, kmirror, mine, held, raw, out, sems):
    loads = [pltpu.make_async_copy(bfac.at[b], raw.at[b], sems.at[b]) for b in range(2)]
    relayout = relayouter(bfac, raw, held, loads)
    stores = []

    def store(source, target):
        c = pltpu.make_async_copy(source, target, sems.at[2 + len(stores)])
        c.start()
        stores.append(c)

    def keep(slot, value, target):
        out[slot] = value
        store(out.at[slot], target)

    for c in loads:
        c.start()
    for b in range(2):
        relayout(b)
        store(held.at[b], mine.at[b])
    k, s = flags(own, 0, 0)
    keep(0, product(held, 0, held, 0, s, k), kband.at[0, 0])
    k, s = flags(own, 0, 1)
    value = product(held, 0, held, 1, s, k)
    keep(1, value, kband.at[0, 1])
    keep(2, value.T, kmirror.at[1, 0])
    k, s = flags(own, 1, 0)
    keep(3, product(held, 1, held, 1, s, k), kband.at[1, 0])
    for c in stores:
        c.wait()


def fast_kernel(own, below, mine, other, kband_in, kmirror_in, kband, kmirror, held, theirs, raw, out, sems):
    _, is_odd = position()
    loads = [pltpu.make_async_copy(other.at[b], raw.at[b], sems.at[b]) for b in range(2)]
    held_load = pltpu.make_async_copy(mine, held, sems.at[2])
    relayout = relayouter(other, raw, theirs, loads)
    for c in (*loads, held_load):
        c.start()

    def get(block, r):
        return tuple(jnp.where(is_odd, a, b) for a, b in zip(flags(below, block, r), flags(own, block, r)))

    b = boundary(get)
    relayout(0)
    relayout(1)
    held_load.wait()
    close = jnp.where(is_odd, 0, 1)
    pick = lambda x, y: jnp.where(is_odd, x, y)
    out[0] = product(held, 1 - close, theirs, 1 - close, pick(b["s3"], b["s1"]), pick(b["m3"], b["m1"]))
    out[1] = product(held, close, theirs, 1 - close, b["s2"], b["m2"])
    out[2] = product(held, close, theirs, close, pick(b["s1"], b["s3"]), pick(b["m1"], b["m3"]))

    def put(targets):
        run([pltpu.make_async_copy(out.at[j], ref, sems.at[3 + j]) for j, ref in enumerate(targets)])

    @pl.when(is_odd)
    def _():
        put([kmirror.at[1, 1], kmirror.at[0, 0], kmirror.at[0, 1]])

    @pl.when(jnp.logical_not(is_odd))
    def _():
        put([kband.at[0, 2], kband.at[1, 1], kband.at[1, 2]])


def first_products_kernel(
    n, own, below, got, mine, back, steps, near, second, extra, rest, lives, case, far_window, near_window, second_window, staged, sems
):
    me, is_odd = position()
    b = slow_boundary(own, below)
    exists = jnp.where(is_odd, me < n - 1, me > 0)
    short = sum((b["half"] > c).astype(jnp.int32) for c in UP[:-1])
    long = len(UP) + sum((b["half"] > c).astype(jnp.int32) for c in BOTH[:-1])
    which = lax.shift_right_logical(jnp.where(is_odd, me, me - 1) - 1, 1)
    splits = exists & (b["split"] > 0)
    is_long = b["split"] > UP[-1]
    case[0] = jnp.where(splits, 1 + which * len(UP + BOTH) + jnp.where(is_long, long, short), 0)
    case[1] = jnp.where(splits & is_long, 1 + which, 0)

    @pl.when(splits)
    def _():
        at = jnp.minimum(b["low"], UNITS)
        run([pltpu.make_async_copy(mine.at[jnp.where(is_odd, 1, 0), :, :, lanes(at, UNITS)], staged, sems.at[3])])
        lower, upper = b["low"] - at, b["low"] - at + b["half"]
        sent = jnp.where(is_odd, lower, upper)
        kept = jnp.where(is_odd, upper, lower)
        count = jnp.where(is_odd, b["split"] - b["half"], b["half"])

        def some(u, carry):
            alive = jnp.where(u < count, 1.0, 0.0).astype(rest.dtype)
            for i in range(2):
                extra[i, :, lanes(u)] = staged[i, :, lanes(jnp.minimum(sent + u, UNITS - 1))]
                rest[i, lanes(u), :] = (staged[i, :, lanes(jnp.minimum(kept + u, UNITS - 1))] * alive).T
            return carry

        lax.fori_loop(0, SPARE, some, 0)

    @pl.when(jnp.logical_not(is_odd))
    def _():
        rows = mine.shape[2]
        at = b["first"]
        loads = [
            pltpu.make_async_copy(mine.at[1, :, :, lanes(at, UNITS)], far_window, sems.at[0]),
            pltpu.make_async_copy(mine.at[0, :, :, lanes(at, UNITS)], near_window, sems.at[1]),
            pltpu.make_async_copy(mine.at[0, :, :, lanes(b["second"], UNITS)], second_window, sems.at[2]),
        ]
        for c in loads:
            c.start()
        left = [got[pl.ds(i * rows, rows), :] for i in range(2)]

        def against(ref, scale):
            return sum(times(left[i], ref[i] * scale) for i in range(2))

        loads[0].wait()
        value = against(far_window, counted(at, at, at + UNITS * b["m3"]))
        back[...] = value
        steps[...], whole, power = coded(value)
        lives[0:1, :] = jnp.zeros((1, rows), lives.dtype) + b["m1"].astype(lives.dtype)
        lives[1:2, :] = whole
        lives[2:3, :] = power
        loads[1].wait()
        near[...] = against(near_window, counted(at, b["s2"], b["s2"] + UNITS * b["m2"]))
        loads[2].wait()
        far_lives = b["m1"] > 0
        counts = counted(
            b["second"],
            jnp.where(far_lives, b["second"], b["low"]),
            jnp.where(far_lives, b["second"] + UNITS, b["low"] + b["rest"]),
        )
        for i in range(2):
            second[i] = (second_window[i] * counts).T


def rest_kernel(got, rest, out):
    width = got.shape[2]
    out[...] = sum(jnp.dot(got[i], rest[i, :width, :], preferred_element_type=jnp.float32) for i in range(2))


def coded(value):
    top = jnp.maximum(jnp.max(jnp.abs(value), axis=0, keepdims=True), 1e-30)
    power = jnp.ceil(jnp.log2(top)) - 14.0
    unit = jnp.exp2(power)
    whole = jnp.clip(jnp.ceil(top / unit), 1.0, STEPS)
    steps = value * (STEPS / (whole * unit)) + ROUND
    return (steps - ROUND).astype(jnp.int32).astype(jnp.int16), whole, power


def decoded(steps, whole, power):
    return steps * (whole * jnp.exp2(power) * (1.0 / STEPS))


def second_products_kernel(got, second, steps, near, more, lives, results, part, sent):
    _, is_odd = position()

    @pl.when(is_odd)
    def _():
        part[...] = more[...].T

    @pl.when(jnp.logical_not(is_odd))
    def _():
        rows = steps.shape[0]
        sent[pl.ds(2 * rows, rows), :] = steps[...]
        lived, whole, power = (lives[k : k + 1, :] for k in range(3))
        row = lax.broadcasted_iota(jnp.int32, (NOTE, rows), 0)
        scales = jnp.where(row == 4, whole, jnp.where(row == 5, power, 0.0))
        value = sum(jnp.dot(got[i], second[i], preferred_element_type=jnp.float32) for i in range(2))
        for k, block in enumerate((value * lived, near[...] + more[...] + value * (1.0 - lived))):
            (results, part)[k][...] = block
            sent[pl.ds(k * rows, rows), :], whole, power = coded(block)
            scales = jnp.where(row == 2 * k, whole, jnp.where(row == 2 * k + 1, power, scales))
        sent[pl.ds(3 * rows, NOTE), :] = scales.astype(jnp.int32).astype(jnp.int16)


def mirror_kernel(case, back, results, part, kmirror_in, kmirror, out, sems):
    _, is_odd = position()

    @pl.when(jnp.logical_not(is_odd))
    def _():
        out[0] = back[...].T
        out[1] = results[...].T
        targets = [kmirror.at[1, 1], kmirror.at[0, 1]]
        run([pltpu.make_async_copy(out.at[j], ref, sems.at[j]) for j, ref in enumerate(targets)])

        @pl.when(case[1] == 0)
        def _():
            out[2] = part[...].T
            run([pltpu.make_async_copy(out.at[2], kmirror.at[0, 0], sems.at[2])])


def last_kernel(case, got, part, other, kband_in, kmirror_in, kband, kmirror, out, mine, theirs, sems):
    _, is_odd = position()
    due = case[1] > 0

    loads = [pltpu.make_async_copy(part, mine, sems.at[3]), pltpu.make_async_copy(other, theirs, sems.at[4])]

    @pl.when(due)
    def _():
        for c in loads:
            c.start()

    @pl.when(is_odd)
    def _():
        rows = out.shape[1]
        scales = got[pl.ds(3 * rows, NOTE), :].astype(jnp.int32).astype(jnp.float32)
        copies = [
            pltpu.make_async_copy(out.at[k], kband.at[index], sems.at[k])
            for k, index in enumerate(((0, 2), (1, 1), (1, 2)))
        ]
        for k in (0, 2, 1):
            steps = got[pl.ds(k * rows, rows), :].astype(jnp.int32).astype(jnp.float32)
            out[k] = decoded(steps, scales[2 * k : 2 * k + 1], scales[2 * k + 1 : 2 * k + 2])
            if k == 1:

                @pl.when(due)
                def _():
                    for c in loads:
                        c.wait()
                    out[1] = mine[...] + theirs[...]

            copies[k].start()
        for c in copies:
            c.wait()

    @pl.when(jnp.logical_not(is_odd) & due)
    def _():
        for c in loads:
            c.wait()
        out[0] = (mine[...] + theirs[...]).T
        run([pltpu.make_async_copy(out.at[0], kmirror.at[0, 0], sems.at[0])])


def call(kernel, outs, ins, out_specs, scratch, flops=0, moved=0, aliases=None, vmem=40):
    inner = kernel.func if isinstance(kernel, functools.partial) else kernel
    return pl.pallas_call(
        kernel,
        out_shape=outs,
        in_specs=ins,
        out_specs=out_specs,
        scratch_shapes=scratch,
        input_output_aliases=aliases or {},
        compiler_params=pltpu.CompilerParams(vmem_limit_bytes=vmem * 2**20),
        cost_estimate=pl.CostEstimate(flops=flops, bytes_accessed=moved, transcendentals=0),
        name=inner.__name__,
    )


def per_device(bfac, pair_mask, dom_start):
    n = lax.axis_size("wide")
    _, rows, orbitals, fitting = bfac.shape
    upward = [(i, i + 1) for i in range(1, n - 1, 2)]
    downward = [(j, i) for i, j in upward]
    fast = [p for i in range(0, n, 2) for p in ((i, i + 1), (i + 1, i))]
    f32, bf16 = jnp.float32, bfac.dtype
    shape = jax.ShapeDtypeStruct
    dma = pltpu.SemaphoreType.DMA
    square = shape((rows, rows), f32)
    window = shape((orbitals, rows, DOM), bf16)
    raw_block = pltpu.VMEM((rows, orbitals, fitting), bf16)

    whole = (orbitals * rows + NOTE, DOM)
    parts = 4
    first = call(
        first_kernel,
        shape(whole, bf16),
        [SMEM, SMEM, HBM],
        HBM,
        [raw_block, pltpu.VMEM(whole, bf16), dma((parts,)), dma((parts * orbitals + 1,))],
        vmem=60,
    )(pair_mask, dom_start, bfac)
    first_got = lax.ppermute(first, "wide", upward)

    second, own, zero = call(
        second_kernel,
        (window, shape((8, DSTEP), jnp.int32), shape((1,), jnp.int32)),
        [SMEM, SMEM, HBM],
        (VMEM, VMEM, SMEM),
        [raw_block, dma((8,))],
        vmem=57,
    )(pair_mask, dom_start, lax.optimization_barrier((bfac, first))[0])
    second_got = lax.ppermute(second, "wide", upward)

    band = shape((2, 3, rows, rows), f32)
    mirror = shape((2, 2, rows, rows), f32)
    both = shape((2, orbitals, rows, fitting), bf16)
    spare = shape((orbitals, rows, SPARE * DSTEP), bf16)
    blocks = pltpu.VMEM((2, orbitals, rows, fitting), bf16)
    raw_blocks = pltpu.VMEM((2, rows, orbitals, fitting), bf16)

    def inner(own, bfac):
        below = lax.ppermute(own, "wide", [(i, i + 1) for i in range(0, n, 2)])
        other = lax.ppermute(bfac, "wide", fast)
        kband, kmirror, mine = call(
            own_kernel,
            (band, mirror, both),
            [SMEM, HBM],
            (HBM, HBM, HBM),
            [blocks, raw_blocks, pltpu.VMEM((4, rows, rows), f32), dma((8,))],
            2**31,
            2**25,
            vmem=40,
        )(own, bfac)
        kband, kmirror = call(
            fast_kernel,
            (band, mirror),
            [SMEM, SMEM, HBM, HBM, HBM, HBM],
            (HBM, HBM),
            [blocks, blocks, raw_blocks, pltpu.VMEM((3, rows, rows), f32), dma((6,))],
            2**31,
            2**25,
            {4: 0, 5: 1},
            vmem=32,
        )(own, below, mine, other, kband, kmirror)
        return kband, kmirror, mine

    def unused(own, bfac):
        return tuple(jnp.zeros(o.shape, o.dtype) for o in (band, mirror, both))

    own, bfac, _ = lax.optimization_barrier((own, bfac, second))
    kband, kmirror, mine = lax.cond(zero[0] == 0, inner, unused, own, bfac)

    below = first_got[orbitals * rows : orbitals * rows + 8, :DSTEP].astype(jnp.int32)
    staged = pltpu.VMEM((orbitals, rows, DOM), bf16)
    back, steps, near, second_window, extra, rest_window, lives, case = call(
        functools.partial(first_products_kernel, n),
        (
            square,
            shape((rows, rows), jnp.int16),
            square,
            shape((orbitals, DOM, rows), bf16),
            spare,
            shape((orbitals, SPARE * DSTEP, rows), bf16),
            shape((8, rows), f32),
            shape((2,), jnp.int32),
        ),
        [SMEM, SMEM, VMEM, HBM],
        (VMEM, VMEM, VMEM, VMEM, VMEM, VMEM, VMEM, SMEM),
        [staged, staged, staged, staged, dma((4,))],
        2**31,
        2**22,
        vmem=16,
    )(own, below, first_got, mine)

    def nothing(*_):
        return jnp.zeros((rows, rows), f32)

    def pair_of(lower):
        return [(lower, lower + 1), (lower + 1, lower)]

    def rest(lower, count, pairs):
        def branch(extra, rest_window):
            got = lax.ppermute(extra[:, :, : count * DSTEP], "wide", pairs)
            return call(rest_kernel, square, [VMEM, VMEM], VMEM, [], 2**26 * count, 2**19 * count, vmem=8)(
                got, rest_window
            )

        return branch

    def parts_of(lower):
        return lambda part: lax.ppermute(part, "wide", pair_of(lower))

    lowers = range(1, n - 1, 2)
    branches = [nothing]
    for i in lowers:
        branches += [rest(i, c, [(i, i + 1)]) for c in UP] + [rest(i, c, pair_of(i)) for c in BOTH]
    more = lax.switch(case[0], branches, extra, rest_window)

    results, part, sent = call(
        second_products_kernel,
        (square, square, shape((3 * rows + NOTE, rows), jnp.int16)),
        [VMEM] * 6,
        (VMEM, VMEM, VMEM),
        [],
        2**30,
        2**22,
        vmem=12,
    )(second_got, second_window, steps, near, more, lives)
    sent_got = lax.ppermute(sent, "wide", downward)
    kmirror = call(
        mirror_kernel,
        mirror,
        [SMEM, VMEM, VMEM, VMEM, HBM],
        HBM,
        [pltpu.VMEM((3, rows, rows), f32), dma((3,))],
        0,
        2**20,
        {4: 0},
        vmem=8,
    )(case, back, results, part, kmirror)
    part, kmirror = lax.optimization_barrier((part, kmirror))
    other_part = lax.switch(case[1], [nothing] + [parts_of(i) for i in lowers], part)
    return call(
        last_kernel,
        (band, mirror),
        [SMEM, VMEM, HBM, HBM, HBM, HBM],
        (HBM, HBM),
        [
            pltpu.VMEM((3, rows, rows), f32),
            pltpu.VMEM((rows, rows), f32),
            pltpu.VMEM((rows, rows), f32),
            dma((5,)),
        ],
        0,
        2**20,
        {4: 0, 5: 1},
        vmem=8,
    )(case, sent_got, part, other_part, kband, kmirror)


def solution(mesh):
    placed = (P("wide", None, "groups", None), P("wide", None), P("wide", None))
    return jax.shard_map(
        per_device,
        mesh=mesh,
        in_specs=placed,
        out_specs=(
            P(("groups", "wide"), None, None, None),
            P(("groups", "wide"), None, None, None),
        ),
        check_vma=False,
    )
```

```python
import functools

import jax
import jax.numpy as jnp
from jax import lax
from jax.experimental import pallas as pl
from jax.experimental.pallas import tpu as pltpu
from jax.sharding import PartitionSpec as P

DOM = 2048
DSTEP = 128
UNITS = DOM // DSTEP
UP = (2, 4, 6)
BOTH = (4, 6, 8)
SPARE = 8
PER = 12
NOTE = 16
STEPS = 32767.0
ROUND = 1.5 * 2.0**23
VMEM = pl.BlockSpec(memory_space=pltpu.VMEM)
SMEM = pl.BlockSpec(memory_space=pltpu.SMEM)
HBM = pl.BlockSpec(memory_space=pltpu.HBM)


def flags(screen, block, r):
    at = block * 3 + r
    return screen[0, at], screen[0, at + PER // 2]


def boundary(get):
    m1, s1 = get(0, 2)
    m2, s2 = get(1, 1)
    m3, s3 = get(1, 2)
    first = jnp.where(m3 > 0, s3, s2)
    low = jnp.where(first <= s2, jnp.maximum(s2, first + UNITS), s2)
    high = jnp.where(first <= s2, s2 + UNITS, jnp.minimum(s2 + UNITS, first))
    rest = jnp.maximum(high - low, 0) * m2
    second = jnp.where(m1 > 0, s1, jnp.minimum(low, UNITS))
    split = rest * m1
    half = jnp.where(split > UP[-1], lax.shift_right_logical(split + 1, 1), split)
    return dict(
        m1=m1, s1=s1, m2=m2, s2=s2, m3=m3, s3=s3, first=first, low=low, rest=rest, second=second, split=split, half=half
    )


def position():
    me = lax.axis_index("wide")
    return me, lax.rem(me, 2) == 1


def slow_boundary(own, below):
    _, is_odd = position()

    def get(block, r):
        return tuple(jnp.where(is_odd, a, b) for a, b in zip(flags(own, block, r), flags(below, block, r)))

    return boundary(get)


def lanes(unit, count=1):
    return pl.ds(pl.multiple_of(unit * DSTEP, DSTEP), count * DSTEP)


def counted(unit, first, last):
    at = unit + lax.shift_right_logical(lax.broadcasted_iota(jnp.int32, (1, DOM), 1), DSTEP.bit_length() - 1)
    return jnp.where((at >= first) & (at < last), 1.0, 0.0).astype(jnp.bfloat16)


def times(left, right):
    return lax.dot_general(left, right, (((1,), (1,)), ((), ())), preferred_element_type=jnp.float32)


def swapped(values):
    return jnp.swapaxes(values, 0, 1)


def run(copies):
    for c in copies:
        c.start()
    for c in copies:
        c.wait()


def load_parts(block, raw, sems):
    parts = sems.shape[0]
    step = raw.shape[0] // parts
    return [
        pltpu.make_async_copy(block.at[pl.ds(q * step, step)], raw.at[pl.ds(q * step, step)], sems.at[q])
        for q in range(parts)
    ]


def screen_rows(pair_mask, dom_start):
    column = lax.broadcasted_iota(jnp.int32, (8, DSTEP), 1)
    value = jnp.zeros((8, DSTEP), jnp.int32)
    for at in range(PER):
        source = pair_mask if at < PER // 2 else dom_start
        block, r = divmod(at % (PER // 2), 3)
        value = jnp.where(column == at, source[block, r], value)
    return value


def first_kernel(pair_mask, dom_start, bfac, out, raw, made, sems, out_sems):
    _, is_odd = position()
    rows = raw.shape[0]

    @pl.when(is_odd)
    def _():
        loads = load_parts(bfac.at[1], raw, sems)
        for c in loads:
            c.start()
        at = boundary(lambda block, r: (pair_mask[block, r], dom_start[block, r]))["first"]
        stores = []

        def store(first, count):
            piece = pl.ds(first, count)
            c = pltpu.make_async_copy(made.at[piece], out.at[piece], out_sems.at[len(stores)])
            c.start()
            stores.append(c)

        value = screen_rows(pair_mask, dom_start)
        made[2 * rows :, :] = jnp.zeros((NOTE, DOM), made.dtype)
        made[2 * rows :, :DSTEP] = jnp.concatenate([value, value], 0).astype(jnp.float32).astype(made.dtype)
        store(2 * rows, NOTE)
        step = rows // len(loads)
        for q, c in enumerate(loads):
            c.wait()
            part = swapped(raw[pl.ds(q * step, step), :, lanes(at, UNITS)])
            for i in range(2):
                made[pl.ds(i * rows + q * step, step), :] = part[i]
                store(i * rows + q * step, step)
        for c in stores:
            c.wait()


def second_kernel(pair_mask, dom_start, bfac, out, own, zero, raw, sems):
    _, is_odd = position()
    own[...] = screen_rows(pair_mask, dom_start)
    zero[0] = jnp.minimum(pair_mask[0, 0], 0)

    @pl.when(is_odd)
    def _():
        b = boundary(lambda block, r: (pair_mask[block, r], dom_start[block, r]))
        loads = load_parts(bfac.at[jnp.where(b["m1"] > 0, 0, 1)], raw, sems)
        for c in loads:
            c.start()
        step = raw.shape[0] // len(loads)
        for q, c in enumerate(loads):
            c.wait()
            rows = pl.ds(q * step, step)
            out[:, rows, :] = swapped(raw[rows, :, lanes(b["second"], UNITS)])


def relayouter(bfac, raw, target, loads):
    step = 32

    def relayout(b):
        loads[b].wait()

        def some(q, carry):
            rows = pl.ds(pl.multiple_of(q * step, step), step)
            target[b, :, rows, :] = swapped(raw[b, rows])
            return carry

        lax.fori_loop(0, bfac.shape[1] // step, some, 0)

    return relayout


def product(left, a, right, b, at, keep):
    value = sum(times(left[a, i, :, lanes(at, UNITS)], right[b, i, :, lanes(at, UNITS)]) for i in range(2))
    return value * keep.astype(jnp.float32)


def own_kernel(own, bfac, kband, kmirror, mine, held, raw, out, sems):
    loads = [pltpu.make_async_copy(bfac.at[b], raw.at[b], sems.at[b]) for b in range(2)]
    relayout = relayouter(bfac, raw, held, loads)
    stores = []

    def store(source, target):
        c = pltpu.make_async_copy(source, target, sems.at[2 + len(stores)])
        c.start()
        stores.append(c)

    def keep(slot, value, target):
        out[slot] = value
        store(out.at[slot], target)

    for c in loads:
        c.start()
    for b in range(2):
        relayout(b)
        store(held.at[b], mine.at[b])
    k, s = flags(own, 0, 0)
    keep(0, product(held, 0, held, 0, s, k), kband.at[0, 0])
    k, s = flags(own, 0, 1)
    value = product(held, 0, held, 1, s, k)
    keep(1, value, kband.at[0, 1])
    keep(2, value.T, kmirror.at[1, 0])
    k, s = flags(own, 1, 0)
    keep(3, product(held, 1, held, 1, s, k), kband.at[1, 0])
    for c in stores:
        c.wait()


def fast_kernel(own, below, mine, other, kband_in, kmirror_in, kband, kmirror, held, theirs, raw, out, sems):
    _, is_odd = position()
    loads = [pltpu.make_async_copy(other.at[b], raw.at[b], sems.at[b]) for b in range(2)]
    held_load = pltpu.make_async_copy(mine, held, sems.at[2])
    relayout = relayouter(other, raw, theirs, loads)
    for c in (*loads, held_load):
        c.start()

    def get(block, r):
        return tuple(jnp.where(is_odd, a, b) for a, b in zip(flags(below, block, r), flags(own, block, r)))

    b = boundary(get)
    relayout(0)
    relayout(1)
    held_load.wait()
    close = jnp.where(is_odd, 0, 1)
    pick = lambda x, y: jnp.where(is_odd, x, y)
    out[0] = product(held, 1 - close, theirs, 1 - close, pick(b["s3"], b["s1"]), pick(b["m3"], b["m1"]))
    out[1] = product(held, close, theirs, 1 - close, b["s2"], b["m2"])
    out[2] = product(held, close, theirs, close, pick(b["s1"], b["s3"]), pick(b["m1"], b["m3"]))

    def put(targets):
        run([pltpu.make_async_copy(out.at[j], ref, sems.at[3 + j]) for j, ref in enumerate(targets)])

    @pl.when(is_odd)
    def _():
        put([kmirror.at[1, 1], kmirror.at[0, 0], kmirror.at[0, 1]])

    @pl.when(jnp.logical_not(is_odd))
    def _():
        put([kband.at[0, 2], kband.at[1, 1], kband.at[1, 2]])


def first_products_kernel(
    n, own, below, got, mine, back, steps, near, second, extra, rest, lives, case, far_window, near_window, second_window, staged, sems
):
    me, is_odd = position()
    b = slow_boundary(own, below)
    exists = jnp.where(is_odd, me < n - 1, me > 0)
    short = sum((b["half"] > c).astype(jnp.int32) for c in UP[:-1])
    long = len(UP) + sum((b["half"] > c).astype(jnp.int32) for c in BOTH[:-1])
    which = lax.shift_right_logical(jnp.where(is_odd, me, me - 1) - 1, 1)
    splits = exists & (b["split"] > 0)
    is_long = b["split"] > UP[-1]
    case[0] = jnp.where(splits, 1 + which * len(UP + BOTH) + jnp.where(is_long, long, short), 0)
    case[1] = jnp.where(splits & is_long, 1 + which, 0)

    @pl.when(splits)
    def _():
        at = jnp.minimum(b["low"], UNITS)
        run([pltpu.make_async_copy(mine.at[jnp.where(is_odd, 1, 0), :, :, lanes(at, UNITS)], staged, sems.at[3])])
        lower, upper = b["low"] - at, b["low"] - at + b["half"]
        sent = jnp.where(is_odd, lower, upper)
        kept = jnp.where(is_odd, upper, lower)
        count = jnp.where(is_odd, b["split"] - b["half"], b["half"])

        def some(u, carry):
            alive = jnp.where(u < count, 1.0, 0.0).astype(rest.dtype)
            for i in range(2):
                extra[i, :, lanes(u)] = staged[i, :, lanes(jnp.minimum(sent + u, UNITS - 1))]
                rest[i, lanes(u), :] = (staged[i, :, lanes(jnp.minimum(kept + u, UNITS - 1))] * alive).T
            return carry

        lax.fori_loop(0, SPARE, some, 0)

    @pl.when(jnp.logical_not(is_odd))
    def _():
        rows = mine.shape[2]
        at = b["first"]
        loads = [
            pltpu.make_async_copy(mine.at[1, :, :, lanes(at, UNITS)], far_window, sems.at[0]),
            pltpu.make_async_copy(mine.at[0, :, :, lanes(at, UNITS)], near_window, sems.at[1]),
            pltpu.make_async_copy(mine.at[0, :, :, lanes(b["second"], UNITS)], second_window, sems.at[2]),
        ]
        for c in loads:
            c.start()
        left = [got[pl.ds(i * rows, rows), :] for i in range(2)]

        def against(ref, scale):
            return sum(times(left[i], ref[i] * scale) for i in range(2))

        loads[0].wait()
        value = against(far_window, counted(at, at, at + UNITS * b["m3"]))
        back[...] = value
        steps[...], whole, power = coded(value)
        lives[0:1, :] = jnp.zeros((1, rows), lives.dtype) + b["m1"].astype(lives.dtype)
        lives[1:2, :] = whole
        lives[2:3, :] = power
        loads[1].wait()
        near[...] = against(near_window, counted(at, b["s2"], b["s2"] + UNITS * b["m2"]))
        loads[2].wait()
        far_lives = b["m1"] > 0
        counts = counted(
            b["second"],
            jnp.where(far_lives, b["second"], b["low"]),
            jnp.where(far_lives, b["second"] + UNITS, b["low"] + b["rest"]),
        )
        for i in range(2):
            second[i] = (second_window[i] * counts).T


def rest_kernel(got, rest, out):
    width = got.shape[2]
    out[...] = sum(jnp.dot(got[i], rest[i, :width, :], preferred_element_type=jnp.float32) for i in range(2))


def coded(value):
    top = jnp.maximum(jnp.max(jnp.abs(value), axis=0, keepdims=True), 1e-30)
    power = jnp.ceil(jnp.log2(top)) - 14.0
    unit = jnp.exp2(power)
    whole = jnp.clip(jnp.ceil(top / unit), 1.0, STEPS)
    steps = value * (STEPS / (whole * unit)) + ROUND
    return (steps - ROUND).astype(jnp.int32).astype(jnp.int16), whole, power


def decoded(steps, whole, power):
    return steps * (whole * jnp.exp2(power) * (1.0 / STEPS))


def second_products_kernel(got, second, steps, near, more, lives, results, part, sent):
    _, is_odd = position()

    @pl.when(is_odd)
    def _():
        part[...] = more[...].T

    @pl.when(jnp.logical_not(is_odd))
    def _():
        rows = steps.shape[0]
        sent[pl.ds(2 * rows, rows), :] = steps[...]
        lived, whole, power = (lives[k : k + 1, :] for k in range(3))
        row = lax.broadcasted_iota(jnp.int32, (NOTE, rows), 0)
        scales = jnp.where(row == 4, whole, jnp.where(row == 5, power, 0.0))
        value = sum(jnp.dot(got[i], second[i], preferred_element_type=jnp.float32) for i in range(2))
        for k, block in enumerate((value * lived, near[...] + more[...] + value * (1.0 - lived))):
            (results, part)[k][...] = block
            sent[pl.ds(k * rows, rows), :], whole, power = coded(block)
            scales = jnp.where(row == 2 * k, whole, jnp.where(row == 2 * k + 1, power, scales))
        sent[pl.ds(3 * rows, NOTE), :] = scales.astype(jnp.int32).astype(jnp.int16)


def mirror_kernel(case, back, results, part, kmirror_in, kmirror, out, sems):
    _, is_odd = position()

    @pl.when(jnp.logical_not(is_odd))
    def _():
        out[0] = back[...].T
        out[1] = results[...].T
        targets = [kmirror.at[1, 1], kmirror.at[0, 1]]
        run([pltpu.make_async_copy(out.at[j], ref, sems.at[j]) for j, ref in enumerate(targets)])

        @pl.when(case[1] == 0)
        def _():
            out[2] = part[...].T
            run([pltpu.make_async_copy(out.at[2], kmirror.at[0, 0], sems.at[2])])


def last_kernel(case, got, part, other, kband_in, kmirror_in, kband, kmirror, out, mine, theirs, sems):
    _, is_odd = position()
    due = case[1] > 0

    loads = [pltpu.make_async_copy(part, mine, sems.at[3]), pltpu.make_async_copy(other, theirs, sems.at[4])]

    @pl.when(due)
    def _():
        for c in loads:
            c.start()

    @pl.when(is_odd)
    def _():
        rows = out.shape[1]
        scales = got[pl.ds(3 * rows, NOTE), :].astype(jnp.int32).astype(jnp.float32)
        copies = [
            pltpu.make_async_copy(out.at[k], kband.at[index], sems.at[k])
            for k, index in enumerate(((0, 2), (1, 1), (1, 2)))
        ]
        for k in (0, 2, 1):
            steps = got[pl.ds(k * rows, rows), :].astype(jnp.int32).astype(jnp.float32)
            out[k] = decoded(steps, scales[2 * k : 2 * k + 1], scales[2 * k + 1 : 2 * k + 2])
            if k == 1:

                @pl.when(due)
                def _():
                    for c in loads:
                        c.wait()
                    out[1] = mine[...] + theirs[...]

            copies[k].start()
        for c in copies:
            c.wait()

    @pl.when(jnp.logical_not(is_odd) & due)
    def _():
        for c in loads:
            c.wait()
        out[0] = (mine[...] + theirs[...]).T
        run([pltpu.make_async_copy(out.at[0], kmirror.at[0, 0], sems.at[0])])


def call(kernel, outs, ins, out_specs, scratch, flops=0, moved=0, aliases=None, vmem=40):
    inner = kernel.func if isinstance(kernel, functools.partial) else kernel
    return pl.pallas_call(
        kernel,
        out_shape=outs,
        in_specs=ins,
        out_specs=out_specs,
        scratch_shapes=scratch,
        input_output_aliases=aliases or {},
        compiler_params=pltpu.CompilerParams(vmem_limit_bytes=vmem * 2**20),
        cost_estimate=pl.CostEstimate(flops=flops, bytes_accessed=moved, transcendentals=0),
        name=inner.__name__,
    )


def per_device(bfac, pair_mask, dom_start):
    n = lax.axis_size("wide")
    _, rows, orbitals, fitting = bfac.shape
    upward = [(i, i + 1) for i in range(1, n - 1, 2)]
    downward = [(j, i) for i, j in upward]
    fast = [p for i in range(0, n, 2) for p in ((i, i + 1), (i + 1, i))]
    f32, bf16 = jnp.float32, bfac.dtype
    shape = jax.ShapeDtypeStruct
    dma = pltpu.SemaphoreType.DMA
    square = shape((rows, rows), f32)
    window = shape((orbitals, rows, DOM), bf16)
    raw_block = pltpu.VMEM((rows, orbitals, fitting), bf16)

    whole = (orbitals * rows + NOTE, DOM)
    parts = 4
    first = call(
        first_kernel,
        shape(whole, bf16),
        [SMEM, SMEM, HBM],
        HBM,
        [raw_block, pltpu.VMEM(whole, bf16), dma((parts,)), dma((parts * orbitals + 1,))],
        vmem=60,
    )(pair_mask, dom_start, bfac)
    first_got = lax.ppermute(first, "wide", upward)

    second, own, zero = call(
        second_kernel,
        (window, shape((8, DSTEP), jnp.int32), shape((1,), jnp.int32)),
        [SMEM, SMEM, HBM],
        (VMEM, VMEM, SMEM),
        [raw_block, dma((8,))],
        vmem=57,
    )(pair_mask, dom_start, lax.optimization_barrier((bfac, first))[0])
    second_got = lax.ppermute(second, "wide", upward)

    band = shape((2, 3, rows, rows), f32)
    mirror = shape((2, 2, rows, rows), f32)
    both = shape((2, orbitals, rows, fitting), bf16)
    spare = shape((orbitals, rows, SPARE * DSTEP), bf16)
    blocks = pltpu.VMEM((2, orbitals, rows, fitting), bf16)
    raw_blocks = pltpu.VMEM((2, rows, orbitals, fitting), bf16)

    def inner(own, bfac):
        below = lax.ppermute(own, "wide", [(i, i + 1) for i in range(0, n, 2)])
        other = lax.ppermute(bfac, "wide", fast)
        kband, kmirror, mine = call(
            own_kernel,
            (band, mirror, both),
            [SMEM, HBM],
            (HBM, HBM, HBM),
            [blocks, raw_blocks, pltpu.VMEM((4, rows, rows), f32), dma((8,))],
            2**31,
            2**25,
            vmem=40,
        )(own, bfac)
        kband, kmirror = call(
            fast_kernel,
            (band, mirror),
            [SMEM, SMEM, HBM, HBM, HBM, HBM],
            (HBM, HBM),
            [blocks, blocks, raw_blocks, pltpu.VMEM((3, rows, rows), f32), dma((6,))],
            2**31,
            2**25,
            {4: 0, 5: 1},
            vmem=32,
        )(own, below, mine, other, kband, kmirror)
        return kband, kmirror, mine

    def unused(own, bfac):
        return tuple(jnp.zeros(o.shape, o.dtype) for o in (band, mirror, both))

    own, bfac, _ = lax.optimization_barrier((own, bfac, second))
    kband, kmirror, mine = lax.cond(zero[0] == 0, inner, unused, own, bfac)

    below = first_got[orbitals * rows : orbitals * rows + 8, :DSTEP].astype(jnp.int32)
    staged = pltpu.VMEM((orbitals, rows, DOM), bf16)
    back, steps, near, second_window, extra, rest_window, lives, case = call(
        functools.partial(first_products_kernel, n),
        (
            square,
            shape((rows, rows), jnp.int16),
            square,
            shape((orbitals, DOM, rows), bf16),
            spare,
            shape((orbitals, SPARE * DSTEP, rows), bf16),
            shape((8, rows), f32),
            shape((2,), jnp.int32),
        ),
        [SMEM, SMEM, VMEM, HBM],
        (VMEM, VMEM, VMEM, VMEM, VMEM, VMEM, VMEM, SMEM),
        [staged, staged, staged, staged, dma((4,))],
        2**31,
        2**22,
        vmem=16,
    )(own, below, first_got, mine)

    def nothing(*_):
        return jnp.zeros((rows, rows), f32)

    def pair_of(lower):
        return [(lower, lower + 1), (lower + 1, lower)]

    def rest(lower, count, pairs):
        def branch(extra, rest_window):
            got = lax.ppermute(extra[:, :, : count * DSTEP], "wide", pairs)
            return call(rest_kernel, square, [VMEM, VMEM], VMEM, [], 2**26 * count, 2**19 * count, vmem=8)(
                got, rest_window
            )

        return branch

    def parts_of(lower):
        return lambda part: lax.ppermute(part, "wide", pair_of(lower))

    lowers = range(1, n - 1, 2)
    branches = [nothing]
    for i in lowers:
        branches += [rest(i, c, [(i, i + 1)]) for c in UP] + [rest(i, c, pair_of(i)) for c in BOTH]
    more = lax.switch(case[0], branches, extra, rest_window)

    results, part, sent = call(
        second_products_kernel,
        (square, square, shape((3 * rows + NOTE, rows), jnp.int16)),
        [VMEM] * 6,
        (VMEM, VMEM, VMEM),
        [],
        2**30,
        2**22,
        vmem=12,
    )(second_got, second_window, steps, near, more, lives)
    sent_got = lax.ppermute(sent, "wide", downward)
    kmirror = call(
        mirror_kernel,
        mirror,
        [SMEM, VMEM, VMEM, VMEM, HBM],
        HBM,
        [pltpu.VMEM((3, rows, rows), f32), dma((3,))],
        0,
        2**20,
        {4: 0},
        vmem=8,
    )(case, back, results, part, kmirror)
    part, kmirror = lax.optimization_barrier((part, kmirror))
    other_part = lax.switch(case[1], [nothing] + [parts_of(i) for i in lowers], part)
    return call(
        last_kernel,
        (band, mirror),
        [SMEM, VMEM, HBM, HBM, HBM, HBM],
        (HBM, HBM),
        [
            pltpu.VMEM((3, rows, rows), f32),
            pltpu.VMEM((rows, rows), f32),
            pltpu.VMEM((rows, rows), f32),
            dma((5,)),
        ],
        0,
        2**20,
        {4: 0, 5: 1},
        vmem=8,
    )(case, sent_got, part, other_part, kband, kmirror)


def solution(mesh):
    placed = (P("wide", None, "groups", None), P("wide", None), P("wide", None))
    return jax.shard_map(
        per_device,
        mesh=mesh,
        in_specs=placed,
        out_specs=(
            P(("groups", "wide"), None, None, None),
            P(("groups", "wide"), None, None, None),
        ),
        check_vma=False,
    )
```
